32 devices in a mesh: dp: 8 (over z, x), fsdp: 4 (over y, core).
Axes of the slice: x: 2, y: 2, z: 4, core: 2. Of those that a mesh axis runs over, the one named last changes fastest.
Arguments:
- token_ids: int32 [2, 128, 128], P(None, ('dp', 'fsdp')), may hold values from 0 to 32127
- pad_mask: int32 [2, 128, 128], P(None, ('dp', 'fsdp')), may hold values from 0 to 1, as said below
- hard_negative: int32 [128], P(('dp', 'fsdp')), may hold values from 0 to 127
- table: float32 [32128, 768], P('dp'), may hold values from -6 to 6
- table_first: float32 [32128, 768], P('dp'), may hold values from -1.5258789e-05 to 1.5258789e-05
- table_second: float32 [32128, 768], P('dp'), may hold values from 7.8065327e-13 to 3.122613e-12
- attn_in: float32 [768, 2304], P(('dp', 'fsdp')), may hold values from -0.21875 to 0.21875
- attn_in_first: float32 [768, 2304], P(('dp', 'fsdp')), may hold values from -3.0517578e-05 to 3.0517578e-05
- attn_in_second: float32 [768, 2304], P(('dp', 'fsdp')), may hold values from 3.122613e-12 to 1.2490452e-11
- attn_out: float32 [768, 768], P(('dp', 'fsdp')), may hold values from -0.4375 to 0.4375
- attn_out_first: float32 [768, 768], P(('dp', 'fsdp')), may hold values from -3.0517578e-05 to 3.0517578e-05
- attn_out_second: float32 [768, 768], P(('dp', 'fsdp')), may hold values from 3.122613e-12 to 1.2490452e-11
- ffn_in: float32 [768, 3072], P(('dp', 'fsdp')), may hold values from -0.21875 to 0.21875
- ffn_in_first: float32 [768, 3072], P(('dp', 'fsdp')), may hold values from -3.0517578e-05 to 3.0517578e-05
- ffn_in_second: float32 [768, 3072], P(('dp', 'fsdp')), may hold values from 3.122613e-12 to 1.2490452e-11
- ffn_out: float32 [3072, 768], P(('dp', 'fsdp')), may hold values from -0.109375 to 0.109375
- ffn_out_first: float32 [3072, 768], P(('dp', 'fsdp')), may hold values from -3.0517578e-05 to 3.0517578e-05
- ffn_out_second: float32 [3072, 768], P(('dp', 'fsdp')), may hold values from 3.122613e-12 to 1.2490452e-11
- proj_head: float32 [768, 768], P(('dp', 'fsdp')), may hold values from -0.21875 to 0.21875
- proj_head_first: float32 [768, 768], P(('dp', 'fsdp')), may hold values from -3.0517578e-05 to 3.0517578e-05
- proj_head_second: float32 [768, 768], P(('dp', 'fsdp')), may hold values from 3.122613e-12 to 1.2490452e-11
- small_params: float32 [2689], replicated, may hold values from -1 to 4, as said below
- small_first: float32 [2689], replicated, may hold values from -4.68417e-05 to 4.68417e-05
- small_second: float32 [2689], replicated, may hold values from 1.23667846e-13 to 1.9984724e-10
Outputs:
- loss_sum: float32 [], replicated
- grad_norm: float32 [], replicated
- next_table_first: float32 [32128, 768], P('dp')
- next_table_second: float32 [32128, 768], P('dp')
- next_table: float32 [32128, 768], P('dp')
- next_attn_in_first: float32 [768, 2304], P(('dp', 'fsdp'))
- next_attn_in_second: float32 [768, 2304], P(('dp', 'fsdp'))
- next_attn_in: float32 [768, 2304], P(('dp', 'fsdp'))
- next_attn_out_first: float32 [768, 768], P(('dp', 'fsdp'))
- next_attn_out_second: float32 [768, 768], P(('dp', 'fsdp'))
- next_attn_out: float32 [768, 768], P(('dp', 'fsdp'))
- next_ffn_in_first: float32 [768, 3072], P(('dp', 'fsdp'))
- next_ffn_in_second: float32 [768, 3072], P(('dp', 'fsdp'))
- next_ffn_in: float32 [768, 3072], P(('dp', 'fsdp'))
- next_ffn_out_first: float32 [3072, 768], P(('dp', 'fsdp'))
- next_ffn_out_second: float32 [3072, 768], P(('dp', 'fsdp'))
- next_ffn_out: float32 [3072, 768], P(('dp', 'fsdp'))
- next_proj_head_first: float32 [768, 768], P(('dp', 'fsdp'))
- next_proj_head_second: float32 [768, 768], P(('dp', 'fsdp'))
- next_proj_head: float32 [768, 768], P(('dp', 'fsdp'))
- next_small_first: float32 [2689], replicated
- next_small_second: float32 [2689], replicated
- next_small: float32 [2689], replicated
The draws below stay inside these ranges and needn't reach their ends.
Inputs may be any that keep to these rules, and one draw needn't show every extreme that they name: `pad_mask`: in each sentence the real tokens are a prefix of one or more; both sentences of the last pair are full (128 real tokens). `small_params`: gains lie in 0.5 to 2.7, biases in -1 to 1, the log scale in 3.5 to 4.
All inputs are finite; a program needn't handle non-finite values.
Results may differ from the reference program's by a relative error of at most 0.014.
The reference program's roundings to bfloat16 on the way count: a program that leaves them out, or rounds other values in their place, can miss the bound.
Values may be sent and summed in bfloat16 or wider, within the bound.
A program may use at most 256 MiB of HBM per device.

```python
import math
from functools import reduce
import jax
import jax.numpy as jnp
import numpy as np
from jax import lax

D = 768
HEADS = 12
HD = 64
FF = 3072
V = 32128
NB = 32
PD = 768
L = 128
STEP = 10
PAIRS = 128
PARAMS = 32344705


def draw_pad_mask(key, part):
    key = jax.random.fold_in(key, 11)
    key_shift, key_length = jax.random.split(key)
    pair_index = jnp.arange(PAIRS, dtype=jnp.int32)
    ceiling = L * (PAIRS + 2 * pair_index) // (3 * PAIRS)
    shifts = jax.random.randint(key_shift, (2, PAIRS), 0, 3)
    limits = jnp.maximum(jnp.right_shift(ceiling[None, :], shifts), 1)
    lengths = 1 + jax.random.randint(key_length, (2, PAIRS), 0, limits)
    lengths = jnp.minimum(lengths, L)
    lengths = lengths.at[:, PAIRS - 1].set(L)
    return (jnp.arange(L, dtype=jnp.int32)[None, None, :] < lengths[:, :, None]).astype(jnp.int32)


def draw_small_params(key, part):
    key = jax.random.fold_in(key, 7)
    key_gain, key_bias, key_scale = jax.random.split(key, 3)
    ramp = 0.7 + 1.4 * jnp.arange(D, dtype=jnp.float32) / D
    gain_rows = ramp[None, :] * jax.random.uniform(key_gain, (3, D), jnp.float32, 0.85, 1.18)
    bias_rows = jax.random.uniform(key_bias, (NB * HEADS,), jnp.float32, -1.0, 1.0)
    log_scale = jax.random.uniform(key_scale, (1,), jnp.float32, 3.5, 4.0)
    return jnp.concatenate([gain_rows.reshape(-1), bias_rows, log_scale])


def segment_row(gain_value, bias_value):
    return jnp.concatenate([jnp.full((3 * D,), gain_value, jnp.float32), jnp.full((NB * HEADS,), bias_value, jnp.float32), jnp.full((1,), gain_value, jnp.float32)])


def draw_small_first(key, part):
    key = jax.random.fold_in(key, 13)
    scale_row = segment_row(0.0444, 0.0044) * PARAMS ** (-0.5)
    values = jax.random.truncated_normal(key, -6.0, 6.0, (3 * D + NB * HEADS + 1,), jnp.float32)
    return values * scale_row


def draw_small_second(key, part):
    key = jax.random.fold_in(key, 17)
    floor_row = segment_row(0.001616, 4e-06) / PARAMS
    spread = jax.random.uniform(key, (3 * D + NB * HEADS + 1,), jnp.float32, 0.0, math.log(4.0))
    return floor_row * jnp.exp(spread)


def place_ends(values, rng, low, high):
    dims = values.shape
    place = [jax.random.randint(jax.random.fold_in(rng, axis), (), 0, dims[axis]) for axis in range(len(dims))]
    values = values.at[tuple(place)].set(low)
    longest = dims.index(max(dims))
    place[longest] = (place[longest] + 1) % dims[longest]
    return values.at[tuple(place)].set(high)


def level_of(key, dims, cuts, smallest, top_value):
    factor_of = 1.0
    for axis_at, parts in cuts:
        draws = jax.random.uniform(jax.random.fold_in(jax.random.fold_in(key, 6), axis_at), (parts,), jnp.float32, smallest / len(cuts), top_value / len(cuts))
        factor_of = factor_of * jnp.repeat(jnp.exp(draws), dims[axis_at] // parts).reshape((-1,) + (1,) * (len(dims) - 1 - axis_at))
    return factor_of


def rank_bounds(number_of, lean):
    weights = [(1 << 20) // math.isqrt(standing ** lean) + 1 for standing in range(1, number_of + 1)]
    scale = 1 + sum(weights) // (1 << 30)
    return np.cumsum(np.array([max(1, weight // scale) for weight in weights]))


def ranked_ids(stream_key, extent, number_of, lean):
    grid = rank_bounds(number_of, lean)
    lot = jax.random.randint(jax.random.fold_in(stream_key, 1), extent, 0, int(grid[number_of - 1]))
    standing = jnp.searchsorted(jnp.asarray(grid, jnp.int32), lot, side="right")
    return jax.random.permutation(jax.random.fold_in(stream_key, 2), number_of)[standing].astype(jnp.int32)


def centred(rng, extent, scale, limit, pieces=(), held_as=jnp.bfloat16):
    array = jax.random.normal(rng, extent, jnp.float32) * scale
    if len(pieces) > 0:
        array = level_of(rng, extent, pieces, -0.22, 0.18) * array
    return jnp.clip(array, min=-limit, max=limit).astype(held_as)


def setup_inputs(seed: int = 0) -> dict:
    keys = jax.random.split(jax.random.key(seed), 25)
    return {
        "token_ids": place_ends(ranked_ids(keys[0], (2, PAIRS, L), V, 2), jax.random.fold_in(keys[0], 3), 0, V - 1).astype(jnp.int32),
        "pad_mask": draw_pad_mask(jax.random.fold_in(keys[24], 71), 0),
        "hard_negative": place_ends(jax.random.randint(keys[2], (PAIRS,), 0, PAIRS), jax.random.fold_in(keys[2], 1), 0, PAIRS - 1).astype(jnp.int32),
        "table": centred(keys[3], (V, D), 1.0, 6.0, ((0, 8),), jnp.float32),
        "table_first": centred(keys[4], (V, D), (0.00555 * PARAMS ** -0.5), 1.52587890625e-05, ((0, 8),), jnp.float32),
        "table_second": jnp.clip(jnp.exp(math.log(3.1226130622202808e-12) - 1.3862944 * jax.random.uniform(keys[5], (V, D), jnp.float32) ** level_of(keys[5], (V, D), ((0, 8),), -0.2, 0.2)), 7.806532655550702e-13, 3.1226130622202808e-12),
        "attn_in": centred(keys[6], (D, 3 * D), D ** -0.5, 0.21875, ((0, 32),), jnp.float32),
        "attn_in_first": centred(keys[7], (D, 3 * D), (0.0111 * PARAMS ** -0.5), 3.0517578125e-05, ((0, 32),), jnp.float32),
        "attn_in_second": jnp.clip(jnp.exp(math.log(1.2490452248881123e-11) - 1.3862944 * jax.random.uniform(keys[8], (D, 3 * D), jnp.float32) ** level_of(keys[8], (D, 3 * D), ((0, 32),), -0.2, 0.2)), 3.1226130622202808e-12, 1.2490452248881123e-11),
        "attn_out": centred(keys[9], (D, D), (D // 4) ** -0.5, 0.4375, ((0, 32),), jnp.float32),
        "attn_out_first": centred(keys[10], (D, D), (0.0111 * PARAMS ** -0.5), 3.0517578125e-05, ((0, 32),), jnp.float32),
        "attn_out_second": jnp.clip(jnp.exp(math.log(1.2490452248881123e-11) - 1.3862944 * jax.random.uniform(keys[11], (D, D), jnp.float32) ** level_of(keys[11], (D, D), ((0, 32),), -0.2, 0.2)), 3.1226130622202808e-12, 1.2490452248881123e-11),
        "ffn_in": centred(keys[12], (D, FF), D ** -0.5, 0.21875, ((0, 32),), jnp.float32),
        "ffn_in_first": centred(keys[13], (D, FF), (0.0111 * PARAMS ** -0.5), 3.0517578125e-05, ((0, 32),), jnp.float32),
        "ffn_in_second": jnp.clip(jnp.exp(math.log(1.2490452248881123e-11) - 1.3862944 * jax.random.uniform(keys[14], (D, FF), jnp.float32) ** level_of(keys[14], (D, FF), ((0, 32),), -0.2, 0.2)), 3.1226130622202808e-12, 1.2490452248881123e-11),
        "ffn_out": centred(keys[15], (FF, D), FF ** -0.5, 0.109375, ((0, 32),), jnp.float32),
        "ffn_out_first": centred(keys[16], (FF, D), (0.0111 * PARAMS ** -0.5), 3.0517578125e-05, ((0, 32),), jnp.float32),
        "ffn_out_second": jnp.clip(jnp.exp(math.log(1.2490452248881123e-11) - 1.3862944 * jax.random.uniform(keys[17], (FF, D), jnp.float32) ** level_of(keys[17], (FF, D), ((0, 32),), -0.2, 0.2)), 3.1226130622202808e-12, 1.2490452248881123e-11),
        "proj_head": centred(keys[18], (D, PD), D ** -0.5, 0.21875, ((0, 32),), jnp.float32),
        "proj_head_first": centred(keys[19], (D, PD), (0.0111 * PARAMS ** -0.5), 3.0517578125e-05, ((0, 32),), jnp.float32),
        "proj_head_second": jnp.clip(jnp.exp(math.log(1.2490452248881123e-11) - 1.3862944 * jax.random.uniform(keys[20], (D, PD), jnp.float32) ** level_of(keys[20], (D, PD), ((0, 32),), -0.2, 0.2)), 3.1226130622202808e-12, 1.2490452248881123e-11),
        "small_params": draw_small_params(jax.random.fold_in(keys[24], 71), 0),
        "small_first": draw_small_first(jax.random.fold_in(keys[24], 71), 0),
        "small_second": draw_small_second(jax.random.fold_in(keys[24], 71), 0),
    }


EPS = 1e-06
SCALE = 0.125
MARGIN = 0.2
CLIP = 0.1
BETA_ONE = 0.9
BETA_TWO = 0.99
ADAM_EPS = 1e-08
RATES = (3.0, 0.1, 0.2, 0.1, 0.05, 0.1, 1.0)
DECAYS = (0.001, 0.001, 0.001, 0.001, 0.001, 0.001, 0.0)
group_size = 32
HIGH = lax.Precision.HIGHEST

@jax.custom_vjp
def low(v):
    return lax.optimization_barrier(v.astype(jnp.bfloat16)).astype(jnp.float32)

@jax.custom_vjp
def low_back(v):
    return v

def low_keep(v):
    return (low(v), None)

def low_pass(kept, grad):
    return (grad,)

def back_keep(v):
    return (v, None)

def back_low(kept, grad):
    return (low(grad),)
low.defvjp(low_keep, low_pass)
low_back.defvjp(back_keep, back_low)

def bucket_table(length, count):
    position = np.arange(length)
    relative = position[None, :] - position[:, None]
    half = count // 2
    base_part = (relative > 0).astype(np.int64) * half
    distance = np.abs(relative)
    exact = half // 2
    safe_dist = np.maximum(distance, 1)
    large = exact + (np.log(safe_dist / exact) / np.log(length / exact) * (half - exact)).astype(np.int64)
    large = np.minimum(large, half - 1)
    return base_part + np.where(distance < exact, distance, large)

def rms_norm(inputs, gain_row):
    return inputs * lax.rsqrt(lax.optimization_barrier(jnp.mean(inputs * inputs, -1, keepdims=True)) + EPS) * gain_row

def encode(seq_pair, weights, gain_rows, bias_full):
    group_ids, group_mask = seq_pair
    table, attn_in, attn_out, ffn_in, ffn_out, proj_head = weights
    group_count = group_ids.shape[0]
    token_rows = low_back(table[group_ids])
    normed = low(rms_norm(token_rows, gain_rows[0]))
    mixed_proj = low(low_back(jnp.einsum('gld,de->gle', normed, attn_in, precision=HIGH)))
    mixed_proj = mixed_proj.reshape(group_count, L, 3, HEADS, HD)
    keep_add = jnp.where(group_mask > 0, 0.0, -1000000000.0)
    scores = jnp.einsum('gqhd,gkhd->ghqk', mixed_proj[:, :, 0], mixed_proj[:, :, 1], precision=HIGH) * SCALE
    scores = low_back(scores + bias_full[None] + keep_add[:, None, None, :])
    prob_low = low(jax.nn.softmax(scores, axis=-1))
    attended = low(low_back(jnp.einsum('ghqk,gkhd->gqhd', prob_low, mixed_proj[:, :, 2], precision=HIGH)))
    attended = attended.reshape(group_count, L, D)
    after_attn = token_rows + low_back(jnp.einsum('gld,de->gle', attended, attn_out, precision=HIGH))
    normed_two = low(rms_norm(after_attn, gain_rows[1]))
    pre_act = low_back(jnp.einsum('gld,df->glf', normed_two, ffn_in, precision=HIGH))
    hidden = low(jax.nn.gelu(pre_act))
    final_rows = after_attn + low_back(jnp.einsum('glf,fd->gld', hidden, ffn_out, precision=HIGH))
    mask_weight = group_mask.astype(jnp.float32)[:, :, None]
    pooled = lax.optimization_barrier(jnp.sum(rms_norm(final_rows, gain_rows[2]) * mask_weight, 1)) / lax.optimization_barrier(jnp.sum(mask_weight, 1))
    projected = low_back(jnp.dot(low(pooled), proj_head, precision=HIGH))
    return projected * lax.rsqrt(lax.optimization_barrier(jnp.sum(projected * projected, -1, keepdims=True)) + EPS)

def total_loss(masters, token_ids, pad_mask, hard_negative):
    weights = tuple((low(matrix) for matrix in masters[:6]))
    small = masters[6]
    gain_rows = small[:3 * D].reshape(3, D)
    bias_table = small[3 * D:3 * D + NB * HEADS].reshape(NB, HEADS)
    log_scale = small[3 * D + NB * HEADS]
    buckets = jnp.asarray(bucket_table(L, NB), jnp.int32)
    bias_full = jnp.transpose(bias_table[buckets], (2, 0, 1))
    ids_grouped = token_ids.reshape(-1, group_size, L)
    mask_grouped = pad_mask.reshape(-1, group_size, L)
    encoder = jax.checkpoint(lambda seq_pair: encode(seq_pair, weights, gain_rows, bias_full))
    unit_rows = lax.map(encoder, (ids_grouped, mask_grouped)).reshape(2, PAIRS, PD)
    queries = low(low_back(unit_rows[0]))
    passages = low(low_back(unit_rows[1]))
    similar = low_back(jnp.dot(queries, passages.T, precision=HIGH))
    columns = jnp.arange(PAIRS, dtype=jnp.int32)
    own_mask = (columns[:, None] == columns[None, :]).astype(jnp.float32)
    negative = (hard_negative[:, None] == columns[None, :]).astype(jnp.float32)
    logits = jnp.exp(log_scale) * similar - MARGIN * own_mask
    diagonal = lax.optimization_barrier(jnp.sum(logits * own_mask, 1))
    hardest = lax.optimization_barrier(jnp.sum(logits * negative, 1))
    return jnp.sum(jax.nn.logsumexp(logits, axis=1) - diagonal + jax.nn.softplus(hardest - diagonal))

def adam_update(param, first_moment, second_moment, gradient, factor, rate, decay):
    clipped = gradient * factor
    first_new = BETA_ONE * first_moment + (1.0 - BETA_ONE) * clipped
    second_new = BETA_TWO * second_moment + (1.0 - BETA_TWO) * clipped * clipped
    direction = first_new / (1.0 - BETA_ONE ** STEP) / (jnp.sqrt(second_new / (1.0 - BETA_TWO ** STEP)) + ADAM_EPS)
    return (first_new, second_new, param - rate * (direction + decay * param))

def reference(token_ids, pad_mask, hard_negative, table, table_first, table_second, attn_in, attn_in_first, attn_in_second, attn_out, attn_out_first, attn_out_second, ffn_in, ffn_in_first, ffn_in_second, ffn_out, ffn_out_first, ffn_out_second, proj_head, proj_head_first, proj_head_second, small_params, small_first, small_second):
    masters = (table, attn_in, attn_out, ffn_in, ffn_out, proj_head, small_params)
    firsts = (table_first, attn_in_first, attn_out_first, ffn_in_first, ffn_out_first, proj_head_first, small_first)
    seconds = (table_second, attn_in_second, attn_out_second, ffn_in_second, ffn_out_second, proj_head_second, small_second)
    loss_value, pull_back = jax.vjp(lambda *params: total_loss(params, token_ids, pad_mask, hard_negative), *masters)
    gradients = pull_back(jnp.ones_like(loss_value))
    squares = [jnp.sum(grad * grad) for grad in gradients]
    norm_value = jnp.sqrt(reduce(lambda left_side, right_side: left_side + right_side, squares))
    factor = jnp.minimum(1.0, CLIP / (norm_value + 1e-06))
    updated = [adam_update(masters[kind_index], firsts[kind_index], seconds[kind_index], gradients[kind_index], factor, RATES[kind_index], DECAYS[kind_index]) for kind_index in range(7)]
    table_parts, inner_parts, outer_parts, up_parts, down_parts, head_parts, small_parts = updated
    return (loss_value, norm_value, table_parts[0], table_parts[1], table_parts[2], inner_parts[0], inner_parts[1], inner_parts[2], outer_parts[0], outer_parts[1], outer_parts[2], up_parts[0], up_parts[1], up_parts[2], down_parts[0], down_parts[1], down_parts[2], head_parts[0], head_parts[1], head_parts[2], small_parts[0], small_parts[1], small_parts[2])
```

```python
import functools

import jax
import jax.numpy as jnp
import numpy as np
from jax import lax
from jax.experimental import pallas as pl
from jax.experimental.pallas import tpu as pltpu
from jax.sharding import PartitionSpec as P

D = 768
HEADS = 12
HD = 64
NB = 32
L = 128
STEP = 10


EPS = 1e-06
SCALE = 0.125
MARGIN = 0.2
CLIP = 0.1
BETA_ONE = 0.9
BETA_TWO = 0.99
ADAM_EPS = 1e-08
RATES = (3.0, 0.1, 0.2, 0.1, 0.05, 0.1, 1.0)
DECAYS = (0.001, 0.001, 0.001, 0.001, 0.001, 0.001, 0.0)
HIGH = lax.Precision.HIGHEST
MESH = pl.DeviceIdType.MESH
CAP = 128


def bucket_table(length, count):
    position = np.arange(length)
    relative = position[None, :] - position[:, None]
    half = count // 2
    base_part = (relative > 0).astype(np.int64) * half
    distance = np.abs(relative)
    exact = half // 2
    safe_dist = np.maximum(distance, 1)
    large = exact + (np.log(safe_dist / exact) / np.log(length / exact) * (half - exact)).astype(
        np.int64
    )
    large = np.minimum(large, half - 1)
    return base_part + np.where(distance < exact, distance, large)


def matmul(left_side, right_side):
    return jnp.dot(left_side, right_side, preferred_element_type=jnp.float32)


def matmul_tn(left_side, right_side):
    return lax.dot_general(
        left_side, right_side, (((0,), (0,)), ((), ())), preferred_element_type=jnp.float32
    )


def matmul_nt(left_side, right_side):
    return lax.dot_general(
        left_side, right_side, (((1,), (1,)), ((), ())), preferred_element_type=jnp.float32
    )


def normalize(inputs, gain_row):
    factor = lax.rsqrt(jnp.mean(inputs * inputs, -1, keepdims=True) + EPS)
    return (inputs * factor * gain_row, factor)


def normalize_back(grad_out, inputs, factor, gain_row):
    scaled = grad_out * gain_row
    grad_gain = jnp.sum(grad_out * inputs * factor, 0)
    grad_in = factor * (
        scaled - inputs * factor * factor * jnp.mean(scaled * inputs, -1, keepdims=True)
    )
    return (grad_in, grad_gain)


def attention_scores(mixed_proj, mask_rows, bias_full):
    keep_add = jnp.where(mask_rows > 0, 0.0, -1000000000.0).astype(jnp.float32)
    scores = jnp.einsum(
        "bqhd,bkhd->bhqk",
        mixed_proj[:, :, 0],
        mixed_proj[:, :, 1],
        preferred_element_type=jnp.float32,
    )
    return scores * SCALE + bias_full[None] + keep_add[:, None, None, :]


def layer_forward(token_rows, mask_rows, weights, gain_rows, bias_full):
    attn_in, attn_out, ffn_in, ffn_out = weights
    seq_count, length = mask_rows.shape
    width = token_rows.shape[1]
    normed_one, factor_one = normalize(token_rows, gain_rows[0])
    act_one = normed_one.astype(jnp.bfloat16)
    mixed_proj = (
        matmul(act_one, attn_in).astype(jnp.bfloat16).reshape(seq_count, length, 3, HEADS, HD)
    )
    scores = attention_scores(mixed_proj, mask_rows, bias_full)
    row_max = jnp.max(scores, -1, keepdims=True)
    log_total = row_max + jnp.log(jnp.sum(jnp.exp(scores - row_max), -1, keepdims=True))
    prob_low = jnp.exp(scores - log_total).astype(jnp.bfloat16)
    attended = jnp.einsum(
        "bhqk,bkhd->bqhd", prob_low, mixed_proj[:, :, 2], preferred_element_type=jnp.float32
    )
    attended = attended.astype(jnp.bfloat16).reshape(-1, width)
    after_attn = token_rows + matmul(attended, attn_out)
    normed_two, factor_two = normalize(after_attn, gain_rows[1])
    act_two = normed_two.astype(jnp.bfloat16)
    pre_act = matmul(act_two, ffn_in)
    hidden = jax.nn.gelu(pre_act).astype(jnp.bfloat16)
    final_rows = after_attn + matmul(hidden, ffn_out)
    kept = (
        token_rows,
        factor_one,
        act_one,
        mixed_proj,
        log_total,
        attended,
        after_attn,
        factor_two,
        act_two,
        pre_act,
        hidden,
    )
    return (final_rows, kept)


def layer_backward(grad_final, kept, mask_rows, weights, gain_rows, bias_full):
    (
        token_rows,
        factor_one,
        act_one,
        mixed_proj,
        log_total,
        attended,
        after_attn,
        factor_two,
        act_two,
        pre_act,
        hidden,
    ) = kept
    attn_in, attn_out, ffn_in, ffn_out = weights
    seq_count, length = mask_rows.shape
    branch = grad_final.astype(jnp.bfloat16)
    grad_ffn_out = matmul_tn(hidden, branch)
    grad_hidden = matmul_nt(branch, ffn_out)
    _, gelu_pull = jax.vjp(jax.nn.gelu, pre_act)
    grad_pre = gelu_pull(grad_hidden)[0].astype(jnp.bfloat16)
    grad_ffn_in = matmul_tn(act_two, grad_pre)
    grad_act_two = matmul_nt(grad_pre, ffn_in)
    grad_mid, gain_two = normalize_back(grad_act_two, after_attn, factor_two, gain_rows[1])
    grad_after = grad_final + grad_mid
    branch = grad_after.astype(jnp.bfloat16)
    grad_attn_out = matmul_tn(attended, branch)
    grad_attended = (
        matmul_nt(branch, attn_out).astype(jnp.bfloat16).reshape(seq_count, length, HEADS, HD)
    )
    scores = attention_scores(mixed_proj, mask_rows, bias_full)
    prob_full = jnp.exp(scores - log_total)
    prob_low = prob_full.astype(jnp.bfloat16)
    queries = mixed_proj[:, :, 0]
    key_rows = mixed_proj[:, :, 1]
    grad_probs = jnp.einsum(
        "bqhd,bkhd->bhqk", grad_attended, mixed_proj[:, :, 2], preferred_element_type=jnp.float32
    )
    grad_values = jnp.einsum(
        "bhqk,bqhd->bkhd", prob_low, grad_attended, preferred_element_type=jnp.float32
    )
    grad_scores = prob_full * (grad_probs - jnp.sum(prob_full * grad_probs, -1, keepdims=True))
    grad_scores = grad_scores.astype(jnp.bfloat16)
    grad_bias = jnp.sum(grad_scores, 0, dtype=jnp.float32)
    grad_queries = (
        jnp.einsum("bhqk,bkhd->bqhd", grad_scores, key_rows, preferred_element_type=jnp.float32)
        * SCALE
    )
    grad_keys = (
        jnp.einsum("bhqk,bqhd->bkhd", grad_scores, queries, preferred_element_type=jnp.float32)
        * SCALE
    )
    grad_mixed = (
        jnp.stack([grad_queries, grad_keys, grad_values], 2)
        .astype(jnp.bfloat16)
        .reshape(seq_count * length, -1)
    )
    grad_attn_in = matmul_tn(act_one, grad_mixed)
    grad_act_one = matmul_nt(grad_mixed, attn_in)
    grad_low, gain_one = normalize_back(grad_act_one, token_rows, factor_one, gain_rows[0])
    grad_rows = grad_after + grad_low
    return (
        grad_rows,
        (grad_attn_in, grad_attn_out, grad_ffn_in, grad_ffn_out),
        gain_one,
        gain_two,
        grad_bias,
    )


def adam_update(param, first_moment, second_moment, gradient, factor, rate, decay):
    clipped = gradient * factor
    first_new = BETA_ONE * first_moment + (1.0 - BETA_ONE) * clipped
    second_new = BETA_TWO * second_moment + (1.0 - BETA_TWO) * clipped * clipped
    direction = (
        first_new
        / (1.0 - BETA_ONE**STEP)
        / (jnp.sqrt(second_new / (1.0 - BETA_TWO**STEP)) + ADAM_EPS)
    )
    return (first_new, second_new, param - rate * (direction + decay * param))


class Grid:
    def __init__(self):
        self.dp, self.fs = lax.axis_size("dp"), lax.axis_size("fsdp")
        self.total = self.dp * self.fs
        self.wide = self.fs // 2
        self.tall = self.dp // self.wide

    def here(self):
        d, f = lax.axis_index("dp"), lax.axis_index("fsdp")
        return d // self.wide, lax.rem(d, self.wide), f // 2, lax.rem(f, 2)

    def device(self, z, x, y, core):
        return (z * self.wide + x, y * 2 + core)

    def flat(self, z, x, y, core):
        return (z * self.wide + x) * self.fs + y * 2 + core

    def peer(self, index):
        return (index // self.fs, lax.rem(index, self.fs))


def greet(device, when=None):
    barrier = pltpu.get_barrier_semaphore()

    def signal():
        pl.semaphore_signal(barrier, inc=1, device_id=device, device_id_type=MESH)

    if when is None:
        signal()
    else:
        pl.when(when)(signal)


def meet(count):
    pl.semaphore_wait(pltpu.get_barrier_semaphore(), count)


def exchange_kernel(grid, spread, src, out, send_sem, recv_sem, own_sem):
    me = lax.axis_index("dp") * grid.fs + lax.axis_index("fsdp")
    own = pltpu.make_async_copy(src.at[me] if spread else src, out.at[me], own_sem)
    own.start()

    @pl.loop(1, grid.total)
    def _(step):
        greet(grid.peer(lax.rem(me + step, grid.total)))

    meet(count=grid.total - 1)

    def copy(peer, slot):
        return pltpu.make_async_remote_copy(
            src_ref=src.at[peer] if spread else src,
            dst_ref=out.at[slot],
            send_sem=send_sem.at[peer],
            recv_sem=recv_sem.at[slot],
            device_id=grid.peer(peer),
            device_id_type=MESH,
        )

    @pl.loop(1, grid.total)
    def _(step):
        copy(lax.rem(me + step, grid.total), me).start()

    own.wait()

    @pl.loop(1, grid.total)
    def _(step):
        peer = lax.rem(me + step, grid.total)
        copy(peer, peer).wait_recv()
        copy(peer, peer).wait_send()


def exchange(src, spread, number):
    grid = Grid()
    block = src.shape[1:] if spread else src.shape
    return pl.pallas_call(
        functools.partial(exchange_kernel, grid, spread),
        out_shape=jax.ShapeDtypeStruct((grid.total,) + block, src.dtype),
        in_specs=[pl.BlockSpec(memory_space=pltpu.VMEM)],
        out_specs=pl.BlockSpec(memory_space=pltpu.VMEM),
        scratch_shapes=[
            pltpu.SemaphoreType.DMA((grid.total,)),
            pltpu.SemaphoreType.DMA((grid.total,)),
            pltpu.SemaphoreType.DMA,
        ],
        compiler_params=pltpu.CompilerParams(collective_id=number, has_side_effects=True),
    )(src)


def gather_kernel(grid, count, *refs):
    srcs, rows, outs, got_rows = refs[:count], refs[count], refs[count + 1 : 2 * count + 1], refs[2 * count + 1]
    send_sem, recv_sem, own_sem, row_send, row_recv, row_own = refs[2 * count + 2 :]
    z, x, y, core = grid.here()
    tall = grid.tall
    d, f = lax.axis_index("dp"), lax.axis_index("fsdp")
    ux, uy = lax.rem(x + 1 - core, 2), lax.rem(y + core, 2)
    vx, vy = lax.rem(x + core, 2), lax.rem(y + 1 - core, 2)
    up, down = grid.device(z + 1, x, y, core), grid.device(z - 1, x, y, core)
    u_device, v_device = grid.device(z, ux, uy, core), grid.device(z, vx, vy, core)
    sibling = grid.device(z, x, y, 1 - core)
    has_up, has_down = z < tall - 1, z > 0
    me = grid.flat(z, x, y, core)
    local = [pltpu.make_async_copy(srcs[m], outs[m].at[me], own_sem.at[m]) for m in range(count)]
    local.append(pltpu.make_async_copy(rows.at[d], got_rows.at[d], row_own))
    for item in local:
        item.start()

    @pl.loop(1, grid.dp)
    def _(step):
        greet((lax.rem(d + step, grid.dp), f))

    greet(v_device)
    greet(sibling)
    greet(u_device)
    meet(count=grid.dp + 2)

    def row_copy(peer, slot):
        return pltpu.make_async_remote_copy(
            src_ref=rows.at[peer],
            dst_ref=got_rows.at[slot],
            send_sem=row_send.at[peer],
            recv_sem=row_recv.at[slot],
            device_id=(peer, f),
            device_id_type=MESH,
        )

    def copy(m, shard, device, way, own):
        return pltpu.make_async_remote_copy(
            src_ref=srcs[m] if own else outs[m].at[shard],
            dst_ref=outs[m].at[shard],
            send_sem=send_sem.at[way, m, shard],
            recv_sem=recv_sem.at[m, shard],
            device_id=device,
            device_id_type=MESH,
        )

    def send(shard, device, way, own=False):
        for m in range(count):
            copy(m, shard, device, way, own).start()

    def arrived(shard):
        for m in range(count):
            copy(m, shard, sibling, 4, False).wait_recv()

    def sent(shard, device, way):
        for m in range(count):
            copy(m, shard, device, way, False).wait_send()

    @pl.when(has_up)
    def _():
        send(me, up, 0, True)

    @pl.when(has_down)
    def _():
        send(me, down, 1, True)

    send(me, u_device, 2, True)
    send(me, v_device, 3, True)
    send(me, sibling, 4, True)

    @pl.loop(1, grid.dp)
    def _(step):
        row_copy(lax.rem(d + step, grid.dp), d).start()

    def pass_z(k):
        low, high = z - k, z + k

        @pl.when(low >= 0)
        def _():
            shard = grid.flat(low, x, y, core)
            arrived(shard)

            @pl.when(has_up)
            def _():
                send(shard, up, 0)

            send(shard, u_device, 2)
            send(shard, v_device, 3)
            send(shard, sibling, 4)

        @pl.when(high < tall)
        def _():
            shard = grid.flat(high, x, y, core)
            arrived(shard)

            @pl.when(has_down)
            def _():
                send(shard, down, 1)

            send(shard, u_device, 2)
            send(shard, v_device, 3)
            send(shard, sibling, 4)

    def both(k, action):
        pl.when(z - k >= 0)(lambda: action(z - k))
        if k:
            pl.when(z + k < tall)(lambda: action(z + k))

    def pass_u(level):
        shard = grid.flat(level, ux, uy, core)
        arrived(shard)
        send(shard, v_device, 3)
        send(shard, sibling, 4)

    def pass_v(level):
        shard = grid.flat(level, vx, vy, core)
        arrived(shard)
        send(shard, sibling, 4)

    def pass_far(level):
        shard = grid.flat(level, 1 - x, 1 - y, core)
        arrived(shard)
        send(shard, sibling, 4)

    for k in range(tall + 1):
        if 0 < k < tall:
            pass_z(k)
        if k < tall:
            both(k, pass_u)
            both(k, pass_v)
        if k:
            both(k - 1, pass_far)

    @pl.loop(1, grid.dp)
    def _(step):
        peer = lax.rem(d + step, grid.dp)
        row_copy(peer, peer).wait_recv()
        row_copy(peer, peer).wait_send()

    @pl.loop(0, tall)
    def _(level):
        for xx in range(2):
            for yy in range(2):
                arrived(grid.flat(level, xx, yy, 1 - core))
                sent(grid.flat(level, xx, yy, core), sibling, 4)
        shard, other = grid.flat(level, x, y, core), grid.flat(level, ux, uy, core)

        @pl.when((level <= z) & has_up)
        def _():
            sent(shard, up, 0)

        @pl.when((level >= z) & has_down)
        def _():
            sent(shard, down, 1)

        sent(shard, u_device, 2)
        sent(shard, v_device, 3)
        sent(other, v_device, 3)

    for item in local:
        item.wait()


def gather(srcs, rows, number):
    grid = Grid()
    count = len(srcs)
    anywhere = pl.BlockSpec(memory_space=pl.ANY)
    results = pl.pallas_call(
        functools.partial(gather_kernel, grid, count),
        out_shape=[jax.ShapeDtypeStruct((grid.total,) + src.shape, src.dtype) for src in srcs]
        + [jax.ShapeDtypeStruct(rows.shape, rows.dtype)],
        in_specs=[anywhere] * (count + 1),
        out_specs=[anywhere] * (count + 1),
        scratch_shapes=[
            pltpu.SemaphoreType.DMA((5, count, grid.total)),
            pltpu.SemaphoreType.DMA((count, grid.total)),
            pltpu.SemaphoreType.DMA((count,)),
            pltpu.SemaphoreType.DMA((grid.dp,)),
            pltpu.SemaphoreType.DMA((grid.dp,)),
            pltpu.SemaphoreType.DMA,
        ],
        compiler_params=pltpu.CompilerParams(collective_id=number, has_side_effects=True),
    )(*srcs, rows)
    return (results[:count], results[count])


def scatter_kernel(grid, count, *refs):
    srcs, outs, refs = refs[:count], refs[count : 2 * count], refs[2 * count :]
    acc, from_sibling, from_v, from_u, from_low, from_high = [
        refs[k * count : (k + 1) * count] for k in range(6)
    ]
    load_sem, side_send, side_recv, v_send, v_recv, u_send, u_recv, z_send, low_recv, high_recv = refs[6 * count :]
    z, x, y, core = grid.here()
    tall = grid.tall
    ux, uy = lax.rem(x + 1 - core, 2), lax.rem(y + core, 2)
    vx, vy = lax.rem(x + core, 2), lax.rem(y + 1 - core, 2)
    up, down = grid.device(z + 1, x, y, core), grid.device(z - 1, x, y, core)
    u_device, v_device = grid.device(z, ux, uy, core), grid.device(z, vx, vy, core)
    sibling = grid.device(z, x, y, 1 - core)
    has_up, has_down = z < tall - 1, z > 0
    greet(u_device)
    greet(v_device)
    greet(sibling)
    greet(up, has_up)
    greet(down, has_down)

    def each(action):
        for m in range(count):
            action(m)

    def slot(level, along_v, along_u):
        return (level * 2 + along_v) * 2 + along_u

    def place(along_v, along_u):
        if along_v and along_u:
            return 1 - x, 1 - y
        if along_v:
            return vx, vy
        if along_u:
            return ux, uy
        return x, y

    def load(m, level, along_v, along_u):
        xx, yy = place(along_v, along_u)
        where = slot(level, along_v, along_u)
        return pltpu.make_async_copy(
            srcs[m].at[grid.flat(level, xx, yy, core)], acc[m].at[where], load_sem.at[m, where]
        )

    def side(m, level, along_v, along_u):
        xx, yy = place(along_v, along_u)
        return pltpu.make_async_remote_copy(
            src_ref=srcs[m].at[grid.flat(level, xx, yy, 1 - core)],
            dst_ref=from_sibling[m].at[slot(level, along_u, along_v)],
            send_sem=side_send.at[m, slot(level, along_u, along_v)],
            recv_sem=side_recv.at[m, slot(level, along_u, along_v)],
            device_id=sibling,
            device_id_type=MESH,
        )

    def v_copy(m, level, along_u):
        return pltpu.make_async_remote_copy(
            src_ref=acc[m].at[slot(level, 1, along_u)],
            dst_ref=from_v[m].at[level * 2 + along_u],
            send_sem=v_send.at[m, level * 2 + along_u],
            recv_sem=v_recv.at[m, level * 2 + along_u],
            device_id=v_device,
            device_id_type=MESH,
        )

    def u_copy(m, level):
        return pltpu.make_async_remote_copy(
            src_ref=acc[m].at[slot(level, 0, 1)],
            dst_ref=from_u[m].at[level],
            send_sem=u_send.at[m, level],
            recv_sem=u_recv.at[m, level],
            device_id=u_device,
            device_id_type=MESH,
        )

    def z_copy(m, level, upward):
        return pltpu.make_async_remote_copy(
            src_ref=acc[m].at[slot(level, 0, 0)],
            dst_ref=(from_low if upward else from_high)[m].at[level],
            send_sem=z_send.at[m, level],
            recv_sem=(low_recv if upward else high_recv).at[m, level],
            device_id=up if upward else down,
            device_id_type=MESH,
        )

    def add(m, where, other, at):
        total = acc[m][where].astype(jnp.float32) + other[m][at].astype(jnp.float32)
        acc[m][where] = total.astype(jnp.bfloat16)

    def levels(action):
        @pl.loop(0, 2 * tall)
        def _(step):
            far = tall - 1 - step // 2
            level = jnp.where(lax.rem(step, 2) == 0, z - far, z + far)
            use = (level >= 0) & (level < tall) & ((far > 0) | (lax.rem(step, 2) == 0))

            @pl.when(use)
            def _():
                action(level)

    def begin(level):
        for along_v in (1, 0):
            for along_u in (1, 0):
                each(lambda m: load(m, level, along_v, along_u).start())

    levels(begin)
    meet(count=3 + has_up.astype(jnp.int32) + has_down.astype(jnp.int32))

    def begin_side(kinds):
        def run(level):
            for along_v, along_u in kinds:
                each(lambda m: side(m, level, along_v, along_u).start())

        return run

    levels(begin_side(((1, 1), (0, 1))))
    levels(begin_side(((1, 0), (0, 0))))

    def take(level, along_v, along_u):
        where = slot(level, along_v, along_u)

        def run(m):
            load(m, level, along_v, along_u).wait()
            side(m, level, along_u, along_v).wait_recv()
            add(m, where, from_sibling, where)

        each(run)

    def first(level):
        for along_u in (1, 0):
            take(level, 1, along_u)
            each(lambda m: v_copy(m, level, along_u).start())

    levels(first)

    def second(level):
        for along_u in (1, 0):
            take(level, 0, along_u)

            def run(m):
                v_copy(m, level, along_u).wait_recv()
                add(m, slot(level, 0, along_u), from_v, level * 2 + along_u)
                if along_u:
                    u_copy(m, level).start()

            each(run)

    levels(second)

    def third(level):
        where = slot(level, 0, 0)

        def run(m):
            u_copy(m, level).wait_recv()
            add(m, where, from_u, level)

        each(run)

        @pl.when((level >= z) & has_down)
        def _():
            def run(m):
                z_copy(m, level, True).wait_recv()
                add(m, where, from_low, level)

            each(run)

        @pl.when((level <= z) & has_up)
        def _():
            def run(m):
                z_copy(m, level, False).wait_recv()
                add(m, where, from_high, level)

            each(run)

        @pl.when(level > z)
        def _():
            each(lambda m: z_copy(m, level, True).start())

        @pl.when(level < z)
        def _():
            each(lambda m: z_copy(m, level, False).start())

    levels(third)

    def finish(m):
        outs[m][...] = acc[m][slot(z, 0, 0)].astype(jnp.float32)

    each(finish)

    def drain(level):
        for along_v in (0, 1):
            for along_u in (0, 1):
                each(lambda m: side(m, level, along_v, along_u).wait_send())
        for along_u in (0, 1):
            each(lambda m: v_copy(m, level, along_u).wait_send())
        each(lambda m: u_copy(m, level).wait_send())

        @pl.when(level != z)
        def _():
            each(lambda m: z_copy(m, level, True).wait_send())

    levels(drain)


def scatter(srcs, number):
    grid = Grid()
    count = len(srcs)
    tall = grid.tall
    blocks = [src.shape[1:] for src in srcs]
    buffers = [
        pltpu.VMEM((number_of,) + block, jnp.bfloat16)
        for number_of in (4 * tall, 4 * tall, 2 * tall, tall, tall, tall)
        for block in blocks
    ]
    semaphores = [
        pltpu.SemaphoreType.DMA((count, number_of))
        for number_of in (4 * tall, 4 * tall, 4 * tall, 2 * tall, 2 * tall, tall, tall, tall, tall, tall)
    ]
    return pl.pallas_call(
        functools.partial(scatter_kernel, grid, count),
        out_shape=[jax.ShapeDtypeStruct(block, jnp.float32) for block in blocks],
        in_specs=[pl.BlockSpec(memory_space=pl.ANY)] * count,
        out_specs=[pl.BlockSpec(memory_space=pltpu.VMEM)] * count,
        scratch_shapes=buffers + semaphores,
        compiler_params=pltpu.CompilerParams(
            collective_id=number, has_side_effects=True, vmem_limit_bytes=56 * 1024 * 1024
        ),
    )(*srcs)


def rows_kernel(grid, src, out, own_sem, line_send, side_send, y_send, recv_sem):
    d, f = lax.axis_index("dp"), lax.axis_index("fsdp")
    me = d * grid.fs + f
    f_side = f + 1 - 2 * lax.rem(f, 2)
    f_y = lax.rem(f + 2, grid.fs)
    f_y_side = lax.rem(f_side + 2, grid.fs)
    own = pltpu.make_async_copy(src.at[d], out.at[me], own_sem)
    own.start()

    @pl.loop(1, grid.dp)
    def _(step):
        greet((lax.rem(d + step, grid.dp), f))

    greet((d, f_side))
    greet((d, f_y))
    meet(count=grid.dp + 1)

    def line(peer, slot):
        return pltpu.make_async_remote_copy(
            src_ref=src.at[peer],
            dst_ref=out.at[slot],
            send_sem=line_send.at[peer],
            recv_sem=recv_sem.at[slot],
            device_id=(peer, f),
            device_id_type=MESH,
        )

    def onward(slot, column, sem, own_block):
        return pltpu.make_async_remote_copy(
            src_ref=src.at[d] if own_block else out.at[slot],
            dst_ref=out.at[slot],
            send_sem=sem.at[slot],
            recv_sem=recv_sem.at[slot],
            device_id=(d, column),
            device_id_type=MESH,
        )

    onward(me, f_y, y_send, True).start()
    onward(me, f_side, side_send, True).start()

    @pl.loop(1, grid.dp)
    def _(step):
        peer = lax.rem(d + step, grid.dp)
        line(peer, me).start()

    @pl.loop(1, grid.dp)
    def _(step):
        slot = lax.rem(d + grid.dp - step, grid.dp) * grid.fs + f
        line(d, slot).wait_recv()
        onward(slot, f_y, y_send, False).start()
        onward(slot, f_side, side_send, False).start()

    @pl.loop(0, grid.dp)
    def _(step):
        slot = lax.rem(d + grid.dp - step, grid.dp) * grid.fs + f_y
        line(d, slot).wait_recv()
        onward(slot, f_side, side_send, False).start()

    @pl.loop(0, grid.dp)
    def _(step):
        line(d, step * grid.fs + f_side).wait_recv()
        line(d, step * grid.fs + f_y_side).wait_recv()
        onward(step * grid.fs + f, f_y, y_send, False).wait_send()
        onward(step * grid.fs + f, f_side, side_send, False).wait_send()
        onward(step * grid.fs + f_y, f_side, side_send, False).wait_send()

    @pl.loop(1, grid.dp)
    def _(step):
        line(lax.rem(d + step, grid.dp), me).wait_send()

    own.wait()


def share_rows(src, number):
    grid = Grid()
    return pl.pallas_call(
        functools.partial(rows_kernel, grid),
        out_shape=jax.ShapeDtypeStruct((grid.total,) + src.shape[1:], src.dtype),
        in_specs=[pl.BlockSpec(memory_space=pl.ANY)],
        out_specs=pl.BlockSpec(memory_space=pl.ANY),
        scratch_shapes=[
            pltpu.SemaphoreType.DMA,
            pltpu.SemaphoreType.DMA((grid.dp,)),
            pltpu.SemaphoreType.DMA((grid.total,)),
            pltpu.SemaphoreType.DMA((grid.total,)),
            pltpu.SemaphoreType.DMA((grid.total,)),
        ],
        compiler_params=pltpu.CompilerParams(collective_id=number, has_side_effects=True),
    )(src)


def spread_kernel(vocab_rows, ids_ref, rows_ref, out_ref, square_ref):
    block = out_ref.shape[0]
    base = pl.program_id(0) * block
    place = base + lax.broadcasted_iota(jnp.int32, (block, ids_ref.shape[1]), 0)
    hot = jnp.where(place == ids_ref[...], 1.0, 0.0).astype(jnp.bfloat16)
    total = matmul(hot, rows_ref[...])
    low = total.astype(jnp.bfloat16)
    out_ref[...] = low
    wide = low.astype(jnp.float32)
    part = jnp.sum((wide * wide).reshape(block // 8, 8, D), 0)

    @pl.when(pl.program_id(0) == 0)
    def _():
        square_ref[...] = jnp.zeros_like(square_ref)

    square_ref[...] += part


def spread_rows(ids, rows, vocab_rows):
    count = rows.shape[0]
    block = 512
    steps = -(-vocab_rows // block)
    return pl.pallas_call(
        functools.partial(spread_kernel, vocab_rows),
        grid=(steps,),
        out_shape=[
            jax.ShapeDtypeStruct((vocab_rows, D), jnp.bfloat16),
            jax.ShapeDtypeStruct((8, D), jnp.float32),
        ],
        in_specs=[
            pl.BlockSpec((1, count), lambda i: (0, 0)),
            pl.BlockSpec((count, D), lambda i: (0, 0)),
        ],
        out_specs=[pl.BlockSpec((block, D), lambda i: (i, 0)), pl.BlockSpec((8, D), lambda i: (0, 0))],
        compiler_params=pltpu.CompilerParams(vmem_limit_bytes=48 * 1024 * 1024),
    )(ids.reshape(1, count), rows)


def plain_body(
    token_ids,
    pad_mask,
    hard_negative,
    table,
    table_first,
    table_second,
    attn_in,
    attn_in_first,
    attn_in_second,
    attn_out,
    attn_out_first,
    attn_out_second,
    ffn_in,
    ffn_in_first,
    ffn_in_second,
    ffn_out,
    ffn_out_first,
    ffn_out_second,
    proj_head,
    proj_head_first,
    proj_head_second,
    small_params,
    small_first,
    small_second,
):
    dp_count = lax.axis_size("dp")
    fsdp_count = lax.axis_size("fsdp")
    device_flat = lax.axis_index("dp") * fsdp_count + lax.axis_index("fsdp")
    pairs_here = token_ids.shape[1]
    pairs_total = pairs_here * dp_count * fsdp_count
    seq_count = 2 * pairs_here
    vocab_rows = table.shape[0]
    row_base = lax.axis_index("dp") * vocab_rows
    gain_rows = small_params[: 3 * D].reshape(3, D)
    bias_table = small_params[3 * D : 3 * D + NB * HEADS].reshape(NB, HEADS)
    log_scale = small_params[3 * D + NB * HEADS]
    buckets = jnp.asarray(bucket_table(L, NB).reshape(-1), jnp.int32)
    bucket_hot = (buckets[:, None] == jnp.arange(NB, dtype=jnp.int32)[None, :]).astype(jnp.float32)
    bias_full = (
        jnp.dot(bucket_hot, bias_table, precision=HIGH).reshape(L, L, HEADS).transpose(2, 0, 1)
    )
    mask_rows = pad_mask.reshape(seq_count, L)
    ids_flat = token_ids.reshape(-1)
    table_low = table.astype(jnp.bfloat16)
    ids_all = lax.all_gather(ids_flat, "dp", axis=0, tiled=True)
    picked = ids_all - row_base
    inside = (picked >= 0) & (picked < vocab_rows)
    chosen = jnp.take(table_low, jnp.clip(picked, 0, vocab_rows - 1), axis=0)
    embedded = lax.psum_scatter(
        jnp.where(inside[:, None], chosen.astype(jnp.float32), 0.0).astype(jnp.bfloat16),
        "dp",
        scatter_dimension=0,
        tiled=True,
    ).astype(jnp.float32)
    shards = (
        attn_in.astype(jnp.bfloat16),
        attn_out.astype(jnp.bfloat16),
        ffn_in.astype(jnp.bfloat16),
        ffn_out.astype(jnp.bfloat16),
        proj_head.astype(jnp.bfloat16),
    )
    gathered = (
        lax.all_gather(shards[0], ("dp", "fsdp"), axis=0, tiled=True),
        lax.all_gather(shards[1], ("dp", "fsdp"), axis=0, tiled=True),
        lax.all_gather(shards[2], ("dp", "fsdp"), axis=0, tiled=True),
        lax.all_gather(shards[3], ("dp", "fsdp"), axis=0, tiled=True),
        lax.all_gather(shards[4], ("dp", "fsdp"), axis=0, tiled=True),
    )
    final_rows, kept = layer_forward(embedded, mask_rows, gathered[:4], gain_rows, bias_full)
    normed_three, factor_three = normalize(final_rows, gain_rows[2])
    mask_weight = mask_rows.astype(jnp.float32)[:, :, None]
    counts = jnp.sum(mask_weight, 1)
    pooled = jnp.sum(normed_three.reshape(seq_count, L, D) * mask_weight, 1) / counts
    pooled_low = pooled.astype(jnp.bfloat16)
    projected = matmul(pooled_low, gathered[4])
    proj_factor = lax.rsqrt(jnp.sum(projected * projected, -1, keepdims=True) + EPS)
    unit_rows = projected * proj_factor
    unit_low = unit_rows.astype(jnp.bfloat16)
    mine_query = unit_low[:pairs_here]
    all_pass = lax.all_gather(unit_low[pairs_here:], ("dp", "fsdp"), axis=0, tiled=True)
    similar = matmul_nt(mine_query, all_pass)
    sim_scale = jnp.exp(log_scale)
    columns = jnp.arange(pairs_total, dtype=jnp.int32)
    own_index = device_flat * pairs_here + jnp.arange(pairs_here, dtype=jnp.int32)
    own_mask = (columns[None, :] == own_index[:, None]).astype(jnp.float32)
    negative = (columns[None, :] == hard_negative[:, None]).astype(jnp.float32)
    logits = sim_scale * similar - MARGIN * own_mask
    diagonal = jnp.sum(logits * own_mask, 1)
    hardest = jnp.sum(logits * negative, 1)
    row_max = jnp.max(logits, 1, keepdims=True)
    log_total = row_max + jnp.log(jnp.sum(jnp.exp(logits - row_max), 1, keepdims=True))
    loss_local = jnp.sum(log_total[:, 0] - diagonal + jax.nn.softplus(hardest - diagonal))
    hinge_gate = jax.nn.sigmoid(hardest - diagonal)
    grad_logits = (
        jnp.exp(logits - log_total) - own_mask + hinge_gate[:, None] * (negative - own_mask)
    )
    grad_log_scale = sim_scale * jnp.sum(grad_logits * similar)
    grad_similar = (sim_scale * grad_logits).astype(jnp.bfloat16)
    grad_query = matmul(grad_similar, all_pass).astype(jnp.bfloat16)
    grad_pass_terms = matmul_tn(grad_similar, mine_query)
    grad_pass = lax.psum_scatter(
        grad_pass_terms, ("dp", "fsdp"), scatter_dimension=0, tiled=True
    ).astype(jnp.bfloat16)
    grad_units = jnp.concatenate([grad_query, grad_pass], 0).astype(jnp.float32)
    grad_proj = (
        proj_factor * (grad_units - unit_rows * jnp.sum(grad_units * unit_rows, -1, keepdims=True))
    ).astype(jnp.bfloat16)
    gathered_back = (
        lax.all_gather(shards[0], ("dp", "fsdp"), axis=0, tiled=True),
        lax.all_gather(shards[1], ("dp", "fsdp"), axis=0, tiled=True),
        lax.all_gather(shards[2], ("dp", "fsdp"), axis=0, tiled=True),
        lax.all_gather(shards[3], ("dp", "fsdp"), axis=0, tiled=True),
        lax.all_gather(shards[4], ("dp", "fsdp"), axis=0, tiled=True),
    )
    grad_proj_head = matmul_tn(pooled_low, grad_proj)
    grad_pooled = matmul_nt(grad_proj, gathered_back[4])
    grad_normed = ((grad_pooled / counts)[:, None, :] * mask_weight).reshape(-1, D)
    grad_final, gain_three = normalize_back(grad_normed, final_rows, factor_three, gain_rows[2])
    grad_rows, matrix_grads, gain_one, gain_two, grad_bias = layer_backward(
        grad_final, kept, mask_rows, gathered_back[:4], gain_rows, bias_full
    )
    attn_in_grad, attn_out_grad, ffn_in_grad, ffn_out_grad = matrix_grads
    grad_bias_table = jnp.dot(grad_bias.reshape(HEADS, L * L), bucket_hot, precision=HIGH).T
    small_local = jnp.concatenate(
        [gain_one, gain_two, gain_three, grad_bias_table.reshape(-1), grad_log_scale[None]]
    )
    small_grad = lax.psum(small_local, ("dp", "fsdp"))
    weight_grads = (
        lax.psum_scatter(attn_in_grad, ("dp", "fsdp"), scatter_dimension=0, tiled=True),
        lax.psum_scatter(attn_out_grad, ("dp", "fsdp"), scatter_dimension=0, tiled=True),
        lax.psum_scatter(ffn_in_grad, ("dp", "fsdp"), scatter_dimension=0, tiled=True),
        lax.psum_scatter(ffn_out_grad, ("dp", "fsdp"), scatter_dimension=0, tiled=True),
        lax.psum_scatter(grad_proj_head, ("dp", "fsdp"), scatter_dimension=0, tiled=True),
    )
    rows_back = lax.all_gather(grad_rows.astype(jnp.bfloat16), "dp", axis=0, tiled=True)
    turn_count = dp_count // 4
    block_rows = rows_back.shape[0] // turn_count

    def add_block(running, piece_pair):
        block_grads, block_ids = piece_pair
        local_ids = block_ids - row_base
        inside = (local_ids >= 0) & (local_ids < vocab_rows)
        segment = jnp.where(inside, local_ids, vocab_rows)
        summed = jax.ops.segment_sum(
            block_grads.astype(jnp.float32), segment, num_segments=vocab_rows + 1
        )
        return (running + summed[:vocab_rows], None)

    table_full, _ = lax.scan(
        add_block,
        jnp.zeros((vocab_rows, D), jnp.float32),
        (rows_back.reshape(turn_count, block_rows, D), ids_all.reshape(turn_count, block_rows)),
    )
    table_grad = lax.psum(table_full.astype(jnp.bfloat16), "fsdp").astype(jnp.float32)
    owned = (table_grad,) + tuple(weight_grads)
    squares = jnp.sum(table_grad * table_grad) / fsdp_count
    for gradient in weight_grads:
        squares = squares + jnp.sum(gradient * gradient)
    total_squares, loss_sum = lax.psum((squares, loss_local), ("dp", "fsdp"))
    norm_value = jnp.sqrt(total_squares + jnp.sum(small_grad * small_grad))
    factor = jnp.minimum(1.0, CLIP / (norm_value + 1e-06))
    masters = (table, attn_in, attn_out, ffn_in, ffn_out, proj_head, small_params)
    firsts = (
        table_first,
        attn_in_first,
        attn_out_first,
        ffn_in_first,
        ffn_out_first,
        proj_head_first,
        small_first,
    )
    seconds = (
        table_second,
        attn_in_second,
        attn_out_second,
        ffn_in_second,
        ffn_out_second,
        proj_head_second,
        small_second,
    )
    gradients = owned + (small_grad,)
    results = [loss_sum, norm_value]
    for kind_index in range(7):
        results.extend(
            adam_update(
                masters[kind_index],
                firsts[kind_index],
                seconds[kind_index],
                gradients[kind_index],
                factor,
                RATES[kind_index],
                DECAYS[kind_index],
            )
        )
    return tuple(results)


def fits(mesh):
    return mesh.shape["fsdp"] == 4 and mesh.shape["dp"] == 8


def dense_rows(ids_flat, table, row_base):
    vocab_rows = table.shape[0]
    ids_all = lax.all_gather(ids_flat, "dp", axis=0, tiled=True)
    picked = ids_all - row_base
    inside = (picked >= 0) & (picked < vocab_rows)
    chosen = jnp.take(table.astype(jnp.bfloat16), jnp.clip(picked, 0, vocab_rows - 1), axis=0)
    return lax.psum_scatter(
        jnp.where(inside[:, None], chosen.astype(jnp.float32), 0.0).astype(jnp.bfloat16),
        "dp",
        scatter_dimension=0,
        tiled=True,
    ).astype(jnp.float32)


def dense_table_grad(ids_flat, grad_low, vocab_rows, row_base):
    ids_all = lax.all_gather(ids_flat, "dp", axis=0, tiled=True)
    rows_back = lax.all_gather(grad_low, "dp", axis=0, tiled=True)
    turn_count = lax.axis_size("dp") // 4
    block_rows = rows_back.shape[0] // turn_count

    def add_block(running, piece_pair):
        block_grads, block_ids = piece_pair
        local_ids = block_ids - row_base
        inside = (local_ids >= 0) & (local_ids < vocab_rows)
        segment = jnp.where(inside, local_ids, vocab_rows)
        summed = jax.ops.segment_sum(
            block_grads.astype(jnp.float32), segment, num_segments=vocab_rows + 1
        )
        return (running + summed[:vocab_rows], None)

    table_full, _ = lax.scan(
        add_block,
        jnp.zeros((vocab_rows, D), jnp.float32),
        (rows_back.reshape(turn_count, block_rows, D), ids_all.reshape(turn_count, block_rows)),
    )
    return lax.psum(table_full.astype(jnp.bfloat16), "fsdp")


def once(flag, make, value):
    return lax.while_loop(lambda state: state[0], lambda state: (False, make(state[1])), (flag, value))[1]


def fast_body(
    token_ids,
    pad_mask,
    hard_negative,
    table,
    table_first,
    table_second,
    attn_in,
    attn_in_first,
    attn_in_second,
    attn_out,
    attn_out_first,
    attn_out_second,
    ffn_in,
    ffn_in_first,
    ffn_in_second,
    ffn_out,
    ffn_out_first,
    ffn_out_second,
    proj_head,
    proj_head_first,
    proj_head_second,
    small_params,
    small_first,
    small_second,
):
    dp_count = lax.axis_size("dp")
    fsdp_count = lax.axis_size("fsdp")
    total = dp_count * fsdp_count
    column = lax.axis_index("fsdp")
    device_flat = lax.axis_index("dp") * fsdp_count + column
    pairs_here = token_ids.shape[1]
    pairs_total = pairs_here * total
    seq_count = 2 * pairs_here
    vocab_rows = table.shape[0]
    row_base = lax.axis_index("dp") * vocab_rows
    gain_rows = small_params[: 3 * D].reshape(3, D)
    bias_table = small_params[3 * D : 3 * D + NB * HEADS].reshape(NB, HEADS)
    log_scale = small_params[3 * D + NB * HEADS]
    buckets = jnp.asarray(bucket_table(L, NB).reshape(-1), jnp.int32)
    bucket_hot = (buckets[:, None] == jnp.arange(NB, dtype=jnp.int32)[None, :]).astype(jnp.float32)
    bias_full = (
        jnp.dot(bucket_hot, bias_table, precision=HIGH).reshape(L, L, HEADS).transpose(2, 0, 1)
    )
    mask_rows = pad_mask.reshape(seq_count, L)
    ids_flat = token_ids.reshape(-1)
    tokens = ids_flat.shape[0]

    order = jnp.arange(tokens, dtype=jnp.int32)
    owner = ids_flat // vocab_rows
    earlier = (ids_flat[None, :] == ids_flat[:, None]) & (order[None, :] < order[:, None])
    first = ~jnp.any(earlier, 1)
    below = (owner[None, :] == owner[:, None]) & (ids_flat[None, :] < ids_flat[:, None]) & first[None, :]
    rank = jnp.sum(below.astype(jnp.int32), 1)
    spilled = jnp.any(rank >= CAP)
    slot = jnp.where(rank < CAP, owner * CAP + rank, -1)
    slots = jnp.arange(dp_count * CAP, dtype=jnp.int32)
    lists = jnp.max(
        jnp.where(slot[None, :] == slots[:, None], (ids_flat - owner * vocab_rows)[None, :], -1), 1
    ).reshape(dp_count, 1, 1, CAP)
    lists = jnp.broadcast_to(lists, (dp_count, fsdp_count, 1, CAP)).reshape(total, 1, CAP)
    extra = jnp.zeros((7, 128), jnp.int32)
    extra = extra.at[0, :pairs_here].set(hard_negative).at[1, 0].set(spilled.astype(jnp.int32))
    message = jnp.concatenate([lists, jnp.broadcast_to(extra[None], (total, 7, 128))], 1)
    heard = exchange(message, True, 1)
    asked = heard[:, 0, :]
    negatives = heard[:, 1, :pairs_here].reshape(-1)
    any_spilled = jnp.max(heard[:, 2, 0]) > 0

    mine_asked = lax.dynamic_index_in_dim(
        asked.reshape(dp_count, fsdp_count, CAP), column, 1, keepdims=False
    )
    answers = jnp.take(table, jnp.maximum(mine_asked.reshape(-1), 0), axis=0).astype(jnp.bfloat16)
    shards = (
        attn_in.astype(jnp.bfloat16),
        attn_out.astype(jnp.bfloat16),
        ffn_in.astype(jnp.bfloat16),
        ffn_out.astype(jnp.bfloat16),
        proj_head.astype(jnp.bfloat16),
    )
    gathered, found = gather(shards, answers.reshape(dp_count, CAP, D), 2)
    gathered = [matrix.reshape(-1, matrix.shape[-1]) for matrix in gathered]
    slot_hot = (slot[:, None] == slots[None, :]).astype(jnp.bfloat16)
    embedded = matmul(slot_hot, found.reshape(dp_count * CAP, D))
    embedded = once(any_spilled, lambda _: dense_rows(ids_flat, table, row_base), embedded)

    final_rows, kept = layer_forward(embedded, mask_rows, gathered[:4], gain_rows, bias_full)
    normed_three, factor_three = normalize(final_rows, gain_rows[2])
    mask_weight = mask_rows.astype(jnp.float32)[:, :, None]
    counts = jnp.sum(mask_weight, 1)
    pooled = jnp.sum(normed_three.reshape(seq_count, L, D) * mask_weight, 1) / counts
    pooled_low = pooled.astype(jnp.bfloat16)
    projected = matmul(pooled_low, gathered[4])
    proj_factor = lax.rsqrt(jnp.sum(projected * projected, -1, keepdims=True) + EPS)
    unit_rows = projected * proj_factor
    unit_low = unit_rows.astype(jnp.bfloat16)
    all_units = exchange(unit_low.reshape(2 * seq_count, D // 2), False, 3)
    all_units = all_units.reshape(total, 2, pairs_here, D)
    all_query = all_units[:, 0].reshape(pairs_total, D)
    all_pass = all_units[:, 1].reshape(pairs_total, D)
    similar = matmul_nt(all_query, all_pass)
    sim_scale = jnp.exp(log_scale)
    columns = jnp.arange(pairs_total, dtype=jnp.int32)
    own_mask = (columns[None, :] == columns[:, None]).astype(jnp.float32)
    negative = (columns[None, :] == negatives[:, None]).astype(jnp.float32)
    logits = sim_scale * similar - MARGIN * own_mask
    diagonal = jnp.sum(logits * own_mask, 1)
    hardest = jnp.sum(logits * negative, 1)
    row_max = jnp.max(logits, 1, keepdims=True)
    log_total = row_max + jnp.log(jnp.sum(jnp.exp(logits - row_max), 1, keepdims=True))
    loss_sum = jnp.sum(log_total[:, 0] - diagonal + jax.nn.softplus(hardest - diagonal))
    hinge_gate = jax.nn.sigmoid(hardest - diagonal)
    grad_logits = (
        jnp.exp(logits - log_total) - own_mask + hinge_gate[:, None] * (negative - own_mask)
    )
    grad_log_scale = sim_scale * jnp.sum(grad_logits * similar)
    grad_similar = (sim_scale * grad_logits).astype(jnp.bfloat16)
    own_first = device_flat * pairs_here
    mine_rows = lax.dynamic_slice_in_dim(grad_similar, own_first, pairs_here, 0)
    mine_columns = lax.dynamic_slice_in_dim(grad_similar, own_first, pairs_here, 1)
    grad_query = matmul(mine_rows, all_pass).astype(jnp.bfloat16)
    grad_pass = matmul_tn(mine_columns, all_query).astype(jnp.bfloat16)
    grad_units = jnp.concatenate([grad_query, grad_pass], 0).astype(jnp.float32)
    grad_proj = (
        proj_factor * (grad_units - unit_rows * jnp.sum(grad_units * unit_rows, -1, keepdims=True))
    ).astype(jnp.bfloat16)
    grad_proj_head = matmul_tn(pooled_low, grad_proj)
    grad_pooled = matmul_nt(grad_proj, gathered[4])
    grad_normed = ((grad_pooled / counts)[:, None, :] * mask_weight).reshape(-1, D)
    grad_final, gain_three = normalize_back(grad_normed, final_rows, factor_three, gain_rows[2])
    grad_rows, matrix_grads, gain_one, gain_two, grad_bias = layer_backward(
        grad_final, kept, mask_rows, gathered[:4], gain_rows, bias_full
    )
    grad_bias_table = jnp.dot(grad_bias.reshape(HEADS, L * L), bucket_hot, precision=HIGH).T
    partials = [
        grad.astype(jnp.bfloat16).reshape(total, -1, grad.shape[1])
        for grad in (*matrix_grads, grad_proj_head)
    ]
    weight_grads = scatter(partials, 4)

    grad_low = grad_rows.astype(jnp.bfloat16)
    slot_sums = matmul_tn(slot_hot, grad_low).astype(jnp.bfloat16).reshape(dp_count, CAP, D)
    all_rows = share_rows(slot_sums, 5)
    table_grad, table_squares = spread_rows(
        asked.reshape(-1), all_rows.reshape(total * CAP, D), vocab_rows
    )
    table_squares = jnp.sum(table_squares)
    table_grad, table_squares = once(
        any_spilled, lambda _: with_squares(dense_table_grad(ids_flat, grad_low, vocab_rows, row_base)), (table_grad, table_squares)
    )
    squares = table_squares / fsdp_count
    for gradient in weight_grads:
        squares = squares + jnp.sum(gradient * gradient)
    small_local = jnp.concatenate(
        [gain_one, gain_two, gain_three, grad_bias_table.reshape(-1), squares[None]]
    )
    width = -(-small_local.shape[0] // 1024) * 8
    small_local = jnp.pad(small_local, (0, width * 128 - small_local.shape[0]))
    summed = jnp.sum(exchange(small_local.reshape(width, 128), False, 6), 0).reshape(-1)
    small_size = small_params.shape[0]
    total_squares = summed[small_size - 1]
    small_grad = jnp.concatenate([summed[: small_size - 1], grad_log_scale[None]])
    norm_value = jnp.sqrt(total_squares + jnp.sum(small_grad * small_grad))
    factor = jnp.minimum(1.0, CLIP / (norm_value + 1e-06))
    updates = (
        (table, table_first, table_second, table_grad.astype(jnp.float32)),
        (attn_in, attn_in_first, attn_in_second, weight_grads[0]),
        (attn_out, attn_out_first, attn_out_second, weight_grads[1]),
        (ffn_in, ffn_in_first, ffn_in_second, weight_grads[2]),
        (ffn_out, ffn_out_first, ffn_out_second, weight_grads[3]),
        (proj_head, proj_head_first, proj_head_second, weight_grads[4]),
        (small_params, small_first, small_second, small_grad),
    )
    results = [loss_sum, norm_value]
    for kind_index, arrays in enumerate(updates):
        results.extend(adam_update(*arrays, factor, RATES[kind_index], DECAYS[kind_index]))
    return tuple(results)


def with_squares(table_grad):
    wide = table_grad.astype(jnp.float32)
    return (table_grad, jnp.sum(wide * wide))


def solution(mesh):
    program = fast_body if fits(mesh) else plain_body
    return jax.shard_map(
        program,
        mesh=mesh,
        in_specs=(
            P(None, ("dp", "fsdp"), None),
            P(None, ("dp", "fsdp"), None),
            P(("dp", "fsdp")),
            P("dp", None),
            P("dp", None),
            P("dp", None),
            P(("dp", "fsdp"), None),
            P(("dp", "fsdp"), None),
            P(("dp", "fsdp"), None),
            P(("dp", "fsdp"), None),
            P(("dp", "fsdp"), None),
            P(("dp", "fsdp"), None),
            P(("dp", "fsdp"), None),
            P(("dp", "fsdp"), None),
            P(("dp", "fsdp"), None),
            P(("dp", "fsdp"), None),
            P(("dp", "fsdp"), None),
            P(("dp", "fsdp"), None),
            P(("dp", "fsdp"), None),
            P(("dp", "fsdp"), None),
            P(("dp", "fsdp"), None),
            P(),
            P(),
            P(),
        ),
        out_specs=(
            P(),
            P(),
            P("dp", None),
            P("dp", None),
            P("dp", None),
            P(("dp", "fsdp"), None),
            P(("dp", "fsdp"), None),
            P(("dp", "fsdp"), None),
            P(("dp", "fsdp"), None),
            P(("dp", "fsdp"), None),
            P(("dp", "fsdp"), None),
            P(("dp", "fsdp"), None),
            P(("dp", "fsdp"), None),
            P(("dp", "fsdp"), None),
            P(("dp", "fsdp"), None),
            P(("dp", "fsdp"), None),
            P(("dp", "fsdp"), None),
            P(("dp", "fsdp"), None),
            P(("dp", "fsdp"), None),
            P(("dp", "fsdp"), None),
            P(),
            P(),
            P(),
        ),
        check_vma=False,
    )
```

```python
import functools

import jax
import jax.numpy as jnp
import numpy as np
from jax import lax
from jax.experimental import pallas as pl
from jax.experimental.pallas import tpu as pltpu
from jax.sharding import PartitionSpec as P

D = 768
HEADS = 12
HD = 64
NB = 32
L = 128
STEP = 10


EPS = 1e-06
SCALE = 0.125
MARGIN = 0.2
CLIP = 0.1
BETA_ONE = 0.9
BETA_TWO = 0.99
ADAM_EPS = 1e-08
RATES = (3.0, 0.1, 0.2, 0.1, 0.05, 0.1, 1.0)
DECAYS = (0.001, 0.001, 0.001, 0.001, 0.001, 0.001, 0.0)
HIGH = lax.Precision.HIGHEST
MESH = pl.DeviceIdType.MESH
CAP = 128


def bucket_table(length, count):
    position = np.arange(length)
    relative = position[None, :] - position[:, None]
    half = count // 2
    base_part = (relative > 0).astype(np.int64) * half
    distance = np.abs(relative)
    exact = half // 2
    safe_dist = np.maximum(distance, 1)
    large = exact + (np.log(safe_dist / exact) / np.log(length / exact) * (half - exact)).astype(
        np.int64
    )
    large = np.minimum(large, half - 1)
    return base_part + np.where(distance < exact, distance, large)


def matmul(left_side, right_side):
    return jnp.dot(left_side, right_side, preferred_element_type=jnp.float32)


def matmul_tn(left_side, right_side):
    return lax.dot_general(
        left_side, right_side, (((0,), (0,)), ((), ())), preferred_element_type=jnp.float32
    )


def matmul_nt(left_side, right_side):
    return lax.dot_general(
        left_side, right_side, (((1,), (1,)), ((), ())), preferred_element_type=jnp.float32
    )


def normalize(inputs, gain_row):
    factor = lax.rsqrt(jnp.mean(inputs * inputs, -1, keepdims=True) + EPS)
    return (inputs * factor * gain_row, factor)


def normalize_back(grad_out, inputs, factor, gain_row):
    scaled = grad_out * gain_row
    grad_gain = jnp.sum(grad_out * inputs * factor, 0)
    grad_in = factor * (
        scaled - inputs * factor * factor * jnp.mean(scaled * inputs, -1, keepdims=True)
    )
    return (grad_in, grad_gain)


def attention_scores(mixed_proj, mask_rows, bias_full):
    keep_add = jnp.where(mask_rows > 0, 0.0, -1000000000.0).astype(jnp.float32)
    scores = jnp.einsum(
        "bqhd,bkhd->bhqk",
        mixed_proj[:, :, 0],
        mixed_proj[:, :, 1],
        preferred_element_type=jnp.float32,
    )
    return scores * SCALE + bias_full[None] + keep_add[:, None, None, :]


def layer_forward(token_rows, mask_rows, weights, gain_rows, bias_full):
    attn_in, attn_out, ffn_in, ffn_out = weights
    seq_count, length = mask_rows.shape
    width = token_rows.shape[1]
    normed_one, factor_one = normalize(token_rows, gain_rows[0])
    act_one = normed_one.astype(jnp.bfloat16)
    mixed_proj = (
        matmul(act_one, attn_in).astype(jnp.bfloat16).reshape(seq_count, length, 3, HEADS, HD)
    )
    scores = attention_scores(mixed_proj, mask_rows, bias_full)
    row_max = jnp.max(scores, -1, keepdims=True)
    log_total = row_max + jnp.log(jnp.sum(jnp.exp(scores - row_max), -1, keepdims=True))
    prob_low = jnp.exp(scores - log_total).astype(jnp.bfloat16)
    attended = jnp.einsum(
        "bhqk,bkhd->bqhd", prob_low, mixed_proj[:, :, 2], preferred_element_type=jnp.float32
    )
    attended = attended.astype(jnp.bfloat16).reshape(-1, width)
    after_attn = token_rows + matmul(attended, attn_out)
    normed_two, factor_two = normalize(after_attn, gain_rows[1])
    act_two = normed_two.astype(jnp.bfloat16)
    pre_act = matmul(act_two, ffn_in)
    hidden = jax.nn.gelu(pre_act).astype(jnp.bfloat16)
    final_rows = after_attn + matmul(hidden, ffn_out)
    kept = (
        token_rows,
        factor_one,
        act_one,
        mixed_proj,
        log_total,
        attended,
        after_attn,
        factor_two,
        act_two,
        pre_act,
        hidden,
    )
    return (final_rows, kept)


def layer_backward(grad_final, kept, mask_rows, weights, gain_rows, bias_full):
    (
        token_rows,
        factor_one,
        act_one,
        mixed_proj,
        log_total,
        attended,
        after_attn,
        factor_two,
        act_two,
        pre_act,
        hidden,
    ) = kept
    attn_in, attn_out, ffn_in, ffn_out = weights
    seq_count, length = mask_rows.shape
    branch = grad_final.astype(jnp.bfloat16)
    grad_ffn_out = matmul_tn(hidden, branch)
    grad_hidden = matmul_nt(branch, ffn_out)
    _, gelu_pull = jax.vjp(jax.nn.gelu, pre_act)
    grad_pre = gelu_pull(grad_hidden)[0].astype(jnp.bfloat16)
    grad_ffn_in = matmul_tn(act_two, grad_pre)
    grad_act_two = matmul_nt(grad_pre, ffn_in)
    grad_mid, gain_two = normalize_back(grad_act_two, after_attn, factor_two, gain_rows[1])
    grad_after = grad_final + grad_mid
    branch = grad_after.astype(jnp.bfloat16)
    grad_attn_out = matmul_tn(attended, branch)
    grad_attended = (
        matmul_nt(branch, attn_out).astype(jnp.bfloat16).reshape(seq_count, length, HEADS, HD)
    )
    scores = attention_scores(mixed_proj, mask_rows, bias_full)
    prob_full = jnp.exp(scores - log_total)
    prob_low = prob_full.astype(jnp.bfloat16)
    queries = mixed_proj[:, :, 0]
    key_rows = mixed_proj[:, :, 1]
    grad_probs = jnp.einsum(
        "bqhd,bkhd->bhqk", grad_attended, mixed_proj[:, :, 2], preferred_element_type=jnp.float32
    )
    grad_values = jnp.einsum(
        "bhqk,bqhd->bkhd", prob_low, grad_attended, preferred_element_type=jnp.float32
    )
    grad_scores = prob_full * (grad_probs - jnp.sum(prob_full * grad_probs, -1, keepdims=True))
    grad_scores = grad_scores.astype(jnp.bfloat16)
    grad_bias = jnp.sum(grad_scores, 0, dtype=jnp.float32)
    grad_queries = (
        jnp.einsum("bhqk,bkhd->bqhd", grad_scores, key_rows, preferred_element_type=jnp.float32)
        * SCALE
    )
    grad_keys = (
        jnp.einsum("bhqk,bqhd->bkhd", grad_scores, queries, preferred_element_type=jnp.float32)
        * SCALE
    )
    grad_mixed = (
        jnp.stack([grad_queries, grad_keys, grad_values], 2)
        .astype(jnp.bfloat16)
        .reshape(seq_count * length, -1)
    )
    grad_attn_in = matmul_tn(act_one, grad_mixed)
    grad_act_one = matmul_nt(grad_mixed, attn_in)
    grad_low, gain_one = normalize_back(grad_act_one, token_rows, factor_one, gain_rows[0])
    grad_rows = grad_after + grad_low
    return (
        grad_rows,
        (grad_attn_in, grad_attn_out, grad_ffn_in, grad_ffn_out),
        gain_one,
        gain_two,
        grad_bias,
    )


def adam_update(param, first_moment, second_moment, gradient, factor, rate, decay):
    clipped = gradient * factor
    first_new = BETA_ONE * first_moment + (1.0 - BETA_ONE) * clipped
    second_new = BETA_TWO * second_moment + (1.0 - BETA_TWO) * clipped * clipped
    direction = (
        first_new
        / (1.0 - BETA_ONE**STEP)
        / (jnp.sqrt(second_new / (1.0 - BETA_TWO**STEP)) + ADAM_EPS)
    )
    return (first_new, second_new, param - rate * (direction + decay * param))


class Grid:
    def __init__(self):
        self.dp, self.fs = lax.axis_size("dp"), lax.axis_size("fsdp")
        self.total = self.dp * self.fs
        self.wide = self.fs // 2
        self.tall = self.dp // self.wide

    def here(self):
        d, f = lax.axis_index("dp"), lax.axis_index("fsdp")
        return d // self.wide, lax.rem(d, self.wide), f // 2, lax.rem(f, 2)

    def device(self, z, x, y, core):
        return (z * self.wide + x, y * 2 + core)

    def flat(self, z, x, y, core):
        return (z * self.wide + x) * self.fs + y * 2 + core

    def peer(self, index):
        return (index // self.fs, lax.rem(index, self.fs))


def greet(device, when=None):
    barrier = pltpu.get_barrier_semaphore()

    def signal():
        pl.semaphore_signal(barrier, inc=1, device_id=device, device_id_type=MESH)

    if when is None:
        signal()
    else:
        pl.when(when)(signal)


def meet(count):
    pl.semaphore_wait(pltpu.get_barrier_semaphore(), count)


def exchange_kernel(grid, spread, src, out, send_sem, recv_sem, own_sem):
    me = lax.axis_index("dp") * grid.fs + lax.axis_index("fsdp")
    own = pltpu.make_async_copy(src.at[me] if spread else src, out.at[me], own_sem)
    own.start()

    @pl.loop(1, grid.total)
    def _(step):
        greet(grid.peer(lax.rem(me + step, grid.total)))

    meet(count=grid.total - 1)

    def copy(peer, slot):
        return pltpu.make_async_remote_copy(
            src_ref=src.at[peer] if spread else src,
            dst_ref=out.at[slot],
            send_sem=send_sem.at[peer],
            recv_sem=recv_sem.at[slot],
            device_id=grid.peer(peer),
            device_id_type=MESH,
        )

    @pl.loop(1, grid.total)
    def _(step):
        copy(lax.rem(me + step, grid.total), me).start()

    own.wait()

    @pl.loop(1, grid.total)
    def _(step):
        peer = lax.rem(me + step, grid.total)
        copy(peer, peer).wait_recv()
        copy(peer, peer).wait_send()


def exchange(src, spread, number):
    grid = Grid()
    block = src.shape[1:] if spread else src.shape
    return pl.pallas_call(
        functools.partial(exchange_kernel, grid, spread),
        out_shape=jax.ShapeDtypeStruct((grid.total,) + block, src.dtype),
        in_specs=[pl.BlockSpec(memory_space=pltpu.VMEM)],
        out_specs=pl.BlockSpec(memory_space=pltpu.VMEM),
        scratch_shapes=[
            pltpu.SemaphoreType.DMA((grid.total,)),
            pltpu.SemaphoreType.DMA((grid.total,)),
            pltpu.SemaphoreType.DMA,
        ],
        compiler_params=pltpu.CompilerParams(collective_id=number, has_side_effects=True),
    )(src)


def gather_kernel(grid, count, *refs):
    srcs, rows, outs, got_rows = refs[:count], refs[count], refs[count + 1 : 2 * count + 1], refs[2 * count + 1]
    send_sem, recv_sem, own_sem, row_send, row_recv, row_own = refs[2 * count + 2 :]
    z, x, y, core = grid.here()
    tall = grid.tall
    d, f = lax.axis_index("dp"), lax.axis_index("fsdp")
    ux, uy = lax.rem(x + 1 - core, 2), lax.rem(y + core, 2)
    vx, vy = lax.rem(x + core, 2), lax.rem(y + 1 - core, 2)
    up, down = grid.device(z + 1, x, y, core), grid.device(z - 1, x, y, core)
    u_device, v_device = grid.device(z, ux, uy, core), grid.device(z, vx, vy, core)
    sibling = grid.device(z, x, y, 1 - core)
    has_up, has_down = z < tall - 1, z > 0
    me = grid.flat(z, x, y, core)
    local = [pltpu.make_async_copy(srcs[m], outs[m].at[me], own_sem.at[m]) for m in range(count)]
    local.append(pltpu.make_async_copy(rows.at[d], got_rows.at[d], row_own))
    for item in local:
        item.start()

    @pl.loop(1, grid.dp)
    def _(step):
        greet((lax.rem(d + step, grid.dp), f))

    greet(v_device)
    greet(sibling)
    greet(u_device)
    meet(count=grid.dp + 2)

    def row_copy(peer, slot):
        return pltpu.make_async_remote_copy(
            src_ref=rows.at[peer],
            dst_ref=got_rows.at[slot],
            send_sem=row_send.at[peer],
            recv_sem=row_recv.at[slot],
            device_id=(peer, f),
            device_id_type=MESH,
        )

    def copy(m, shard, device, way, own):
        return pltpu.make_async_remote_copy(
            src_ref=srcs[m] if own else outs[m].at[shard],
            dst_ref=outs[m].at[shard],
            send_sem=send_sem.at[way, m, shard],
            recv_sem=recv_sem.at[m, shard],
            device_id=device,
            device_id_type=MESH,
        )

    def send(shard, device, way, own=False):
        for m in range(count):
            copy(m, shard, device, way, own).start()

    def arrived(shard):
        for m in range(count):
            copy(m, shard, sibling, 4, False).wait_recv()

    def sent(shard, device, way):
        for m in range(count):
            copy(m, shard, device, way, False).wait_send()

    @pl.when(has_up)
    def _():
        send(me, up, 0, True)

    @pl.when(has_down)
    def _():
        send(me, down, 1, True)

    send(me, u_device, 2, True)
    send(me, v_device, 3, True)
    send(me, sibling, 4, True)

    @pl.loop(1, grid.dp)
    def _(step):
        row_copy(lax.rem(d + step, grid.dp), d).start()

    def pass_z(k):
        low, high = z - k, z + k

        @pl.when(low >= 0)
        def _():
            shard = grid.flat(low, x, y, core)
            arrived(shard)

            @pl.when(has_up)
            def _():
                send(shard, up, 0)

            send(shard, u_device, 2)
            send(shard, v_device, 3)
            send(shard, sibling, 4)

        @pl.when(high < tall)
        def _():
            shard = grid.flat(high, x, y, core)
            arrived(shard)

            @pl.when(has_down)
            def _():
                send(shard, down, 1)

            send(shard, u_device, 2)
            send(shard, v_device, 3)
            send(shard, sibling, 4)

    def both(k, action):
        pl.when(z - k >= 0)(lambda: action(z - k))
        if k:
            pl.when(z + k < tall)(lambda: action(z + k))

    def pass_u(level):
        shard = grid.flat(level, ux, uy, core)
        arrived(shard)
        send(shard, v_device, 3)
        send(shard, sibling, 4)

    def pass_v(level):
        shard = grid.flat(level, vx, vy, core)
        arrived(shard)
        send(shard, sibling, 4)

    def pass_far(level):
        shard = grid.flat(level, 1 - x, 1 - y, core)
        arrived(shard)
        send(shard, sibling, 4)

    for k in range(tall + 1):
        if 0 < k < tall:
            pass_z(k)
        if k < tall:
            both(k, pass_u)
            both(k, pass_v)
        if k:
            both(k - 1, pass_far)

    @pl.loop(1, grid.dp)
    def _(step):
        peer = lax.rem(d + step, grid.dp)
        row_copy(peer, peer).wait_recv()
        row_copy(peer, peer).wait_send()

    @pl.loop(0, tall)
    def _(level):
        for xx in range(2):
            for yy in range(2):
                arrived(grid.flat(level, xx, yy, 1 - core))
                sent(grid.flat(level, xx, yy, core), sibling, 4)
        shard, other = grid.flat(level, x, y, core), grid.flat(level, ux, uy, core)

        @pl.when((level <= z) & has_up)
        def _():
            sent(shard, up, 0)

        @pl.when((level >= z) & has_down)
        def _():
            sent(shard, down, 1)

        sent(shard, u_device, 2)
        sent(shard, v_device, 3)
        sent(other, v_device, 3)

    for item in local:
        item.wait()


def gather(srcs, rows, number):
    grid = Grid()
    count = len(srcs)
    anywhere = pl.BlockSpec(memory_space=pl.ANY)
    results = pl.pallas_call(
        functools.partial(gather_kernel, grid, count),
        out_shape=[jax.ShapeDtypeStruct((grid.total,) + src.shape, src.dtype) for src in srcs]
        + [jax.ShapeDtypeStruct(rows.shape, rows.dtype)],
        in_specs=[anywhere] * (count + 1),
        out_specs=[anywhere] * (count + 1),
        scratch_shapes=[
            pltpu.SemaphoreType.DMA((5, count, grid.total)),
            pltpu.SemaphoreType.DMA((count, grid.total)),
            pltpu.SemaphoreType.DMA((count,)),
            pltpu.SemaphoreType.DMA((grid.dp,)),
            pltpu.SemaphoreType.DMA((grid.dp,)),
            pltpu.SemaphoreType.DMA,
        ],
        compiler_params=pltpu.CompilerParams(collective_id=number, has_side_effects=True),
    )(*srcs, rows)
    return (results[:count], results[count])


ROW_BLOCK = 512


def finish_kernel(grid, count, *refs):
    srcs, (sums, ids, small) = refs[:count], refs[count : count + 3]
    refs = refs[count + 3 :]
    outs, (table_out, small_out, square_out) = refs[:count], refs[count : count + 3]
    refs = refs[count + 3 :]
    acc, from_side, from_v, from_u, from_low, from_high = [
        refs[k * count : (k + 1) * count] for k in range(6)
    ]
    refs = refs[6 * count :]
    rows, small_all, square_mine, square_all = refs[:4]
    load_sem, side_send, side_recv, v_send, v_recv, u_send, u_recv, z_send, low_recv, high_recv = refs[4:14]
    row_own, line_send, on_send, row_recv, small_send, small_recv, square_send, square_recv = refs[14:]
    z, x, y, core = grid.here()
    tall = grid.tall
    d, f = lax.axis_index("dp"), lax.axis_index("fsdp")
    me = d * grid.fs + f
    up, down = grid.device(z + 1, x, y, core), grid.device(z - 1, x, y, core)
    has_up, has_down = z < tall - 1, z > 0
    ux, uy = lax.rem(x + 1 - core, 2), lax.rem(y + core, 2)
    vx, vy = lax.rem(x + core, 2), lax.rem(y + 1 - core, 2)
    u_device, v_device = grid.device(z, ux, uy, core), grid.device(z, vx, vy, core)
    sibling = grid.device(z, x, y, 1 - core)
    f_side = y * 2 + 1 - core
    f_y = (1 - y) * 2 + core
    f_far = (1 - y) * 2 + 1 - core

    @pl.loop(1, grid.total)
    def _(step):
        greet(grid.peer(lax.rem(me + step, grid.total)))

    def each(action):
        for m in range(count):
            action(m)

    def level_of(j):
        tables = []
        for own in range(tall):
            tables.append(sorted(range(tall), key=lambda level: (-abs(level - own), -level))[j])
        value = tables[0]
        for own in range(1, tall):
            value = jnp.where(z == own, tables[own], value)
        return value

    def load(m, level):
        return pltpu.make_async_copy(
            srcs[m].at[level, :, :, core], acc[m].at[level], load_sem.at[m, level]
        )

    def side(m, level):
        return pltpu.make_async_remote_copy(
            src_ref=srcs[m].at[level, :, :, 1 - core],
            dst_ref=from_side[m].at[level],
            send_sem=side_send.at[m, level],
            recv_sem=side_recv.at[m, level],
            device_id=sibling,
            device_id_type=MESH,
        )

    def v_copy(m, level, along_u):
        xx, yy = (1 - x, 1 - y) if along_u else (vx, vy)
        return pltpu.make_async_remote_copy(
            src_ref=acc[m].at[level, xx, yy],
            dst_ref=from_v[m].at[level, along_u],
            send_sem=v_send.at[m, level, along_u],
            recv_sem=v_recv.at[m, level, along_u],
            device_id=v_device,
            device_id_type=MESH,
        )

    def u_copy(m, level):
        return pltpu.make_async_remote_copy(
            src_ref=acc[m].at[level, ux, uy],
            dst_ref=from_u[m].at[level],
            send_sem=u_send.at[m, level],
            recv_sem=u_recv.at[m, level],
            device_id=u_device,
            device_id_type=MESH,
        )

    def z_copy(m, level, upward):
        return pltpu.make_async_remote_copy(
            src_ref=acc[m].at[level, x, y],
            dst_ref=(from_low if upward else from_high)[m].at[level],
            send_sem=z_send.at[m, level],
            recv_sem=(low_recv if upward else high_recv).at[m, level],
            device_id=up if upward else down,
            device_id_type=MESH,
        )

    def line(peer, slot):
        return pltpu.make_async_remote_copy(
            src_ref=sums.at[peer],
            dst_ref=rows.at[slot],
            send_sem=line_send.at[peer],
            recv_sem=row_recv.at[slot],
            device_id=(peer, f),
            device_id_type=MESH,
        )

    def onward(slot, to_side, own_block=False):
        return pltpu.make_async_remote_copy(
            src_ref=sums.at[d] if own_block else rows.at[slot],
            dst_ref=rows.at[slot],
            send_sem=on_send.at[1 if to_side else 0, slot],
            recv_sem=row_recv.at[slot],
            device_id=(d, f_side if to_side else f_y),
            device_id_type=MESH,
        )

    def small_copy(peer, slot):
        return pltpu.make_async_remote_copy(
            src_ref=small,
            dst_ref=small_all.at[slot],
            send_sem=small_send.at[peer],
            recv_sem=small_recv.at[slot],
            device_id=grid.peer(peer),
            device_id_type=MESH,
        )

    def square_copy(peer, slot):
        return pltpu.make_async_remote_copy(
            src_ref=square_mine,
            dst_ref=square_all.at[slot],
            send_sem=square_send.at[peer],
            recv_sem=square_recv.at[slot],
            device_id=grid.peer(peer),
            device_id_type=MESH,
        )

    levels = [level_of(j) for j in range(tall)]
    own_rows = pltpu.make_async_copy(sums.at[d], rows.at[me], row_own)
    own_rows.start()
    for level in levels:
        each(lambda m: load(m, level).start())
    meet(grid.total - 1)

    @pl.loop(1, grid.dp)
    def _(step):
        line(lax.rem(d + step, grid.dp), me).start()

    for level in levels:
        each(lambda m: side(m, level).start())
    onward(me, False, True).start()
    onward(me, True, True).start()

    @pl.loop(1, grid.total)
    def _(step):
        small_copy(lax.rem(me + step, grid.total), me).start()

    small_all[me] = small[...]

    def first(j):
        level = levels[j]

        def run(m):
            load(m, level).wait()
            side(m, level).wait_recv()
            for xx in range(2):
                for yy in range(2):
                    total = acc[m][level, xx, yy].astype(jnp.float32) + from_side[m][level, xx, yy].astype(jnp.float32)
                    acc[m][level, xx, yy] = total.astype(jnp.bfloat16)
            v_copy(m, level, 1).start()
            v_copy(m, level, 0).start()

        each(run)

    def add(m, level, xx, yy, other):
        total = acc[m][level, xx, yy].astype(jnp.float32) + other.astype(jnp.float32)
        acc[m][level, xx, yy] = total.astype(jnp.bfloat16)

    def second(j):
        level = levels[j]

        def run(m):
            v_copy(m, level, 1).wait_recv()
            add(m, level, ux, uy, from_v[m][level, 1])
            u_copy(m, level).start()

        each(run)

    def second_own(j):
        level = levels[j]

        def run(m):
            v_copy(m, level, 0).wait_recv()
            add(m, level, x, y, from_v[m][level, 0])

        each(run)

    def third(j):
        level = levels[j]

        def run(m):
            u_copy(m, level).wait_recv()
            add(m, level, x, y, from_u[m][level])

            @pl.when((level >= z) & has_down)
            def _():
                z_copy(m, level, True).wait_recv()
                add(m, level, x, y, from_low[m][level])

            @pl.when((level <= z) & has_up)
            def _():
                z_copy(m, level, False).wait_recv()
                add(m, level, x, y, from_high[m][level])

            @pl.when(level > z)
            def _():
                z_copy(m, level, True).start()

            @pl.when(level < z)
            def _():
                z_copy(m, level, False).start()

        each(run)

    def pass_lines():
        @pl.loop(1, grid.dp)
        def _(step):
            slot = lax.rem(d + grid.dp - step, grid.dp) * grid.fs + f
            line(d, slot).wait_recv()
            onward(slot, False).start()
            onward(slot, True).start()

    def pass_y():
        @pl.loop(0, grid.dp)
        def _(step):
            slot = lax.rem(d + grid.dp - step, grid.dp) * grid.fs + f_y
            line(d, slot).wait_recv()
            onward(slot, True).start()

    def rows_in():
        own_rows.wait()

        @pl.loop(0, grid.dp)
        def _(step):
            line(d, step * grid.fs + f_side).wait_recv()
            line(d, step * grid.fs + f_far).wait_recv()

    table_rows = table_out.shape[0]
    whole_blocks = table_rows // ROW_BLOCK
    square_mine[...] = jnp.zeros_like(square_mine)

    def fold(values):
        n, lanes = values.shape
        part = jnp.sum(values.reshape(n // 8, 8, lanes), 0)
        total = part[:, :128]
        for at in range(128, lanes, 128):
            total = total + part[:, at : at + 128]
        return total

    def spread(start, size):
        per = rows.shape[1]
        group = 8
        total = jnp.zeros((size, D), jnp.float32)
        for g in range(0, grid.total, group):
            place = start + lax.broadcasted_iota(jnp.int32, (size, group * per), 0)
            wanted = ids[:, g * per : (g + group) * per]
            hot = jnp.where(place == wanted, 1.0, 0.0).astype(jnp.bfloat16)
            total = total + matmul(hot, rows[g : g + group].reshape(group * per, D))
        low = total.astype(jnp.bfloat16)
        table_out[pl.ds(start, size), :] = low
        wide = low.astype(jnp.float32)
        square_mine[8:16, :] += fold(wide * wide)

    def spread_blocks(first_block, last_block):
        @pl.loop(first_block, last_block)
        def _(block):
            spread(pl.multiple_of(block * ROW_BLOCK, ROW_BLOCK), ROW_BLOCK)

    for j in range(tall):
        first(j)
    pass_lines()
    second(0)
    second_own(0)
    second(1)
    second_own(1)
    third(0)
    pass_y()
    second(2)
    second_own(2)
    third(1)
    second(3)
    second_own(3)
    rows_in()
    spread_blocks(0, whole_blocks // 2)
    third(2)
    spread_blocks(whole_blocks // 2, whole_blocks)
    if table_rows % ROW_BLOCK:
        spread(whole_blocks * ROW_BLOCK, table_rows % ROW_BLOCK)
    third(3)

    def give(m):
        wide = acc[m][z, x, y].astype(jnp.float32)
        outs[m][...] = wide
        square_mine[0:8, :] += fold(wide * wide)

    each(give)

    @pl.loop(1, grid.total)
    def _(step):
        square_copy(lax.rem(me + step, grid.total), me).start()

    square_all[me] = square_mine[...]

    @pl.loop(1, grid.total)
    def _(step):
        peer = lax.rem(me + step, grid.total)
        small_copy(peer, peer).wait_recv()

    small_out[...] = jnp.sum(small_all[...], 0)

    for level in levels:
        each(lambda m: side(m, level).wait_send())
        each(lambda m: v_copy(m, level, 0).wait_send())
        each(lambda m: v_copy(m, level, 1).wait_send())
        each(lambda m: u_copy(m, level).wait_send())

        @pl.when(level != z)
        def _():
            each(lambda m: z_copy(m, level, True).wait_send())

    @pl.loop(0, grid.dp)
    def _(step):
        onward(step * grid.fs + f, False).wait_send()
        onward(step * grid.fs + f, True).wait_send()
        onward(step * grid.fs + f_y, True).wait_send()

    @pl.loop(1, grid.dp)
    def _(step):
        line(lax.rem(d + step, grid.dp), me).wait_send()

    @pl.loop(1, grid.total)
    def _(step):
        peer = lax.rem(me + step, grid.total)
        square_copy(peer, peer).wait_recv()
        square_copy(peer, peer).wait_send()
        small_copy(peer, peer).wait_send()

    square_out[...] = jnp.sum(square_all[...], 0)


def finish(srcs, sums, ids, small, vocab_rows, number):
    grid = Grid()
    count = len(srcs)
    tall = grid.tall
    blocks = [src.shape[1:] for src in srcs]
    srcs = [src.reshape((tall, 2, 2, 2) + src.shape[1:]) for src in srcs]
    leads = ((tall, 2, 2), (tall, 2, 2), (tall, 2), (tall,), (tall,), (tall,))
    buffers = [pltpu.VMEM(lead + block, jnp.bfloat16) for lead in leads for block in blocks]
    cap = sums.shape[1]
    buffers += [
        pltpu.VMEM((grid.total, cap, D), jnp.bfloat16),
        pltpu.VMEM((grid.total,) + small.shape, jnp.float32),
        pltpu.VMEM((16, 128), jnp.float32),
        pltpu.VMEM((grid.total, 16, 128), jnp.float32),
    ]
    dma = pltpu.SemaphoreType.DMA
    by_level = dma((count, tall))
    semaphores = [by_level, by_level, by_level, dma((count, tall, 2)), dma((count, tall, 2))] + [by_level] * 5
    by_device = dma((grid.total,))
    semaphores += [dma, dma((grid.dp,)), dma((2, grid.total)), by_device, by_device, by_device, by_device, by_device]
    anywhere, inside = pl.BlockSpec(memory_space=pl.ANY), pl.BlockSpec(memory_space=pltpu.VMEM)
    results = pl.pallas_call(
        functools.partial(finish_kernel, grid, count),
        out_shape=[jax.ShapeDtypeStruct(block, jnp.float32) for block in blocks]
        + [
            jax.ShapeDtypeStruct((vocab_rows, D), jnp.bfloat16),
            jax.ShapeDtypeStruct(small.shape, jnp.float32),
            jax.ShapeDtypeStruct((16, 128), jnp.float32),
        ],
        in_specs=[anywhere] * (count + 1) + [inside] * 2,
        out_specs=[inside] * (count + 3),
        scratch_shapes=buffers + semaphores,
        compiler_params=pltpu.CompilerParams(
            collective_id=number, has_side_effects=True, vmem_limit_bytes=62 * 1024 * 1024
        ),
    )(*srcs, sums, ids.reshape(1, -1), small)
    return (results[:count], *results[count:])


def plain_body(
    token_ids,
    pad_mask,
    hard_negative,
    table,
    table_first,
    table_second,
    attn_in,
    attn_in_first,
    attn_in_second,
    attn_out,
    attn_out_first,
    attn_out_second,
    ffn_in,
    ffn_in_first,
    ffn_in_second,
    ffn_out,
    ffn_out_first,
    ffn_out_second,
    proj_head,
    proj_head_first,
    proj_head_second,
    small_params,
    small_first,
    small_second,
):
    dp_count = lax.axis_size("dp")
    fsdp_count = lax.axis_size("fsdp")
    device_flat = lax.axis_index("dp") * fsdp_count + lax.axis_index("fsdp")
    pairs_here = token_ids.shape[1]
    pairs_total = pairs_here * dp_count * fsdp_count
    seq_count = 2 * pairs_here
    vocab_rows = table.shape[0]
    row_base = lax.axis_index("dp") * vocab_rows
    gain_rows = small_params[: 3 * D].reshape(3, D)
    bias_table = small_params[3 * D : 3 * D + NB * HEADS].reshape(NB, HEADS)
    log_scale = small_params[3 * D + NB * HEADS]
    buckets = jnp.asarray(bucket_table(L, NB).reshape(-1), jnp.int32)
    bucket_hot = (buckets[:, None] == jnp.arange(NB, dtype=jnp.int32)[None, :]).astype(jnp.float32)
    bias_full = (
        jnp.dot(bucket_hot, bias_table, precision=HIGH).reshape(L, L, HEADS).transpose(2, 0, 1)
    )
    mask_rows = pad_mask.reshape(seq_count, L)
    ids_flat = token_ids.reshape(-1)
    table_low = table.astype(jnp.bfloat16)
    ids_all = lax.all_gather(ids_flat, "dp", axis=0, tiled=True)
    picked = ids_all - row_base
    inside = (picked >= 0) & (picked < vocab_rows)
    chosen = jnp.take(table_low, jnp.clip(picked, 0, vocab_rows - 1), axis=0)
    embedded = lax.psum_scatter(
        jnp.where(inside[:, None], chosen.astype(jnp.float32), 0.0).astype(jnp.bfloat16),
        "dp",
        scatter_dimension=0,
        tiled=True,
    ).astype(jnp.float32)
    shards = (
        attn_in.astype(jnp.bfloat16),
        attn_out.astype(jnp.bfloat16),
        ffn_in.astype(jnp.bfloat16),
        ffn_out.astype(jnp.bfloat16),
        proj_head.astype(jnp.bfloat16),
    )
    gathered = (
        lax.all_gather(shards[0], ("dp", "fsdp"), axis=0, tiled=True),
        lax.all_gather(shards[1], ("dp", "fsdp"), axis=0, tiled=True),
        lax.all_gather(shards[2], ("dp", "fsdp"), axis=0, tiled=True),
        lax.all_gather(shards[3], ("dp", "fsdp"), axis=0, tiled=True),
        lax.all_gather(shards[4], ("dp", "fsdp"), axis=0, tiled=True),
    )
    final_rows, kept = layer_forward(embedded, mask_rows, gathered[:4], gain_rows, bias_full)
    normed_three, factor_three = normalize(final_rows, gain_rows[2])
    mask_weight = mask_rows.astype(jnp.float32)[:, :, None]
    counts = jnp.sum(mask_weight, 1)
    pooled = jnp.sum(normed_three.reshape(seq_count, L, D) * mask_weight, 1) / counts
    pooled_low = pooled.astype(jnp.bfloat16)
    projected = matmul(pooled_low, gathered[4])
    proj_factor = lax.rsqrt(jnp.sum(projected * projected, -1, keepdims=True) + EPS)
    unit_rows = projected * proj_factor
    unit_low = unit_rows.astype(jnp.bfloat16)
    mine_query = unit_low[:pairs_here]
    all_pass = lax.all_gather(unit_low[pairs_here:], ("dp", "fsdp"), axis=0, tiled=True)
    similar = matmul_nt(mine_query, all_pass)
    sim_scale = jnp.exp(log_scale)
    columns = jnp.arange(pairs_total, dtype=jnp.int32)
    own_index = device_flat * pairs_here + jnp.arange(pairs_here, dtype=jnp.int32)
    own_mask = (columns[None, :] == own_index[:, None]).astype(jnp.float32)
    negative = (columns[None, :] == hard_negative[:, None]).astype(jnp.float32)
    logits = sim_scale * similar - MARGIN * own_mask
    diagonal = jnp.sum(logits * own_mask, 1)
    hardest = jnp.sum(logits * negative, 1)
    row_max = jnp.max(logits, 1, keepdims=True)
    log_total = row_max + jnp.log(jnp.sum(jnp.exp(logits - row_max), 1, keepdims=True))
    loss_local = jnp.sum(log_total[:, 0] - diagonal + jax.nn.softplus(hardest - diagonal))
    hinge_gate = jax.nn.sigmoid(hardest - diagonal)
    grad_logits = (
        jnp.exp(logits - log_total) - own_mask + hinge_gate[:, None] * (negative - own_mask)
    )
    grad_log_scale = sim_scale * jnp.sum(grad_logits * similar)
    grad_similar = (sim_scale * grad_logits).astype(jnp.bfloat16)
    grad_query = matmul(grad_similar, all_pass).astype(jnp.bfloat16)
    grad_pass_terms = matmul_tn(grad_similar, mine_query)
    grad_pass = lax.psum_scatter(
        grad_pass_terms, ("dp", "fsdp"), scatter_dimension=0, tiled=True
    ).astype(jnp.bfloat16)
    grad_units = jnp.concatenate([grad_query, grad_pass], 0).astype(jnp.float32)
    grad_proj = (
        proj_factor * (grad_units - unit_rows * jnp.sum(grad_units * unit_rows, -1, keepdims=True))
    ).astype(jnp.bfloat16)
    gathered_back = (
        lax.all_gather(shards[0], ("dp", "fsdp"), axis=0, tiled=True),
        lax.all_gather(shards[1], ("dp", "fsdp"), axis=0, tiled=True),
        lax.all_gather(shards[2], ("dp", "fsdp"), axis=0, tiled=True),
        lax.all_gather(shards[3], ("dp", "fsdp"), axis=0, tiled=True),
        lax.all_gather(shards[4], ("dp", "fsdp"), axis=0, tiled=True),
    )
    grad_proj_head = matmul_tn(pooled_low, grad_proj)
    grad_pooled = matmul_nt(grad_proj, gathered_back[4])
    grad_normed = ((grad_pooled / counts)[:, None, :] * mask_weight).reshape(-1, D)
    grad_final, gain_three = normalize_back(grad_normed, final_rows, factor_three, gain_rows[2])
    grad_rows, matrix_grads, gain_one, gain_two, grad_bias = layer_backward(
        grad_final, kept, mask_rows, gathered_back[:4], gain_rows, bias_full
    )
    attn_in_grad, attn_out_grad, ffn_in_grad, ffn_out_grad = matrix_grads
    grad_bias_table = jnp.dot(grad_bias.reshape(HEADS, L * L), bucket_hot, precision=HIGH).T
    small_local = jnp.concatenate(
        [gain_one, gain_two, gain_three, grad_bias_table.reshape(-1), grad_log_scale[None]]
    )
    small_grad = lax.psum(small_local, ("dp", "fsdp"))
    weight_grads = (
        lax.psum_scatter(attn_in_grad, ("dp", "fsdp"), scatter_dimension=0, tiled=True),
        lax.psum_scatter(attn_out_grad, ("dp", "fsdp"), scatter_dimension=0, tiled=True),
        lax.psum_scatter(ffn_in_grad, ("dp", "fsdp"), scatter_dimension=0, tiled=True),
        lax.psum_scatter(ffn_out_grad, ("dp", "fsdp"), scatter_dimension=0, tiled=True),
        lax.psum_scatter(grad_proj_head, ("dp", "fsdp"), scatter_dimension=0, tiled=True),
    )
    rows_back = lax.all_gather(grad_rows.astype(jnp.bfloat16), "dp", axis=0, tiled=True)
    turn_count = dp_count // 4
    block_rows = rows_back.shape[0] // turn_count

    def add_block(running, piece_pair):
        block_grads, block_ids = piece_pair
        local_ids = block_ids - row_base
        inside = (local_ids >= 0) & (local_ids < vocab_rows)
        segment = jnp.where(inside, local_ids, vocab_rows)
        summed = jax.ops.segment_sum(
            block_grads.astype(jnp.float32), segment, num_segments=vocab_rows + 1
        )
        return (running + summed[:vocab_rows], None)

    table_full, _ = lax.scan(
        add_block,
        jnp.zeros((vocab_rows, D), jnp.float32),
        (rows_back.reshape(turn_count, block_rows, D), ids_all.reshape(turn_count, block_rows)),
    )
    table_grad = lax.psum(table_full.astype(jnp.bfloat16), "fsdp").astype(jnp.float32)
    owned = (table_grad,) + tuple(weight_grads)
    squares = jnp.sum(table_grad * table_grad) / fsdp_count
    for gradient in weight_grads:
        squares = squares + jnp.sum(gradient * gradient)
    total_squares, loss_sum = lax.psum((squares, loss_local), ("dp", "fsdp"))
    norm_value = jnp.sqrt(total_squares + jnp.sum(small_grad * small_grad))
    factor = jnp.minimum(1.0, CLIP / (norm_value + 1e-06))
    masters = (table, attn_in, attn_out, ffn_in, ffn_out, proj_head, small_params)
    firsts = (
        table_first,
        attn_in_first,
        attn_out_first,
        ffn_in_first,
        ffn_out_first,
        proj_head_first,
        small_first,
    )
    seconds = (
        table_second,
        attn_in_second,
        attn_out_second,
        ffn_in_second,
        ffn_out_second,
        proj_head_second,
        small_second,
    )
    gradients = owned + (small_grad,)
    results = [loss_sum, norm_value]
    for kind_index in range(7):
        results.extend(
            adam_update(
                masters[kind_index],
                firsts[kind_index],
                seconds[kind_index],
                gradients[kind_index],
                factor,
                RATES[kind_index],
                DECAYS[kind_index],
            )
        )
    return tuple(results)


def fits(mesh):
    return mesh.shape["fsdp"] == 4 and mesh.shape["dp"] == 8


def dense_rows(ids_flat, table, row_base):
    vocab_rows = table.shape[0]
    ids_all = lax.all_gather(ids_flat, "dp", axis=0, tiled=True)
    picked = ids_all - row_base
    inside = (picked >= 0) & (picked < vocab_rows)
    chosen = jnp.take(table.astype(jnp.bfloat16), jnp.clip(picked, 0, vocab_rows - 1), axis=0)
    return lax.psum_scatter(
        jnp.where(inside[:, None], chosen.astype(jnp.float32), 0.0).astype(jnp.bfloat16),
        "dp",
        scatter_dimension=0,
        tiled=True,
    ).astype(jnp.float32)


def dense_table_grad(ids_flat, grad_low, vocab_rows, row_base):
    ids_all = lax.all_gather(ids_flat, "dp", axis=0, tiled=True)
    rows_back = lax.all_gather(grad_low, "dp", axis=0, tiled=True)
    turn_count = lax.axis_size("dp") // 4
    block_rows = rows_back.shape[0] // turn_count

    def add_block(running, piece_pair):
        block_grads, block_ids = piece_pair
        local_ids = block_ids - row_base
        inside = (local_ids >= 0) & (local_ids < vocab_rows)
        segment = jnp.where(inside, local_ids, vocab_rows)
        summed = jax.ops.segment_sum(
            block_grads.astype(jnp.float32), segment, num_segments=vocab_rows + 1
        )
        return (running + summed[:vocab_rows], None)

    table_full, _ = lax.scan(
        add_block,
        jnp.zeros((vocab_rows, D), jnp.float32),
        (rows_back.reshape(turn_count, block_rows, D), ids_all.reshape(turn_count, block_rows)),
    )
    return lax.psum(table_full.astype(jnp.bfloat16), "fsdp")


def once(flag, make, value):
    return lax.while_loop(lambda state: state[0], lambda state: (False, make(state[1])), (flag, value))[1]


def fast_body(
    token_ids,
    pad_mask,
    hard_negative,
    table,
    table_first,
    table_second,
    attn_in,
    attn_in_first,
    attn_in_second,
    attn_out,
    attn_out_first,
    attn_out_second,
    ffn_in,
    ffn_in_first,
    ffn_in_second,
    ffn_out,
    ffn_out_first,
    ffn_out_second,
    proj_head,
    proj_head_first,
    proj_head_second,
    small_params,
    small_first,
    small_second,
):
    dp_count = lax.axis_size("dp")
    fsdp_count = lax.axis_size("fsdp")
    total = dp_count * fsdp_count
    column = lax.axis_index("fsdp")
    device_flat = lax.axis_index("dp") * fsdp_count + column
    pairs_here = token_ids.shape[1]
    pairs_total = pairs_here * total
    seq_count = 2 * pairs_here
    vocab_rows = table.shape[0]
    row_base = lax.axis_index("dp") * vocab_rows
    gain_rows = small_params[: 3 * D].reshape(3, D)
    bias_table = small_params[3 * D : 3 * D + NB * HEADS].reshape(NB, HEADS)
    log_scale = small_params[3 * D + NB * HEADS]
    buckets = jnp.asarray(bucket_table(L, NB).reshape(-1), jnp.int32)
    bucket_hot = (buckets[:, None] == jnp.arange(NB, dtype=jnp.int32)[None, :]).astype(jnp.float32)
    bias_full = (
        jnp.dot(bucket_hot, bias_table, precision=HIGH).reshape(L, L, HEADS).transpose(2, 0, 1)
    )
    mask_rows = pad_mask.reshape(seq_count, L)
    ids_flat = token_ids.reshape(-1)
    tokens = ids_flat.shape[0]

    order = jnp.arange(tokens, dtype=jnp.int32)
    owner = ids_flat // vocab_rows
    earlier = (ids_flat[None, :] == ids_flat[:, None]) & (order[None, :] < order[:, None])
    first = ~jnp.any(earlier, 1)
    below = (owner[None, :] == owner[:, None]) & (ids_flat[None, :] < ids_flat[:, None]) & first[None, :]
    rank = jnp.sum(below.astype(jnp.int32), 1)
    spilled = jnp.any(rank >= CAP)
    slot = jnp.where(rank < CAP, owner * CAP + rank, -1)
    slots = jnp.arange(dp_count * CAP, dtype=jnp.int32)
    lists = jnp.max(
        jnp.where(slot[None, :] == slots[:, None], (ids_flat - owner * vocab_rows)[None, :], -1), 1
    ).reshape(dp_count, 1, 1, CAP)
    lists = jnp.broadcast_to(lists, (dp_count, fsdp_count, 1, CAP)).reshape(total, 1, CAP)
    extra = jnp.zeros((7, 128), jnp.int32)
    extra = extra.at[0, :pairs_here].set(hard_negative).at[1, 0].set(spilled.astype(jnp.int32))
    message = jnp.concatenate([lists, jnp.broadcast_to(extra[None], (total, 7, 128))], 1)
    heard = exchange(message, True, 1)
    asked = heard[:, 0, :]
    negatives = heard[:, 1, :pairs_here].reshape(-1)
    any_spilled = jnp.max(heard[:, 2, 0]) > 0

    mine_asked = lax.dynamic_index_in_dim(
        asked.reshape(dp_count, fsdp_count, CAP), column, 1, keepdims=False
    )
    answers = jnp.take(table, jnp.maximum(mine_asked.reshape(-1), 0), axis=0).astype(jnp.bfloat16)
    shards = (
        attn_in.astype(jnp.bfloat16),
        attn_out.astype(jnp.bfloat16),
        ffn_in.astype(jnp.bfloat16),
        ffn_out.astype(jnp.bfloat16),
        proj_head.astype(jnp.bfloat16),
    )
    gathered, found = gather(shards, answers.reshape(dp_count, CAP, D), 2)
    gathered = [matrix.reshape(-1, matrix.shape[-1]) for matrix in gathered]
    slot_hot = (slot[:, None] == slots[None, :]).astype(jnp.bfloat16)
    embedded = matmul(slot_hot, found.reshape(dp_count * CAP, D))
    embedded = once(any_spilled, lambda _: dense_rows(ids_flat, table, row_base), embedded)

    final_rows, kept = layer_forward(embedded, mask_rows, gathered[:4], gain_rows, bias_full)
    normed_three, factor_three = normalize(final_rows, gain_rows[2])
    mask_weight = mask_rows.astype(jnp.float32)[:, :, None]
    counts = jnp.sum(mask_weight, 1)
    pooled = jnp.sum(normed_three.reshape(seq_count, L, D) * mask_weight, 1) / counts
    pooled_low = pooled.astype(jnp.bfloat16)
    projected = matmul(pooled_low, gathered[4])
    proj_factor = lax.rsqrt(jnp.sum(projected * projected, -1, keepdims=True) + EPS)
    unit_rows = projected * proj_factor
    unit_low = unit_rows.astype(jnp.bfloat16)
    all_units = exchange(unit_low.reshape(2 * seq_count, D // 2), False, 3)
    all_units = all_units.reshape(total, 2, pairs_here, D)
    all_query = all_units[:, 0].reshape(pairs_total, D)
    all_pass = all_units[:, 1].reshape(pairs_total, D)
    similar = matmul_nt(all_query, all_pass)
    sim_scale = jnp.exp(log_scale)
    columns = jnp.arange(pairs_total, dtype=jnp.int32)
    own_mask = (columns[None, :] == columns[:, None]).astype(jnp.float32)
    negative = (columns[None, :] == negatives[:, None]).astype(jnp.float32)
    logits = sim_scale * similar - MARGIN * own_mask
    diagonal = jnp.sum(logits * own_mask, 1)
    hardest = jnp.sum(logits * negative, 1)
    row_max = jnp.max(logits, 1, keepdims=True)
    log_total = row_max + jnp.log(jnp.sum(jnp.exp(logits - row_max), 1, keepdims=True))
    loss_sum = jnp.sum(log_total[:, 0] - diagonal + jax.nn.softplus(hardest - diagonal))
    hinge_gate = jax.nn.sigmoid(hardest - diagonal)
    grad_logits = (
        jnp.exp(logits - log_total) - own_mask + hinge_gate[:, None] * (negative - own_mask)
    )
    grad_log_scale = sim_scale * jnp.sum(grad_logits * similar)
    grad_similar = (sim_scale * grad_logits).astype(jnp.bfloat16)
    own_first = device_flat * pairs_here
    mine_rows = lax.dynamic_slice_in_dim(grad_similar, own_first, pairs_here, 0)
    mine_columns = lax.dynamic_slice_in_dim(grad_similar, own_first, pairs_here, 1)
    grad_query = matmul(mine_rows, all_pass).astype(jnp.bfloat16)
    grad_pass = matmul_tn(mine_columns, all_query).astype(jnp.bfloat16)
    grad_units = jnp.concatenate([grad_query, grad_pass], 0).astype(jnp.float32)
    grad_proj = (
        proj_factor * (grad_units - unit_rows * jnp.sum(grad_units * unit_rows, -1, keepdims=True))
    ).astype(jnp.bfloat16)
    grad_proj_head = matmul_tn(pooled_low, grad_proj)
    grad_pooled = matmul_nt(grad_proj, gathered[4])
    grad_normed = ((grad_pooled / counts)[:, None, :] * mask_weight).reshape(-1, D)
    grad_final, gain_three = normalize_back(grad_normed, final_rows, factor_three, gain_rows[2])
    grad_rows, matrix_grads, gain_one, gain_two, grad_bias = layer_backward(
        grad_final, kept, mask_rows, gathered[:4], gain_rows, bias_full
    )
    grad_bias_table = jnp.dot(grad_bias.reshape(HEADS, L * L), bucket_hot, precision=HIGH).T
    partials = [
        grad.astype(jnp.bfloat16).reshape(total, -1, grad.shape[1])
        for grad in (*matrix_grads, grad_proj_head)
    ]
    small_local = jnp.concatenate([gain_one, gain_two, gain_three, grad_bias_table.reshape(-1)])
    width = -(-small_local.shape[0] // 1024) * 8
    small_local = jnp.pad(small_local, (0, width * 128 - small_local.shape[0]))
    grad_low = grad_rows.astype(jnp.bfloat16)
    slot_sums = matmul_tn(slot_hot, grad_low).astype(jnp.bfloat16).reshape(dp_count, CAP, D)
    weight_grads, table_grad, summed, squares = finish(
        partials, slot_sums, asked.reshape(-1), small_local.reshape(width, 128), vocab_rows, 4
    )
    table_squares = jnp.sum(squares[8:])
    table_grad, table_squares = once(
        any_spilled,
        lambda _: with_squares(dense_table_grad(ids_flat, grad_low, vocab_rows, row_base)),
        (table_grad, table_squares),
    )
    small_size = small_params.shape[0]
    total_squares = jnp.sum(squares[:8]) + table_squares / fsdp_count
    small_grad = jnp.concatenate([summed.reshape(-1)[: small_size - 1], grad_log_scale[None]])
    norm_value = jnp.sqrt(total_squares + jnp.sum(small_grad * small_grad))
    factor = jnp.minimum(1.0, CLIP / (norm_value + 1e-06))
    updates = (
        (table, table_first, table_second, table_grad.astype(jnp.float32)),
        (attn_in, attn_in_first, attn_in_second, weight_grads[0]),
        (attn_out, attn_out_first, attn_out_second, weight_grads[1]),
        (ffn_in, ffn_in_first, ffn_in_second, weight_grads[2]),
        (ffn_out, ffn_out_first, ffn_out_second, weight_grads[3]),
        (proj_head, proj_head_first, proj_head_second, weight_grads[4]),
        (small_params, small_first, small_second, small_grad),
    )
    results = [loss_sum, norm_value]
    for kind_index, arrays in enumerate(updates):
        results.extend(adam_update(*arrays, factor, RATES[kind_index], DECAYS[kind_index]))
    return tuple(results)


def with_squares(table_grad):
    wide = table_grad.astype(jnp.float32)
    return (table_grad, lax.psum(jnp.sum(wide * wide), ("dp", "fsdp")))


def solution(mesh):
    program = fast_body if fits(mesh) else plain_body
    return jax.shard_map(
        program,
        mesh=mesh,
        in_specs=(
            P(None, ("dp", "fsdp"), None),
            P(None, ("dp", "fsdp"), None),
            P(("dp", "fsdp")),
            P("dp", None),
            P("dp", None),
            P("dp", None),
            P(("dp", "fsdp"), None),
            P(("dp", "fsdp"), None),
            P(("dp", "fsdp"), None),
            P(("dp", "fsdp"), None),
            P(("dp", "fsdp"), None),
            P(("dp", "fsdp"), None),
            P(("dp", "fsdp"), None),
            P(("dp", "fsdp"), None),
            P(("dp", "fsdp"), None),
            P(("dp", "fsdp"), None),
            P(("dp", "fsdp"), None),
            P(("dp", "fsdp"), None),
            P(("dp", "fsdp"), None),
            P(("dp", "fsdp"), None),
            P(("dp", "fsdp"), None),
            P(),
            P(),
            P(),
        ),
        out_specs=(
            P(),
            P(),
            P("dp", None),
            P("dp", None),
            P("dp", None),
            P(("dp", "fsdp"), None),
            P(("dp", "fsdp"), None),
            P(("dp", "fsdp"), None),
            P(("dp", "fsdp"), None),
            P(("dp", "fsdp"), None),
            P(("dp", "fsdp"), None),
            P(("dp", "fsdp"), None),
            P(("dp", "fsdp"), None),
            P(("dp", "fsdp"), None),
            P(("dp", "fsdp"), None),
            P(("dp", "fsdp"), None),
            P(("dp", "fsdp"), None),
            P(("dp", "fsdp"), None),
            P(("dp", "fsdp"), None),
            P(("dp", "fsdp"), None),
            P(),
            P(),
            P(),
        ),
        check_vma=False,
    )
```

```python
import functools

import jax
import jax.numpy as jnp
import numpy as np
from jax import lax
from jax.experimental import pallas as pl
from jax.experimental.pallas import tpu as pltpu
from jax.sharding import PartitionSpec as P

D = 768
HEADS = 12
HD = 64
NB = 32
L = 128
STEP = 10


EPS = 1e-06
SCALE = 0.125
MARGIN = 0.2
CLIP = 0.1
BETA_ONE = 0.9
BETA_TWO = 0.99
ADAM_EPS = 1e-08
RATES = (3.0, 0.1, 0.2, 0.1, 0.05, 0.1, 1.0)
DECAYS = (0.001, 0.001, 0.001, 0.001, 0.001, 0.001, 0.0)
HIGH = lax.Precision.HIGHEST
MESH = pl.DeviceIdType.MESH
CAP = 128


def bucket_table(length, count):
    position = np.arange(length)
    relative = position[None, :] - position[:, None]
    half = count // 2
    base_part = (relative > 0).astype(np.int64) * half
    distance = np.abs(relative)
    exact = half // 2
    safe_dist = np.maximum(distance, 1)
    large = exact + (np.log(safe_dist / exact) / np.log(length / exact) * (half - exact)).astype(
        np.int64
    )
    large = np.minimum(large, half - 1)
    return base_part + np.where(distance < exact, distance, large)


def matmul(left_side, right_side):
    return jnp.dot(left_side, right_side, preferred_element_type=jnp.float32)


def matmul_tn(left_side, right_side):
    return lax.dot_general(
        left_side, right_side, (((0,), (0,)), ((), ())), preferred_element_type=jnp.float32
    )


def matmul_nt(left_side, right_side):
    return lax.dot_general(
        left_side, right_side, (((1,), (1,)), ((), ())), preferred_element_type=jnp.float32
    )


def normalize(inputs, gain_row):
    factor = lax.rsqrt(jnp.mean(inputs * inputs, -1, keepdims=True) + EPS)
    return (inputs * factor * gain_row, factor)


def normalize_back(grad_out, inputs, factor, gain_row):
    scaled = grad_out * gain_row
    grad_gain = jnp.sum(grad_out * inputs * factor, 0)
    grad_in = factor * (
        scaled - inputs * factor * factor * jnp.mean(scaled * inputs, -1, keepdims=True)
    )
    return (grad_in, grad_gain)


def attention_scores(mixed_proj, mask_rows, bias_full):
    keep_add = jnp.where(mask_rows > 0, 0.0, -1000000000.0).astype(jnp.float32)
    scores = jnp.einsum(
        "bqhd,bkhd->bhqk",
        mixed_proj[:, :, 0],
        mixed_proj[:, :, 1],
        preferred_element_type=jnp.float32,
    )
    return scores * SCALE + bias_full[None] + keep_add[:, None, None, :]


def layer_forward(token_rows, mask_rows, weights, gain_rows, bias_full):
    attn_in, attn_out, ffn_in, ffn_out = weights
    seq_count, length = mask_rows.shape
    width = token_rows.shape[1]
    normed_one, factor_one = normalize(token_rows, gain_rows[0])
    act_one = normed_one.astype(jnp.bfloat16)
    mixed_proj = (
        matmul(act_one, attn_in).astype(jnp.bfloat16).reshape(seq_count, length, 3, HEADS, HD)
    )
    scores = attention_scores(mixed_proj, mask_rows, bias_full)
    row_max = jnp.max(scores, -1, keepdims=True)
    log_total = row_max + jnp.log(jnp.sum(jnp.exp(scores - row_max), -1, keepdims=True))
    prob_low = jnp.exp(scores - log_total).astype(jnp.bfloat16)
    attended = jnp.einsum(
        "bhqk,bkhd->bqhd", prob_low, mixed_proj[:, :, 2], preferred_element_type=jnp.float32
    )
    attended = attended.astype(jnp.bfloat16).reshape(-1, width)
    after_attn = token_rows + matmul(attended, attn_out)
    normed_two, factor_two = normalize(after_attn, gain_rows[1])
    act_two = normed_two.astype(jnp.bfloat16)
    pre_act = matmul(act_two, ffn_in)
    hidden = jax.nn.gelu(pre_act).astype(jnp.bfloat16)
    final_rows = after_attn + matmul(hidden, ffn_out)
    kept = (
        token_rows,
        factor_one,
        act_one,
        mixed_proj,
        log_total,
        attended,
        after_attn,
        factor_two,
        act_two,
        pre_act,
        hidden,
    )
    return (final_rows, kept)


def layer_backward(grad_final, kept, mask_rows, weights, gain_rows, bias_full):
    (
        token_rows,
        factor_one,
        act_one,
        mixed_proj,
        log_total,
        attended,
        after_attn,
        factor_two,
        act_two,
        pre_act,
        hidden,
    ) = kept
    attn_in, attn_out, ffn_in, ffn_out = weights
    seq_count, length = mask_rows.shape
    branch = grad_final.astype(jnp.bfloat16)
    grad_ffn_out = matmul_tn(hidden, branch)
    grad_hidden = matmul_nt(branch, ffn_out)
    _, gelu_pull = jax.vjp(jax.nn.gelu, pre_act)
    grad_pre = gelu_pull(grad_hidden)[0].astype(jnp.bfloat16)
    grad_ffn_in = matmul_tn(act_two, grad_pre)
    grad_act_two = matmul_nt(grad_pre, ffn_in)
    grad_mid, gain_two = normalize_back(grad_act_two, after_attn, factor_two, gain_rows[1])
    grad_after = grad_final + grad_mid
    branch = grad_after.astype(jnp.bfloat16)
    grad_attn_out = matmul_tn(attended, branch)
    grad_attended = (
        matmul_nt(branch, attn_out).astype(jnp.bfloat16).reshape(seq_count, length, HEADS, HD)
    )
    scores = attention_scores(mixed_proj, mask_rows, bias_full)
    prob_full = jnp.exp(scores - log_total)
    prob_low = prob_full.astype(jnp.bfloat16)
    queries = mixed_proj[:, :, 0]
    key_rows = mixed_proj[:, :, 1]
    grad_probs = jnp.einsum(
        "bqhd,bkhd->bhqk", grad_attended, mixed_proj[:, :, 2], preferred_element_type=jnp.float32
    )
    grad_values = jnp.einsum(
        "bhqk,bqhd->bkhd", prob_low, grad_attended, preferred_element_type=jnp.float32
    )
    grad_scores = prob_full * (grad_probs - jnp.sum(prob_full * grad_probs, -1, keepdims=True))
    grad_scores = grad_scores.astype(jnp.bfloat16)
    grad_bias = jnp.sum(grad_scores, 0, dtype=jnp.float32)
    grad_queries = (
        jnp.einsum("bhqk,bkhd->bqhd", grad_scores, key_rows, preferred_element_type=jnp.float32)
        * SCALE
    )
    grad_keys = (
        jnp.einsum("bhqk,bqhd->bkhd", grad_scores, queries, preferred_element_type=jnp.float32)
        * SCALE
    )
    grad_mixed = (
        jnp.stack([grad_queries, grad_keys, grad_values], 2)
        .astype(jnp.bfloat16)
        .reshape(seq_count * length, -1)
    )
    grad_attn_in = matmul_tn(act_one, grad_mixed)
    grad_act_one = matmul_nt(grad_mixed, attn_in)
    grad_low, gain_one = normalize_back(grad_act_one, token_rows, factor_one, gain_rows[0])
    grad_rows = grad_after + grad_low
    return (
        grad_rows,
        (grad_attn_in, grad_attn_out, grad_ffn_in, grad_ffn_out),
        gain_one,
        gain_two,
        grad_bias,
    )


def adam_update(param, first_moment, second_moment, gradient, factor, rate, decay):
    clipped = gradient * factor
    first_new = BETA_ONE * first_moment + (1.0 - BETA_ONE) * clipped
    second_new = BETA_TWO * second_moment + (1.0 - BETA_TWO) * clipped * clipped
    direction = (
        first_new
        / (1.0 - BETA_ONE**STEP)
        / (jnp.sqrt(second_new / (1.0 - BETA_TWO**STEP)) + ADAM_EPS)
    )
    return (first_new, second_new, param - rate * (direction + decay * param))


class Grid:
    def __init__(self):
        self.dp, self.fs = lax.axis_size("dp"), lax.axis_size("fsdp")
        self.total = self.dp * self.fs
        self.wide = self.fs // 2
        self.tall = self.dp // self.wide

    def here(self):
        d, f = lax.axis_index("dp"), lax.axis_index("fsdp")
        return d // self.wide, lax.rem(d, self.wide), f // 2, lax.rem(f, 2)

    def device(self, z, x, y, core):
        return (z * self.wide + x, y * 2 + core)

    def flat(self, z, x, y, core):
        return (z * self.wide + x) * self.fs + y * 2 + core

    def peer(self, index):
        return (index // self.fs, lax.rem(index, self.fs))


def greet(device, when=None):
    barrier = pltpu.get_barrier_semaphore()

    def signal():
        pl.semaphore_signal(barrier, inc=1, device_id=device, device_id_type=MESH)

    if when is None:
        signal()
    else:
        pl.when(when)(signal)


def meet(count):
    pl.semaphore_wait(pltpu.get_barrier_semaphore(), count)


def exchange_kernel(grid, spread, src, out, send_sem, recv_sem, own_sem):
    me = lax.axis_index("dp") * grid.fs + lax.axis_index("fsdp")
    own = pltpu.make_async_copy(src.at[me] if spread else src, out.at[me], own_sem)
    own.start()

    @pl.loop(1, grid.total)
    def _(step):
        greet(grid.peer(lax.rem(me + step, grid.total)))

    meet(count=grid.total - 1)

    def copy(peer, slot):
        return pltpu.make_async_remote_copy(
            src_ref=src.at[peer] if spread else src,
            dst_ref=out.at[slot],
            send_sem=send_sem.at[peer],
            recv_sem=recv_sem.at[slot],
            device_id=grid.peer(peer),
            device_id_type=MESH,
        )

    @pl.loop(1, grid.total)
    def _(step):
        copy(lax.rem(me + step, grid.total), me).start()

    own.wait()

    @pl.loop(1, grid.total)
    def _(step):
        peer = lax.rem(me + step, grid.total)
        copy(peer, peer).wait_recv()
        copy(peer, peer).wait_send()


def exchange(src, spread, number):
    grid = Grid()
    block = src.shape[1:] if spread else src.shape
    return pl.pallas_call(
        functools.partial(exchange_kernel, grid, spread),
        out_shape=jax.ShapeDtypeStruct((grid.total,) + block, src.dtype),
        in_specs=[pl.BlockSpec(memory_space=pltpu.VMEM)],
        out_specs=pl.BlockSpec(memory_space=pltpu.VMEM),
        scratch_shapes=[
            pltpu.SemaphoreType.DMA((grid.total,)),
            pltpu.SemaphoreType.DMA((grid.total,)),
            pltpu.SemaphoreType.DMA,
        ],
        compiler_params=pltpu.CompilerParams(collective_id=number, has_side_effects=True),
    )(src)


def gather_kernel(grid, count, *refs):
    srcs, rows, outs, got_rows = refs[:count], refs[count], refs[count + 1 : 2 * count + 1], refs[2 * count + 1]
    send_sem, recv_sem, own_sem, row_send, row_recv, row_own = refs[2 * count + 2 :]
    z, x, y, core = grid.here()
    tall = grid.tall
    d, f = lax.axis_index("dp"), lax.axis_index("fsdp")
    ux, uy = lax.rem(x + 1 - core, 2), lax.rem(y + core, 2)
    vx, vy = lax.rem(x + core, 2), lax.rem(y + 1 - core, 2)
    up, down = grid.device(z + 1, x, y, core), grid.device(z - 1, x, y, core)
    u_device, v_device = grid.device(z, ux, uy, core), grid.device(z, vx, vy, core)
    sibling = grid.device(z, x, y, 1 - core)
    has_up, has_down = z < tall - 1, z > 0
    me = grid.flat(z, x, y, core)
    local = [pltpu.make_async_copy(srcs[m], outs[m].at[me], own_sem.at[m]) for m in range(count)]
    local.append(pltpu.make_async_copy(rows.at[d], got_rows.at[d], row_own))
    for item in local:
        item.start()

    @pl.loop(1, grid.dp)
    def _(step):
        greet((lax.rem(d + step, grid.dp), f))

    greet(v_device)
    greet(sibling)
    greet(u_device)
    meet(count=grid.dp + 2)

    def row_copy(peer, slot):
        return pltpu.make_async_remote_copy(
            src_ref=rows.at[peer],
            dst_ref=got_rows.at[slot],
            send_sem=row_send.at[peer],
            recv_sem=row_recv.at[slot],
            device_id=(peer, f),
            device_id_type=MESH,
        )

    def copy(m, shard, device, way, own):
        return pltpu.make_async_remote_copy(
            src_ref=srcs[m] if own else outs[m].at[shard],
            dst_ref=outs[m].at[shard],
            send_sem=send_sem.at[way, m, shard],
            recv_sem=recv_sem.at[m, shard],
            device_id=device,
            device_id_type=MESH,
        )

    def send(shard, device, way, own=False):
        for m in range(count):
            copy(m, shard, device, way, own).start()

    def arrived(shard):
        for m in range(count):
            copy(m, shard, sibling, 4, False).wait_recv()

    def sent(shard, device, way):
        for m in range(count):
            copy(m, shard, device, way, False).wait_send()

    @pl.when(has_up)
    def _():
        send(me, up, 0, True)

    @pl.when(has_down)
    def _():
        send(me, down, 1, True)

    send(me, u_device, 2, True)
    send(me, v_device, 3, True)
    send(me, sibling, 4, True)

    @pl.loop(1, grid.dp)
    def _(step):
        row_copy(lax.rem(d + step, grid.dp), d).start()

    def pass_z(k):
        low, high = z - k, z + k

        @pl.when(low >= 0)
        def _():
            shard = grid.flat(low, x, y, core)
            arrived(shard)

            @pl.when(has_up)
            def _():
                send(shard, up, 0)

            send(shard, u_device, 2)
            send(shard, v_device, 3)
            send(shard, sibling, 4)

        @pl.when(high < tall)
        def _():
            shard = grid.flat(high, x, y, core)
            arrived(shard)

            @pl.when(has_down)
            def _():
                send(shard, down, 1)

            send(shard, u_device, 2)
            send(shard, v_device, 3)
            send(shard, sibling, 4)

    def both(k, action):
        pl.when(z - k >= 0)(lambda: action(z - k))
        if k:
            pl.when(z + k < tall)(lambda: action(z + k))

    def pass_u(level):
        shard = grid.flat(level, ux, uy, core)
        arrived(shard)
        send(shard, v_device, 3)
        send(shard, sibling, 4)

    def pass_v(level):
        shard = grid.flat(level, vx, vy, core)
        arrived(shard)
        send(shard, sibling, 4)

    def pass_far(level):
        shard = grid.flat(level, 1 - x, 1 - y, core)
        arrived(shard)
        send(shard, sibling, 4)

    for k in range(tall + 1):
        if 0 < k < tall:
            pass_z(k)
        if k < tall:
            both(k, pass_u)
            both(k, pass_v)
        if k:
            both(k - 1, pass_far)

    @pl.loop(1, grid.dp)
    def _(step):
        peer = lax.rem(d + step, grid.dp)
        row_copy(peer, peer).wait_recv()
        row_copy(peer, peer).wait_send()

    @pl.loop(0, tall)
    def _(level):
        for xx in range(2):
            for yy in range(2):
                arrived(grid.flat(level, xx, yy, 1 - core))
                sent(grid.flat(level, xx, yy, core), sibling, 4)
        shard, other = grid.flat(level, x, y, core), grid.flat(level, ux, uy, core)

        @pl.when((level <= z) & has_up)
        def _():
            sent(shard, up, 0)

        @pl.when((level >= z) & has_down)
        def _():
            sent(shard, down, 1)

        sent(shard, u_device, 2)
        sent(shard, v_device, 3)
        sent(other, v_device, 3)

    for item in local:
        item.wait()


def gather(srcs, rows, number):
    grid = Grid()
    count = len(srcs)
    anywhere = pl.BlockSpec(memory_space=pl.ANY)
    results = pl.pallas_call(
        functools.partial(gather_kernel, grid, count),
        out_shape=[jax.ShapeDtypeStruct((grid.total,) + src.shape, src.dtype) for src in srcs]
        + [jax.ShapeDtypeStruct(rows.shape, rows.dtype)],
        in_specs=[anywhere] * (count + 1),
        out_specs=[anywhere] * (count + 1),
        scratch_shapes=[
            pltpu.SemaphoreType.DMA((5, count, grid.total)),
            pltpu.SemaphoreType.DMA((count, grid.total)),
            pltpu.SemaphoreType.DMA((count,)),
            pltpu.SemaphoreType.DMA((grid.dp,)),
            pltpu.SemaphoreType.DMA((grid.dp,)),
            pltpu.SemaphoreType.DMA,
        ],
        compiler_params=pltpu.CompilerParams(collective_id=number, has_side_effects=True),
    )(*srcs, rows)
    return (results[:count], results[count])


ROW_BLOCK = 512


def finish_kernel(grid, count, *refs):
    srcs, (sums, ids, small) = refs[:count], refs[count : count + 3]
    refs = refs[count + 3 :]
    outs, (table_out, small_out, square_out) = refs[:count], refs[count : count + 3]
    refs = refs[count + 3 :]
    acc, from_side, from_v, from_u, from_low, from_high = [
        refs[k * count : (k + 1) * count] for k in range(6)
    ]
    refs = refs[6 * count :]
    rows, small_all, square_mine, square_all = refs[:4]
    load_sem, side_send, side_recv, v_send, v_recv, u_send, u_recv, z_send, low_recv, high_recv = refs[4:14]
    row_own, line_send, on_send, row_recv, small_send, small_recv, square_send, square_recv = refs[14:]
    z, x, y, core = grid.here()
    tall = grid.tall
    d, f = lax.axis_index("dp"), lax.axis_index("fsdp")
    me = d * grid.fs + f
    up, down = grid.device(z + 1, x, y, core), grid.device(z - 1, x, y, core)
    has_up, has_down = z < tall - 1, z > 0
    ux, uy = lax.rem(x + 1 - core, 2), lax.rem(y + core, 2)
    vx, vy = lax.rem(x + core, 2), lax.rem(y + 1 - core, 2)
    u_device, v_device = grid.device(z, ux, uy, core), grid.device(z, vx, vy, core)
    sibling = grid.device(z, x, y, 1 - core)
    f_side = y * 2 + 1 - core
    f_y = (1 - y) * 2 + core
    f_far = (1 - y) * 2 + 1 - core

    @pl.loop(1, grid.total)
    def _(step):
        greet(grid.peer(lax.rem(me + step, grid.total)))

    def each(action):
        for m in range(count):
            action(m)

    def level_of(j):
        tables = []
        for own in range(tall):
            tables.append(sorted(range(tall), key=lambda level: (-abs(level - own), -level))[j])
        value = tables[0]
        for own in range(1, tall):
            value = jnp.where(z == own, tables[own], value)
        return value

    def load(m, level):
        return pltpu.make_async_copy(
            srcs[m].at[level, :, :, core], acc[m].at[level], load_sem.at[m, level]
        )

    def side(m, level):
        return pltpu.make_async_remote_copy(
            src_ref=srcs[m].at[level, :, :, 1 - core],
            dst_ref=from_side[m].at[level],
            send_sem=side_send.at[m, level],
            recv_sem=side_recv.at[m, level],
            device_id=sibling,
            device_id_type=MESH,
        )

    def v_copy(m, level, along_u):
        xx, yy = (1 - x, 1 - y) if along_u else (vx, vy)
        return pltpu.make_async_remote_copy(
            src_ref=acc[m].at[level, xx, yy],
            dst_ref=from_v[m].at[level, along_u],
            send_sem=v_send.at[m, level, along_u],
            recv_sem=v_recv.at[m, level, along_u],
            device_id=v_device,
            device_id_type=MESH,
        )

    def u_copy(m, level):
        return pltpu.make_async_remote_copy(
            src_ref=acc[m].at[level, ux, uy],
            dst_ref=from_u[m].at[level],
            send_sem=u_send.at[m, level],
            recv_sem=u_recv.at[m, level],
            device_id=u_device,
            device_id_type=MESH,
        )

    def z_copy(m, level, upward):
        return pltpu.make_async_remote_copy(
            src_ref=acc[m].at[level, x, y],
            dst_ref=(from_low if upward else from_high)[m].at[level],
            send_sem=z_send.at[m, level],
            recv_sem=(low_recv if upward else high_recv).at[m, level],
            device_id=up if upward else down,
            device_id_type=MESH,
        )

    def line(peer, slot):
        return pltpu.make_async_remote_copy(
            src_ref=sums.at[peer],
            dst_ref=rows.at[slot],
            send_sem=line_send.at[peer],
            recv_sem=row_recv.at[slot],
            device_id=(peer, f),
            device_id_type=MESH,
        )

    def onward(slot, to_side, own_block=False):
        return pltpu.make_async_remote_copy(
            src_ref=sums.at[d] if own_block else rows.at[slot],
            dst_ref=rows.at[slot],
            send_sem=on_send.at[1 if to_side else 0, slot],
            recv_sem=row_recv.at[slot],
            device_id=(d, f_side if to_side else f_y),
            device_id_type=MESH,
        )

    def small_copy(peer, slot):
        return pltpu.make_async_remote_copy(
            src_ref=small,
            dst_ref=small_all.at[slot],
            send_sem=small_send.at[peer],
            recv_sem=small_recv.at[slot],
            device_id=grid.peer(peer),
            device_id_type=MESH,
        )

    def square_copy(peer, slot):
        return pltpu.make_async_remote_copy(
            src_ref=square_mine,
            dst_ref=square_all.at[slot],
            send_sem=square_send.at[peer],
            recv_sem=square_recv.at[slot],
            device_id=grid.peer(peer),
            device_id_type=MESH,
        )

    levels = [level_of(j) for j in range(tall)]
    own_rows = pltpu.make_async_copy(sums.at[d], rows.at[me], row_own)
    own_rows.start()
    for level in levels:
        each(lambda m: load(m, level).start())
    meet(grid.total - 1)

    @pl.loop(1, grid.dp)
    def _(step):
        line(lax.rem(d + step, grid.dp), me).start()

    for level in levels:
        each(lambda m: side(m, level).start())
    onward(me, False, True).start()
    onward(me, True, True).start()

    @pl.loop(1, grid.total)
    def _(step):
        small_copy(lax.rem(me + step, grid.total), me).start()

    small_all[me] = small[...]

    def first(j):
        level = levels[j]

        def run(m):
            load(m, level).wait()
            side(m, level).wait_recv()
            for xx in range(2):
                for yy in range(2):
                    total = acc[m][level, xx, yy].astype(jnp.float32) + from_side[m][level, xx, yy].astype(jnp.float32)
                    acc[m][level, xx, yy] = total.astype(jnp.bfloat16)
            v_copy(m, level, 1).start()
            v_copy(m, level, 0).start()

        each(run)

    def add(m, level, xx, yy, other):
        total = acc[m][level, xx, yy].astype(jnp.float32) + other.astype(jnp.float32)
        acc[m][level, xx, yy] = total.astype(jnp.bfloat16)

    def second(j):
        level = levels[j]

        def run(m):
            v_copy(m, level, 1).wait_recv()
            add(m, level, ux, uy, from_v[m][level, 1])
            u_copy(m, level).start()

        each(run)

    def second_own(j):
        level = levels[j]

        def run(m):
            v_copy(m, level, 0).wait_recv()
            add(m, level, x, y, from_v[m][level, 0])

        each(run)

    def third(j):
        level = levels[j]

        def run(m):
            u_copy(m, level).wait_recv()
            add(m, level, x, y, from_u[m][level])

            @pl.when((level >= z) & has_down)
            def _():
                z_copy(m, level, True).wait_recv()
                add(m, level, x, y, from_low[m][level])

            @pl.when((level <= z) & has_up)
            def _():
                z_copy(m, level, False).wait_recv()
                add(m, level, x, y, from_high[m][level])

            @pl.when(level > z)
            def _():
                z_copy(m, level, True).start()

            @pl.when(level < z)
            def _():
                z_copy(m, level, False).start()

        each(run)

    def pass_lines():
        @pl.loop(1, grid.dp)
        def _(step):
            slot = lax.rem(d + grid.dp - step, grid.dp) * grid.fs + f
            line(d, slot).wait_recv()
            onward(slot, False).start()
            onward(slot, True).start()

    def pass_y():
        @pl.loop(0, grid.dp)
        def _(step):
            slot = lax.rem(d + grid.dp - step, grid.dp) * grid.fs + f_y
            line(d, slot).wait_recv()
            onward(slot, True).start()

    def rows_in():
        own_rows.wait()

        @pl.loop(0, grid.dp)
        def _(step):
            line(d, step * grid.fs + f_side).wait_recv()
            line(d, step * grid.fs + f_far).wait_recv()

    table_rows = table_out.shape[0]
    whole_blocks = table_rows // ROW_BLOCK
    square_mine[...] = jnp.zeros_like(square_mine)

    def fold(values):
        n, lanes = values.shape
        part = jnp.sum(values.reshape(n // 8, 8, lanes), 0)
        total = part[:, :128]
        for at in range(128, lanes, 128):
            total = total + part[:, at : at + 128]
        return total

    def spread(start, size):
        per = rows.shape[1]
        group = 8
        total = jnp.zeros((size, D), jnp.float32)
        for g in range(0, grid.total, group):
            place = start + lax.broadcasted_iota(jnp.int32, (size, group * per), 0)
            wanted = ids[:, g * per : (g + group) * per]
            hot = jnp.where(place == wanted, 1.0, 0.0).astype(jnp.bfloat16)
            total = total + matmul(hot, rows[g : g + group].reshape(group * per, D))
        low = total.astype(jnp.bfloat16)
        table_out[pl.ds(start, size), :] = low
        wide = low.astype(jnp.float32)
        square_mine[8:16, :] += fold(wide * wide)

    def spread_blocks(first_block, last_block):
        @pl.loop(first_block, last_block)
        def _(block):
            spread(pl.multiple_of(block * ROW_BLOCK, ROW_BLOCK), ROW_BLOCK)

    for j in range(tall):
        first(j)
    pass_lines()
    second(0)
    second_own(0)
    second(1)
    second_own(1)
    third(0)
    pass_y()
    second(2)
    second_own(2)
    third(1)
    second(3)
    second_own(3)
    rows_in()
    spread_blocks(0, whole_blocks // 2)
    third(2)
    spread_blocks(whole_blocks // 2, whole_blocks)
    if table_rows % ROW_BLOCK:
        spread(whole_blocks * ROW_BLOCK, table_rows % ROW_BLOCK)
    third(3)

    def give(m):
        wide = acc[m][z, x, y].astype(jnp.float32)
        outs[m][...] = wide
        square_mine[0:8, :] += fold(wide * wide)

    each(give)

    @pl.loop(1, grid.total)
    def _(step):
        square_copy(lax.rem(me + step, grid.total), me).start()

    square_all[me] = square_mine[...]

    @pl.loop(1, grid.total)
    def _(step):
        peer = lax.rem(me + step, grid.total)
        small_copy(peer, peer).wait_recv()

    small_out[...] = jnp.sum(small_all[...], 0)

    for level in levels:
        each(lambda m: side(m, level).wait_send())
        each(lambda m: v_copy(m, level, 0).wait_send())
        each(lambda m: v_copy(m, level, 1).wait_send())
        each(lambda m: u_copy(m, level).wait_send())

        @pl.when(level != z)
        def _():
            each(lambda m: z_copy(m, level, True).wait_send())

    @pl.loop(0, grid.dp)
    def _(step):
        onward(step * grid.fs + f, False).wait_send()
        onward(step * grid.fs + f, True).wait_send()
        onward(step * grid.fs + f_y, True).wait_send()

    @pl.loop(1, grid.dp)
    def _(step):
        line(lax.rem(d + step, grid.dp), me).wait_send()

    @pl.loop(1, grid.total)
    def _(step):
        peer = lax.rem(me + step, grid.total)
        square_copy(peer, peer).wait_recv()
        square_copy(peer, peer).wait_send()
        small_copy(peer, peer).wait_send()

    square_out[...] = jnp.sum(square_all[...], 0)


def finish(srcs, sums, ids, small, vocab_rows, number):
    grid = Grid()
    count = len(srcs)
    tall = grid.tall
    blocks = [src.shape[1:] for src in srcs]
    srcs = [src.reshape((tall, 2, 2, 2) + src.shape[1:]) for src in srcs]
    leads = ((tall, 2, 2), (tall, 2, 2), (tall, 2), (tall,), (tall,), (tall,))
    buffers = [pltpu.VMEM(lead + block, jnp.bfloat16) for lead in leads for block in blocks]
    cap = sums.shape[1]
    buffers += [
        pltpu.VMEM((grid.total, cap, D), jnp.bfloat16),
        pltpu.VMEM((grid.total,) + small.shape, jnp.float32),
        pltpu.VMEM((16, 128), jnp.float32),
        pltpu.VMEM((grid.total, 16, 128), jnp.float32),
    ]
    dma = pltpu.SemaphoreType.DMA
    by_level = dma((count, tall))
    semaphores = [by_level, by_level, by_level, dma((count, tall, 2)), dma((count, tall, 2))] + [by_level] * 5
    by_device = dma((grid.total,))
    semaphores += [dma, dma((grid.dp,)), dma((2, grid.total)), by_device, by_device, by_device, by_device, by_device]
    anywhere, inside = pl.BlockSpec(memory_space=pl.ANY), pl.BlockSpec(memory_space=pltpu.VMEM)
    results = pl.pallas_call(
        functools.partial(finish_kernel, grid, count),
        out_shape=[jax.ShapeDtypeStruct(block, jnp.float32) for block in blocks]
        + [
            jax.ShapeDtypeStruct((vocab_rows, D), jnp.bfloat16),
            jax.ShapeDtypeStruct(small.shape, jnp.float32),
            jax.ShapeDtypeStruct((16, 128), jnp.float32),
        ],
        in_specs=[anywhere] * (count + 1) + [inside] * 2,
        out_specs=[inside] * (count + 3),
        scratch_shapes=buffers + semaphores,
        compiler_params=pltpu.CompilerParams(
            collective_id=number, has_side_effects=True, vmem_limit_bytes=62 * 1024 * 1024
        ),
    )(*srcs, sums, ids.reshape(1, -1), small)
    return (results[:count], *results[count:])


WIDE = 3 * D
PACKED = WIDE + D + 4 * D + D
TILE_SEQS = 4


def lane_is(shape, low, high):
    lanes = lax.broadcasted_iota(jnp.int32, shape, len(shape) - 1)
    return (lanes >= low) & (lanes < high)


def gelu_parts(t):
    inner = np.float32(np.sqrt(2 / np.pi)) * (t + 0.044715 * (t * t * t))
    tan = jnp.tanh(inner)
    return 0.5 * (1.0 + tan), tan


def forward_kernel(
    x0_ref,
    mask_col_ref,
    gains_ref,
    bias_ref,
    packed_hbm,
    down_hbm,
    mixed_ref,
    attended_ref,
    total_ref,
    after_ref,
    pre_ref,
    final_ref,
    pooled_ref,
    projected_ref,
    packed,
    down,
    load_sem,
):
    step = pl.program_id(0)
    tile_seqs = x0_ref.shape[0] // L
    edges = (0, WIDE, WIDE + D, WIDE + 5 * D, PACKED)

    def load(k):
        if k == 4:
            return pltpu.make_async_copy(down_hbm, down, load_sem.at[k])
        part = pl.ds(edges[k], edges[k + 1] - edges[k])
        return pltpu.make_async_copy(packed_hbm.at[:, part], packed.at[:, part], load_sem.at[k])

    def loaded(k):
        @pl.when(step == 0)
        def _():
            load(k).wait()

    @pl.when(step == 0)
    def _():
        for k in (0, 1, 2, 4, 3):
            load(k).start()

    x0 = x0_ref[...]
    act_one = normalize(x0, gains_ref[0:1, :])[0].astype(jnp.bfloat16)
    loaded(0)
    for at in range(0, WIDE, D):
        mixed_ref[:, at : at + D] = matmul(act_one, packed[:, at : at + D]).astype(jnp.bfloat16)

    zero = jnp.zeros((), jnp.bfloat16)
    for s in range(tile_seqs):
        rows = slice(s * L, (s + 1) * L)
        keep = jnp.where(mask_col_ref[rows, :] > 0, 0.0, -1000000000.0)
        for pair in range(HEADS // 2):
            at = pair * 128
            query = mixed_ref[rows, at : at + 128]
            key = mixed_ref[rows, D + at : D + at + 128]
            value = mixed_ref[rows, 2 * D + at : 2 * D + at + 128]
            mine = lane_is((L, 128), 0, HD)
            keys = jnp.concatenate([jnp.where(mine, key, zero), jnp.where(mine, zero, key)], 0)
            scores = (matmul_nt(keys, query) * SCALE).reshape(2, L, L)
            scores = scores + bias_ref[2 * pair : 2 * pair + 2] + keep[None]
            row_max = jnp.max(scores, 1, keepdims=True)
            powers = jnp.exp(scores - row_max)
            row_sum = jnp.sum(powers, 1, keepdims=True)
            prob = (powers * (1.0 / row_sum)).astype(jnp.bfloat16)
            total_ref[s, 2 * pair : 2 * pair + 2, :] = (row_max + jnp.log(row_sum))[:, 0, :]
            flipped = jnp.transpose(value)
            both = jnp.concatenate([matmul(flipped[:HD], prob[0]), matmul(flipped[HD:], prob[1])], 0)
            both = jnp.transpose(both)
            attended_ref[rows, at : at + 128] = both.astype(jnp.bfloat16)

    loaded(1)
    after = x0 + matmul(attended_ref[...], packed[:, WIDE : WIDE + D])
    after_ref[...] = after
    act_two = normalize(after, gains_ref[1:2, :])[0].astype(jnp.bfloat16)
    loaded(2)
    loaded(4)
    final = after
    for j in range(4):
        at = WIDE + D + j * D
        pre = matmul(act_two, packed[:, at : at + D])
        pre_ref[:, j * D : (j + 1) * D] = pre
        hidden = (pre * gelu_parts(pre)[0]).astype(jnp.bfloat16)
        final = final + matmul(hidden, down[j * D : (j + 1) * D, :])
    final_ref[...] = final
    normed = normalize(final, gains_ref[2:3, :])[0]
    weight = mask_col_ref[...]
    for s in range(tile_seqs):
        rows = slice(s * L, (s + 1) * L)
        count = jnp.sum(weight[rows], 0, keepdims=True)
        row = jnp.sum(normed[rows] * weight[rows], 0, keepdims=True) / count
        pooled_ref[pl.ds(step * tile_seqs + s, 1), :] = row

    @pl.when(step == pl.num_programs(0) - 1)
    def _():
        load(3).wait()
        projected_ref[...] = matmul(pooled_ref[...].astype(jnp.bfloat16), packed[:, PACKED - D :])


def run_forward(x0, mask_col, gains, bias_full, packed, down):
    tokens = x0.shape[0]
    seqs = tokens // L
    tile = TILE_SEQS * L
    steps = tokens // tile

    def rows(width):
        return pl.BlockSpec((tile, width), lambda i: (i, 0))

    def whole(*shape):
        return pl.BlockSpec(shape, lambda i: (0,) * len(shape), pipeline_mode=pl.Buffered(1))

    def kept(width, dtype):
        return jax.ShapeDtypeStruct((tokens, width), dtype)

    anywhere = pl.BlockSpec(memory_space=pl.ANY)
    return pl.pallas_call(
        forward_kernel,
        grid=(steps,),
        out_shape=[
            kept(WIDE, jnp.bfloat16),
            kept(D, jnp.bfloat16),
            jax.ShapeDtypeStruct((seqs, HEADS, L), jnp.float32),
            kept(D, jnp.float32),
            kept(4 * D, jnp.float32),
            kept(D, jnp.float32),
            jax.ShapeDtypeStruct((seqs, D), jnp.float32),
            jax.ShapeDtypeStruct((seqs, D), jnp.float32),
        ],
        in_specs=[
            rows(D),
            rows(1),
            whole(3, D),
            whole(HEADS, L, L),
            anywhere,
            anywhere,
        ],
        out_specs=[rows(WIDE), rows(D), pl.BlockSpec((TILE_SEQS, HEADS, L), lambda i: (i, 0, 0)), rows(D), rows(4 * D), rows(D), whole(seqs, D), whole(seqs, D)],
        scratch_shapes=[
            pltpu.VMEM((D, PACKED), jnp.bfloat16),
            pltpu.VMEM((4 * D, D), jnp.bfloat16),
            pltpu.SemaphoreType.DMA((5,)),
        ],
        compiler_params=pltpu.CompilerParams(vmem_limit_bytes=60 * 1024 * 1024),
    )(x0, mask_col, gains, bias_full, packed, down)


BACK_SEQS = 2


def backward_kernel(
    x0_ref,
    mask_col_ref,
    mixed_ref,
    attended,
    total_ref,
    after_ref,
    pre_hbm,
    final_ref,
    gains_ref,
    bias_ref,
    pooled_ref,
    grad_proj_ref,
    packed_hbm,
    down_hbm,
    rows_ref,
    grad_gains_ref,
    grad_bias_ref,
    grad_packed_hbm,
    grad_down_hbm,
    packed,
    down,
    hidden,
    grad_pre,
    act_one,
    act_two,
    branch_two,
    branch_one,
    grad_mixed,
    grad_pooled,
    stage,
    pre_buffer,
    load_sem,
    store_sem,
    pre_sem,
):
    step = pl.program_id(0)
    tile_seqs = x0_ref.shape[0] // L
    tile = tile_seqs * L
    base = pl.multiple_of(step * tile, tile)
    edges = (0, WIDE, WIDE + D, WIDE + 5 * D, PACKED)

    def load(k):
        if k == 4:
            return pltpu.make_async_copy(down_hbm, down, load_sem.at[k])
        part = pl.ds(edges[k], edges[k + 1] - edges[k])
        to = stage.at[0] if k == 3 else packed.at[:, part]
        return pltpu.make_async_copy(packed_hbm.at[:, part], to, load_sem.at[k])

    def loaded(k):
        @pl.when(step == 0)
        def _():
            load(k).wait()

    def load_pre(number):
        start = pl.multiple_of(number // 4 * tile, tile)
        across = pl.multiple_of(lax.rem(number, 4) * D, D)
        slot = lax.rem(number, 2)
        return pltpu.make_async_copy(
            pre_hbm.at[pl.ds(start, tile), pl.ds(across, D)], pre_buffer.at[slot], pre_sem.at[slot]
        )

    @pl.when(step == 0)
    def _():
        load_pre(0).start()
        for k in (3, 4, 2, 1, 0):
            load(k).start()
        grad_gains_ref[...] = jnp.zeros_like(grad_gains_ref)
        grad_bias_ref[...] = jnp.zeros_like(grad_bias_ref)
        load(3).wait()
        grad_pooled[...] = matmul_nt(grad_proj_ref[...], stage[0])

    def gain_back(k, grad_out, inputs):
        gain = gains_ref[k : k + 1, :]
        factor = lax.rsqrt(jnp.mean(inputs * inputs, -1, keepdims=True) + EPS)
        scaled = grad_out * gain
        grad_gains_ref[k : k + 1, :] += jnp.sum(grad_out * inputs * factor, 0, keepdims=True)
        return factor * (
            scaled - inputs * (factor * factor * jnp.mean(scaled * inputs, -1, keepdims=True))
        )

    rows = pl.ds(base, tile)
    weight = mask_col_ref[...]
    pieces = []
    for s in range(tile_seqs):
        part = weight[s * L : (s + 1) * L]
        count = jnp.sum(part, 0, keepdims=True)
        pieces.append(part * (grad_pooled[pl.ds(step * tile_seqs + s, 1), :] / count))
    grad_final = gain_back(2, jnp.concatenate(pieces, 0), final_ref[...])
    branch = grad_final.astype(jnp.bfloat16)
    branch_two[rows, :] = branch
    loaded(4)
    loaded(2)
    grad_act = jnp.zeros((tile, D), jnp.float32)
    for j in range(4):
        part = slice(j * D, (j + 1) * D)
        grad_hidden = matmul_nt(branch, down[part, :])
        number = step * 4 + j
        pl.when(number + 1 < pl.num_programs(0) * 4)(lambda: load_pre(number + 1).start())
        load_pre(number).wait()
        pre = pre_buffer[j % 2]
        half, tan = gelu_parts(pre)
        hidden[rows, part] = (pre * half).astype(jnp.bfloat16)
        slope = np.float32(np.sqrt(2 / np.pi)) * (1.0 + (3 * 0.044715) * (pre * pre))
        grad_part = (grad_hidden * (half + 0.5 * pre * (1.0 - tan * tan) * slope)).astype(jnp.bfloat16)
        grad_pre[rows, part] = grad_part
        at = WIDE + D + j * D
        grad_act = grad_act + matmul_nt(grad_part, packed[:, at : at + D])
    after = after_ref[...]
    act_two[rows, :] = normalize(after, gains_ref[1:2, :])[0].astype(jnp.bfloat16)
    grad_after = grad_final + gain_back(1, grad_act, after)
    branch = grad_after.astype(jnp.bfloat16)
    branch_one[rows, :] = branch
    loaded(1)
    grad_attended = matmul_nt(branch, packed[:, WIDE : WIDE + D]).astype(jnp.bfloat16)
    zero = jnp.zeros((), jnp.bfloat16)
    mine = lane_is((L, 128), 0, HD)
    for s in range(tile_seqs):
        part = slice(s * L, (s + 1) * L)
        here = pl.ds(pl.multiple_of(base + s * L, L), L)
        keep = jnp.where(weight[part] > 0, 0.0, -1000000000.0)
        for pair in range(HEADS // 2):
            at = pair * 128
            query = mixed_ref[part, at : at + 128]
            key = mixed_ref[part, D + at : D + at + 128]
            value = mixed_ref[part, 2 * D + at : 2 * D + at + 128]
            grad_out = grad_attended[part, at : at + 128]
            keys = jnp.concatenate([jnp.where(mine, key, zero), jnp.where(mine, zero, key)], 0)
            values = jnp.concatenate([jnp.where(mine, value, zero), jnp.where(mine, zero, value)], 0)
            scores = (matmul_nt(keys, query) * SCALE).reshape(2, L, L)
            scores = scores + bias_ref[2 * pair : 2 * pair + 2] + keep[None]
            prob = jnp.exp(scores - total_ref[s, 2 * pair : 2 * pair + 2, :][:, None, :])
            grad_prob = matmul_nt(values, grad_out).reshape(2, L, L)
            mean = jnp.sum(prob * grad_prob, 1, keepdims=True)
            grad_scores = (prob * (grad_prob - mean)).astype(jnp.bfloat16)
            grad_bias_ref[2 * pair : 2 * pair + 2] += grad_scores.astype(jnp.float32)
            prob_low = prob.astype(jnp.bfloat16)
            flipped = jnp.transpose(key)
            grad_query = jnp.concatenate(
                [matmul(flipped[:HD], grad_scores[0]), matmul(flipped[HD:], grad_scores[1])], 0
            )
            grad_mixed[here, at : at + 128] = (jnp.transpose(grad_query) * SCALE).astype(jnp.bfloat16)
            grad_keys = matmul(grad_scores.reshape(2 * L, L), query)
            grad_key = jnp.where(mine, grad_keys[:L], grad_keys[L:]) * SCALE
            grad_mixed[here, D + at : D + at + 128] = grad_key.astype(jnp.bfloat16)
            grad_values = matmul(prob_low.reshape(2 * L, L), grad_out)
            grad_value = jnp.where(mine, grad_values[:L], grad_values[L:])
            grad_mixed[here, 2 * D + at : 2 * D + at + 128] = grad_value.astype(jnp.bfloat16)
    loaded(0)
    x0 = x0_ref[...]
    act_one[rows, :] = normalize(x0, gains_ref[0:1, :])[0].astype(jnp.bfloat16)
    grad_act = matmul_nt(grad_mixed[rows, :], packed[:, :WIDE])
    rows_ref[...] = (grad_after + gain_back(0, grad_act, x0)).astype(jnp.bfloat16)

    @pl.when(step == pl.num_programs(0) - 1)
    def _():
        jobs = []
        for j in range(4):
            part = slice(j * D, (j + 1) * D)
            jobs.append((hidden, part, branch_two, slice(0, D), grad_down_hbm.at[pl.ds(j * D, D), :]))
        for j in range(4):
            part = slice(j * D, (j + 1) * D)
            jobs.append((act_two, slice(0, D), grad_pre, part, grad_packed_hbm.at[:, pl.ds(WIDE + D + j * D, D)]))
        jobs.append((attended, slice(0, D), branch_one, slice(0, D), grad_packed_hbm.at[:, pl.ds(WIDE, D)]))
        for j in range(3):
            part = slice(j * D, (j + 1) * D)
            jobs.append((act_one, slice(0, D), grad_mixed, part, grad_packed_hbm.at[:, pl.ds(j * D, D)]))
        copies = []
        for number, (left, left_part, right, right_part, to) in enumerate(jobs):
            slot = number % 2
            if number >= 2:
                copies[number - 2].wait()
            stage[slot] = matmul_tn(left[:, left_part], right[:, right_part]).astype(jnp.bfloat16)
            copies.append(pltpu.make_async_copy(stage.at[slot], to, store_sem.at[slot]))
            copies[-1].start()
        copies[-2].wait()
        stage[0] = matmul_tn(pooled_ref[...].astype(jnp.bfloat16), grad_proj_ref[...]).astype(jnp.bfloat16)
        last = pltpu.make_async_copy(stage.at[0], grad_packed_hbm.at[:, pl.ds(PACKED - D, D)], store_sem.at[0])
        last.start()
        copies[-1].wait()
        last.wait()


def run_backward(
    x0, mask_col, mixed, attended, totals, after, pre, final, gains, bias_full, pooled, grad_proj, packed, down
):
    tokens = x0.shape[0]
    seqs = tokens // L
    tile = BACK_SEQS * L
    steps = tokens // tile

    def rows(width, **mode):
        return pl.BlockSpec((tile, width), lambda i: (i, 0), **mode)

    def whole(*shape):
        return pl.BlockSpec(shape, lambda i: (0,) * len(shape), pipeline_mode=pl.Buffered(1))

    def low(*shape):
        return pltpu.VMEM(shape, jnp.bfloat16)

    anywhere = pl.BlockSpec(memory_space=pl.ANY)
    return pl.pallas_call(
        backward_kernel,
        grid=(steps,),
        out_shape=[
            jax.ShapeDtypeStruct((tokens, D), jnp.bfloat16),
            jax.ShapeDtypeStruct((3, D), jnp.float32),
            jax.ShapeDtypeStruct((HEADS, L, L), jnp.float32),
            jax.ShapeDtypeStruct(packed.shape, jnp.bfloat16),
            jax.ShapeDtypeStruct(down.shape, jnp.bfloat16),
        ],
        in_specs=[
            rows(D),
            rows(1),
            rows(WIDE),
            whole(tokens, D),
            pl.BlockSpec((BACK_SEQS, HEADS, L), lambda i: (i, 0, 0)),
            rows(D),
            anywhere,
            rows(D),
            whole(3, D),
            whole(HEADS, L, L),
            whole(seqs, D),
            whole(seqs, D),
            anywhere,
            anywhere,
        ],
        out_specs=[rows(D), whole(3, D), whole(HEADS, L, L), anywhere, anywhere],
        scratch_shapes=[
            low(D, PACKED - D),
            low(4 * D, D),
            low(tokens, 4 * D),
            low(tokens, 4 * D),
            low(tokens, D),
            low(tokens, D),
            low(tokens, D),
            low(tokens, D),
            low(tokens, WIDE),
            pltpu.VMEM((seqs, D), jnp.float32),
            low(2, D, D),
            pltpu.VMEM((2, tile, D), jnp.float32),
            pltpu.SemaphoreType.DMA((5,)),
            pltpu.SemaphoreType.DMA((2,)),
            pltpu.SemaphoreType.DMA((2,)),
        ],
        compiler_params=pltpu.CompilerParams(vmem_limit_bytes=62 * 1024 * 1024),
    )(x0, mask_col, mixed, attended, totals, after, pre, final, gains, bias_full, pooled, grad_proj, packed, down)


def loss_kernel(
    grid, pairs_here, projected_ref, target_ref, scale_ref, grad_ref, loss_ref, mine, others, grads, send_sem, recv_sem
):
    me = lax.axis_index("dp") * grid.fs + lax.axis_index("fsdp")
    each = 2 * pairs_here
    half = D // 2

    @pl.loop(1, grid.total)
    def _(step):
        greet(grid.peer(lax.rem(me + step, grid.total)))

    projected = projected_ref[...]
    factor = lax.rsqrt(jnp.sum(projected * projected, -1, keepdims=True) + EPS)
    unit = projected * factor
    mine[...] = jnp.concatenate([unit[:, :half], unit[:, half:]], 0).astype(jnp.bfloat16)
    meet(grid.total - 1)

    def copy(peer, slot):
        return pltpu.make_async_remote_copy(
            src_ref=mine,
            dst_ref=others.at[slot],
            send_sem=send_sem.at[peer],
            recv_sem=recv_sem.at[slot],
            device_id=grid.peer(peer),
            device_id_type=MESH,
        )

    @pl.loop(1, grid.total)
    def _(step):
        copy(lax.rem(me + step, grid.total), me).start()

    others[me] = mine[...]

    @pl.loop(1, grid.total)
    def _(step):
        peer = lax.rem(me + step, grid.total)
        copy(peer, peer).wait_recv()

    count = grid.total * each
    wide = others[...].astype(jnp.float32)
    units = jnp.concatenate(
        [wide[:, :each].reshape(count, half), wide[:, each:].reshape(count, half)], 1
    ).astype(jnp.bfloat16)
    similar = matmul_nt(units, units)
    row = lax.broadcasted_iota(jnp.int32, (count, count), 0)
    column = lax.broadcasted_iota(jnp.int32, (count, count), 1)
    used = (lax.rem(row, each) < pairs_here) & (lax.rem(column, each) >= pairs_here)
    own = used & (column == row + pairs_here)
    negative = used & (column == target_ref[...])
    sim_scale = jnp.exp(scale_ref[...])
    own_mask = jnp.where(own, 1.0, 0.0)
    negative_mask = jnp.where(negative, 1.0, 0.0)
    logits = sim_scale * similar - MARGIN * own_mask
    diagonal = jnp.sum(logits * own_mask, 1, keepdims=True)
    hardest = jnp.sum(logits * negative_mask, 1, keepdims=True)
    row_max = jnp.max(jnp.where(used, logits, -3e38), 1, keepdims=True)
    powers = jnp.where(used, jnp.exp(jnp.minimum(logits - row_max, 0.0)), 0.0)
    row_sum = jnp.sum(powers, 1, keepdims=True)
    is_query = lax.rem(lax.broadcasted_iota(jnp.int32, (count, 1), 0), each) < pairs_here
    gap = hardest - diagonal
    softplus = jnp.maximum(gap, 0.0) + jnp.log(1.0 + jnp.exp(-jnp.abs(gap)))
    row_sum = jnp.where(is_query, row_sum, 1.0)
    losses = jnp.where(is_query, row_max + jnp.log(row_sum) - diagonal + softplus, 0.0)
    gate = 1.0 / (1.0 + jnp.exp(-gap))
    grad_logits = jnp.where(
        used, powers / row_sum - own_mask + gate * (negative_mask - own_mask), 0.0
    )
    loss_ref[0:1, :] = jnp.broadcast_to(jnp.sum(losses, 0, keepdims=True), (1, 128))
    grad_scale = sim_scale * jnp.sum(
        jnp.sum(grad_logits * similar, 1, keepdims=True), 0, keepdims=True
    )
    loss_ref[1:2, :] = jnp.broadcast_to(grad_scale, (1, 128))
    loss_ref[2:8, :] = jnp.zeros((6, 128), jnp.float32)
    grad_similar = sim_scale * grad_logits
    grads[...] = grad_similar + jnp.transpose(grad_similar)
    first = pl.multiple_of(me * each, each)
    grad_units = matmul(grads[pl.ds(first, each), :].astype(jnp.bfloat16), units)
    grad_units = grad_units.astype(jnp.bfloat16).astype(jnp.float32)
    grad_ref[...] = (
        factor * (grad_units - unit * jnp.sum(grad_units * unit, -1, keepdims=True))
    ).astype(jnp.bfloat16)

    @pl.loop(1, grid.total)
    def _(step):
        peer = lax.rem(me + step, grid.total)
        copy(peer, peer).wait_send()


def run_loss(projected, target, log_scale, number):
    grid = Grid()
    each = projected.shape[0]
    count = grid.total * each
    inside = pl.BlockSpec(memory_space=pltpu.VMEM)
    dma = pltpu.SemaphoreType.DMA((grid.total,))
    return pl.pallas_call(
        functools.partial(loss_kernel, grid, each // 2),
        out_shape=[
            jax.ShapeDtypeStruct((each, D), jnp.bfloat16),
            jax.ShapeDtypeStruct((8, 128), jnp.float32),
        ],
        in_specs=[inside] * 3,
        out_specs=[inside] * 2,
        scratch_shapes=[
            pltpu.VMEM((2 * each, D // 2), jnp.bfloat16),
            pltpu.VMEM((grid.total, 2 * each, D // 2), jnp.bfloat16),
            pltpu.VMEM((count, count), jnp.float32),
            dma,
            dma,
        ],
        compiler_params=pltpu.CompilerParams(collective_id=number, has_side_effects=True),
    )(projected, target, log_scale)


def plain_body(
    token_ids,
    pad_mask,
    hard_negative,
    table,
    table_first,
    table_second,
    attn_in,
    attn_in_first,
    attn_in_second,
    attn_out,
    attn_out_first,
    attn_out_second,
    ffn_in,
    ffn_in_first,
    ffn_in_second,
    ffn_out,
    ffn_out_first,
    ffn_out_second,
    proj_head,
    proj_head_first,
    proj_head_second,
    small_params,
    small_first,
    small_second,
):
    dp_count = lax.axis_size("dp")
    fsdp_count = lax.axis_size("fsdp")
    device_flat = lax.axis_index("dp") * fsdp_count + lax.axis_index("fsdp")
    pairs_here = token_ids.shape[1]
    pairs_total = pairs_here * dp_count * fsdp_count
    seq_count = 2 * pairs_here
    vocab_rows = table.shape[0]
    row_base = lax.axis_index("dp") * vocab_rows
    gain_rows = small_params[: 3 * D].reshape(3, D)
    bias_table = small_params[3 * D : 3 * D + NB * HEADS].reshape(NB, HEADS)
    log_scale = small_params[3 * D + NB * HEADS]
    buckets = jnp.asarray(bucket_table(L, NB).reshape(-1), jnp.int32)
    bucket_hot = (buckets[:, None] == jnp.arange(NB, dtype=jnp.int32)[None, :]).astype(jnp.float32)
    bias_full = (
        jnp.dot(bucket_hot, bias_table, precision=HIGH).reshape(L, L, HEADS).transpose(2, 0, 1)
    )
    mask_rows = pad_mask.reshape(seq_count, L)
    ids_flat = token_ids.reshape(-1)
    table_low = table.astype(jnp.bfloat16)
    ids_all = lax.all_gather(ids_flat, "dp", axis=0, tiled=True)
    picked = ids_all - row_base
    inside = (picked >= 0) & (picked < vocab_rows)
    chosen = jnp.take(table_low, jnp.clip(picked, 0, vocab_rows - 1), axis=0)
    embedded = lax.psum_scatter(
        jnp.where(inside[:, None], chosen.astype(jnp.float32), 0.0).astype(jnp.bfloat16),
        "dp",
        scatter_dimension=0,
        tiled=True,
    ).astype(jnp.float32)
    shards = (
        attn_in.astype(jnp.bfloat16),
        attn_out.astype(jnp.bfloat16),
        ffn_in.astype(jnp.bfloat16),
        ffn_out.astype(jnp.bfloat16),
        proj_head.astype(jnp.bfloat16),
    )
    gathered = (
        lax.all_gather(shards[0], ("dp", "fsdp"), axis=0, tiled=True),
        lax.all_gather(shards[1], ("dp", "fsdp"), axis=0, tiled=True),
        lax.all_gather(shards[2], ("dp", "fsdp"), axis=0, tiled=True),
        lax.all_gather(shards[3], ("dp", "fsdp"), axis=0, tiled=True),
        lax.all_gather(shards[4], ("dp", "fsdp"), axis=0, tiled=True),
    )
    final_rows, kept = layer_forward(embedded, mask_rows, gathered[:4], gain_rows, bias_full)
    normed_three, factor_three = normalize(final_rows, gain_rows[2])
    mask_weight = mask_rows.astype(jnp.float32)[:, :, None]
    counts = jnp.sum(mask_weight, 1)
    pooled = jnp.sum(normed_three.reshape(seq_count, L, D) * mask_weight, 1) / counts
    pooled_low = pooled.astype(jnp.bfloat16)
    projected = matmul(pooled_low, gathered[4])
    proj_factor = lax.rsqrt(jnp.sum(projected * projected, -1, keepdims=True) + EPS)
    unit_rows = projected * proj_factor
    unit_low = unit_rows.astype(jnp.bfloat16)
    mine_query = unit_low[:pairs_here]
    all_pass = lax.all_gather(unit_low[pairs_here:], ("dp", "fsdp"), axis=0, tiled=True)
    similar = matmul_nt(mine_query, all_pass)
    sim_scale = jnp.exp(log_scale)
    columns = jnp.arange(pairs_total, dtype=jnp.int32)
    own_index = device_flat * pairs_here + jnp.arange(pairs_here, dtype=jnp.int32)
    own_mask = (columns[None, :] == own_index[:, None]).astype(jnp.float32)
    negative = (columns[None, :] == hard_negative[:, None]).astype(jnp.float32)
    logits = sim_scale * similar - MARGIN * own_mask
    diagonal = jnp.sum(logits * own_mask, 1)
    hardest = jnp.sum(logits * negative, 1)
    row_max = jnp.max(logits, 1, keepdims=True)
    log_total = row_max + jnp.log(jnp.sum(jnp.exp(logits - row_max), 1, keepdims=True))
    loss_local = jnp.sum(log_total[:, 0] - diagonal + jax.nn.softplus(hardest - diagonal))
    hinge_gate = jax.nn.sigmoid(hardest - diagonal)
    grad_logits = (
        jnp.exp(logits - log_total) - own_mask + hinge_gate[:, None] * (negative - own_mask)
    )
    grad_log_scale = sim_scale * jnp.sum(grad_logits * similar)
    grad_similar = (sim_scale * grad_logits).astype(jnp.bfloat16)
    grad_query = matmul(grad_similar, all_pass).astype(jnp.bfloat16)
    grad_pass_terms = matmul_tn(grad_similar, mine_query)
    grad_pass = lax.psum_scatter(
        grad_pass_terms, ("dp", "fsdp"), scatter_dimension=0, tiled=True
    ).astype(jnp.bfloat16)
    grad_units = jnp.concatenate([grad_query, grad_pass], 0).astype(jnp.float32)
    grad_proj = (
        proj_factor * (grad_units - unit_rows * jnp.sum(grad_units * unit_rows, -1, keepdims=True))
    ).astype(jnp.bfloat16)
    gathered_back = (
        lax.all_gather(shards[0], ("dp", "fsdp"), axis=0, tiled=True),
        lax.all_gather(shards[1], ("dp", "fsdp"), axis=0, tiled=True),
        lax.all_gather(shards[2], ("dp", "fsdp"), axis=0, tiled=True),
        lax.all_gather(shards[3], ("dp", "fsdp"), axis=0, tiled=True),
        lax.all_gather(shards[4], ("dp", "fsdp"), axis=0, tiled=True),
    )
    grad_proj_head = matmul_tn(pooled_low, grad_proj)
    grad_pooled = matmul_nt(grad_proj, gathered_back[4])
    grad_normed = ((grad_pooled / counts)[:, None, :] * mask_weight).reshape(-1, D)
    grad_final, gain_three = normalize_back(grad_normed, final_rows, factor_three, gain_rows[2])
    grad_rows, matrix_grads, gain_one, gain_two, grad_bias = layer_backward(
        grad_final, kept, mask_rows, gathered_back[:4], gain_rows, bias_full
    )
    attn_in_grad, attn_out_grad, ffn_in_grad, ffn_out_grad = matrix_grads
    grad_bias_table = jnp.dot(grad_bias.reshape(HEADS, L * L), bucket_hot, precision=HIGH).T
    small_local = jnp.concatenate(
        [gain_one, gain_two, gain_three, grad_bias_table.reshape(-1), grad_log_scale[None]]
    )
    small_grad = lax.psum(small_local, ("dp", "fsdp"))
    weight_grads = (
        lax.psum_scatter(attn_in_grad, ("dp", "fsdp"), scatter_dimension=0, tiled=True),
        lax.psum_scatter(attn_out_grad, ("dp", "fsdp"), scatter_dimension=0, tiled=True),
        lax.psum_scatter(ffn_in_grad, ("dp", "fsdp"), scatter_dimension=0, tiled=True),
        lax.psum_scatter(ffn_out_grad, ("dp", "fsdp"), scatter_dimension=0, tiled=True),
        lax.psum_scatter(grad_proj_head, ("dp", "fsdp"), scatter_dimension=0, tiled=True),
    )
    rows_back = lax.all_gather(grad_rows.astype(jnp.bfloat16), "dp", axis=0, tiled=True)
    turn_count = dp_count // 4
    block_rows = rows_back.shape[0] // turn_count

    def add_block(running, piece_pair):
        block_grads, block_ids = piece_pair
        local_ids = block_ids - row_base
        inside = (local_ids >= 0) & (local_ids < vocab_rows)
        segment = jnp.where(inside, local_ids, vocab_rows)
        summed = jax.ops.segment_sum(
            block_grads.astype(jnp.float32), segment, num_segments=vocab_rows + 1
        )
        return (running + summed[:vocab_rows], None)

    table_full, _ = lax.scan(
        add_block,
        jnp.zeros((vocab_rows, D), jnp.float32),
        (rows_back.reshape(turn_count, block_rows, D), ids_all.reshape(turn_count, block_rows)),
    )
    table_grad = lax.psum(table_full.astype(jnp.bfloat16), "fsdp").astype(jnp.float32)
    owned = (table_grad,) + tuple(weight_grads)
    squares = jnp.sum(table_grad * table_grad) / fsdp_count
    for gradient in weight_grads:
        squares = squares + jnp.sum(gradient * gradient)
    total_squares, loss_sum = lax.psum((squares, loss_local), ("dp", "fsdp"))
    norm_value = jnp.sqrt(total_squares + jnp.sum(small_grad * small_grad))
    factor = jnp.minimum(1.0, CLIP / (norm_value + 1e-06))
    masters = (table, attn_in, attn_out, ffn_in, ffn_out, proj_head, small_params)
    firsts = (
        table_first,
        attn_in_first,
        attn_out_first,
        ffn_in_first,
        ffn_out_first,
        proj_head_first,
        small_first,
    )
    seconds = (
        table_second,
        attn_in_second,
        attn_out_second,
        ffn_in_second,
        ffn_out_second,
        proj_head_second,
        small_second,
    )
    gradients = owned + (small_grad,)
    results = [loss_sum, norm_value]
    for kind_index in range(7):
        results.extend(
            adam_update(
                masters[kind_index],
                firsts[kind_index],
                seconds[kind_index],
                gradients[kind_index],
                factor,
                RATES[kind_index],
                DECAYS[kind_index],
            )
        )
    return tuple(results)


def fits(mesh):
    return mesh.shape["fsdp"] == 4 and mesh.shape["dp"] == 8


def dense_rows(ids_flat, table, row_base):
    vocab_rows = table.shape[0]
    ids_all = lax.all_gather(ids_flat, "dp", axis=0, tiled=True)
    picked = ids_all - row_base
    inside = (picked >= 0) & (picked < vocab_rows)
    chosen = jnp.take(table.astype(jnp.bfloat16), jnp.clip(picked, 0, vocab_rows - 1), axis=0)
    return lax.psum_scatter(
        jnp.where(inside[:, None], chosen.astype(jnp.float32), 0.0).astype(jnp.bfloat16),
        "dp",
        scatter_dimension=0,
        tiled=True,
    ).astype(jnp.float32)


def dense_table_grad(ids_flat, grad_low, vocab_rows, row_base):
    ids_all = lax.all_gather(ids_flat, "dp", axis=0, tiled=True)
    rows_back = lax.all_gather(grad_low, "dp", axis=0, tiled=True)
    turn_count = lax.axis_size("dp") // 4
    block_rows = rows_back.shape[0] // turn_count

    def add_block(running, piece_pair):
        block_grads, block_ids = piece_pair
        local_ids = block_ids - row_base
        inside = (local_ids >= 0) & (local_ids < vocab_rows)
        segment = jnp.where(inside, local_ids, vocab_rows)
        summed = jax.ops.segment_sum(
            block_grads.astype(jnp.float32), segment, num_segments=vocab_rows + 1
        )
        return (running + summed[:vocab_rows], None)

    table_full, _ = lax.scan(
        add_block,
        jnp.zeros((vocab_rows, D), jnp.float32),
        (rows_back.reshape(turn_count, block_rows, D), ids_all.reshape(turn_count, block_rows)),
    )
    return lax.psum(table_full.astype(jnp.bfloat16), "fsdp")


def once(flag, make, value):
    return lax.while_loop(lambda state: state[0], lambda state: (False, make(state[1])), (flag, value))[1]


def fast_body(
    token_ids,
    pad_mask,
    hard_negative,
    table,
    table_first,
    table_second,
    attn_in,
    attn_in_first,
    attn_in_second,
    attn_out,
    attn_out_first,
    attn_out_second,
    ffn_in,
    ffn_in_first,
    ffn_in_second,
    ffn_out,
    ffn_out_first,
    ffn_out_second,
    proj_head,
    proj_head_first,
    proj_head_second,
    small_params,
    small_first,
    small_second,
):
    dp_count = lax.axis_size("dp")
    fsdp_count = lax.axis_size("fsdp")
    total = dp_count * fsdp_count
    column = lax.axis_index("fsdp")
    device_flat = lax.axis_index("dp") * fsdp_count + column
    pairs_here = token_ids.shape[1]
    pairs_total = pairs_here * total
    seq_count = 2 * pairs_here
    vocab_rows = table.shape[0]
    row_base = lax.axis_index("dp") * vocab_rows
    gain_rows = small_params[: 3 * D].reshape(3, D)
    bias_table = small_params[3 * D : 3 * D + NB * HEADS].reshape(NB, HEADS)
    log_scale = small_params[3 * D + NB * HEADS]
    buckets = jnp.asarray(bucket_table(L, NB).T.reshape(-1), jnp.int32)
    bucket_hot = (buckets[:, None] == jnp.arange(NB, dtype=jnp.int32)[None, :]).astype(jnp.float32)
    bias_full = (
        jnp.dot(bucket_hot, bias_table, precision=HIGH).reshape(L, L, HEADS).transpose(2, 0, 1)
    )
    mask_rows = pad_mask.reshape(seq_count, L)
    ids_flat = token_ids.reshape(-1)
    tokens = ids_flat.shape[0]

    order = jnp.arange(tokens, dtype=jnp.int32)
    owner = ids_flat // vocab_rows
    earlier = (ids_flat[None, :] == ids_flat[:, None]) & (order[None, :] < order[:, None])
    first = ~jnp.any(earlier, 1)
    below = (owner[None, :] == owner[:, None]) & (ids_flat[None, :] < ids_flat[:, None]) & first[None, :]
    rank = jnp.sum(below.astype(jnp.int32), 1)
    spilled = jnp.any(rank >= CAP)
    slot = jnp.where(rank < CAP, owner * CAP + rank, -1)
    slots = jnp.arange(dp_count * CAP, dtype=jnp.int32)
    lists = jnp.max(
        jnp.where(slot[None, :] == slots[:, None], (ids_flat - owner * vocab_rows)[None, :], -1), 1
    ).reshape(dp_count, 1, 1, CAP)
    lists = jnp.broadcast_to(lists, (dp_count, fsdp_count, 1, CAP)).reshape(total, 1, CAP)
    extra = jnp.zeros((7, 128), jnp.int32)
    extra = extra.at[0, :pairs_here].set(hard_negative).at[1, 0].set(spilled.astype(jnp.int32))
    message = jnp.concatenate([lists, jnp.broadcast_to(extra[None], (total, 7, 128))], 1)
    heard = exchange(message, True, 1)
    asked = heard[:, 0, :]
    negatives = heard[:, 1, :pairs_here].reshape(-1)
    any_spilled = jnp.max(heard[:, 2, 0]) > 0

    mine_asked = lax.dynamic_index_in_dim(
        asked.reshape(dp_count, fsdp_count, CAP), column, 1, keepdims=False
    )
    answers = jnp.take(table, jnp.maximum(mine_asked.reshape(-1), 0), axis=0).astype(jnp.bfloat16)
    shards = (
        jnp.concatenate([attn_in, attn_out, ffn_in, proj_head], 1).astype(jnp.bfloat16),
        ffn_out.astype(jnp.bfloat16),
    )
    gathered, found = gather(shards, answers.reshape(dp_count, CAP, D), 2)
    packed, down = [matrix.reshape(-1, matrix.shape[-1]) for matrix in gathered]
    slot_hot = (slot[:, None] == slots[None, :]).astype(jnp.bfloat16)
    embedded = matmul(slot_hot, found.reshape(dp_count * CAP, D))
    embedded = once(any_spilled, lambda _: dense_rows(ids_flat, table, row_base), embedded)

    mask_col = mask_rows.astype(jnp.float32).reshape(tokens, 1)
    *kept, pooled, projected = run_forward(embedded, mask_col, gain_rows, bias_full, packed, down)
    target = negatives // pairs_here * seq_count + pairs_here + negatives % pairs_here
    target = jnp.concatenate(
        [target.reshape(total, pairs_here), jnp.full((total, pairs_here), -1, jnp.int32)], 1
    ).reshape(-1, 1)
    grad_proj, loss_parts = run_loss(projected, target, log_scale.reshape(1, 1), 3)
    loss_sum, grad_log_scale = loss_parts[0, 0], loss_parts[1, 0]
    grad_low, grad_gains, grad_bias, grad_packed, grad_down = run_backward(
        embedded, mask_col, *kept, gain_rows, bias_full, pooled, grad_proj, packed, down
    )
    grad_bias_table = jnp.dot(grad_bias.reshape(HEADS, L * L), bucket_hot, precision=HIGH).T
    partials = [grad.reshape(total, -1, grad.shape[1]) for grad in (grad_packed, grad_down)]
    small_local = jnp.concatenate([grad_gains.reshape(-1), grad_bias_table.reshape(-1)])
    width = -(-small_local.shape[0] // 1024) * 8
    small_local = jnp.pad(small_local, (0, width * 128 - small_local.shape[0]))
    slot_sums = matmul_tn(slot_hot, grad_low).astype(jnp.bfloat16).reshape(dp_count, CAP, D)
    weight_grads, table_grad, summed, squares = finish(
        partials, slot_sums, asked.reshape(-1), small_local.reshape(width, 128), vocab_rows, 4
    )
    table_squares = jnp.sum(squares[8:])
    table_grad, table_squares = once(
        any_spilled,
        lambda _: with_squares(dense_table_grad(ids_flat, grad_low, vocab_rows, row_base)),
        (table_grad, table_squares),
    )
    small_size = small_params.shape[0]
    total_squares = jnp.sum(squares[:8]) + table_squares / fsdp_count
    small_grad = jnp.concatenate([summed.reshape(-1)[: small_size - 1], grad_log_scale[None]])
    norm_value = jnp.sqrt(total_squares + jnp.sum(small_grad * small_grad))
    factor = jnp.minimum(1.0, CLIP / (norm_value + 1e-06))
    grad_in, grad_out, grad_up, grad_head = jnp.split(
        weight_grads[0], (WIDE, WIDE + D, WIDE + 5 * D), 1
    )
    updates = (
        (table, table_first, table_second, table_grad.astype(jnp.float32)),
        (attn_in, attn_in_first, attn_in_second, grad_in),
        (attn_out, attn_out_first, attn_out_second, grad_out),
        (ffn_in, ffn_in_first, ffn_in_second, grad_up),
        (ffn_out, ffn_out_first, ffn_out_second, weight_grads[1]),
        (proj_head, proj_head_first, proj_head_second, grad_head),
        (small_params, small_first, small_second, small_grad),
    )
    results = [loss_sum, norm_value]
    for kind_index, arrays in enumerate(updates):
        results.extend(adam_update(*arrays, factor, RATES[kind_index], DECAYS[kind_index]))
    return tuple(results)


def with_squares(table_grad):
    wide = table_grad.astype(jnp.float32)
    return (table_grad, lax.psum(jnp.sum(wide * wide), ("dp", "fsdp")))


def solution(mesh):
    program = fast_body if fits(mesh) else plain_body
    return jax.shard_map(
        program,
        mesh=mesh,
        in_specs=(
            P(None, ("dp", "fsdp"), None),
            P(None, ("dp", "fsdp"), None),
            P(("dp", "fsdp")),
            P("dp", None),
            P("dp", None),
            P("dp", None),
            P(("dp", "fsdp"), None),
            P(("dp", "fsdp"), None),
            P(("dp", "fsdp"), None),
            P(("dp", "fsdp"), None),
            P(("dp", "fsdp"), None),
            P(("dp", "fsdp"), None),
            P(("dp", "fsdp"), None),
            P(("dp", "fsdp"), None),
            P(("dp", "fsdp"), None),
            P(("dp", "fsdp"), None),
            P(("dp", "fsdp"), None),
            P(("dp", "fsdp"), None),
            P(("dp", "fsdp"), None),
            P(("dp", "fsdp"), None),
            P(("dp", "fsdp"), None),
            P(),
            P(),
            P(),
        ),
        out_specs=(
            P(),
            P(),
            P("dp", None),
            P("dp", None),
            P("dp", None),
            P(("dp", "fsdp"), None),
            P(("dp", "fsdp"), None),
            P(("dp", "fsdp"), None),
            P(("dp", "fsdp"), None),
            P(("dp", "fsdp"), None),
            P(("dp", "fsdp"), None),
            P(("dp", "fsdp"), None),
            P(("dp", "fsdp"), None),
            P(("dp", "fsdp"), None),
            P(("dp", "fsdp"), None),
            P(("dp", "fsdp"), None),
            P(("dp", "fsdp"), None),
            P(("dp", "fsdp"), None),
            P(("dp", "fsdp"), None),
            P(("dp", "fsdp"), None),
            P(),
            P(),
            P(),
        ),
        check_vma=False,
    )
```

```python
import functools

import jax
import jax.numpy as jnp
import numpy as np
from jax import lax
from jax.experimental import pallas as pl
from jax.experimental.pallas import tpu as pltpu
from jax.sharding import PartitionSpec as P

D = 768
HEADS = 12
HD = 64
NB = 32
L = 128
STEP = 10


EPS = 1e-06
SCALE = 0.125
MARGIN = 0.2
CLIP = 0.1
BETA_ONE = 0.9
BETA_TWO = 0.99
ADAM_EPS = 1e-08
RATES = (3.0, 0.1, 0.2, 0.1, 0.05, 0.1, 1.0)
DECAYS = (0.001, 0.001, 0.001, 0.001, 0.001, 0.001, 0.0)
HIGH = lax.Precision.HIGHEST
MESH = pl.DeviceIdType.MESH
CAP = 112


def bucket_table(length, count):
    position = np.arange(length)
    relative = position[None, :] - position[:, None]
    half = count // 2
    base_part = (relative > 0).astype(np.int64) * half
    distance = np.abs(relative)
    exact = half // 2
    safe_dist = np.maximum(distance, 1)
    large = exact + (np.log(safe_dist / exact) / np.log(length / exact) * (half - exact)).astype(
        np.int64
    )
    large = np.minimum(large, half - 1)
    return base_part + np.where(distance < exact, distance, large)


def matmul(left_side, right_side):
    return jnp.dot(left_side, right_side, preferred_element_type=jnp.float32)


def matmul_tn(left_side, right_side):
    return lax.dot_general(
        left_side, right_side, (((0,), (0,)), ((), ())), preferred_element_type=jnp.float32
    )


def matmul_nt(left_side, right_side):
    return lax.dot_general(
        left_side, right_side, (((1,), (1,)), ((), ())), preferred_element_type=jnp.float32
    )


def normalize(inputs, gain_row):
    factor = lax.rsqrt(jnp.mean(inputs * inputs, -1, keepdims=True) + EPS)
    return (inputs * factor * gain_row, factor)


def normalize_back(grad_out, inputs, factor, gain_row):
    scaled = grad_out * gain_row
    grad_gain = jnp.sum(grad_out * inputs * factor, 0)
    grad_in = factor * (
        scaled - inputs * factor * factor * jnp.mean(scaled * inputs, -1, keepdims=True)
    )
    return (grad_in, grad_gain)


def attention_scores(mixed_proj, mask_rows, bias_full):
    keep_add = jnp.where(mask_rows > 0, 0.0, -1000000000.0).astype(jnp.float32)
    scores = jnp.einsum(
        "bqhd,bkhd->bhqk",
        mixed_proj[:, :, 0],
        mixed_proj[:, :, 1],
        preferred_element_type=jnp.float32,
    )
    return scores * SCALE + bias_full[None] + keep_add[:, None, None, :]


def layer_forward(token_rows, mask_rows, weights, gain_rows, bias_full):
    attn_in, attn_out, ffn_in, ffn_out = weights
    seq_count, length = mask_rows.shape
    width = token_rows.shape[1]
    normed_one, factor_one = normalize(token_rows, gain_rows[0])
    act_one = normed_one.astype(jnp.bfloat16)
    mixed_proj = (
        matmul(act_one, attn_in).astype(jnp.bfloat16).reshape(seq_count, length, 3, HEADS, HD)
    )
    scores = attention_scores(mixed_proj, mask_rows, bias_full)
    row_max = jnp.max(scores, -1, keepdims=True)
    log_total = row_max + jnp.log(jnp.sum(jnp.exp(scores - row_max), -1, keepdims=True))
    prob_low = jnp.exp(scores - log_total).astype(jnp.bfloat16)
    attended = jnp.einsum(
        "bhqk,bkhd->bqhd", prob_low, mixed_proj[:, :, 2], preferred_element_type=jnp.float32
    )
    attended = attended.astype(jnp.bfloat16).reshape(-1, width)
    after_attn = token_rows + matmul(attended, attn_out)
    normed_two, factor_two = normalize(after_attn, gain_rows[1])
    act_two = normed_two.astype(jnp.bfloat16)
    pre_act = matmul(act_two, ffn_in)
    hidden = jax.nn.gelu(pre_act).astype(jnp.bfloat16)
    final_rows = after_attn + matmul(hidden, ffn_out)
    kept = (
        token_rows,
        factor_one,
        act_one,
        mixed_proj,
        log_total,
        attended,
        after_attn,
        factor_two,
        act_two,
        pre_act,
        hidden,
    )
    return (final_rows, kept)


def layer_backward(grad_final, kept, mask_rows, weights, gain_rows, bias_full):
    (
        token_rows,
        factor_one,
        act_one,
        mixed_proj,
        log_total,
        attended,
        after_attn,
        factor_two,
        act_two,
        pre_act,
        hidden,
    ) = kept
    attn_in, attn_out, ffn_in, ffn_out = weights
    seq_count, length = mask_rows.shape
    branch = grad_final.astype(jnp.bfloat16)
    grad_ffn_out = matmul_tn(hidden, branch)
    grad_hidden = matmul_nt(branch, ffn_out)
    _, gelu_pull = jax.vjp(jax.nn.gelu, pre_act)
    grad_pre = gelu_pull(grad_hidden)[0].astype(jnp.bfloat16)
    grad_ffn_in = matmul_tn(act_two, grad_pre)
    grad_act_two = matmul_nt(grad_pre, ffn_in)
    grad_mid, gain_two = normalize_back(grad_act_two, after_attn, factor_two, gain_rows[1])
    grad_after = grad_final + grad_mid
    branch = grad_after.astype(jnp.bfloat16)
    grad_attn_out = matmul_tn(attended, branch)
    grad_attended = (
        matmul_nt(branch, attn_out).astype(jnp.bfloat16).reshape(seq_count, length, HEADS, HD)
    )
    scores = attention_scores(mixed_proj, mask_rows, bias_full)
    prob_full = jnp.exp(scores - log_total)
    prob_low = prob_full.astype(jnp.bfloat16)
    queries = mixed_proj[:, :, 0]
    key_rows = mixed_proj[:, :, 1]
    grad_probs = jnp.einsum(
        "bqhd,bkhd->bhqk", grad_attended, mixed_proj[:, :, 2], preferred_element_type=jnp.float32
    )
    grad_values = jnp.einsum(
        "bhqk,bqhd->bkhd", prob_low, grad_attended, preferred_element_type=jnp.float32
    )
    grad_scores = prob_full * (grad_probs - jnp.sum(prob_full * grad_probs, -1, keepdims=True))
    grad_scores = grad_scores.astype(jnp.bfloat16)
    grad_bias = jnp.sum(grad_scores, 0, dtype=jnp.float32)
    grad_queries = (
        jnp.einsum("bhqk,bkhd->bqhd", grad_scores, key_rows, preferred_element_type=jnp.float32)
        * SCALE
    )
    grad_keys = (
        jnp.einsum("bhqk,bqhd->bkhd", grad_scores, queries, preferred_element_type=jnp.float32)
        * SCALE
    )
    grad_mixed = (
        jnp.stack([grad_queries, grad_keys, grad_values], 2)
        .astype(jnp.bfloat16)
        .reshape(seq_count * length, -1)
    )
    grad_attn_in = matmul_tn(act_one, grad_mixed)
    grad_act_one = matmul_nt(grad_mixed, attn_in)
    grad_low, gain_one = normalize_back(grad_act_one, token_rows, factor_one, gain_rows[0])
    grad_rows = grad_after + grad_low
    return (
        grad_rows,
        (grad_attn_in, grad_attn_out, grad_ffn_in, grad_ffn_out),
        gain_one,
        gain_two,
        grad_bias,
    )


def adam_update(param, first_moment, second_moment, gradient, factor, rate, decay):
    clipped = gradient * factor
    first_new = BETA_ONE * first_moment + (1.0 - BETA_ONE) * clipped
    second_new = BETA_TWO * second_moment + (1.0 - BETA_TWO) * clipped * clipped
    direction = (
        first_new
        / (1.0 - BETA_ONE**STEP)
        / (jnp.sqrt(second_new / (1.0 - BETA_TWO**STEP)) + ADAM_EPS)
    )
    return (first_new, second_new, param - rate * (direction + decay * param))


class Grid:
    def __init__(self):
        self.dp, self.fs = lax.axis_size("dp"), lax.axis_size("fsdp")
        self.total = self.dp * self.fs
        self.wide = self.fs // 2
        self.tall = self.dp // self.wide

    def here(self):
        d, f = lax.axis_index("dp"), lax.axis_index("fsdp")
        return d // self.wide, lax.rem(d, self.wide), f // 2, lax.rem(f, 2)

    def device(self, z, x, y, core):
        return (z * self.wide + x, y * 2 + core)

    def flat(self, z, x, y, core):
        return (z * self.wide + x) * self.fs + y * 2 + core

    def peer(self, index):
        return (index // self.fs, lax.rem(index, self.fs))


def greet(device, when=None):
    barrier = pltpu.get_barrier_semaphore()

    def signal():
        pl.semaphore_signal(barrier, inc=1, device_id=device, device_id_type=MESH)

    if when is None:
        signal()
    else:
        pl.when(when)(signal)


def meet(count):
    pl.semaphore_wait(pltpu.get_barrier_semaphore(), count)


ROW_BLOCK = 512
WIDE = 3 * D
PACKED = WIDE + D + 4 * D + D
TILE_SEQS = 4


def head_kernel(
    grid,
    col_ref,
    row_ref,
    negative_ref,
    in_ref,
    out_ref,
    up_ref,
    proj_ref,
    down_ref,
    table_hbm,
    packed_out,
    down_out,
    heard,
    slot_ref,
    x0_ref,
    packed_mine,
    down_mine,
    table,
    total,
    answers,
    found,
    messages,
    send_sem,
    recv_sem,
    own_sem,
    row_send,
    row_recv,
    note_send,
    note_recv,
    note_on,
    table_sem,
):
    srcs, outs = (packed_mine, down_mine), (packed_out, down_out)
    count = 2
    z, x, y, core = grid.here()
    tall = grid.tall
    d, f = lax.axis_index("dp"), lax.axis_index("fsdp")
    ux, uy = lax.rem(x + 1 - core, 2), lax.rem(y + core, 2)
    vx, vy = lax.rem(x + core, 2), lax.rem(y + 1 - core, 2)
    up, down = grid.device(z + 1, x, y, core), grid.device(z - 1, x, y, core)
    u_device, v_device = grid.device(z, ux, uy, core), grid.device(z, vx, vy, core)
    sibling = grid.device(z, x, y, 1 - core)
    has_up, has_down = z < tall - 1, z > 0
    me = grid.flat(z, x, y, core)
    f_side, f_y, f_far = y * 2 + 1 - core, (1 - y) * 2 + core, (1 - y) * 2 + 1 - core

    @pl.loop(1, grid.dp)
    def _(step):
        greet((lax.rem(d + step, grid.dp), f))

    greet((d, f_y))
    greet(sibling)
    vocab_rows = table_hbm.shape[0]
    fetch = pltpu.make_async_copy(table_hbm, table.at[pl.ds(0, vocab_rows), :], table_sem)
    fetch.start()
    at = 0
    for ref in (in_ref, out_ref, up_ref, proj_ref):
        packed_mine[:, at : at + ref.shape[1]] = ref[...].astype(jnp.bfloat16)
        at += ref.shape[1]
    down_mine[...] = down_ref[...].astype(jnp.bfloat16)
    local = [pltpu.make_async_copy(srcs[m], outs[m].at[me], own_sem.at[m]) for m in range(count)]
    for item in local:
        item.start()
    meet(grid.dp + 1)

    def copy(m, shard, device, way, own):
        return pltpu.make_async_remote_copy(
            src_ref=srcs[m] if own else outs[m].at[shard],
            dst_ref=outs[m].at[shard],
            send_sem=send_sem.at[way, m, shard],
            recv_sem=recv_sem.at[m, shard],
            device_id=device,
            device_id_type=MESH,
        )

    def send(shard, device, way, own=False):
        for m in range(count):
            copy(m, shard, device, way, own).start()

    def arrived(shard):
        for m in range(count):
            copy(m, shard, sibling, 4, False).wait_recv()

    def sent(shard, device, way):
        for m in range(count):
            copy(m, shard, device, way, False).wait_send()

    @pl.when(has_up)
    def _():
        send(me, up, 0, True)

    @pl.when(has_down)
    def _():
        send(me, down, 1, True)

    send(me, u_device, 2, True)
    send(me, v_device, 3, True)
    send(me, sibling, 4, True)

    tokens = col_ref.shape[0]
    chunk = 128
    ids_row = row_ref[...]
    place_row = lax.broadcasted_iota(jnp.int32, (chunk, tokens), 1)
    place_col = lax.broadcasted_iota(jnp.int32, (chunk, tokens), 0)

    def see(step, repeated):
        start = pl.multiple_of(step * chunk, chunk)
        again = (col_ref[pl.ds(start, chunk), :] == ids_row) & (place_col + start < place_row)
        return jnp.maximum(repeated, jnp.max(jnp.where(again, 1.0, 0.0), 0, keepdims=True))

    repeated = lax.fori_loop(0, tokens // chunk, see, jnp.zeros((1, tokens), jnp.float32))
    firsts = jnp.where(repeated > 0.5, -1.0, ids_row)
    lane = lax.broadcasted_iota(jnp.int32, (chunk, 128), 1).astype(jnp.float32)

    def rank_some(step, carry):
        listed, most = carry
        start = pl.multiple_of(step * chunk, chunk)
        ids = col_ref[pl.ds(start, chunk), :]
        owner = jnp.zeros_like(ids)
        for other in range(1, grid.dp):
            owner = owner + jnp.where(ids >= float(other * vocab_rows), 1.0, 0.0)
        first_id = owner * float(vocab_rows)
        rank = jnp.sum(jnp.where((firsts >= first_id) & (firsts < ids), 1.0, 0.0), 1, keepdims=True)
        slot = jnp.where(rank < float(CAP), owner * float(CAP) + rank, -1.0)
        slot_ref[pl.ds(start, chunk), :] = slot
        rows = []
        for other in range(grid.dp):
            hit = (slot == lane + float(other * CAP)) & (lane < float(CAP))
            rows.append(jnp.max(jnp.where(hit, ids - first_id + 1.0, 0.0), 0, keepdims=True))
        return (jnp.maximum(listed, jnp.concatenate(rows, 0)), jnp.maximum(most, jnp.max(rank, 0, keepdims=True)))

    listed, most = lax.fori_loop(
        0,
        tokens // chunk,
        rank_some,
        (jnp.zeros((grid.dp, 128), jnp.float32), jnp.zeros((1, 1), jnp.float32)),
    )
    spilled = jnp.broadcast_to(jnp.where(most >= float(CAP), 1.0, 0.0), (1, 128))
    rest = jnp.concatenate([negative_ref[...], spilled, jnp.zeros((5, 128), jnp.float32)], 0)
    for other in range(grid.dp):
        messages[other] = jnp.concatenate([listed[other : other + 1] - 1.0, rest], 0)

    def note(peer, slot):
        return pltpu.make_async_remote_copy(
            src_ref=messages.at[peer],
            dst_ref=heard.at[slot],
            send_sem=note_send.at[peer],
            recv_sem=note_recv.at[slot],
            device_id=(peer, f),
            device_id_type=MESH,
        )

    def note_onward(slot, to_side):
        return pltpu.make_async_remote_copy(
            src_ref=heard.at[slot],
            dst_ref=heard.at[slot],
            send_sem=note_on.at[1 if to_side else 0, slot],
            recv_sem=note_recv.at[slot],
            device_id=(d, f_side if to_side else f_y),
            device_id_type=MESH,
        )

    @pl.loop(1, grid.dp)
    def _(step):
        note(lax.rem(d + step, grid.dp), me).start()

    heard[me] = messages[d]

    def row_copy(peer, slot):
        return pltpu.make_async_remote_copy(
            src_ref=answers.at[peer],
            dst_ref=found.at[slot],
            send_sem=row_send.at[peer],
            recv_sem=row_recv.at[slot],
            device_id=(peer, f),
            device_id_type=MESH,
        )

    def pass_z(k):
        low, high = z - k, z + k

        @pl.when(low >= 0)
        def _():
            shard = grid.flat(low, x, y, core)
            arrived(shard)

            @pl.when(has_up)
            def _():
                send(shard, up, 0)

            send(shard, u_device, 2)
            send(shard, v_device, 3)
            send(shard, sibling, 4)

        @pl.when(high < tall)
        def _():
            shard = grid.flat(high, x, y, core)
            arrived(shard)

            @pl.when(has_down)
            def _():
                send(shard, down, 1)

            send(shard, u_device, 2)
            send(shard, v_device, 3)
            send(shard, sibling, 4)

    def both(k, action):
        pl.when(z - k >= 0)(lambda: action(z - k))
        if k:
            pl.when(z + k < tall)(lambda: action(z + k))

    def pass_u(level):
        shard = grid.flat(level, ux, uy, core)
        arrived(shard)
        send(shard, v_device, 3)
        send(shard, sibling, 4)

    def pass_v(level):
        shard = grid.flat(level, vx, vy, core)
        arrived(shard)
        send(shard, sibling, 4)

    def pass_far(level):
        shard = grid.flat(level, 1 - x, 1 - y, core)
        arrived(shard)
        send(shard, sibling, 4)

    both(0, pass_u)

    @pl.loop(1, grid.dp)
    def _(step):
        note(d, lax.rem(d + step, grid.dp) * grid.fs + f).wait_recv()

    @pl.loop(0, grid.dp)
    def _(peer):
        note_onward(peer * grid.fs + f, False).start()
        note_onward(peer * grid.fs + f, True).start()

    pass_z(1)
    fetch.wait()
    padding = table.shape[0] - vocab_rows
    if padding:
        table[vocab_rows:, :] = jnp.zeros((padding, D), jnp.float32)
    asked = jnp.concatenate([heard[peer * grid.fs + f, 0:1, :] for peer in range(grid.dp)], 0)
    asked = jnp.transpose(asked)
    block = ROW_BLOCK
    total[...] = jnp.zeros_like(total)
    lanes = lax.broadcasted_iota(jnp.int32, (CAP, block), 1).astype(jnp.float32)

    def pick(step):
        start = pl.multiple_of(step * block, block)
        some = table[pl.ds(start, block), :].astype(jnp.bfloat16)
        wanted = lanes + (step * block).astype(jnp.float32)
        hot = jnp.concatenate(
            [
                jnp.where(asked[:CAP, peer : peer + 1] == wanted, 1.0, 0.0)
                for peer in range(grid.dp)
            ],
            0,
        ).astype(jnp.bfloat16)
        total[...] += matmul(hot, some)

    steps = table.shape[0] // block
    pl.loop(0, steps)(pick)
    answers[...] = total[...].reshape(answers.shape).astype(jnp.bfloat16)
    found[d] = answers[d]

    @pl.loop(1, grid.dp)
    def _(step):
        row_copy(lax.rem(d + step, grid.dp), d).start()

    both(0, pass_v)
    for k in range(1, tall + 1):
        if 1 < k < tall:
            pass_z(k)
        if k < tall:
            both(k, pass_u)
            both(k, pass_v)
        both(k - 1, pass_far)

    @pl.loop(1, grid.dp)
    def _(step):
        row_copy(d, lax.rem(d + step, grid.dp)).wait_recv()

    slots = grid.dp * CAP
    some = tokens // 4
    wide_lane = lax.broadcasted_iota(jnp.int32, (some, slots), 1).astype(jnp.float32)
    rows = found[...].reshape(slots, D)

    @pl.loop(0, 4)
    def _(step):
        start = pl.multiple_of(step * some, some)
        hot = jnp.where(slot_ref[pl.ds(start, some), :] == wide_lane, 1.0, 0.0).astype(jnp.bfloat16)
        x0_ref[pl.ds(start, some), :] = matmul(hot, rows)

    @pl.loop(0, grid.dp)
    def _(peer):
        note(d, peer * grid.fs + f_y).wait_recv()
        note_onward(peer * grid.fs + f_y, True).start()

    @pl.loop(0, grid.dp)
    def _(peer):
        note(d, peer * grid.fs + f_side).wait_recv()
        note(d, peer * grid.fs + f_far).wait_recv()
        note_onward(peer * grid.fs + f, False).wait_send()
        note_onward(peer * grid.fs + f, True).wait_send()
        note_onward(peer * grid.fs + f_y, True).wait_send()

    @pl.loop(1, grid.dp)
    def _(step):
        peer = lax.rem(d + step, grid.dp)
        row_copy(peer, d).wait_send()
        note(peer, me).wait_send()

    @pl.loop(0, tall)
    def _(level):
        for xx in range(2):
            for yy in range(2):
                arrived(grid.flat(level, xx, yy, 1 - core))
                sent(grid.flat(level, xx, yy, core), sibling, 4)
        shard, other = grid.flat(level, x, y, core), grid.flat(level, ux, uy, core)

        @pl.when((level <= z) & has_up)
        def _():
            sent(shard, up, 0)

        @pl.when((level >= z) & has_down)
        def _():
            sent(shard, down, 1)

        sent(shard, u_device, 2)
        sent(shard, v_device, 3)
        sent(other, v_device, 3)

    for item in local:
        item.wait()


def run_head(ids, negatives, attn_in, attn_out, ffn_in, proj_head, ffn_out, table, number):
    grid = Grid()
    tokens = ids.shape[0]
    wide = ids.astype(jnp.float32)
    row = jnp.zeros((1, 128), jnp.float32).at[0, : negatives.shape[0]].set(negatives.astype(jnp.float32))
    shapes = ((attn_in.shape[0], PACKED), ffn_out.shape)
    blocks = -(-table.shape[0] // ROW_BLOCK)
    anywhere, inside = pl.BlockSpec(memory_space=pl.ANY), pl.BlockSpec(memory_space=pltpu.VMEM)
    dma = pltpu.SemaphoreType.DMA
    line, everyone = dma((grid.dp,)), dma((grid.total,))
    return pl.pallas_call(
        functools.partial(head_kernel, grid),
        out_shape=[jax.ShapeDtypeStruct((grid.total,) + shape, jnp.bfloat16) for shape in shapes]
        + [
            jax.ShapeDtypeStruct((grid.total, 8, 128), jnp.float32),
            jax.ShapeDtypeStruct((tokens, 1), jnp.float32),
            jax.ShapeDtypeStruct((tokens, D), jnp.float32),
        ],
        in_specs=[inside] * 8 + [anywhere],
        out_specs=[anywhere] * 2 + [inside] * 3,
        scratch_shapes=[pltpu.VMEM(shape, jnp.bfloat16) for shape in shapes]
        + [
            pltpu.VMEM((blocks * ROW_BLOCK, D), jnp.float32),
            pltpu.VMEM((grid.dp * CAP, D), jnp.float32),
            pltpu.VMEM((grid.dp, CAP, D), jnp.bfloat16),
            pltpu.VMEM((grid.dp, CAP, D), jnp.bfloat16),
            pltpu.VMEM((grid.dp, 8, 128), jnp.float32),
            dma((5, 2, grid.total)),
            dma((2, grid.total)),
            dma((2,)),
            line,
            line,
            line,
            everyone,
            dma((2, grid.total)),
            dma,
        ],
        compiler_params=pltpu.CompilerParams(
            collective_id=number, has_side_effects=True, vmem_limit_bytes=48 * 1024 * 1024
        ),
    )(wide.reshape(tokens, 1), wide.reshape(1, tokens), row, attn_in, attn_out, ffn_in, proj_head, ffn_out, table)


def lane_is(shape, low, high):
    lanes = lax.broadcasted_iota(jnp.int32, shape, len(shape) - 1)
    return (lanes >= low) & (lanes < high)


def gelu_parts(t):
    inner = np.float32(np.sqrt(2 / np.pi)) * (t + 0.044715 * (t * t * t))
    tan = jnp.tanh(inner)
    return 0.5 * (1.0 + tan), tan


def forward_kernel(
    x0_ref,
    mask_col_ref,
    gains_ref,
    bias_ref,
    packed_hbm,
    down_hbm,
    mixed_ref,
    attended_ref,
    total_ref,
    after_ref,
    pre_ref,
    final_ref,
    pooled_ref,
    projected_ref,
    packed,
    down,
    load_sem,
):
    step = pl.program_id(0)
    tile_seqs = x0_ref.shape[0] // L
    edges = (0, WIDE, WIDE + D, WIDE + 5 * D, PACKED)

    def load(k):
        if k == 4:
            return pltpu.make_async_copy(down_hbm, down, load_sem.at[k])
        part = pl.ds(edges[k], edges[k + 1] - edges[k])
        return pltpu.make_async_copy(packed_hbm.at[:, part], packed.at[:, part], load_sem.at[k])

    def loaded(k):
        @pl.when(step == 0)
        def _():
            load(k).wait()

    @pl.when(step == 0)
    def _():
        for k in (0, 1, 2, 4, 3):
            load(k).start()

    x0 = x0_ref[...]
    act_one = normalize(x0, gains_ref[0:1, :])[0].astype(jnp.bfloat16)
    loaded(0)
    for at in range(0, WIDE, D):
        mixed_ref[:, at : at + D] = matmul(act_one, packed[:, at : at + D]).astype(jnp.bfloat16)

    zero = jnp.zeros((), jnp.bfloat16)
    for s in range(tile_seqs):
        rows = slice(s * L, (s + 1) * L)
        keep = jnp.where(mask_col_ref[rows, :] > 0, 0.0, -1000000000.0)
        for pair in range(HEADS // 2):
            at = pair * 128
            query = mixed_ref[rows, at : at + 128]
            key = mixed_ref[rows, D + at : D + at + 128]
            value = mixed_ref[rows, 2 * D + at : 2 * D + at + 128]
            mine = lane_is((L, 128), 0, HD)
            keys = jnp.concatenate([jnp.where(mine, key, zero), jnp.where(mine, zero, key)], 0)
            scores = (matmul_nt(keys, query) * SCALE).reshape(2, L, L)
            scores = scores + bias_ref[2 * pair : 2 * pair + 2] + keep[None]
            row_max = jnp.max(scores, 1, keepdims=True)
            powers = jnp.exp(scores - row_max)
            row_sum = jnp.sum(powers, 1, keepdims=True)
            prob = (powers * (1.0 / row_sum)).astype(jnp.bfloat16)
            total_ref[s, 2 * pair : 2 * pair + 2, :] = (row_max + jnp.log(row_sum))[:, 0, :]
            flipped = jnp.transpose(value)
            both = jnp.concatenate([matmul(flipped[:HD], prob[0]), matmul(flipped[HD:], prob[1])], 0)
            both = jnp.transpose(both)
            attended_ref[rows, at : at + 128] = both.astype(jnp.bfloat16)

    loaded(1)
    after = x0 + matmul(attended_ref[...], packed[:, WIDE : WIDE + D])
    after_ref[...] = after
    act_two = normalize(after, gains_ref[1:2, :])[0].astype(jnp.bfloat16)
    loaded(2)
    loaded(4)
    final = after
    for j in range(4):
        at = WIDE + D + j * D
        pre = matmul(act_two, packed[:, at : at + D])
        pre_ref[:, j * D : (j + 1) * D] = pre
        hidden = (pre * gelu_parts(pre)[0]).astype(jnp.bfloat16)
        final = final + matmul(hidden, down[j * D : (j + 1) * D, :])
    final_ref[...] = final
    normed = normalize(final, gains_ref[2:3, :])[0]
    weight = mask_col_ref[...]
    for s in range(tile_seqs):
        rows = slice(s * L, (s + 1) * L)
        count = jnp.sum(weight[rows], 0, keepdims=True)
        row = jnp.sum(normed[rows] * weight[rows], 0, keepdims=True) / count
        pooled_ref[pl.ds(step * tile_seqs + s, 1), :] = row

    @pl.when(step == pl.num_programs(0) - 1)
    def _():
        load(3).wait()
        projected_ref[...] = matmul(pooled_ref[...].astype(jnp.bfloat16), packed[:, PACKED - D :])


def run_forward(x0, mask_col, gains, bias_full, packed, down):
    tokens = x0.shape[0]
    seqs = tokens // L
    tile = TILE_SEQS * L
    steps = tokens // tile

    def rows(width):
        return pl.BlockSpec((tile, width), lambda i: (i, 0))

    def whole(*shape):
        return pl.BlockSpec(shape, lambda i: (0,) * len(shape), pipeline_mode=pl.Buffered(1))

    def kept(width, dtype):
        return jax.ShapeDtypeStruct((tokens, width), dtype)

    anywhere = pl.BlockSpec(memory_space=pl.ANY)
    return pl.pallas_call(
        forward_kernel,
        grid=(steps,),
        out_shape=[
            kept(WIDE, jnp.bfloat16),
            kept(D, jnp.bfloat16),
            jax.ShapeDtypeStruct((seqs, HEADS, L), jnp.float32),
            kept(D, jnp.float32),
            kept(4 * D, jnp.float32),
            kept(D, jnp.float32),
            jax.ShapeDtypeStruct((seqs, D), jnp.float32),
            jax.ShapeDtypeStruct((seqs, D), jnp.float32),
        ],
        in_specs=[
            rows(D),
            rows(1),
            whole(3, D),
            whole(HEADS, L, L),
            anywhere,
            anywhere,
        ],
        out_specs=[rows(WIDE), rows(D), pl.BlockSpec((TILE_SEQS, HEADS, L), lambda i: (i, 0, 0)), rows(D), rows(4 * D), rows(D), whole(seqs, D), whole(seqs, D)],
        scratch_shapes=[
            pltpu.VMEM((D, PACKED), jnp.bfloat16),
            pltpu.VMEM((4 * D, D), jnp.bfloat16),
            pltpu.SemaphoreType.DMA((5,)),
        ],
        compiler_params=pltpu.CompilerParams(vmem_limit_bytes=60 * 1024 * 1024),
    )(x0, mask_col, gains, bias_full, packed, down)


def loss_kernel(
    grid, pairs_here, projected_ref, target_ref, scale_ref, grad_ref, loss_ref, mine, others, grads, send_sem, recv_sem
):
    me = lax.axis_index("dp") * grid.fs + lax.axis_index("fsdp")
    each = 2 * pairs_here
    half = D // 2

    @pl.loop(1, grid.total)
    def _(step):
        greet(grid.peer(lax.rem(me + step, grid.total)))

    projected = projected_ref[...]
    factor = lax.rsqrt(jnp.sum(projected * projected, -1, keepdims=True) + EPS)
    unit = projected * factor
    mine[...] = jnp.concatenate([unit[:, :half], unit[:, half:]], 0).astype(jnp.bfloat16)
    meet(grid.total - 1)

    def copy(peer, slot):
        return pltpu.make_async_remote_copy(
            src_ref=mine,
            dst_ref=others.at[slot],
            send_sem=send_sem.at[peer],
            recv_sem=recv_sem.at[slot],
            device_id=grid.peer(peer),
            device_id_type=MESH,
        )

    @pl.loop(1, grid.total)
    def _(step):
        copy(lax.rem(me + step, grid.total), me).start()

    others[me] = mine[...]

    @pl.loop(1, grid.total)
    def _(step):
        peer = lax.rem(me + step, grid.total)
        copy(peer, peer).wait_recv()

    count = grid.total * each
    wide = others[...].astype(jnp.float32)
    units = jnp.concatenate(
        [wide[:, :each].reshape(count, half), wide[:, each:].reshape(count, half)], 1
    ).astype(jnp.bfloat16)
    similar = matmul_nt(units, units)
    row = lax.broadcasted_iota(jnp.int32, (count, count), 0)
    column = lax.broadcasted_iota(jnp.int32, (count, count), 1)
    used = (lax.rem(row, each) < pairs_here) & (lax.rem(column, each) >= pairs_here)
    own = used & (column == row + pairs_here)
    negative = used & (column == target_ref[...])
    sim_scale = jnp.exp(scale_ref[...])
    own_mask = jnp.where(own, 1.0, 0.0)
    negative_mask = jnp.where(negative, 1.0, 0.0)
    logits = sim_scale * similar - MARGIN * own_mask
    diagonal = jnp.sum(logits * own_mask, 1, keepdims=True)
    hardest = jnp.sum(logits * negative_mask, 1, keepdims=True)
    row_max = jnp.max(jnp.where(used, logits, -3e38), 1, keepdims=True)
    powers = jnp.where(used, jnp.exp(jnp.minimum(logits - row_max, 0.0)), 0.0)
    row_sum = jnp.sum(powers, 1, keepdims=True)
    is_query = lax.rem(lax.broadcasted_iota(jnp.int32, (count, 1), 0), each) < pairs_here
    gap = hardest - diagonal
    softplus = jnp.maximum(gap, 0.0) + jnp.log(1.0 + jnp.exp(-jnp.abs(gap)))
    row_sum = jnp.where(is_query, row_sum, 1.0)
    losses = jnp.where(is_query, row_max + jnp.log(row_sum) - diagonal + softplus, 0.0)
    gate = 1.0 / (1.0 + jnp.exp(-gap))
    grad_logits = jnp.where(
        used, powers / row_sum - own_mask + gate * (negative_mask - own_mask), 0.0
    )
    loss_ref[0:1, :] = jnp.broadcast_to(jnp.sum(losses, 0, keepdims=True), (1, 128))
    grad_scale = sim_scale * jnp.sum(
        jnp.sum(grad_logits * similar, 1, keepdims=True), 0, keepdims=True
    )
    loss_ref[1:2, :] = jnp.broadcast_to(grad_scale, (1, 128))
    loss_ref[2:8, :] = jnp.zeros((6, 128), jnp.float32)
    grad_similar = sim_scale * grad_logits
    grads[...] = grad_similar + jnp.transpose(grad_similar)
    first = pl.multiple_of(me * each, each)
    grad_units = matmul(grads[pl.ds(first, each), :].astype(jnp.bfloat16), units)
    grad_units = grad_units.astype(jnp.bfloat16).astype(jnp.float32)
    grad_ref[...] = (
        factor * (grad_units - unit * jnp.sum(grad_units * unit, -1, keepdims=True))
    ).astype(jnp.bfloat16)

    @pl.loop(1, grid.total)
    def _(step):
        peer = lax.rem(me + step, grid.total)
        copy(peer, peer).wait_send()


def run_loss(projected, target, log_scale, number):
    grid = Grid()
    each = projected.shape[0]
    count = grid.total * each
    inside = pl.BlockSpec(memory_space=pltpu.VMEM)
    dma = pltpu.SemaphoreType.DMA((grid.total,))
    return pl.pallas_call(
        functools.partial(loss_kernel, grid, each // 2),
        out_shape=[
            jax.ShapeDtypeStruct((each, D), jnp.bfloat16),
            jax.ShapeDtypeStruct((8, 128), jnp.float32),
        ],
        in_specs=[inside] * 3,
        out_specs=[inside] * 2,
        scratch_shapes=[
            pltpu.VMEM((2 * each, D // 2), jnp.bfloat16),
            pltpu.VMEM((grid.total, 2 * each, D // 2), jnp.bfloat16),
            pltpu.VMEM((count, count), jnp.float32),
            dma,
            dma,
        ],
        compiler_params=pltpu.CompilerParams(collective_id=number, has_side_effects=True),
    )(projected, target, log_scale)


BACK_SEQS = 2


def backward_kernel(
    x0_ref,
    mask_col_ref,
    mixed_ref,
    attended,
    total_ref,
    after_ref,
    pre_hbm,
    final_ref,
    gains_ref,
    bias_ref,
    pooled_ref,
    grad_proj_ref,
    packed_hbm,
    down_hbm,
    rows_ref,
    grad_gains_ref,
    grad_bias_ref,
    grad_packed_hbm,
    grad_down_hbm,
    packed,
    down,
    hidden,
    grad_pre,
    act_one,
    act_two,
    branch_two,
    branch_one,
    grad_mixed,
    grad_pooled,
    stage,
    pre_buffer,
    load_sem,
    store_sem,
    pre_sem,
):
    step = pl.program_id(0)
    tile_seqs = x0_ref.shape[0] // L
    tile = tile_seqs * L
    base = pl.multiple_of(step * tile, tile)
    edges = (0, WIDE, WIDE + D, WIDE + 5 * D, PACKED)

    def load(k):
        if k == 4:
            return pltpu.make_async_copy(down_hbm, down, load_sem.at[k])
        part = pl.ds(edges[k], edges[k + 1] - edges[k])
        to = stage.at[0] if k == 3 else packed.at[:, part]
        return pltpu.make_async_copy(packed_hbm.at[:, part], to, load_sem.at[k])

    def loaded(k):
        @pl.when(step == 0)
        def _():
            load(k).wait()

    def load_pre(number):
        start = pl.multiple_of(number // 4 * tile, tile)
        across = pl.multiple_of(lax.rem(number, 4) * D, D)
        slot = lax.rem(number, 2)
        return pltpu.make_async_copy(
            pre_hbm.at[pl.ds(start, tile), pl.ds(across, D)], pre_buffer.at[slot], pre_sem.at[slot]
        )

    @pl.when(step == 0)
    def _():
        load_pre(0).start()
        for k in (3, 4, 2, 1, 0):
            load(k).start()
        grad_gains_ref[...] = jnp.zeros_like(grad_gains_ref)
        grad_bias_ref[...] = jnp.zeros_like(grad_bias_ref)
        load(3).wait()
        grad_pooled[...] = matmul_nt(grad_proj_ref[...], stage[0])

    def gain_back(k, grad_out, inputs):
        gain = gains_ref[k : k + 1, :]
        factor = lax.rsqrt(jnp.mean(inputs * inputs, -1, keepdims=True) + EPS)
        scaled = grad_out * gain
        grad_gains_ref[k : k + 1, :] += jnp.sum(grad_out * inputs * factor, 0, keepdims=True)
        return factor * (
            scaled - inputs * (factor * factor * jnp.mean(scaled * inputs, -1, keepdims=True))
        )

    rows = pl.ds(base, tile)
    weight = mask_col_ref[...]
    pieces = []
    for s in range(tile_seqs):
        part = weight[s * L : (s + 1) * L]
        count = jnp.sum(part, 0, keepdims=True)
        pieces.append(part * (grad_pooled[pl.ds(step * tile_seqs + s, 1), :] / count))
    grad_final = gain_back(2, jnp.concatenate(pieces, 0), final_ref[...])
    branch = grad_final.astype(jnp.bfloat16)
    branch_two[rows, :] = branch
    loaded(4)
    loaded(2)
    grad_act = jnp.zeros((tile, D), jnp.float32)
    for j in range(4):
        part = slice(j * D, (j + 1) * D)
        grad_hidden = matmul_nt(branch, down[part, :])
        number = step * 4 + j
        pl.when(number + 1 < pl.num_programs(0) * 4)(lambda: load_pre(number + 1).start())
        load_pre(number).wait()
        pre = pre_buffer[j % 2]
        half, tan = gelu_parts(pre)
        hidden[rows, part] = (pre * half).astype(jnp.bfloat16)
        slope = np.float32(np.sqrt(2 / np.pi)) * (1.0 + (3 * 0.044715) * (pre * pre))
        grad_part = (grad_hidden * (half + 0.5 * pre * (1.0 - tan * tan) * slope)).astype(jnp.bfloat16)
        grad_pre[rows, part] = grad_part
        at = WIDE + D + j * D
        grad_act = grad_act + matmul_nt(grad_part, packed[:, at : at + D])
    after = after_ref[...]
    act_two[rows, :] = normalize(after, gains_ref[1:2, :])[0].astype(jnp.bfloat16)
    grad_after = grad_final + gain_back(1, grad_act, after)
    branch = grad_after.astype(jnp.bfloat16)
    branch_one[rows, :] = branch
    loaded(1)
    grad_attended = matmul_nt(branch, packed[:, WIDE : WIDE + D]).astype(jnp.bfloat16)
    zero = jnp.zeros((), jnp.bfloat16)
    mine = lane_is((L, 128), 0, HD)
    for s in range(tile_seqs):
        part = slice(s * L, (s + 1) * L)
        here = pl.ds(pl.multiple_of(base + s * L, L), L)
        keep = jnp.where(weight[part] > 0, 0.0, -1000000000.0)
        for pair in range(HEADS // 2):
            at = pair * 128
            query = mixed_ref[part, at : at + 128]
            key = mixed_ref[part, D + at : D + at + 128]
            value = mixed_ref[part, 2 * D + at : 2 * D + at + 128]
            grad_out = grad_attended[part, at : at + 128]
            keys = jnp.concatenate([jnp.where(mine, key, zero), jnp.where(mine, zero, key)], 0)
            values = jnp.concatenate([jnp.where(mine, value, zero), jnp.where(mine, zero, value)], 0)
            scores = (matmul_nt(keys, query) * SCALE).reshape(2, L, L)
            scores = scores + bias_ref[2 * pair : 2 * pair + 2] + keep[None]
            prob = jnp.exp(scores - total_ref[s, 2 * pair : 2 * pair + 2, :][:, None, :])
            grad_prob = matmul_nt(values, grad_out).reshape(2, L, L)
            mean = jnp.sum(prob * grad_prob, 1, keepdims=True)
            grad_scores = (prob * (grad_prob - mean)).astype(jnp.bfloat16)
            grad_bias_ref[2 * pair : 2 * pair + 2] += grad_scores.astype(jnp.float32)
            prob_low = prob.astype(jnp.bfloat16)
            flipped = jnp.transpose(key)
            grad_query = jnp.concatenate(
                [matmul(flipped[:HD], grad_scores[0]), matmul(flipped[HD:], grad_scores[1])], 0
            )
            grad_mixed[here, at : at + 128] = (jnp.transpose(grad_query) * SCALE).astype(jnp.bfloat16)
            grad_keys = matmul(grad_scores.reshape(2 * L, L), query)
            grad_key = jnp.where(mine, grad_keys[:L], grad_keys[L:]) * SCALE
            grad_mixed[here, D + at : D + at + 128] = grad_key.astype(jnp.bfloat16)
            grad_values = matmul(prob_low.reshape(2 * L, L), grad_out)
            grad_value = jnp.where(mine, grad_values[:L], grad_values[L:])
            grad_mixed[here, 2 * D + at : 2 * D + at + 128] = grad_value.astype(jnp.bfloat16)
    loaded(0)
    x0 = x0_ref[...]
    act_one[rows, :] = normalize(x0, gains_ref[0:1, :])[0].astype(jnp.bfloat16)
    grad_act = matmul_nt(grad_mixed[rows, :], packed[:, :WIDE])
    rows_ref[...] = (grad_after + gain_back(0, grad_act, x0)).astype(jnp.bfloat16)

    @pl.when(step == pl.num_programs(0) - 1)
    def _():
        jobs = []
        for j in range(4):
            part = slice(j * D, (j + 1) * D)
            jobs.append((hidden, part, branch_two, slice(0, D), grad_down_hbm.at[pl.ds(j * D, D), :]))
        for j in range(4):
            part = slice(j * D, (j + 1) * D)
            jobs.append((act_two, slice(0, D), grad_pre, part, grad_packed_hbm.at[:, pl.ds(WIDE + D + j * D, D)]))
        jobs.append((attended, slice(0, D), branch_one, slice(0, D), grad_packed_hbm.at[:, pl.ds(WIDE, D)]))
        for j in range(3):
            part = slice(j * D, (j + 1) * D)
            jobs.append((act_one, slice(0, D), grad_mixed, part, grad_packed_hbm.at[:, pl.ds(j * D, D)]))
        copies = []
        for number, (left, left_part, right, right_part, to) in enumerate(jobs):
            slot = number % 2
            if number >= 2:
                copies[number - 2].wait()
            stage[slot] = matmul_tn(left[:, left_part], right[:, right_part]).astype(jnp.bfloat16)
            copies.append(pltpu.make_async_copy(stage.at[slot], to, store_sem.at[slot]))
            copies[-1].start()
        copies[-2].wait()
        stage[0] = matmul_tn(pooled_ref[...].astype(jnp.bfloat16), grad_proj_ref[...]).astype(jnp.bfloat16)
        last = pltpu.make_async_copy(stage.at[0], grad_packed_hbm.at[:, pl.ds(PACKED - D, D)], store_sem.at[0])
        last.start()
        copies[-1].wait()
        last.wait()


def run_backward(
    x0, mask_col, mixed, attended, totals, after, pre, final, gains, bias_full, pooled, grad_proj, packed, down
):
    tokens = x0.shape[0]
    seqs = tokens // L
    tile = BACK_SEQS * L
    steps = tokens // tile

    def rows(width, **mode):
        return pl.BlockSpec((tile, width), lambda i: (i, 0), **mode)

    def whole(*shape):
        return pl.BlockSpec(shape, lambda i: (0,) * len(shape), pipeline_mode=pl.Buffered(1))

    def low(*shape):
        return pltpu.VMEM(shape, jnp.bfloat16)

    anywhere = pl.BlockSpec(memory_space=pl.ANY)
    return pl.pallas_call(
        backward_kernel,
        grid=(steps,),
        out_shape=[
            jax.ShapeDtypeStruct((tokens, D), jnp.bfloat16),
            jax.ShapeDtypeStruct((3, D), jnp.float32),
            jax.ShapeDtypeStruct((HEADS, L, L), jnp.float32),
            jax.ShapeDtypeStruct(packed.shape, jnp.bfloat16),
            jax.ShapeDtypeStruct(down.shape, jnp.bfloat16),
        ],
        in_specs=[
            rows(D),
            rows(1),
            rows(WIDE),
            whole(tokens, D),
            pl.BlockSpec((BACK_SEQS, HEADS, L), lambda i: (i, 0, 0)),
            rows(D),
            anywhere,
            rows(D),
            whole(3, D),
            whole(HEADS, L, L),
            whole(seqs, D),
            whole(seqs, D),
            anywhere,
            anywhere,
        ],
        out_specs=[rows(D), whole(3, D), whole(HEADS, L, L), anywhere, anywhere],
        scratch_shapes=[
            low(D, PACKED - D),
            low(4 * D, D),
            low(tokens, 4 * D),
            low(tokens, 4 * D),
            low(tokens, D),
            low(tokens, D),
            low(tokens, D),
            low(tokens, D),
            low(tokens, WIDE),
            pltpu.VMEM((seqs, D), jnp.float32),
            low(2, D, D),
            pltpu.VMEM((2, tile, D), jnp.float32),
            pltpu.SemaphoreType.DMA((5,)),
            pltpu.SemaphoreType.DMA((2,)),
            pltpu.SemaphoreType.DMA((2,)),
        ],
        compiler_params=pltpu.CompilerParams(vmem_limit_bytes=62 * 1024 * 1024),
    )(x0, mask_col, mixed, attended, totals, after, pre, final, gains, bias_full, pooled, grad_proj, packed, down)


def finish_kernel(grid, count, *refs):
    srcs, (sums, ids, small) = refs[:count], refs[count : count + 3]
    refs = refs[count + 3 :]
    outs, (table_out, small_out, square_out) = refs[:count], refs[count : count + 3]
    refs = refs[count + 3 :]
    acc, from_side, from_v, from_u, from_low, from_high = [
        refs[k * count : (k + 1) * count] for k in range(6)
    ]
    refs = refs[6 * count :]
    rows, small_stage, small_in, square_stage, square_in = refs[:5]
    refs = refs[1:]
    load_sem, side_send, side_recv, v_send, v_recv, u_send, u_recv, z_send, low_recv, high_recv = refs[4:14]
    row_own, line_send, on_send, row_recv, small_send, small_recv, square_send, square_recv = refs[14:]
    z, x, y, core = grid.here()
    tall = grid.tall
    d, f = lax.axis_index("dp"), lax.axis_index("fsdp")
    me = d * grid.fs + f
    up, down = grid.device(z + 1, x, y, core), grid.device(z - 1, x, y, core)
    has_up, has_down = z < tall - 1, z > 0
    ux, uy = lax.rem(x + 1 - core, 2), lax.rem(y + core, 2)
    vx, vy = lax.rem(x + core, 2), lax.rem(y + 1 - core, 2)
    u_device, v_device = grid.device(z, ux, uy, core), grid.device(z, vx, vy, core)
    sibling = grid.device(z, x, y, 1 - core)
    f_side = y * 2 + 1 - core
    f_y = (1 - y) * 2 + core
    f_far = (1 - y) * 2 + 1 - core

    for level in range(tall):
        small_in[3 + level] = jnp.zeros(small.shape, jnp.float32)
        square_in[3 + level] = jnp.zeros((16, 128), jnp.float32)
    x_device, y_device = grid.device(z, 1 - x, y, core), grid.device(z, x, 1 - y, core)

    @pl.loop(1, grid.dp)
    def _(step):
        greet((lax.rem(d + step, grid.dp), f))

    greet(y_device)
    greet(sibling)

    def each(action):
        for m in range(count):
            action(m)

    def level_of(j):
        tables = []
        for own in range(tall):
            tables.append(sorted(range(tall), key=lambda level: (-abs(level - own), -level))[j])
        value = tables[0]
        for own in range(1, tall):
            value = jnp.where(z == own, tables[own], value)
        return value

    def load(m, level):
        return pltpu.make_async_copy(
            srcs[m].at[level, :, :, core], acc[m].at[level], load_sem.at[m, level]
        )

    def side(m, level):
        return pltpu.make_async_remote_copy(
            src_ref=srcs[m].at[level, :, :, 1 - core],
            dst_ref=from_side[m].at[level],
            send_sem=side_send.at[m, level],
            recv_sem=side_recv.at[m, level],
            device_id=sibling,
            device_id_type=MESH,
        )

    def v_copy(m, level, along_u):
        xx, yy = (1 - x, 1 - y) if along_u else (vx, vy)
        return pltpu.make_async_remote_copy(
            src_ref=acc[m].at[level, xx, yy],
            dst_ref=from_v[m].at[level, along_u],
            send_sem=v_send.at[m, level, along_u],
            recv_sem=v_recv.at[m, level, along_u],
            device_id=v_device,
            device_id_type=MESH,
        )

    def u_copy(m, level):
        return pltpu.make_async_remote_copy(
            src_ref=acc[m].at[level, ux, uy],
            dst_ref=from_u[m].at[level],
            send_sem=u_send.at[m, level],
            recv_sem=u_recv.at[m, level],
            device_id=u_device,
            device_id_type=MESH,
        )

    def z_copy(m, level, upward):
        return pltpu.make_async_remote_copy(
            src_ref=acc[m].at[level, x, y],
            dst_ref=(from_low if upward else from_high)[m].at[level],
            send_sem=z_send.at[m, level],
            recv_sem=(low_recv if upward else high_recv).at[m, level],
            device_id=up if upward else down,
            device_id_type=MESH,
        )

    def line(peer, slot):
        return pltpu.make_async_remote_copy(
            src_ref=sums.at[peer],
            dst_ref=rows.at[slot],
            send_sem=line_send.at[peer],
            recv_sem=row_recv.at[slot],
            device_id=(peer, f),
            device_id_type=MESH,
        )

    def onward(slot, to_side, own_block=False):
        return pltpu.make_async_remote_copy(
            src_ref=sums.at[d] if own_block else rows.at[slot],
            dst_ref=rows.at[slot],
            send_sem=on_send.at[1 if to_side else 0, slot],
            recv_sem=row_recv.at[slot],
            device_id=(d, f_side if to_side else f_y),
            device_id_type=MESH,
        )

    def total_of(stage, inbox, send_sem, recv_sem):
        partners = (sibling, x_device, y_device)

        def copy(r):
            return pltpu.make_async_remote_copy(
                src_ref=stage.at[r],
                dst_ref=inbox.at[r],
                send_sem=send_sem.at[r],
                recv_sem=recv_sem.at[r],
                device_id=partners[r],
                device_id_type=MESH,
            )

        def z_send(level, slot):
            return pltpu.make_async_remote_copy(
                src_ref=stage.at[3],
                dst_ref=inbox.at[3 + slot],
                send_sem=send_sem.at[3 + level],
                recv_sem=recv_sem.at[3 + slot],
                device_id=grid.device(level, x, y, core),
                device_id_type=MESH,
            )

        def others(action):
            @pl.loop(1, tall)
            def _(step):
                action(lax.rem(z + step, tall))

        def send(r):
            if r < 3:
                copy(r).start()
            else:
                others(lambda level: z_send(level, z).start())

        def take(r):
            if r < 3:
                copy(r).wait_recv()
                stage[r + 1] = stage[r] + inbox[r]
                send(r + 1)
            else:
                others(lambda level: z_send(level, level).wait_recv())

        def result():
            total = stage[3]
            for level in range(tall):
                total = total + jnp.where(z == level, 0.0, inbox[3 + level])
            for r in range(3):
                copy(r).wait_send()
            others(lambda level: z_send(level, level).wait_send())
            return total

        return send, take, result

    small_stage[0] = small[...]
    small_sends, small_take, small_result = total_of(small_stage, small_in, small_send, small_recv)
    square_sends, square_take, square_result = total_of(square_stage, square_in, square_send, square_recv)
    levels = [level_of(j) for j in range(tall)]
    own_rows = pltpu.make_async_copy(sums.at[d], rows.at[me], row_own)
    own_rows.start()
    for level in levels:
        each(lambda m: load(m, level).start())
    meet(grid.dp + 1)
    small_sends(0)

    @pl.loop(1, grid.dp)
    def _(step):
        line(lax.rem(d + step, grid.dp), me).start()

    for level in levels:
        each(lambda m: side(m, level).start())
    onward(me, False, True).start()
    onward(me, True, True).start()

    def first(j):
        level = levels[j]

        def run(m):
            load(m, level).wait()
            side(m, level).wait_recv()
            for xx in range(2):
                for yy in range(2):
                    total = acc[m][level, xx, yy].astype(jnp.float32) + from_side[m][level, xx, yy].astype(jnp.float32)
                    acc[m][level, xx, yy] = total.astype(jnp.bfloat16)
            v_copy(m, level, 1).start()
            v_copy(m, level, 0).start()

        each(run)

    def add(m, level, xx, yy, other):
        total = acc[m][level, xx, yy].astype(jnp.float32) + other.astype(jnp.float32)
        acc[m][level, xx, yy] = total.astype(jnp.bfloat16)

    def second(j):
        level = levels[j]

        def run(m):
            v_copy(m, level, 1).wait_recv()
            add(m, level, ux, uy, from_v[m][level, 1])
            u_copy(m, level).start()

        each(run)

    def second_own(j):
        level = levels[j]

        def run(m):
            v_copy(m, level, 0).wait_recv()
            add(m, level, x, y, from_v[m][level, 0])

        each(run)

    def third(j):
        level = levels[j]

        def run(m):
            u_copy(m, level).wait_recv()
            add(m, level, x, y, from_u[m][level])

            @pl.when((level >= z) & has_down)
            def _():
                z_copy(m, level, True).wait_recv()
                add(m, level, x, y, from_low[m][level])

            @pl.when((level <= z) & has_up)
            def _():
                z_copy(m, level, False).wait_recv()
                add(m, level, x, y, from_high[m][level])

            @pl.when(level > z)
            def _():
                z_copy(m, level, True).start()

            @pl.when(level < z)
            def _():
                z_copy(m, level, False).start()

        each(run)

    def pass_lines():
        @pl.loop(1, grid.dp)
        def _(step):
            slot = lax.rem(d + grid.dp - step, grid.dp) * grid.fs + f
            line(d, slot).wait_recv()
            onward(slot, False).start()
            onward(slot, True).start()

    def pass_y():
        @pl.loop(0, grid.dp)
        def _(step):
            slot = lax.rem(d + grid.dp - step, grid.dp) * grid.fs + f_y
            line(d, slot).wait_recv()
            onward(slot, True).start()

    def rows_in():
        own_rows.wait()

        @pl.loop(0, grid.dp)
        def _(step):
            line(d, step * grid.fs + f_side).wait_recv()
            line(d, step * grid.fs + f_far).wait_recv()

    table_rows = table_out.shape[0]
    whole_blocks = table_rows // ROW_BLOCK
    square_stage[0] = jnp.zeros((16, 128), jnp.float32)

    def fold(values):
        n, lanes = values.shape
        part = jnp.sum(values.reshape(n // 8, 8, lanes), 0)
        total = part[:, :128]
        for at in range(128, lanes, 128):
            total = total + part[:, at : at + 128]
        return total

    def spread(start, size):
        per = rows.shape[1]
        group = 8
        total = jnp.zeros((size, D), jnp.float32)
        for g in range(0, grid.total, group):
            place = (start + lax.broadcasted_iota(jnp.int32, (size, group * per), 0)).astype(jnp.float32)
            wanted = ids[:, g * per : (g + group) * per]
            hot = jnp.where(place == wanted, 1.0, 0.0).astype(jnp.bfloat16)
            total = total + matmul(hot, rows[g : g + group].reshape(group * per, D))
        low = total.astype(jnp.bfloat16)
        table_out[pl.ds(start, size), :] = low
        wide = low.astype(jnp.float32)
        square_stage[0, 8:16, :] += fold(wide * wide)

    def spread_blocks(first_block, last_block):
        @pl.loop(first_block, last_block)
        def _(block):
            spread(pl.multiple_of(block * ROW_BLOCK, ROW_BLOCK), ROW_BLOCK)

    for j in range(tall):
        first(j)
        if j < 3:
            small_take(j)
    pass_lines()
    second(0)
    second_own(0)
    second(1)
    second_own(1)
    third(0)
    pass_y()
    second(2)
    second_own(2)
    third(1)
    second(3)
    second_own(3)
    rows_in()
    spread_blocks(0, whole_blocks // 2)
    third(2)
    spread_blocks(whole_blocks // 2, whole_blocks)
    if table_rows % ROW_BLOCK:
        spread(whole_blocks * ROW_BLOCK, table_rows % ROW_BLOCK)
    third(3)

    def give(m):
        wide = acc[m][z, x, y].astype(jnp.float32)
        outs[m][...] = wide
        square_stage[0, 0:8, :] += fold(wide * wide)

    each(give)

    square_sends(0)
    small_take(3)
    small_out[...] = small_result()
    for r in range(3):
        square_take(r)

    for level in levels:
        each(lambda m: side(m, level).wait_send())
        each(lambda m: v_copy(m, level, 0).wait_send())
        each(lambda m: v_copy(m, level, 1).wait_send())
        each(lambda m: u_copy(m, level).wait_send())

        @pl.when(level != z)
        def _():
            each(lambda m: z_copy(m, level, True).wait_send())

    @pl.loop(0, grid.dp)
    def _(step):
        onward(step * grid.fs + f, False).wait_send()
        onward(step * grid.fs + f, True).wait_send()
        onward(step * grid.fs + f_y, True).wait_send()

    @pl.loop(1, grid.dp)
    def _(step):
        line(lax.rem(d + step, grid.dp), me).wait_send()

    square_take(3)
    square_out[...] = square_result()


def finish(srcs, sums, ids, small, vocab_rows, number):
    grid = Grid()
    count = len(srcs)
    tall = grid.tall
    blocks = [src.shape[1:] for src in srcs]
    srcs = [src.reshape((tall, 2, 2, 2) + src.shape[1:]) for src in srcs]
    leads = ((tall, 2, 2), (tall, 2, 2), (tall, 2), (tall,), (tall,), (tall,))
    buffers = [pltpu.VMEM(lead + block, jnp.bfloat16) for lead in leads for block in blocks]
    cap = sums.shape[1]
    buffers += [
        pltpu.VMEM((grid.total, cap, D), jnp.bfloat16),
        pltpu.VMEM((4,) + small.shape, jnp.float32),
        pltpu.VMEM((3 + tall,) + small.shape, jnp.float32),
        pltpu.VMEM((4, 16, 128), jnp.float32),
        pltpu.VMEM((3 + tall, 16, 128), jnp.float32),
    ]
    dma = pltpu.SemaphoreType.DMA
    by_level = dma((count, tall))
    semaphores = [by_level, by_level, by_level, dma((count, tall, 2)), dma((count, tall, 2))] + [by_level] * 5
    by_device, by_step = dma((grid.total,)), dma((3 + tall,))
    semaphores += [dma, dma((grid.dp,)), dma((2, grid.total)), by_device] + [by_step] * 4
    anywhere, inside = pl.BlockSpec(memory_space=pl.ANY), pl.BlockSpec(memory_space=pltpu.VMEM)
    results = pl.pallas_call(
        functools.partial(finish_kernel, grid, count),
        out_shape=[jax.ShapeDtypeStruct(block, jnp.float32) for block in blocks]
        + [
            jax.ShapeDtypeStruct((vocab_rows, D), jnp.bfloat16),
            jax.ShapeDtypeStruct(small.shape, jnp.float32),
            jax.ShapeDtypeStruct((16, 128), jnp.float32),
        ],
        in_specs=[anywhere] * (count + 1) + [inside] * 2,
        out_specs=[inside] * (count + 3),
        scratch_shapes=buffers + semaphores,
        compiler_params=pltpu.CompilerParams(
            collective_id=number, has_side_effects=True, vmem_limit_bytes=62 * 1024 * 1024
        ),
    )(*srcs, sums, ids.reshape(1, -1), small)
    return (results[:count], *results[count:])


def plain_body(
    token_ids,
    pad_mask,
    hard_negative,
    table,
    table_first,
    table_second,
    attn_in,
    attn_in_first,
    attn_in_second,
    attn_out,
    attn_out_first,
    attn_out_second,
    ffn_in,
    ffn_in_first,
    ffn_in_second,
    ffn_out,
    ffn_out_first,
    ffn_out_second,
    proj_head,
    proj_head_first,
    proj_head_second,
    small_params,
    small_first,
    small_second,
):
    dp_count = lax.axis_size("dp")
    fsdp_count = lax.axis_size("fsdp")
    device_flat = lax.axis_index("dp") * fsdp_count + lax.axis_index("fsdp")
    pairs_here = token_ids.shape[1]
    pairs_total = pairs_here * dp_count * fsdp_count
    seq_count = 2 * pairs_here
    vocab_rows = table.shape[0]
    row_base = lax.axis_index("dp") * vocab_rows
    gain_rows = small_params[: 3 * D].reshape(3, D)
    bias_table = small_params[3 * D : 3 * D + NB * HEADS].reshape(NB, HEADS)
    log_scale = small_params[3 * D + NB * HEADS]
    buckets = jnp.asarray(bucket_table(L, NB).reshape(-1), jnp.int32)
    bucket_hot = (buckets[:, None] == jnp.arange(NB, dtype=jnp.int32)[None, :]).astype(jnp.float32)
    bias_full = (
        jnp.dot(bucket_hot, bias_table, precision=HIGH).reshape(L, L, HEADS).transpose(2, 0, 1)
    )
    mask_rows = pad_mask.reshape(seq_count, L)
    ids_flat = token_ids.reshape(-1)
    table_low = table.astype(jnp.bfloat16)
    ids_all = lax.all_gather(ids_flat, "dp", axis=0, tiled=True)
    picked = ids_all - row_base
    inside = (picked >= 0) & (picked < vocab_rows)
    chosen = jnp.take(table_low, jnp.clip(picked, 0, vocab_rows - 1), axis=0)
    embedded = lax.psum_scatter(
        jnp.where(inside[:, None], chosen.astype(jnp.float32), 0.0).astype(jnp.bfloat16),
        "dp",
        scatter_dimension=0,
        tiled=True,
    ).astype(jnp.float32)
    shards = (
        attn_in.astype(jnp.bfloat16),
        attn_out.astype(jnp.bfloat16),
        ffn_in.astype(jnp.bfloat16),
        ffn_out.astype(jnp.bfloat16),
        proj_head.astype(jnp.bfloat16),
    )
    gathered = (
        lax.all_gather(shards[0], ("dp", "fsdp"), axis=0, tiled=True),
        lax.all_gather(shards[1], ("dp", "fsdp"), axis=0, tiled=True),
        lax.all_gather(shards[2], ("dp", "fsdp"), axis=0, tiled=True),
        lax.all_gather(shards[3], ("dp", "fsdp"), axis=0, tiled=True),
        lax.all_gather(shards[4], ("dp", "fsdp"), axis=0, tiled=True),
    )
    final_rows, kept = layer_forward(embedded, mask_rows, gathered[:4], gain_rows, bias_full)
    normed_three, factor_three = normalize(final_rows, gain_rows[2])
    mask_weight = mask_rows.astype(jnp.float32)[:, :, None]
    counts = jnp.sum(mask_weight, 1)
    pooled = jnp.sum(normed_three.reshape(seq_count, L, D) * mask_weight, 1) / counts
    pooled_low = pooled.astype(jnp.bfloat16)
    projected = matmul(pooled_low, gathered[4])
    proj_factor = lax.rsqrt(jnp.sum(projected * projected, -1, keepdims=True) + EPS)
    unit_rows = projected * proj_factor
    unit_low = unit_rows.astype(jnp.bfloat16)
    mine_query = unit_low[:pairs_here]
    all_pass = lax.all_gather(unit_low[pairs_here:], ("dp", "fsdp"), axis=0, tiled=True)
    similar = matmul_nt(mine_query, all_pass)
    sim_scale = jnp.exp(log_scale)
    columns = jnp.arange(pairs_total, dtype=jnp.int32)
    own_index = device_flat * pairs_here + jnp.arange(pairs_here, dtype=jnp.int32)
    own_mask = (columns[None, :] == own_index[:, None]).astype(jnp.float32)
    negative = (columns[None, :] == hard_negative[:, None]).astype(jnp.float32)
    logits = sim_scale * similar - MARGIN * own_mask
    diagonal = jnp.sum(logits * own_mask, 1)
    hardest = jnp.sum(logits * negative, 1)
    row_max = jnp.max(logits, 1, keepdims=True)
    log_total = row_max + jnp.log(jnp.sum(jnp.exp(logits - row_max), 1, keepdims=True))
    loss_local = jnp.sum(log_total[:, 0] - diagonal + jax.nn.softplus(hardest - diagonal))
    hinge_gate = jax.nn.sigmoid(hardest - diagonal)
    grad_logits = (
        jnp.exp(logits - log_total) - own_mask + hinge_gate[:, None] * (negative - own_mask)
    )
    grad_log_scale = sim_scale * jnp.sum(grad_logits * similar)
    grad_similar = (sim_scale * grad_logits).astype(jnp.bfloat16)
    grad_query = matmul(grad_similar, all_pass).astype(jnp.bfloat16)
    grad_pass_terms = matmul_tn(grad_similar, mine_query)
    grad_pass = lax.psum_scatter(
        grad_pass_terms, ("dp", "fsdp"), scatter_dimension=0, tiled=True
    ).astype(jnp.bfloat16)
    grad_units = jnp.concatenate([grad_query, grad_pass], 0).astype(jnp.float32)
    grad_proj = (
        proj_factor * (grad_units - unit_rows * jnp.sum(grad_units * unit_rows, -1, keepdims=True))
    ).astype(jnp.bfloat16)
    gathered_back = (
        lax.all_gather(shards[0], ("dp", "fsdp"), axis=0, tiled=True),
        lax.all_gather(shards[1], ("dp", "fsdp"), axis=0, tiled=True),
        lax.all_gather(shards[2], ("dp", "fsdp"), axis=0, tiled=True),
        lax.all_gather(shards[3], ("dp", "fsdp"), axis=0, tiled=True),
        lax.all_gather(shards[4], ("dp", "fsdp"), axis=0, tiled=True),
    )
    grad_proj_head = matmul_tn(pooled_low, grad_proj)
    grad_pooled = matmul_nt(grad_proj, gathered_back[4])
    grad_normed = ((grad_pooled / counts)[:, None, :] * mask_weight).reshape(-1, D)
    grad_final, gain_three = normalize_back(grad_normed, final_rows, factor_three, gain_rows[2])
    grad_rows, matrix_grads, gain_one, gain_two, grad_bias = layer_backward(
        grad_final, kept, mask_rows, gathered_back[:4], gain_rows, bias_full
    )
    attn_in_grad, attn_out_grad, ffn_in_grad, ffn_out_grad = matrix_grads
    grad_bias_table = jnp.dot(grad_bias.reshape(HEADS, L * L), bucket_hot, precision=HIGH).T
    small_local = jnp.concatenate(
        [gain_one, gain_two, gain_three, grad_bias_table.reshape(-1), grad_log_scale[None]]
    )
    small_grad = lax.psum(small_local, ("dp", "fsdp"))
    weight_grads = (
        lax.psum_scatter(attn_in_grad, ("dp", "fsdp"), scatter_dimension=0, tiled=True),
        lax.psum_scatter(attn_out_grad, ("dp", "fsdp"), scatter_dimension=0, tiled=True),
        lax.psum_scatter(ffn_in_grad, ("dp", "fsdp"), scatter_dimension=0, tiled=True),
        lax.psum_scatter(ffn_out_grad, ("dp", "fsdp"), scatter_dimension=0, tiled=True),
        lax.psum_scatter(grad_proj_head, ("dp", "fsdp"), scatter_dimension=0, tiled=True),
    )
    rows_back = lax.all_gather(grad_rows.astype(jnp.bfloat16), "dp", axis=0, tiled=True)
    turn_count = dp_count // 4
    block_rows = rows_back.shape[0] // turn_count

    def add_block(running, piece_pair):
        block_grads, block_ids = piece_pair
        local_ids = block_ids - row_base
        inside = (local_ids >= 0) & (local_ids < vocab_rows)
        segment = jnp.where(inside, local_ids, vocab_rows)
        summed = jax.ops.segment_sum(
            block_grads.astype(jnp.float32), segment, num_segments=vocab_rows + 1
        )
        return (running + summed[:vocab_rows], None)

    table_full, _ = lax.scan(
        add_block,
        jnp.zeros((vocab_rows, D), jnp.float32),
        (rows_back.reshape(turn_count, block_rows, D), ids_all.reshape(turn_count, block_rows)),
    )
    table_grad = lax.psum(table_full.astype(jnp.bfloat16), "fsdp").astype(jnp.float32)
    owned = (table_grad,) + tuple(weight_grads)
    squares = jnp.sum(table_grad * table_grad) / fsdp_count
    for gradient in weight_grads:
        squares = squares + jnp.sum(gradient * gradient)
    total_squares, loss_sum = lax.psum((squares, loss_local), ("dp", "fsdp"))
    norm_value = jnp.sqrt(total_squares + jnp.sum(small_grad * small_grad))
    factor = jnp.minimum(1.0, CLIP / (norm_value + 1e-06))
    masters = (table, attn_in, attn_out, ffn_in, ffn_out, proj_head, small_params)
    firsts = (
        table_first,
        attn_in_first,
        attn_out_first,
        ffn_in_first,
        ffn_out_first,
        proj_head_first,
        small_first,
    )
    seconds = (
        table_second,
        attn_in_second,
        attn_out_second,
        ffn_in_second,
        ffn_out_second,
        proj_head_second,
        small_second,
    )
    gradients = owned + (small_grad,)
    results = [loss_sum, norm_value]
    for kind_index in range(7):
        results.extend(
            adam_update(
                masters[kind_index],
                firsts[kind_index],
                seconds[kind_index],
                gradients[kind_index],
                factor,
                RATES[kind_index],
                DECAYS[kind_index],
            )
        )
    return tuple(results)


def fits(mesh):
    return mesh.shape["fsdp"] == 4 and mesh.shape["dp"] == 8


def dense_rows(ids_flat, table, row_base):
    vocab_rows = table.shape[0]
    ids_all = lax.all_gather(ids_flat, "dp", axis=0, tiled=True)
    picked = ids_all - row_base
    inside = (picked >= 0) & (picked < vocab_rows)
    chosen = jnp.take(table.astype(jnp.bfloat16), jnp.clip(picked, 0, vocab_rows - 1), axis=0)
    return lax.psum_scatter(
        jnp.where(inside[:, None], chosen.astype(jnp.float32), 0.0).astype(jnp.bfloat16),
        "dp",
        scatter_dimension=0,
        tiled=True,
    ).astype(jnp.float32)


def dense_table_grad(ids_flat, grad_low, vocab_rows, row_base):
    ids_all = lax.all_gather(ids_flat, "dp", axis=0, tiled=True)
    rows_back = lax.all_gather(grad_low, "dp", axis=0, tiled=True)
    turn_count = lax.axis_size("dp") // 4
    block_rows = rows_back.shape[0] // turn_count

    def add_block(running, piece_pair):
        block_grads, block_ids = piece_pair
        local_ids = block_ids - row_base
        inside = (local_ids >= 0) & (local_ids < vocab_rows)
        segment = jnp.where(inside, local_ids, vocab_rows)
        summed = jax.ops.segment_sum(
            block_grads.astype(jnp.float32), segment, num_segments=vocab_rows + 1
        )
        return (running + summed[:vocab_rows], None)

    table_full, _ = lax.scan(
        add_block,
        jnp.zeros((vocab_rows, D), jnp.float32),
        (rows_back.reshape(turn_count, block_rows, D), ids_all.reshape(turn_count, block_rows)),
    )
    return lax.psum(table_full.astype(jnp.bfloat16), "fsdp")


def once(flag, make, value):
    return lax.while_loop(lambda state: state[0], lambda state: (False, make(state[1])), (flag, value))[1]


def fast_body(
    token_ids,
    pad_mask,
    hard_negative,
    table,
    table_first,
    table_second,
    attn_in,
    attn_in_first,
    attn_in_second,
    attn_out,
    attn_out_first,
    attn_out_second,
    ffn_in,
    ffn_in_first,
    ffn_in_second,
    ffn_out,
    ffn_out_first,
    ffn_out_second,
    proj_head,
    proj_head_first,
    proj_head_second,
    small_params,
    small_first,
    small_second,
):
    dp_count = lax.axis_size("dp")
    fsdp_count = lax.axis_size("fsdp")
    total = dp_count * fsdp_count
    pairs_here = token_ids.shape[1]
    pairs_total = pairs_here * total
    seq_count = 2 * pairs_here
    vocab_rows = table.shape[0]
    row_base = lax.axis_index("dp") * vocab_rows
    gain_rows = small_params[: 3 * D].reshape(3, D)
    bias_table = small_params[3 * D : 3 * D + NB * HEADS].reshape(NB, HEADS)
    log_scale = small_params[3 * D + NB * HEADS]
    buckets = jnp.asarray(bucket_table(L, NB).T.reshape(-1), jnp.int32)
    bucket_hot = (buckets[:, None] == jnp.arange(NB, dtype=jnp.int32)[None, :]).astype(jnp.float32)
    bias_full = (
        jnp.dot(bucket_hot, bias_table, precision=HIGH).reshape(L, L, HEADS).transpose(2, 0, 1)
    )
    mask_rows = pad_mask.reshape(seq_count, L)
    ids_flat = token_ids.reshape(-1)
    tokens = ids_flat.shape[0]

    gathered_packed, gathered_down, heard, slot, embedded = run_head(
        ids_flat, hard_negative, attn_in, attn_out, ffn_in, proj_head, ffn_out, table, 1
    )
    packed = gathered_packed.reshape(-1, PACKED)
    down = gathered_down.reshape(-1, D)
    asked = heard[:, 0, :CAP]
    negatives = heard[:, 1, :pairs_here].reshape(-1).astype(jnp.int32)
    any_spilled = jnp.max(heard[:, 2, 0]) > 0.5
    embedded = once(any_spilled, lambda _: dense_rows(ids_flat, table, row_base), embedded)

    mask_col = mask_rows.astype(jnp.float32).reshape(tokens, 1)
    *kept, pooled, projected = run_forward(embedded, mask_col, gain_rows, bias_full, packed, down)
    target = negatives // pairs_here * seq_count + pairs_here + negatives % pairs_here
    target = jnp.concatenate(
        [target.reshape(total, pairs_here), jnp.full((total, pairs_here), -1, jnp.int32)], 1
    ).reshape(-1, 1)
    grad_proj, loss_parts = run_loss(projected, target, log_scale.reshape(1, 1), 3)
    loss_sum, grad_log_scale = loss_parts[0, 0], loss_parts[1, 0]
    grad_low, grad_gains, grad_bias, grad_packed, grad_down = run_backward(
        embedded, mask_col, *kept, gain_rows, bias_full, pooled, grad_proj, packed, down
    )
    grad_bias_table = jnp.dot(grad_bias.reshape(HEADS, L * L), bucket_hot, precision=HIGH).T
    partials = [grad.reshape(total, -1, grad.shape[1]) for grad in (grad_packed, grad_down)]
    small_local = jnp.concatenate([grad_gains.reshape(-1), grad_bias_table.reshape(-1)])
    width = -(-small_local.shape[0] // 1024) * 8
    small_local = jnp.pad(small_local, (0, width * 128 - small_local.shape[0]))
    slots = jnp.arange(dp_count * CAP, dtype=jnp.int32).astype(jnp.float32)
    slot_hot = (slot == slots[None, :]).astype(jnp.bfloat16)
    slot_sums = matmul_tn(slot_hot, grad_low).astype(jnp.bfloat16).reshape(dp_count, CAP, D)
    weight_grads, table_grad, summed, squares = finish(
        partials, slot_sums, asked.reshape(-1), small_local.reshape(width, 128), vocab_rows, 4
    )
    table_squares = jnp.sum(squares[8:])
    table_grad, table_squares = once(
        any_spilled,
        lambda _: with_squares(dense_table_grad(ids_flat, grad_low, vocab_rows, row_base)),
        (table_grad, table_squares),
    )
    small_size = small_params.shape[0]
    total_squares = jnp.sum(squares[:8]) + table_squares / fsdp_count
    small_grad = jnp.concatenate([summed.reshape(-1)[: small_size - 1], grad_log_scale[None]])
    norm_value = jnp.sqrt(total_squares + jnp.sum(small_grad * small_grad))
    factor = jnp.minimum(1.0, CLIP / (norm_value + 1e-06))
    grad_in, grad_out, grad_up, grad_head = jnp.split(
        weight_grads[0], (WIDE, WIDE + D, WIDE + 5 * D), 1
    )
    updates = (
        (table, table_first, table_second, table_grad.astype(jnp.float32)),
        (attn_in, attn_in_first, attn_in_second, grad_in),
        (attn_out, attn_out_first, attn_out_second, grad_out),
        (ffn_in, ffn_in_first, ffn_in_second, grad_up),
        (ffn_out, ffn_out_first, ffn_out_second, weight_grads[1]),
        (proj_head, proj_head_first, proj_head_second, grad_head),
        (small_params, small_first, small_second, small_grad),
    )
    results = [loss_sum, norm_value]
    for kind_index, arrays in enumerate(updates):
        results.extend(adam_update(*arrays, factor, RATES[kind_index], DECAYS[kind_index]))
    return tuple(results)


def with_squares(table_grad):
    wide = table_grad.astype(jnp.float32)
    return (table_grad, lax.psum(jnp.sum(wide * wide), ("dp", "fsdp")))


def solution(mesh):
    program = fast_body if fits(mesh) else plain_body
    return jax.shard_map(
        program,
        mesh=mesh,
        in_specs=(
            P(None, ("dp", "fsdp"), None),
            P(None, ("dp", "fsdp"), None),
            P(("dp", "fsdp")),
            P("dp", None),
            P("dp", None),
            P("dp", None),
            P(("dp", "fsdp"), None),
            P(("dp", "fsdp"), None),
            P(("dp", "fsdp"), None),
            P(("dp", "fsdp"), None),
            P(("dp", "fsdp"), None),
            P(("dp", "fsdp"), None),
            P(("dp", "fsdp"), None),
            P(("dp", "fsdp"), None),
            P(("dp", "fsdp"), None),
            P(("dp", "fsdp"), None),
            P(("dp", "fsdp"), None),
            P(("dp", "fsdp"), None),
            P(("dp", "fsdp"), None),
            P(("dp", "fsdp"), None),
            P(("dp", "fsdp"), None),
            P(),
            P(),
            P(),
        ),
        out_specs=(
            P(),
            P(),
            P("dp", None),
            P("dp", None),
            P("dp", None),
            P(("dp", "fsdp"), None),
            P(("dp", "fsdp"), None),
            P(("dp", "fsdp"), None),
            P(("dp", "fsdp"), None),
            P(("dp", "fsdp"), None),
            P(("dp", "fsdp"), None),
            P(("dp", "fsdp"), None),
            P(("dp", "fsdp"), None),
            P(("dp", "fsdp"), None),
            P(("dp", "fsdp"), None),
            P(("dp", "fsdp"), None),
            P(("dp", "fsdp"), None),
            P(("dp", "fsdp"), None),
            P(("dp", "fsdp"), None),
            P(("dp", "fsdp"), None),
            P(),
            P(),
            P(),
        ),
        check_vma=False,
    )
```

```python
import functools

import jax
import jax.numpy as jnp
import numpy as np
from jax import lax
from jax.experimental import pallas as pl
from jax.experimental.pallas import tpu as pltpu
from jax.sharding import PartitionSpec as P

D = 768
HEADS = 12
HD = 64
NB = 32
L = 128
STEP = 10


EPS = 1e-06
SCALE = 0.125
MARGIN = 0.2
CLIP = 0.1
BETA_ONE = 0.9
BETA_TWO = 0.99
ADAM_EPS = 1e-08
RATES = (3.0, 0.1, 0.2, 0.1, 0.05, 0.1, 1.0)
DECAYS = (0.001, 0.001, 0.001, 0.001, 0.001, 0.001, 0.0)
HIGH = lax.Precision.HIGHEST
MESH = pl.DeviceIdType.MESH
CAP = 112


def bucket_table(length, count):
    position = np.arange(length)
    relative = position[None, :] - position[:, None]
    half = count // 2
    base_part = (relative > 0).astype(np.int64) * half
    distance = np.abs(relative)
    exact = half // 2
    safe_dist = np.maximum(distance, 1)
    large = exact + (np.log(safe_dist / exact) / np.log(length / exact) * (half - exact)).astype(
        np.int64
    )
    large = np.minimum(large, half - 1)
    return base_part + np.where(distance < exact, distance, large)


def matmul(left_side, right_side):
    return jnp.dot(left_side, right_side, preferred_element_type=jnp.float32)


def matmul_tn(left_side, right_side):
    return lax.dot_general(
        left_side, right_side, (((0,), (0,)), ((), ())), preferred_element_type=jnp.float32
    )


def matmul_nt(left_side, right_side):
    return lax.dot_general(
        left_side, right_side, (((1,), (1,)), ((), ())), preferred_element_type=jnp.float32
    )


def normalize(inputs, gain_row):
    factor = lax.rsqrt(jnp.mean(inputs * inputs, -1, keepdims=True) + EPS)
    return (inputs * factor * gain_row, factor)


def normalize_back(grad_out, inputs, factor, gain_row):
    scaled = grad_out * gain_row
    grad_gain = jnp.sum(grad_out * inputs * factor, 0)
    grad_in = factor * (
        scaled - inputs * factor * factor * jnp.mean(scaled * inputs, -1, keepdims=True)
    )
    return (grad_in, grad_gain)


def attention_scores(mixed_proj, mask_rows, bias_full):
    keep_add = jnp.where(mask_rows > 0, 0.0, -1000000000.0).astype(jnp.float32)
    scores = jnp.einsum(
        "bqhd,bkhd->bhqk",
        mixed_proj[:, :, 0],
        mixed_proj[:, :, 1],
        preferred_element_type=jnp.float32,
    )
    return scores * SCALE + bias_full[None] + keep_add[:, None, None, :]


def layer_forward(token_rows, mask_rows, weights, gain_rows, bias_full):
    attn_in, attn_out, ffn_in, ffn_out = weights
    seq_count, length = mask_rows.shape
    width = token_rows.shape[1]
    normed_one, factor_one = normalize(token_rows, gain_rows[0])
    act_one = normed_one.astype(jnp.bfloat16)
    mixed_proj = (
        matmul(act_one, attn_in).astype(jnp.bfloat16).reshape(seq_count, length, 3, HEADS, HD)
    )
    scores = attention_scores(mixed_proj, mask_rows, bias_full)
    row_max = jnp.max(scores, -1, keepdims=True)
    log_total = row_max + jnp.log(jnp.sum(jnp.exp(scores - row_max), -1, keepdims=True))
    prob_low = jnp.exp(scores - log_total).astype(jnp.bfloat16)
    attended = jnp.einsum(
        "bhqk,bkhd->bqhd", prob_low, mixed_proj[:, :, 2], preferred_element_type=jnp.float32
    )
    attended = attended.astype(jnp.bfloat16).reshape(-1, width)
    after_attn = token_rows + matmul(attended, attn_out)
    normed_two, factor_two = normalize(after_attn, gain_rows[1])
    act_two = normed_two.astype(jnp.bfloat16)
    pre_act = matmul(act_two, ffn_in)
    hidden = jax.nn.gelu(pre_act).astype(jnp.bfloat16)
    final_rows = after_attn + matmul(hidden, ffn_out)
    kept = (
        token_rows,
        factor_one,
        act_one,
        mixed_proj,
        log_total,
        attended,
        after_attn,
        factor_two,
        act_two,
        pre_act,
        hidden,
    )
    return (final_rows, kept)


def layer_backward(grad_final, kept, mask_rows, weights, gain_rows, bias_full):
    (
        token_rows,
        factor_one,
        act_one,
        mixed_proj,
        log_total,
        attended,
        after_attn,
        factor_two,
        act_two,
        pre_act,
        hidden,
    ) = kept
    attn_in, attn_out, ffn_in, ffn_out = weights
    seq_count, length = mask_rows.shape
    branch = grad_final.astype(jnp.bfloat16)
    grad_ffn_out = matmul_tn(hidden, branch)
    grad_hidden = matmul_nt(branch, ffn_out)
    _, gelu_pull = jax.vjp(jax.nn.gelu, pre_act)
    grad_pre = gelu_pull(grad_hidden)[0].astype(jnp.bfloat16)
    grad_ffn_in = matmul_tn(act_two, grad_pre)
    grad_act_two = matmul_nt(grad_pre, ffn_in)
    grad_mid, gain_two = normalize_back(grad_act_two, after_attn, factor_two, gain_rows[1])
    grad_after = grad_final + grad_mid
    branch = grad_after.astype(jnp.bfloat16)
    grad_attn_out = matmul_tn(attended, branch)
    grad_attended = (
        matmul_nt(branch, attn_out).astype(jnp.bfloat16).reshape(seq_count, length, HEADS, HD)
    )
    scores = attention_scores(mixed_proj, mask_rows, bias_full)
    prob_full = jnp.exp(scores - log_total)
    prob_low = prob_full.astype(jnp.bfloat16)
    queries = mixed_proj[:, :, 0]
    key_rows = mixed_proj[:, :, 1]
    grad_probs = jnp.einsum(
        "bqhd,bkhd->bhqk", grad_attended, mixed_proj[:, :, 2], preferred_element_type=jnp.float32
    )
    grad_values = jnp.einsum(
        "bhqk,bqhd->bkhd", prob_low, grad_attended, preferred_element_type=jnp.float32
    )
    grad_scores = prob_full * (grad_probs - jnp.sum(prob_full * grad_probs, -1, keepdims=True))
    grad_scores = grad_scores.astype(jnp.bfloat16)
    grad_bias = jnp.sum(grad_scores, 0, dtype=jnp.float32)
    grad_queries = (
        jnp.einsum("bhqk,bkhd->bqhd", grad_scores, key_rows, preferred_element_type=jnp.float32)
        * SCALE
    )
    grad_keys = (
        jnp.einsum("bhqk,bqhd->bkhd", grad_scores, queries, preferred_element_type=jnp.float32)
        * SCALE
    )
    grad_mixed = (
        jnp.stack([grad_queries, grad_keys, grad_values], 2)
        .astype(jnp.bfloat16)
        .reshape(seq_count * length, -1)
    )
    grad_attn_in = matmul_tn(act_one, grad_mixed)
    grad_act_one = matmul_nt(grad_mixed, attn_in)
    grad_low, gain_one = normalize_back(grad_act_one, token_rows, factor_one, gain_rows[0])
    grad_rows = grad_after + grad_low
    return (
        grad_rows,
        (grad_attn_in, grad_attn_out, grad_ffn_in, grad_ffn_out),
        gain_one,
        gain_two,
        grad_bias,
    )


def adam_update(param, first_moment, second_moment, gradient, factor, rate, decay):
    clipped = gradient * factor
    first_new = BETA_ONE * first_moment + (1.0 - BETA_ONE) * clipped
    second_new = BETA_TWO * second_moment + (1.0 - BETA_TWO) * clipped * clipped
    direction = (
        first_new
        / (1.0 - BETA_ONE**STEP)
        / (jnp.sqrt(second_new / (1.0 - BETA_TWO**STEP)) + ADAM_EPS)
    )
    return (first_new, second_new, param - rate * (direction + decay * param))


class Grid:
    def __init__(self):
        self.dp, self.fs = lax.axis_size("dp"), lax.axis_size("fsdp")
        self.total = self.dp * self.fs
        self.wide = self.fs // 2
        self.tall = self.dp // self.wide

    def here(self):
        d, f = lax.axis_index("dp"), lax.axis_index("fsdp")
        return d // self.wide, lax.rem(d, self.wide), f // 2, lax.rem(f, 2)

    def device(self, z, x, y, core):
        return (z * self.wide + x, y * 2 + core)

    def flat(self, z, x, y, core):
        return (z * self.wide + x) * self.fs + y * 2 + core

    def peer(self, index):
        return (index // self.fs, lax.rem(index, self.fs))


def greet(device, when=None):
    barrier = pltpu.get_barrier_semaphore()

    def signal():
        pl.semaphore_signal(barrier, inc=1, device_id=device, device_id_type=MESH)

    if when is None:
        signal()
    else:
        pl.when(when)(signal)


def meet(count):
    pl.semaphore_wait(pltpu.get_barrier_semaphore(), count)


ROW_BLOCK = 512
WIDE = 3 * D
PACKED = WIDE + D + 4 * D + D
TILE_SEQS = 4


def head_kernel(
    grid,
    col_ref,
    row_ref,
    negative_ref,
    in_ref,
    out_ref,
    up_ref,
    proj_ref,
    down_ref,
    table_hbm,
    packed_out,
    down_out,
    heard,
    slot_ref,
    x0_ref,
    packed_mine,
    down_mine,
    table,
    total,
    answers,
    found,
    messages,
    send_sem,
    recv_sem,
    own_sem,
    row_send,
    row_recv,
    note_send,
    note_recv,
    note_on,
    table_sem,
):
    srcs, outs = (packed_mine, down_mine), (packed_out, down_out)
    count = 2
    z, x, y, core = grid.here()
    tall = grid.tall
    d, f = lax.axis_index("dp"), lax.axis_index("fsdp")
    ux, uy = lax.rem(x + 1 - core, 2), lax.rem(y + core, 2)
    vx, vy = lax.rem(x + core, 2), lax.rem(y + 1 - core, 2)
    up, down = grid.device(z + 1, x, y, core), grid.device(z - 1, x, y, core)
    u_device, v_device = grid.device(z, ux, uy, core), grid.device(z, vx, vy, core)
    sibling = grid.device(z, x, y, 1 - core)
    has_up, has_down = z < tall - 1, z > 0
    me = grid.flat(z, x, y, core)
    f_side, f_y, f_far = y * 2 + 1 - core, (1 - y) * 2 + core, (1 - y) * 2 + 1 - core

    @pl.loop(1, grid.dp)
    def _(step):
        greet((lax.rem(d + step, grid.dp), f))

    greet((d, f_y))
    greet(sibling)
    vocab_rows = table_hbm.shape[0]
    fetch = pltpu.make_async_copy(table_hbm, table.at[pl.ds(0, vocab_rows), :], table_sem)
    fetch.start()
    at = 0
    for ref in (in_ref, out_ref, up_ref, proj_ref):
        packed_mine[:, at : at + ref.shape[1]] = ref[...].astype(jnp.bfloat16)
        at += ref.shape[1]
    down_mine[...] = down_ref[...].astype(jnp.bfloat16)
    local = [pltpu.make_async_copy(srcs[m], outs[m].at[me], own_sem.at[m]) for m in range(count)]
    for item in local:
        item.start()
    meet(grid.dp + 1)

    def copy(m, shard, device, way, own):
        return pltpu.make_async_remote_copy(
            src_ref=srcs[m] if own else outs[m].at[shard],
            dst_ref=outs[m].at[shard],
            send_sem=send_sem.at[way, m, shard],
            recv_sem=recv_sem.at[m, shard],
            device_id=device,
            device_id_type=MESH,
        )

    def send(shard, device, way, own=False):
        for m in range(count):
            copy(m, shard, device, way, own).start()

    def arrived(shard):
        for m in range(count):
            copy(m, shard, sibling, 4, False).wait_recv()

    def sent(shard, device, way):
        for m in range(count):
            copy(m, shard, device, way, False).wait_send()

    @pl.when(has_up)
    def _():
        send(me, up, 0, True)

    @pl.when(has_down)
    def _():
        send(me, down, 1, True)

    send(me, u_device, 2, True)
    send(me, v_device, 3, True)
    send(me, sibling, 4, True)

    tokens = col_ref.shape[0]
    chunk = 128
    ids_row = row_ref[...]
    place_row = lax.broadcasted_iota(jnp.int32, (chunk, tokens), 1)
    place_col = lax.broadcasted_iota(jnp.int32, (chunk, tokens), 0)

    def see(step, repeated):
        start = pl.multiple_of(step * chunk, chunk)
        again = (col_ref[pl.ds(start, chunk), :] == ids_row) & (place_col + start < place_row)
        return jnp.maximum(repeated, jnp.max(jnp.where(again, 1.0, 0.0), 0, keepdims=True))

    repeated = lax.fori_loop(0, tokens // chunk, see, jnp.zeros((1, tokens), jnp.float32))
    firsts = jnp.where(repeated > 0.5, -1.0, ids_row)
    lane = lax.broadcasted_iota(jnp.int32, (chunk, 128), 1).astype(jnp.float32)

    def rank_some(step, carry):
        listed, most = carry
        start = pl.multiple_of(step * chunk, chunk)
        ids = col_ref[pl.ds(start, chunk), :]
        owner = jnp.zeros_like(ids)
        for other in range(1, grid.dp):
            owner = owner + jnp.where(ids >= float(other * vocab_rows), 1.0, 0.0)
        first_id = owner * float(vocab_rows)
        rank = jnp.sum(jnp.where((firsts >= first_id) & (firsts < ids), 1.0, 0.0), 1, keepdims=True)
        slot = jnp.where(rank < float(CAP), owner * float(CAP) + rank, -1.0)
        slot_ref[pl.ds(start, chunk), :] = slot
        rows = []
        for other in range(grid.dp):
            hit = (slot == lane + float(other * CAP)) & (lane < float(CAP))
            rows.append(jnp.max(jnp.where(hit, ids - first_id + 1.0, 0.0), 0, keepdims=True))
        return (jnp.maximum(listed, jnp.concatenate(rows, 0)), jnp.maximum(most, jnp.max(rank, 0, keepdims=True)))

    listed, most = lax.fori_loop(
        0,
        tokens // chunk,
        rank_some,
        (jnp.zeros((grid.dp, 128), jnp.float32), jnp.zeros((1, 1), jnp.float32)),
    )
    spilled = jnp.broadcast_to(jnp.where(most >= float(CAP), 1.0, 0.0), (1, 128))
    rest = jnp.concatenate([negative_ref[...], spilled, jnp.zeros((5, 128), jnp.float32)], 0)
    for other in range(grid.dp):
        messages[other] = jnp.concatenate([listed[other : other + 1] - 1.0, rest], 0)

    def note(peer, slot):
        return pltpu.make_async_remote_copy(
            src_ref=messages.at[peer],
            dst_ref=heard.at[slot],
            send_sem=note_send.at[peer],
            recv_sem=note_recv.at[slot],
            device_id=(peer, f),
            device_id_type=MESH,
        )

    def note_onward(slot, to_side):
        return pltpu.make_async_remote_copy(
            src_ref=heard.at[slot],
            dst_ref=heard.at[slot],
            send_sem=note_on.at[1 if to_side else 0, slot],
            recv_sem=note_recv.at[slot],
            device_id=(d, f_side if to_side else f_y),
            device_id_type=MESH,
        )

    @pl.loop(1, grid.dp)
    def _(step):
        note(lax.rem(d + step, grid.dp), me).start()

    heard[me] = messages[d]

    def row_copy(peer, slot):
        return pltpu.make_async_remote_copy(
            src_ref=answers.at[peer],
            dst_ref=found.at[slot],
            send_sem=row_send.at[peer],
            recv_sem=row_recv.at[slot],
            device_id=(peer, f),
            device_id_type=MESH,
        )

    def pass_z(k):
        low, high = z - k, z + k

        @pl.when(low >= 0)
        def _():
            shard = grid.flat(low, x, y, core)
            arrived(shard)

            @pl.when(has_up)
            def _():
                send(shard, up, 0)

            send(shard, u_device, 2)
            send(shard, v_device, 3)
            send(shard, sibling, 4)

        @pl.when(high < tall)
        def _():
            shard = grid.flat(high, x, y, core)
            arrived(shard)

            @pl.when(has_down)
            def _():
                send(shard, down, 1)

            send(shard, u_device, 2)
            send(shard, v_device, 3)
            send(shard, sibling, 4)

    def both(k, action):
        pl.when(z - k >= 0)(lambda: action(z - k))
        if k:
            pl.when(z + k < tall)(lambda: action(z + k))

    def pass_u(level):
        shard = grid.flat(level, ux, uy, core)
        arrived(shard)
        send(shard, v_device, 3)
        send(shard, sibling, 4)

    def pass_v(level):
        shard = grid.flat(level, vx, vy, core)
        arrived(shard)
        send(shard, sibling, 4)

    def pass_far(level):
        shard = grid.flat(level, 1 - x, 1 - y, core)
        arrived(shard)
        send(shard, sibling, 4)

    both(0, pass_u)

    @pl.loop(1, grid.dp)
    def _(step):
        note(d, lax.rem(d + step, grid.dp) * grid.fs + f).wait_recv()

    @pl.loop(0, grid.dp)
    def _(peer):
        note_onward(peer * grid.fs + f, False).start()
        note_onward(peer * grid.fs + f, True).start()

    pass_z(1)
    fetch.wait()
    padding = table.shape[0] - vocab_rows
    if padding:
        table[vocab_rows:, :] = jnp.zeros((padding, D), jnp.float32)
    asked = jnp.concatenate([heard[peer * grid.fs + f, 0:1, :] for peer in range(grid.dp)], 0)
    asked = jnp.transpose(asked)
    block = ROW_BLOCK
    total[...] = jnp.zeros_like(total)
    lanes = lax.broadcasted_iota(jnp.int32, (CAP, block), 1).astype(jnp.float32)

    def pick(step):
        start = pl.multiple_of(step * block, block)
        some = table[pl.ds(start, block), :].astype(jnp.bfloat16)
        wanted = lanes + (step * block).astype(jnp.float32)
        hot = jnp.concatenate(
            [
                jnp.where(asked[:CAP, peer : peer + 1] == wanted, 1.0, 0.0)
                for peer in range(grid.dp)
            ],
            0,
        ).astype(jnp.bfloat16)
        total[...] += matmul(hot, some)

    steps = table.shape[0] // block
    pl.loop(0, steps)(pick)
    answers[...] = total[...].reshape(answers.shape).astype(jnp.bfloat16)
    found[d] = answers[d]

    @pl.loop(1, grid.dp)
    def _(step):
        row_copy(lax.rem(d + step, grid.dp), d).start()

    both(0, pass_v)
    for k in range(1, tall + 1):
        if 1 < k < tall:
            pass_z(k)
        if k < tall:
            both(k, pass_u)
            both(k, pass_v)
        both(k - 1, pass_far)

    @pl.loop(1, grid.dp)
    def _(step):
        row_copy(d, lax.rem(d + step, grid.dp)).wait_recv()

    slots = grid.dp * CAP
    some = tokens // 4
    wide_lane = lax.broadcasted_iota(jnp.int32, (some, slots), 1).astype(jnp.float32)
    rows = found[...].reshape(slots, D)

    @pl.loop(0, 4)
    def _(step):
        start = pl.multiple_of(step * some, some)
        hot = jnp.where(slot_ref[pl.ds(start, some), :] == wide_lane, 1.0, 0.0).astype(jnp.bfloat16)
        x0_ref[pl.ds(start, some), :] = matmul(hot, rows)

    @pl.loop(0, grid.dp)
    def _(peer):
        note(d, peer * grid.fs + f_y).wait_recv()
        note_onward(peer * grid.fs + f_y, True).start()

    @pl.loop(0, grid.dp)
    def _(peer):
        note(d, peer * grid.fs + f_side).wait_recv()
        note(d, peer * grid.fs + f_far).wait_recv()
        note_onward(peer * grid.fs + f, False).wait_send()
        note_onward(peer * grid.fs + f, True).wait_send()
        note_onward(peer * grid.fs + f_y, True).wait_send()

    @pl.loop(1, grid.dp)
    def _(step):
        peer = lax.rem(d + step, grid.dp)
        row_copy(peer, d).wait_send()
        note(peer, me).wait_send()

    @pl.loop(0, tall)
    def _(level):
        for xx in range(2):
            for yy in range(2):
                arrived(grid.flat(level, xx, yy, 1 - core))
                sent(grid.flat(level, xx, yy, core), sibling, 4)
        shard, other = grid.flat(level, x, y, core), grid.flat(level, ux, uy, core)

        @pl.when((level <= z) & has_up)
        def _():
            sent(shard, up, 0)

        @pl.when((level >= z) & has_down)
        def _():
            sent(shard, down, 1)

        sent(shard, u_device, 2)
        sent(shard, v_device, 3)
        sent(other, v_device, 3)

    for item in local:
        item.wait()


def run_head(ids, negatives, attn_in, attn_out, ffn_in, proj_head, ffn_out, table, number):
    grid = Grid()
    tokens = ids.shape[0]
    wide = ids.astype(jnp.float32)
    row = jnp.zeros((1, 128), jnp.float32).at[0, : negatives.shape[0]].set(negatives.astype(jnp.float32))
    shapes = ((attn_in.shape[0], PACKED), ffn_out.shape)
    blocks = -(-table.shape[0] // ROW_BLOCK)
    anywhere, inside = pl.BlockSpec(memory_space=pl.ANY), pl.BlockSpec(memory_space=pltpu.VMEM)
    dma = pltpu.SemaphoreType.DMA
    line, everyone = dma((grid.dp,)), dma((grid.total,))
    return pl.pallas_call(
        functools.partial(head_kernel, grid),
        out_shape=[jax.ShapeDtypeStruct((grid.total,) + shape, jnp.bfloat16) for shape in shapes]
        + [
            jax.ShapeDtypeStruct((grid.total, 8, 128), jnp.float32),
            jax.ShapeDtypeStruct((tokens, 1), jnp.float32),
            jax.ShapeDtypeStruct((tokens, D), jnp.float32),
        ],
        in_specs=[inside] * 8 + [anywhere],
        out_specs=[anywhere] * 2 + [inside] * 3,
        scratch_shapes=[pltpu.VMEM(shape, jnp.bfloat16) for shape in shapes]
        + [
            pltpu.VMEM((blocks * ROW_BLOCK, D), jnp.float32),
            pltpu.VMEM((grid.dp * CAP, D), jnp.float32),
            pltpu.VMEM((grid.dp, CAP, D), jnp.bfloat16),
            pltpu.VMEM((grid.dp, CAP, D), jnp.bfloat16),
            pltpu.VMEM((grid.dp, 8, 128), jnp.float32),
            dma((5, 2, grid.total)),
            dma((2, grid.total)),
            dma((2,)),
            line,
            line,
            line,
            everyone,
            dma((2, grid.total)),
            dma,
        ],
        compiler_params=pltpu.CompilerParams(
            collective_id=number, has_side_effects=True, vmem_limit_bytes=48 * 1024 * 1024
        ),
    )(wide.reshape(tokens, 1), wide.reshape(1, tokens), row, attn_in, attn_out, ffn_in, proj_head, ffn_out, table)


def lane_is(shape, low, high):
    lanes = lax.broadcasted_iota(jnp.int32, shape, len(shape) - 1)
    return (lanes >= low) & (lanes < high)


def gelu_parts(t):
    inner = np.float32(np.sqrt(2 / np.pi)) * (t + 0.044715 * (t * t * t))
    tan = jnp.tanh(inner)
    return 0.5 * (1.0 + tan), tan


def forward_kernel(
    x0_ref,
    mask_col_ref,
    gains_ref,
    bias_ref,
    packed_hbm,
    down_hbm,
    mixed_ref,
    attended_ref,
    total_ref,
    after_ref,
    pre_ref,
    final_ref,
    pooled_ref,
    projected_ref,
    packed,
    down,
    load_sem,
):
    step = pl.program_id(0)
    tile_seqs = x0_ref.shape[0] // L
    edges = (0, WIDE, WIDE + D, WIDE + 5 * D, PACKED)

    def load(k):
        if k == 4:
            return pltpu.make_async_copy(down_hbm, down, load_sem.at[k])
        part = pl.ds(edges[k], edges[k + 1] - edges[k])
        return pltpu.make_async_copy(packed_hbm.at[:, part], packed.at[:, part], load_sem.at[k])

    def loaded(k):
        @pl.when(step == 0)
        def _():
            load(k).wait()

    @pl.when(step == 0)
    def _():
        for k in (0, 1, 2, 4, 3):
            load(k).start()

    x0 = x0_ref[...]
    act_one = normalize(x0, gains_ref[0:1, :])[0].astype(jnp.bfloat16)
    loaded(0)
    for at in range(0, WIDE, D):
        mixed_ref[:, at : at + D] = matmul(act_one, packed[:, at : at + D]).astype(jnp.bfloat16)

    zero = jnp.zeros((), jnp.bfloat16)
    for s in range(tile_seqs):
        rows = slice(s * L, (s + 1) * L)
        keep = jnp.where(mask_col_ref[rows, :] > 0, 0.0, -1000000000.0)
        for pair in range(HEADS // 2):
            at = pair * 128
            query = mixed_ref[rows, at : at + 128]
            key = mixed_ref[rows, D + at : D + at + 128]
            value = mixed_ref[rows, 2 * D + at : 2 * D + at + 128]
            mine = lane_is((L, 128), 0, HD)
            keys = jnp.concatenate([jnp.where(mine, key, zero), jnp.where(mine, zero, key)], 0)
            scores = (matmul_nt(keys, query) * SCALE).reshape(2, L, L)
            scores = scores + bias_ref[2 * pair : 2 * pair + 2] + keep[None]
            row_max = jnp.max(scores, 1, keepdims=True)
            powers = jnp.exp(scores - row_max)
            row_sum = jnp.sum(powers, 1, keepdims=True)
            prob = (powers * (1.0 / row_sum)).astype(jnp.bfloat16)
            total_ref[s, 2 * pair : 2 * pair + 2, :] = (row_max + jnp.log(row_sum))[:, 0, :]
            flipped = jnp.transpose(value)
            both = jnp.concatenate([matmul(flipped[:HD], prob[0]), matmul(flipped[HD:], prob[1])], 0)
            both = jnp.transpose(both)
            attended_ref[rows, at : at + 128] = both.astype(jnp.bfloat16)

    loaded(1)
    after = x0 + matmul(attended_ref[...], packed[:, WIDE : WIDE + D])
    after_ref[...] = after
    act_two = normalize(after, gains_ref[1:2, :])[0].astype(jnp.bfloat16)
    loaded(2)
    loaded(4)
    final = after
    for j in range(4):
        at = WIDE + D + j * D
        pre = matmul(act_two, packed[:, at : at + D])
        pre_ref[:, j * D : (j + 1) * D] = pre
        hidden = (pre * gelu_parts(pre)[0]).astype(jnp.bfloat16)
        final = final + matmul(hidden, down[j * D : (j + 1) * D, :])
    final_ref[...] = final
    normed = normalize(final, gains_ref[2:3, :])[0]
    weight = mask_col_ref[...]
    for s in range(tile_seqs):
        rows = slice(s * L, (s + 1) * L)
        count = jnp.sum(weight[rows], 0, keepdims=True)
        row = jnp.sum(normed[rows] * weight[rows], 0, keepdims=True) / count
        pooled_ref[pl.ds(step * tile_seqs + s, 1), :] = row

    @pl.when(step == pl.num_programs(0) - 1)
    def _():
        load(3).wait()
        projected_ref[...] = matmul(pooled_ref[...].astype(jnp.bfloat16), packed[:, PACKED - D :])


def run_forward(x0, mask_col, gains, bias_full, packed, down):
    tokens = x0.shape[0]
    seqs = tokens // L
    tile = TILE_SEQS * L
    steps = tokens // tile

    def rows(width):
        return pl.BlockSpec((tile, width), lambda i: (i, 0))

    def whole(*shape):
        return pl.BlockSpec(shape, lambda i: (0,) * len(shape), pipeline_mode=pl.Buffered(1))

    def kept(width, dtype):
        return jax.ShapeDtypeStruct((tokens, width), dtype)

    anywhere = pl.BlockSpec(memory_space=pl.ANY)
    return pl.pallas_call(
        forward_kernel,
        grid=(steps,),
        out_shape=[
            kept(WIDE, jnp.bfloat16),
            kept(D, jnp.bfloat16),
            jax.ShapeDtypeStruct((seqs, HEADS, L), jnp.float32),
            kept(D, jnp.float32),
            kept(4 * D, jnp.float32),
            kept(D, jnp.float32),
            jax.ShapeDtypeStruct((seqs, D), jnp.float32),
            jax.ShapeDtypeStruct((seqs, D), jnp.float32),
        ],
        in_specs=[
            rows(D),
            rows(1),
            whole(3, D),
            whole(HEADS, L, L),
            anywhere,
            anywhere,
        ],
        out_specs=[rows(WIDE), rows(D), pl.BlockSpec((TILE_SEQS, HEADS, L), lambda i: (i, 0, 0)), rows(D), rows(4 * D), rows(D), whole(seqs, D), whole(seqs, D)],
        scratch_shapes=[
            pltpu.VMEM((D, PACKED), jnp.bfloat16),
            pltpu.VMEM((4 * D, D), jnp.bfloat16),
            pltpu.SemaphoreType.DMA((5,)),
        ],
        compiler_params=pltpu.CompilerParams(vmem_limit_bytes=60 * 1024 * 1024),
    )(x0, mask_col, gains, bias_full, packed, down)


def loss_kernel(
    grid, pairs_here, projected_ref, target_ref, scale_ref, grad_ref, loss_ref, mine, others, grads, send_sem, recv_sem
):
    me = lax.axis_index("dp") * grid.fs + lax.axis_index("fsdp")
    each = 2 * pairs_here
    half = D // 2

    @pl.loop(1, grid.total)
    def _(step):
        greet(grid.peer(lax.rem(me + step, grid.total)))

    projected = projected_ref[...]
    factor = lax.rsqrt(jnp.sum(projected * projected, -1, keepdims=True) + EPS)
    unit = projected * factor
    mine[...] = jnp.concatenate([unit[:, :half], unit[:, half:]], 0).astype(jnp.bfloat16)
    meet(grid.total - 1)

    def copy(peer, slot):
        return pltpu.make_async_remote_copy(
            src_ref=mine,
            dst_ref=others.at[slot],
            send_sem=send_sem.at[peer],
            recv_sem=recv_sem.at[slot],
            device_id=grid.peer(peer),
            device_id_type=MESH,
        )

    @pl.loop(1, grid.total)
    def _(step):
        copy(lax.rem(me + step, grid.total), me).start()

    others[me] = mine[...]

    @pl.loop(1, grid.total)
    def _(step):
        peer = lax.rem(me + step, grid.total)
        copy(peer, peer).wait_recv()

    count = grid.total * each
    wide = others[...].astype(jnp.float32)
    units = jnp.concatenate(
        [wide[:, :each].reshape(count, half), wide[:, each:].reshape(count, half)], 1
    ).astype(jnp.bfloat16)
    similar = matmul_nt(units, units)
    row = lax.broadcasted_iota(jnp.int32, (count, count), 0)
    column = lax.broadcasted_iota(jnp.int32, (count, count), 1)
    used = (lax.rem(row, each) < pairs_here) & (lax.rem(column, each) >= pairs_here)
    own = used & (column == row + pairs_here)
    negative = used & (column == target_ref[...])
    sim_scale = jnp.exp(scale_ref[...])
    own_mask = jnp.where(own, 1.0, 0.0)
    negative_mask = jnp.where(negative, 1.0, 0.0)
    logits = sim_scale * similar - MARGIN * own_mask
    diagonal = jnp.sum(logits * own_mask, 1, keepdims=True)
    hardest = jnp.sum(logits * negative_mask, 1, keepdims=True)
    row_max = jnp.max(jnp.where(used, logits, -3e38), 1, keepdims=True)
    powers = jnp.where(used, jnp.exp(jnp.minimum(logits - row_max, 0.0)), 0.0)
    row_sum = jnp.sum(powers, 1, keepdims=True)
    is_query = lax.rem(lax.broadcasted_iota(jnp.int32, (count, 1), 0), each) < pairs_here
    gap = hardest - diagonal
    softplus = jnp.maximum(gap, 0.0) + jnp.log(1.0 + jnp.exp(-jnp.abs(gap)))
    row_sum = jnp.where(is_query, row_sum, 1.0)
    losses = jnp.where(is_query, row_max + jnp.log(row_sum) - diagonal + softplus, 0.0)
    gate = 1.0 / (1.0 + jnp.exp(-gap))
    grad_logits = jnp.where(
        used, powers / row_sum - own_mask + gate * (negative_mask - own_mask), 0.0
    )
    loss_ref[0:1, :] = jnp.broadcast_to(jnp.sum(losses, 0, keepdims=True), (1, 128))
    grad_scale = sim_scale * jnp.sum(
        jnp.sum(grad_logits * similar, 1, keepdims=True), 0, keepdims=True
    )
    loss_ref[1:2, :] = jnp.broadcast_to(grad_scale, (1, 128))
    loss_ref[2:8, :] = jnp.zeros((6, 128), jnp.float32)
    grad_similar = sim_scale * grad_logits
    grads[...] = grad_similar + jnp.transpose(grad_similar)
    first = pl.multiple_of(me * each, each)
    grad_units = matmul(grads[pl.ds(first, each), :].astype(jnp.bfloat16), units)
    grad_units = grad_units.astype(jnp.bfloat16).astype(jnp.float32)
    grad_ref[...] = (
        factor * (grad_units - unit * jnp.sum(grad_units * unit, -1, keepdims=True))
    ).astype(jnp.bfloat16)

    @pl.loop(1, grid.total)
    def _(step):
        peer = lax.rem(me + step, grid.total)
        copy(peer, peer).wait_send()


def run_loss(projected, target, log_scale, number):
    grid = Grid()
    each = projected.shape[0]
    count = grid.total * each
    inside = pl.BlockSpec(memory_space=pltpu.VMEM)
    dma = pltpu.SemaphoreType.DMA((grid.total,))
    return pl.pallas_call(
        functools.partial(loss_kernel, grid, each // 2),
        out_shape=[
            jax.ShapeDtypeStruct((each, D), jnp.bfloat16),
            jax.ShapeDtypeStruct((8, 128), jnp.float32),
        ],
        in_specs=[inside] * 3,
        out_specs=[inside] * 2,
        scratch_shapes=[
            pltpu.VMEM((2 * each, D // 2), jnp.bfloat16),
            pltpu.VMEM((grid.total, 2 * each, D // 2), jnp.bfloat16),
            pltpu.VMEM((count, count), jnp.float32),
            dma,
            dma,
        ],
        compiler_params=pltpu.CompilerParams(collective_id=number, has_side_effects=True),
    )(projected, target, log_scale)


class Tree:

    @staticmethod
    def scratch(grid, blocks):
        count, tall = len(blocks), grid.tall
        leads = ((tall, 2, 2), (tall, 2, 2), (tall, 2), (tall,), (tall,), (tall,))
        dma = pltpu.SemaphoreType.DMA
        level, pair = dma((count, tall)), dma((count, tall, 2))
        buffers = [pltpu.VMEM(lead + block, jnp.bfloat16) for lead in leads for block in blocks]
        return buffers + [level, level, level, pair, pair] + [level] * 5

    @staticmethod
    def size(count):
        return 6 * count + 10

    def __init__(self, grid, srcs, scratch):
        count = len(srcs)
        self.grid, self.count, self.srcs = grid, count, srcs
        self.acc, self.from_side, self.from_v, self.from_u, self.from_low, self.from_high = [
            scratch[k * count : (k + 1) * count] for k in range(6)
        ]
        (
            self.load_sem,
            self.side_send,
            self.side_recv,
            self.v_send,
            self.v_recv,
            self.u_send,
            self.u_recv,
            self.z_send,
            self.low_recv,
            self.high_recv,
        ) = scratch[6 * count :]
        z, x, y, core = self.place = grid.here()
        tall = grid.tall
        self.up, self.down = grid.device(z + 1, x, y, core), grid.device(z - 1, x, y, core)
        self.has_up, self.has_down = z < tall - 1, z > 0
        self.u = lax.rem(x + 1 - core, 2), lax.rem(y + core, 2)
        self.v = lax.rem(x + core, 2), lax.rem(y + 1 - core, 2)
        self.u_device = grid.device(z, *self.u, core)
        self.v_device = grid.device(z, *self.v, core)
        self.sibling = grid.device(z, x, y, 1 - core)
        self.levels = [self.level_of(j) for j in range(tall)]

    def greet_all(self):
        greet(self.u_device)
        greet(self.v_device)
        greet(self.sibling)
        greet(self.up, self.has_up)
        greet(self.down, self.has_down)
        return 3 + self.has_up.astype(jnp.int32) + self.has_down.astype(jnp.int32)

    def each(self, action):
        for m in range(self.count):
            action(m)

    def level_of(self, j):
        tall = self.grid.tall
        tables = [
            sorted(range(tall), key=lambda level: (-abs(level - own), -level))[j] for own in range(tall)
        ]
        value = tables[0]
        for own in range(1, tall):
            value = jnp.where(self.place[0] == own, tables[own], value)
        return value

    def load(self, m, level):
        core = self.place[3]
        return pltpu.make_async_copy(
            self.srcs[m].at[level, :, :, core], self.acc[m].at[level], self.load_sem.at[m, level]
        )

    def remote(self, src, dst, send_sem, recv_sem, device):
        return pltpu.make_async_remote_copy(
            src_ref=src,
            dst_ref=dst,
            send_sem=send_sem,
            recv_sem=recv_sem,
            device_id=device,
            device_id_type=MESH,
        )

    def side(self, m, level):
        return self.remote(
            self.srcs[m].at[level, :, :, 1 - self.place[3]],
            self.from_side[m].at[level],
            self.side_send.at[m, level],
            self.side_recv.at[m, level],
            self.sibling,
        )

    def v_copy(self, m, level, along_u):
        z, x, y, core = self.place
        xx, yy = (1 - x, 1 - y) if along_u else self.v
        return self.remote(
            self.acc[m].at[level, xx, yy],
            self.from_v[m].at[level, along_u],
            self.v_send.at[m, level, along_u],
            self.v_recv.at[m, level, along_u],
            self.v_device,
        )

    def u_copy(self, m, level):
        return self.remote(
            self.acc[m].at[level, self.u[0], self.u[1]],
            self.from_u[m].at[level],
            self.u_send.at[m, level],
            self.u_recv.at[m, level],
            self.u_device,
        )

    def z_copy(self, m, level, upward):
        z, x, y, core = self.place
        return self.remote(
            self.acc[m].at[level, x, y],
            (self.from_low if upward else self.from_high)[m].at[level],
            self.z_send.at[m, level],
            (self.low_recv if upward else self.high_recv).at[m, level],
            self.up if upward else self.down,
        )

    def add(self, m, level, xx, yy, other):
        total = self.acc[m][level, xx, yy].astype(jnp.float32) + other.astype(jnp.float32)
        self.acc[m][level, xx, yy] = total.astype(jnp.bfloat16)

    def loads(self):
        for level in self.levels:
            self.each(lambda m: self.load(m, level).start())

    def sides(self):
        for level in self.levels:
            self.each(lambda m: self.side(m, level).start())

    def first(self, j):
        level = self.levels[j]

        def run(m):
            self.load(m, level).wait()
            self.side(m, level).wait_recv()
            for xx in range(2):
                for yy in range(2):
                    self.add(m, level, xx, yy, self.from_side[m][level, xx, yy])
            self.v_copy(m, level, 1).start()
            self.v_copy(m, level, 0).start()

        self.each(run)

    def second(self, j):
        z, x, y, core = self.place
        level = self.levels[j]

        def run(m):
            self.v_copy(m, level, 1).wait_recv()
            self.add(m, level, self.u[0], self.u[1], self.from_v[m][level, 1])
            self.u_copy(m, level).start()

        def run_own(m):
            self.v_copy(m, level, 0).wait_recv()
            self.add(m, level, x, y, self.from_v[m][level, 0])

        self.each(run)
        self.each(run_own)

    def third(self, j):
        z, x, y, core = self.place
        level = self.levels[j]

        def run(m):
            self.u_copy(m, level).wait_recv()
            self.add(m, level, x, y, self.from_u[m][level])

            @pl.when((level >= z) & self.has_down)
            def _():
                self.z_copy(m, level, True).wait_recv()
                self.add(m, level, x, y, self.from_low[m][level])

            @pl.when((level <= z) & self.has_up)
            def _():
                self.z_copy(m, level, False).wait_recv()
                self.add(m, level, x, y, self.from_high[m][level])

            @pl.when(level > z)
            def _():
                self.z_copy(m, level, True).start()

            @pl.when(level < z)
            def _():
                self.z_copy(m, level, False).start()

        self.each(run)

    def own(self, m):
        z, x, y, core = self.place
        return self.acc[m][z, x, y].astype(jnp.float32)

    def drain(self):
        for level in self.levels:
            self.each(lambda m: self.side(m, level).wait_send())
            self.each(lambda m: self.v_copy(m, level, 0).wait_send())
            self.each(lambda m: self.v_copy(m, level, 1).wait_send())
            self.each(lambda m: self.u_copy(m, level).wait_send())

            @pl.when(level != self.place[0])
            def _():
                self.each(lambda m: self.z_copy(m, level, True).wait_send())


def fold(values):
    n, lanes = values.shape
    part = jnp.sum(values.reshape(n // 8, 8, lanes), 0)
    total = part[:, :128]
    for at in range(128, lanes, 128):
        total = total + part[:, at : at + 128]
    return total


def gain_back(gains_ref, grads_ref, k, grad_out, inputs):
    factor = lax.rsqrt(jnp.mean(inputs * inputs, -1, keepdims=True) + EPS)
    scaled = grad_out * gains_ref[k : k + 1, :]
    grads_ref[k : k + 1, :] += jnp.sum(grad_out * inputs * factor, 0, keepdims=True)
    return factor * (
        scaled - inputs * (factor * factor * jnp.mean(scaled * inputs, -1, keepdims=True))
    )


BACK_SEQS = 2


def ffn_back_kernel(
    final_ref,
    after_ref,
    mask_col_ref,
    gains_ref,
    pooled_ref,
    grad_proj_ref,
    pre_hbm,
    packed_hbm,
    down_hbm,
    grad_after_ref,
    grad_gains_ref,
    grad_up_hbm,
    grad_down_hbm,
    up,
    head,
    down,
    branch,
    act_two,
    wide,
    hidden,
    grad_pre,
    grad_act,
    pre,
    grad_pooled,
    stage,
    load_sem,
    pre_sem,
    store_sem,
):
    tokens = final_ref.shape[0]
    tile = BACK_SEQS * L

    def load(k):
        if k == 0:
            return pltpu.make_async_copy(packed_hbm.at[:, pl.ds(PACKED - D, D)], head, load_sem.at[0])
        if k == 1:
            return pltpu.make_async_copy(down_hbm, down, load_sem.at[1])
        return pltpu.make_async_copy(packed_hbm.at[:, pl.ds(WIDE + D, 4 * D)], up, load_sem.at[2])

    def load_pre(j):
        return pltpu.make_async_copy(pre_hbm.at[:, pl.ds(j * D, D)], pre.at[j % 2], pre_sem.at[j % 2])

    load(0).start()
    load_pre(0).start()
    load(1).start()
    load(2).start()
    grad_gains_ref[...] = jnp.zeros_like(grad_gains_ref)
    load(0).wait()
    grad_pooled[...] = matmul_nt(grad_proj_ref[...], head[...])

    @pl.loop(0, tokens // tile)
    def _(step):
        rows = pl.ds(pl.multiple_of(step * tile, tile), tile)
        weight = mask_col_ref[rows, :]
        pieces = []
        for s in range(BACK_SEQS):
            part = weight[s * L : (s + 1) * L]
            count = jnp.sum(part, 0, keepdims=True)
            pieces.append(part * (grad_pooled[pl.ds(step * BACK_SEQS + s, 1), :] / count))
        grad = gain_back(gains_ref, grad_gains_ref, 2, jnp.concatenate(pieces, 0), final_ref[rows, :])
        grad_after_ref[rows, :] = grad
        branch[rows, :] = grad.astype(jnp.bfloat16)
        act_two[rows, :] = normalize(after_ref[rows, :], gains_ref[1:2, :])[0].astype(jnp.bfloat16)

    stores = []

    def store(value, to):
        slot = len(stores) % 2
        if len(stores) >= 2:
            stores[-2].wait()
        stage[slot] = value.astype(jnp.bfloat16)
        stores.append(pltpu.make_async_copy(stage.at[slot], to, store_sem.at[slot]))
        stores[-1].start()

    load(1).wait()
    for j in range(4):
        part = slice(j * D, (j + 1) * D)
        if j < 3:
            load_pre(j + 1).start()
        wide[...] = matmul_nt(branch[...], down[part, :])
        load_pre(j).wait()

        @pl.loop(0, tokens // tile)
        def _(step):
            rows = pl.ds(pl.multiple_of(step * tile, tile), tile)
            some = pre[j % 2, rows, :]
            half, tan = gelu_parts(some)
            hidden[rows, :] = (some * half).astype(jnp.bfloat16)
            slope = np.float32(np.sqrt(2 / np.pi)) * (1.0 + (3 * 0.044715) * (some * some))
            slope = half + 0.5 * some * (1.0 - tan * tan) * slope
            grad_pre[rows, :] = (wide[rows, :] * slope).astype(jnp.bfloat16)

        if j == 0:
            load(2).wait()
            grad_act[...] = matmul_nt(grad_pre[...], up[:, part])
        else:
            grad_act[...] += matmul_nt(grad_pre[...], up[:, part])
        store(matmul_tn(hidden[...], branch[...]), grad_down_hbm.at[pl.ds(j * D, D), :])
        store(matmul_tn(act_two[...], grad_pre[...]), grad_up_hbm.at[:, pl.ds(j * D, D)])
    store(
        matmul_tn(pooled_ref[...].astype(jnp.bfloat16), grad_proj_ref[...]),
        grad_up_hbm.at[:, pl.ds(4 * D, D)],
    )

    @pl.loop(0, tokens // tile)
    def _(step):
        rows = pl.ds(pl.multiple_of(step * tile, tile), tile)
        grad = gain_back(gains_ref, grad_gains_ref, 1, grad_act[rows, :], after_ref[rows, :])
        grad_after_ref[rows, :] += grad

    stores[-2].wait()
    stores[-1].wait()


def run_ffn_back(final, after, mask_col, gains, pooled, grad_proj, pre, packed, down):
    tokens, seqs = final.shape[0], pooled.shape[0]
    anywhere, inside = pl.BlockSpec(memory_space=pl.ANY), pl.BlockSpec(memory_space=pltpu.VMEM)

    def low(*shape):
        return pltpu.VMEM(shape, jnp.bfloat16)

    def full(*shape):
        return pltpu.VMEM(shape, jnp.float32)

    return pl.pallas_call(
        ffn_back_kernel,
        out_shape=[
            jax.ShapeDtypeStruct((tokens, D), jnp.float32),
            jax.ShapeDtypeStruct((3, D), jnp.float32),
            jax.ShapeDtypeStruct((D, 5 * D), jnp.bfloat16),
            jax.ShapeDtypeStruct((4 * D, D), jnp.bfloat16),
        ],
        in_specs=[inside] * 6 + [anywhere] * 3,
        out_specs=[inside] * 2 + [anywhere] * 2,
        scratch_shapes=[
            low(D, 4 * D),
            low(D, D),
            low(4 * D, D),
            low(tokens, D),
            low(tokens, D),
            full(tokens, D),
            low(tokens, D),
            low(tokens, D),
            full(tokens, D),
            full(2, tokens, D),
            full(seqs, D),
            low(2, D, D),
            pltpu.SemaphoreType.DMA((3,)),
            pltpu.SemaphoreType.DMA((2,)),
            pltpu.SemaphoreType.DMA((2,)),
        ],
        compiler_params=pltpu.CompilerParams(vmem_limit_bytes=62 * 1024 * 1024),
    )(final, after, mask_col, gains, pooled, grad_proj, pre, packed, down)


def attn_back_kernel(grid, *refs):
    x0_ref, mask_col_ref, mixed_ref, attended, total_ref, grad_after_ref, gains_ref, bias_ref, packed_hbm = refs[:9]
    srcs = refs[9:11]
    rows_ref, grad_gains_ref, grad_bias_ref, grad_attn_hbm = refs[11:15]
    outs, square_ref = refs[15:17], refs[17]
    packed, act_one, branch_one, grad_mixed, stage, load_sem, store_sem = refs[18:25]
    tree = Tree(grid, srcs, refs[25:])
    step = pl.program_id(0)
    last_step = pl.num_programs(0) - 1
    tile_seqs = x0_ref.shape[0] // L
    tile = tile_seqs * L
    base = pl.multiple_of(step * tile, tile)

    def load(k):
        part = pl.ds(WIDE, D) if k else pl.ds(0, WIDE)
        return pltpu.make_async_copy(packed_hbm.at[:, part], packed.at[:, part], load_sem.at[k])

    @pl.when(step == 0)
    def _():
        friends = tree.greet_all()
        load(1).start()
        load(0).start()
        tree.loads()
        grad_gains_ref[...] = jnp.zeros_like(grad_gains_ref)
        grad_bias_ref[...] = jnp.zeros_like(grad_bias_ref)
        meet(friends)
        tree.sides()
        load(1).wait()

    rows = pl.ds(base, tile)
    grad_after = grad_after_ref[...]
    weight = mask_col_ref[...]
    branch = grad_after.astype(jnp.bfloat16)
    branch_one[rows, :] = branch
    grad_attended = matmul_nt(branch, packed[:, WIDE:]).astype(jnp.bfloat16)
    act_one[rows, :] = normalize(x0_ref[...], gains_ref[0:1, :])[0].astype(jnp.bfloat16)

    def at_step(number, action, *levels):
        @pl.when(step == number)
        def _():
            for j in levels:
                action(j)

    at_step(0, tree.first, 0, 1)
    at_step(1, tree.second, 0)
    at_step(2, tree.third, 0)
    at_step(3, tree.third, 1)
    zero = jnp.zeros((), jnp.bfloat16)
    mine = lane_is((L, 128), 0, HD)
    for s in range(tile_seqs):
        part = slice(s * L, (s + 1) * L)
        here = pl.ds(pl.multiple_of(base + s * L, L), L)
        keep = jnp.where(weight[part] > 0, 0.0, -1000000000.0)
        for pair in range(HEADS // 2):
            at = pair * 128
            query = mixed_ref[part, at : at + 128]
            key = mixed_ref[part, D + at : D + at + 128]
            value = mixed_ref[part, 2 * D + at : 2 * D + at + 128]
            grad_out = grad_attended[part, at : at + 128]
            keys = jnp.concatenate([jnp.where(mine, key, zero), jnp.where(mine, zero, key)], 0)
            values = jnp.concatenate([jnp.where(mine, value, zero), jnp.where(mine, zero, value)], 0)
            scores = (matmul_nt(keys, query) * SCALE).reshape(2, L, L)
            scores = scores + bias_ref[2 * pair : 2 * pair + 2] + keep[None]
            prob = jnp.exp(scores - total_ref[s, 2 * pair : 2 * pair + 2, :][:, None, :])
            grad_prob = matmul_nt(values, grad_out).reshape(2, L, L)
            mean = jnp.sum(prob * grad_prob, 1, keepdims=True)
            grad_scores = (prob * (grad_prob - mean)).astype(jnp.bfloat16)
            grad_bias_ref[2 * pair : 2 * pair + 2] += grad_scores.astype(jnp.float32)
            prob_low = prob.astype(jnp.bfloat16)
            flipped = jnp.transpose(key)
            grad_query = jnp.concatenate(
                [matmul(flipped[:HD], grad_scores[0]), matmul(flipped[HD:], grad_scores[1])], 0
            )
            grad_mixed[here, at : at + 128] = (jnp.transpose(grad_query) * SCALE).astype(jnp.bfloat16)
            grad_keys = matmul(grad_scores.reshape(2 * L, L), query)
            grad_key = jnp.where(mine, grad_keys[:L], grad_keys[L:]) * SCALE
            grad_mixed[here, D + at : D + at + 128] = grad_key.astype(jnp.bfloat16)
            grad_values = matmul(prob_low.reshape(2 * L, L), grad_out)
            grad_value = jnp.where(mine, grad_values[:L], grad_values[L:])
            grad_mixed[here, 2 * D + at : 2 * D + at + 128] = grad_value.astype(jnp.bfloat16)

    @pl.when(step == 0)
    def _():
        tree.first(2)
        tree.first(3)
        load(0).wait()

    at_step(1, tree.second, 1)
    at_step(2, tree.second, 2)
    at_step(3, tree.second, 3)
    grad_act = matmul_nt(grad_mixed[rows, :], packed[:, :WIDE])
    grad_low = gain_back(gains_ref, grad_gains_ref, 0, grad_act, x0_ref[...])
    rows_ref[...] = (grad_after + grad_low).astype(jnp.bfloat16)

    @pl.when(step == last_step)
    def _():
        tree.third(2)
        jobs = [(attended, branch_one, slice(0, D), 3)]
        for j in range(3):
            jobs.append((act_one, grad_mixed, slice(j * D, (j + 1) * D), j))
        copies = []
        for number, (left, right, part, at) in enumerate(jobs):
            slot = number % 2
            if number >= 2:
                copies[number - 2].wait()
            stage[slot] = matmul_tn(left[...], right[:, part]).astype(jnp.bfloat16)
            to = grad_attn_hbm.at[:, pl.ds(at * D, D)]
            copies.append(pltpu.make_async_copy(stage.at[slot], to, store_sem.at[slot]))
            copies[-1].start()
        tree.third(3)
        square_ref[...] = jnp.zeros_like(square_ref)

        def give(m):
            wide = tree.own(m)
            outs[m][...] = wide
            square_ref[0:8, :] += fold(wide * wide)

        tree.each(give)
        copies[-2].wait()
        copies[-1].wait()
        tree.drain()


def run_attn_back(
    x0, mask_col, mixed, attended, totals, grad_after, gains, bias_full, packed, grad_up, grad_down, number
):
    grid = Grid()
    tokens = x0.shape[0]
    tile = BACK_SEQS * L
    steps = tokens // tile
    srcs = [grad.reshape(grid.total, -1, grad.shape[1]) for grad in (grad_up, grad_down)]
    blocks = [src.shape[1:] for src in srcs]
    srcs = [src.reshape((grid.tall, 2, 2, 2) + src.shape[1:]) for src in srcs]

    def rows(width):
        return pl.BlockSpec((tile, width), lambda i: (i, 0))

    def whole(*shape):
        return pl.BlockSpec(shape, lambda i: (0,) * len(shape), pipeline_mode=pl.Buffered(1))

    def low(*shape):
        return pltpu.VMEM(shape, jnp.bfloat16)

    anywhere = pl.BlockSpec(memory_space=pl.ANY)
    return pl.pallas_call(
        functools.partial(attn_back_kernel, grid),
        grid=(steps,),
        out_shape=[
            jax.ShapeDtypeStruct((tokens, D), jnp.bfloat16),
            jax.ShapeDtypeStruct((1, D), jnp.float32),
            jax.ShapeDtypeStruct((HEADS, L, L), jnp.float32),
            jax.ShapeDtypeStruct((D, WIDE + D), jnp.bfloat16),
        ]
        + [jax.ShapeDtypeStruct(block, jnp.float32) for block in blocks]
        + [jax.ShapeDtypeStruct((16, 128), jnp.float32)],
        in_specs=[
            rows(D),
            rows(1),
            rows(WIDE),
            whole(tokens, D),
            pl.BlockSpec((BACK_SEQS, HEADS, L), lambda i: (i, 0, 0)),
            rows(D),
            whole(3, D),
            whole(HEADS, L, L),
            anywhere,
            anywhere,
            anywhere,
        ],
        out_specs=[rows(D), whole(1, D), whole(HEADS, L, L), anywhere]
        + [whole(*block) for block in blocks]
        + [whole(16, 128)],
        scratch_shapes=[
            low(D, WIDE + D),
            low(tokens, D),
            low(tokens, D),
            low(tokens, WIDE),
            low(2, D, D),
            pltpu.SemaphoreType.DMA((2,)),
            pltpu.SemaphoreType.DMA((2,)),
        ]
        + Tree.scratch(grid, blocks),
        compiler_params=pltpu.CompilerParams(
            collective_id=number, has_side_effects=True, vmem_limit_bytes=62 * 1024 * 1024
        ),
    )(x0, mask_col, mixed, attended, totals, grad_after, gains, bias_full, packed, *srcs)


def finish_kernel(grid, count, *refs):
    srcs, (sums, ids, small, square_ref) = refs[:count], refs[count : count + 4]
    refs = refs[count + 4 :]
    outs, (table_out, small_out, square_out) = refs[:count], refs[count : count + 3]
    refs = refs[count + 3 :]
    tree = Tree(grid, srcs, refs[: Tree.size(count)])
    refs = refs[Tree.size(count) :]
    rows, small_stage, small_in, square_stage, square_in = refs[:5]
    row_own, line_send, on_send, row_recv, small_send, small_recv, square_send, square_recv = refs[5:]
    z, x, y, core = grid.here()
    tall = grid.tall
    d, f = lax.axis_index("dp"), lax.axis_index("fsdp")
    me = d * grid.fs + f
    sibling = tree.sibling
    f_side = y * 2 + 1 - core
    f_y = (1 - y) * 2 + core
    f_far = (1 - y) * 2 + 1 - core
    for level in range(tall):
        small_in[3 + level] = jnp.zeros(small.shape, jnp.float32)
        square_in[3 + level] = jnp.zeros((16, 128), jnp.float32)
    x_device, y_device = grid.device(z, 1 - x, y, core), grid.device(z, x, 1 - y, core)

    @pl.loop(1, grid.dp)
    def _(step):
        greet((lax.rem(d + step, grid.dp), f))

    greet(y_device)
    greet(sibling)

    def line(peer, slot):
        return pltpu.make_async_remote_copy(
            src_ref=sums.at[peer],
            dst_ref=rows.at[slot],
            send_sem=line_send.at[peer],
            recv_sem=row_recv.at[slot],
            device_id=(peer, f),
            device_id_type=MESH,
        )

    def onward(slot, to_side, own_block=False):
        return pltpu.make_async_remote_copy(
            src_ref=sums.at[d] if own_block else rows.at[slot],
            dst_ref=rows.at[slot],
            send_sem=on_send.at[1 if to_side else 0, slot],
            recv_sem=row_recv.at[slot],
            device_id=(d, f_side if to_side else f_y),
            device_id_type=MESH,
        )

    def total_of(stage, inbox, send_sem, recv_sem):
        partners = (sibling, x_device, y_device)

        def copy(r):
            return pltpu.make_async_remote_copy(
                src_ref=stage.at[r],
                dst_ref=inbox.at[r],
                send_sem=send_sem.at[r],
                recv_sem=recv_sem.at[r],
                device_id=partners[r],
                device_id_type=MESH,
            )

        def z_send(level, slot):
            return pltpu.make_async_remote_copy(
                src_ref=stage.at[3],
                dst_ref=inbox.at[3 + slot],
                send_sem=send_sem.at[3 + level],
                recv_sem=recv_sem.at[3 + slot],
                device_id=grid.device(level, x, y, core),
                device_id_type=MESH,
            )

        def others(action):
            @pl.loop(1, tall)
            def _(step):
                action(lax.rem(z + step, tall))

        def send(r):
            if r < 3:
                copy(r).start()
            else:
                others(lambda level: z_send(level, z).start())

        def take(r):
            if r < 3:
                copy(r).wait_recv()
                stage[r + 1] = stage[r] + inbox[r]
                send(r + 1)
            else:
                others(lambda level: z_send(level, level).wait_recv())

        def result():
            total = stage[3]
            for level in range(tall):
                total = total + jnp.where(z == level, 0.0, inbox[3 + level])
            for r in range(3):
                copy(r).wait_send()
            others(lambda level: z_send(level, level).wait_send())
            return total

        return send, take, result

    small_stage[0] = small[...]
    small_sends, small_take, small_result = total_of(small_stage, small_in, small_send, small_recv)
    square_sends, square_take, square_result = total_of(square_stage, square_in, square_send, square_recv)
    own_rows = pltpu.make_async_copy(sums.at[d], rows.at[me], row_own)
    own_rows.start()
    tree.loads()
    meet(grid.dp + 1)
    small_sends(0)

    @pl.loop(1, grid.dp)
    def _(step):
        line(lax.rem(d + step, grid.dp), me).start()

    tree.sides()
    onward(me, False, True).start()
    onward(me, True, True).start()

    def pass_lines():
        @pl.loop(1, grid.dp)
        def _(step):
            slot = lax.rem(d + grid.dp - step, grid.dp) * grid.fs + f
            line(d, slot).wait_recv()
            onward(slot, False).start()
            onward(slot, True).start()

    def pass_y():
        @pl.loop(0, grid.dp)
        def _(step):
            slot = lax.rem(d + grid.dp - step, grid.dp) * grid.fs + f_y
            line(d, slot).wait_recv()
            onward(slot, True).start()

    def rows_in():
        own_rows.wait()

        @pl.loop(0, grid.dp)
        def _(step):
            line(d, step * grid.fs + f_side).wait_recv()
            line(d, step * grid.fs + f_far).wait_recv()

    table_rows = table_out.shape[0]
    whole_blocks = table_rows // ROW_BLOCK
    square_stage[0] = square_ref[...]

    def spread(start, size):
        per = rows.shape[1]
        group = 8
        total = jnp.zeros((size, D), jnp.float32)
        for g in range(0, grid.total, group):
            place = (start + lax.broadcasted_iota(jnp.int32, (size, group * per), 0)).astype(jnp.float32)
            wanted = ids[:, g * per : (g + group) * per]
            hot = jnp.where(place == wanted, 1.0, 0.0).astype(jnp.bfloat16)
            total = total + matmul(hot, rows[g : g + group].reshape(group * per, D))
        low = total.astype(jnp.bfloat16)
        table_out[pl.ds(start, size), :] = low
        wide = low.astype(jnp.float32)
        square_stage[0, 8:16, :] += fold(wide * wide)

    def spread_blocks(first_block, last_block):
        @pl.loop(first_block, last_block)
        def _(block):
            spread(pl.multiple_of(block * ROW_BLOCK, ROW_BLOCK), ROW_BLOCK)

    for j in range(tall):
        tree.first(j)
        if j < 3:
            small_take(j)
    pass_lines()
    tree.second(0)
    tree.second(1)
    tree.third(0)
    pass_y()
    tree.second(2)
    tree.third(1)
    tree.second(3)
    rows_in()
    spread_blocks(0, whole_blocks // 2)
    tree.third(2)
    spread_blocks(whole_blocks // 2, whole_blocks)
    if table_rows % ROW_BLOCK:
        spread(whole_blocks * ROW_BLOCK, table_rows % ROW_BLOCK)
    tree.third(3)

    def give(m):
        wide = tree.own(m)
        outs[m][...] = wide
        square_stage[0, 0:8, :] += fold(wide * wide)

    tree.each(give)

    square_sends(0)
    small_take(3)
    small_out[...] = small_result()
    for r in range(3):
        square_take(r)

    tree.drain()

    @pl.loop(0, grid.dp)
    def _(step):
        onward(step * grid.fs + f, False).wait_send()
        onward(step * grid.fs + f, True).wait_send()
        onward(step * grid.fs + f_y, True).wait_send()

    @pl.loop(1, grid.dp)
    def _(step):
        line(lax.rem(d + step, grid.dp), me).wait_send()

    square_take(3)
    square_out[...] = square_result()


def finish(srcs, sums, ids, small, squares, vocab_rows, number):
    grid = Grid()
    count = len(srcs)
    tall = grid.tall
    blocks = [src.shape[1:] for src in srcs]
    srcs = [src.reshape((tall, 2, 2, 2) + src.shape[1:]) for src in srcs]
    cap = sums.shape[1]
    dma = pltpu.SemaphoreType.DMA
    by_device, by_step = dma((grid.total,)), dma((3 + tall,))
    scratch = Tree.scratch(grid, blocks) + [
        pltpu.VMEM((grid.total, cap, D), jnp.bfloat16),
        pltpu.VMEM((4,) + small.shape, jnp.float32),
        pltpu.VMEM((3 + tall,) + small.shape, jnp.float32),
        pltpu.VMEM((4, 16, 128), jnp.float32),
        pltpu.VMEM((3 + tall, 16, 128), jnp.float32),
        dma,
        dma((grid.dp,)),
        dma((2, grid.total)),
        by_device,
    ]
    anywhere, inside = pl.BlockSpec(memory_space=pl.ANY), pl.BlockSpec(memory_space=pltpu.VMEM)
    results = pl.pallas_call(
        functools.partial(finish_kernel, grid, count),
        out_shape=[jax.ShapeDtypeStruct(block, jnp.float32) for block in blocks]
        + [
            jax.ShapeDtypeStruct((vocab_rows, D), jnp.bfloat16),
            jax.ShapeDtypeStruct(small.shape, jnp.float32),
            jax.ShapeDtypeStruct((16, 128), jnp.float32),
        ],
        in_specs=[anywhere] * (count + 1) + [inside] * 3,
        out_specs=[inside] * (count + 3),
        scratch_shapes=scratch + [by_step] * 4,
        compiler_params=pltpu.CompilerParams(
            collective_id=number, has_side_effects=True, vmem_limit_bytes=62 * 1024 * 1024
        ),
    )(*srcs, sums, ids.reshape(1, -1), small, squares)
    return (results[:count], *results[count:])


def plain_body(
    token_ids,
    pad_mask,
    hard_negative,
    table,
    table_first,
    table_second,
    attn_in,
    attn_in_first,
    attn_in_second,
    attn_out,
    attn_out_first,
    attn_out_second,
    ffn_in,
    ffn_in_first,
    ffn_in_second,
    ffn_out,
    ffn_out_first,
    ffn_out_second,
    proj_head,
    proj_head_first,
    proj_head_second,
    small_params,
    small_first,
    small_second,
):
    dp_count = lax.axis_size("dp")
    fsdp_count = lax.axis_size("fsdp")
    device_flat = lax.axis_index("dp") * fsdp_count + lax.axis_index("fsdp")
    pairs_here = token_ids.shape[1]
    pairs_total = pairs_here * dp_count * fsdp_count
    seq_count = 2 * pairs_here
    vocab_rows = table.shape[0]
    row_base = lax.axis_index("dp") * vocab_rows
    gain_rows = small_params[: 3 * D].reshape(3, D)
    bias_table = small_params[3 * D : 3 * D + NB * HEADS].reshape(NB, HEADS)
    log_scale = small_params[3 * D + NB * HEADS]
    buckets = jnp.asarray(bucket_table(L, NB).reshape(-1), jnp.int32)
    bucket_hot = (buckets[:, None] == jnp.arange(NB, dtype=jnp.int32)[None, :]).astype(jnp.float32)
    bias_full = (
        jnp.dot(bucket_hot, bias_table, precision=HIGH).reshape(L, L, HEADS).transpose(2, 0, 1)
    )
    mask_rows = pad_mask.reshape(seq_count, L)
    ids_flat = token_ids.reshape(-1)
    table_low = table.astype(jnp.bfloat16)
    ids_all = lax.all_gather(ids_flat, "dp", axis=0, tiled=True)
    picked = ids_all - row_base
    inside = (picked >= 0) & (picked < vocab_rows)
    chosen = jnp.take(table_low, jnp.clip(picked, 0, vocab_rows - 1), axis=0)
    embedded = lax.psum_scatter(
        jnp.where(inside[:, None], chosen.astype(jnp.float32), 0.0).astype(jnp.bfloat16),
        "dp",
        scatter_dimension=0,
        tiled=True,
    ).astype(jnp.float32)
    shards = (
        attn_in.astype(jnp.bfloat16),
        attn_out.astype(jnp.bfloat16),
        ffn_in.astype(jnp.bfloat16),
        ffn_out.astype(jnp.bfloat16),
        proj_head.astype(jnp.bfloat16),
    )
    gathered = (
        lax.all_gather(shards[0], ("dp", "fsdp"), axis=0, tiled=True),
        lax.all_gather(shards[1], ("dp", "fsdp"), axis=0, tiled=True),
        lax.all_gather(shards[2], ("dp", "fsdp"), axis=0, tiled=True),
        lax.all_gather(shards[3], ("dp", "fsdp"), axis=0, tiled=True),
        lax.all_gather(shards[4], ("dp", "fsdp"), axis=0, tiled=True),
    )
    final_rows, kept = layer_forward(embedded, mask_rows, gathered[:4], gain_rows, bias_full)
    normed_three, factor_three = normalize(final_rows, gain_rows[2])
    mask_weight = mask_rows.astype(jnp.float32)[:, :, None]
    counts = jnp.sum(mask_weight, 1)
    pooled = jnp.sum(normed_three.reshape(seq_count, L, D) * mask_weight, 1) / counts
    pooled_low = pooled.astype(jnp.bfloat16)
    projected = matmul(pooled_low, gathered[4])
    proj_factor = lax.rsqrt(jnp.sum(projected * projected, -1, keepdims=True) + EPS)
    unit_rows = projected * proj_factor
    unit_low = unit_rows.astype(jnp.bfloat16)
    mine_query = unit_low[:pairs_here]
    all_pass = lax.all_gather(unit_low[pairs_here:], ("dp", "fsdp"), axis=0, tiled=True)
    similar = matmul_nt(mine_query, all_pass)
    sim_scale = jnp.exp(log_scale)
    columns = jnp.arange(pairs_total, dtype=jnp.int32)
    own_index = device_flat * pairs_here + jnp.arange(pairs_here, dtype=jnp.int32)
    own_mask = (columns[None, :] == own_index[:, None]).astype(jnp.float32)
    negative = (columns[None, :] == hard_negative[:, None]).astype(jnp.float32)
    logits = sim_scale * similar - MARGIN * own_mask
    diagonal = jnp.sum(logits * own_mask, 1)
    hardest = jnp.sum(logits * negative, 1)
    row_max = jnp.max(logits, 1, keepdims=True)
    log_total = row_max + jnp.log(jnp.sum(jnp.exp(logits - row_max), 1, keepdims=True))
    loss_local = jnp.sum(log_total[:, 0] - diagonal + jax.nn.softplus(hardest - diagonal))
    hinge_gate = jax.nn.sigmoid(hardest - diagonal)
    grad_logits = (
        jnp.exp(logits - log_total) - own_mask + hinge_gate[:, None] * (negative - own_mask)
    )
    grad_log_scale = sim_scale * jnp.sum(grad_logits * similar)
    grad_similar = (sim_scale * grad_logits).astype(jnp.bfloat16)
    grad_query = matmul(grad_similar, all_pass).astype(jnp.bfloat16)
    grad_pass_terms = matmul_tn(grad_similar, mine_query)
    grad_pass = lax.psum_scatter(
        grad_pass_terms, ("dp", "fsdp"), scatter_dimension=0, tiled=True
    ).astype(jnp.bfloat16)
    grad_units = jnp.concatenate([grad_query, grad_pass], 0).astype(jnp.float32)
    grad_proj = (
        proj_factor * (grad_units - unit_rows * jnp.sum(grad_units * unit_rows, -1, keepdims=True))
    ).astype(jnp.bfloat16)
    gathered_back = (
        lax.all_gather(shards[0], ("dp", "fsdp"), axis=0, tiled=True),
        lax.all_gather(shards[1], ("dp", "fsdp"), axis=0, tiled=True),
        lax.all_gather(shards[2], ("dp", "fsdp"), axis=0, tiled=True),
        lax.all_gather(shards[3], ("dp", "fsdp"), axis=0, tiled=True),
        lax.all_gather(shards[4], ("dp", "fsdp"), axis=0, tiled=True),
    )
    grad_proj_head = matmul_tn(pooled_low, grad_proj)
    grad_pooled = matmul_nt(grad_proj, gathered_back[4])
    grad_normed = ((grad_pooled / counts)[:, None, :] * mask_weight).reshape(-1, D)
    grad_final, gain_three = normalize_back(grad_normed, final_rows, factor_three, gain_rows[2])
    grad_rows, matrix_grads, gain_one, gain_two, grad_bias = layer_backward(
        grad_final, kept, mask_rows, gathered_back[:4], gain_rows, bias_full
    )
    attn_in_grad, attn_out_grad, ffn_in_grad, ffn_out_grad = matrix_grads
    grad_bias_table = jnp.dot(grad_bias.reshape(HEADS, L * L), bucket_hot, precision=HIGH).T
    small_local = jnp.concatenate(
        [gain_one, gain_two, gain_three, grad_bias_table.reshape(-1), grad_log_scale[None]]
    )
    small_grad = lax.psum(small_local, ("dp", "fsdp"))
    weight_grads = (
        lax.psum_scatter(attn_in_grad, ("dp", "fsdp"), scatter_dimension=0, tiled=True),
        lax.psum_scatter(attn_out_grad, ("dp", "fsdp"), scatter_dimension=0, tiled=True),
        lax.psum_scatter(ffn_in_grad, ("dp", "fsdp"), scatter_dimension=0, tiled=True),
        lax.psum_scatter(ffn_out_grad, ("dp", "fsdp"), scatter_dimension=0, tiled=True),
        lax.psum_scatter(grad_proj_head, ("dp", "fsdp"), scatter_dimension=0, tiled=True),
    )
    rows_back = lax.all_gather(grad_rows.astype(jnp.bfloat16), "dp", axis=0, tiled=True)
    turn_count = dp_count // 4
    block_rows = rows_back.shape[0] // turn_count

    def add_block(running, piece_pair):
        block_grads, block_ids = piece_pair
        local_ids = block_ids - row_base
        inside = (local_ids >= 0) & (local_ids < vocab_rows)
        segment = jnp.where(inside, local_ids, vocab_rows)
        summed = jax.ops.segment_sum(
            block_grads.astype(jnp.float32), segment, num_segments=vocab_rows + 1
        )
        return (running + summed[:vocab_rows], None)

    table_full, _ = lax.scan(
        add_block,
        jnp.zeros((vocab_rows, D), jnp.float32),
        (rows_back.reshape(turn_count, block_rows, D), ids_all.reshape(turn_count, block_rows)),
    )
    table_grad = lax.psum(table_full.astype(jnp.bfloat16), "fsdp").astype(jnp.float32)
    owned = (table_grad,) + tuple(weight_grads)
    squares = jnp.sum(table_grad * table_grad) / fsdp_count
    for gradient in weight_grads:
        squares = squares + jnp.sum(gradient * gradient)
    total_squares, loss_sum = lax.psum((squares, loss_local), ("dp", "fsdp"))
    norm_value = jnp.sqrt(total_squares + jnp.sum(small_grad * small_grad))
    factor = jnp.minimum(1.0, CLIP / (norm_value + 1e-06))
    masters = (table, attn_in, attn_out, ffn_in, ffn_out, proj_head, small_params)
    firsts = (
        table_first,
        attn_in_first,
        attn_out_first,
        ffn_in_first,
        ffn_out_first,
        proj_head_first,
        small_first,
    )
    seconds = (
        table_second,
        attn_in_second,
        attn_out_second,
        ffn_in_second,
        ffn_out_second,
        proj_head_second,
        small_second,
    )
    gradients = owned + (small_grad,)
    results = [loss_sum, norm_value]
    for kind_index in range(7):
        results.extend(
            adam_update(
                masters[kind_index],
                firsts[kind_index],
                seconds[kind_index],
                gradients[kind_index],
                factor,
                RATES[kind_index],
                DECAYS[kind_index],
            )
        )
    return tuple(results)


def fits(mesh):
    return mesh.shape["fsdp"] == 4 and mesh.shape["dp"] == 8


def dense_rows(ids_flat, table, row_base):
    vocab_rows = table.shape[0]
    ids_all = lax.all_gather(ids_flat, "dp", axis=0, tiled=True)
    picked = ids_all - row_base
    inside = (picked >= 0) & (picked < vocab_rows)
    chosen = jnp.take(table, jnp.clip(picked, 0, vocab_rows - 1), axis=0)
    return lax.psum_scatter(
        jnp.where(inside[:, None], chosen, 0.0).astype(jnp.bfloat16),
        "dp",
        scatter_dimension=0,
        tiled=True,
    ).astype(jnp.float32)


def dense_table_grad(ids_flat, grad_low, vocab_rows, row_base):
    ids_all = lax.all_gather(ids_flat, "dp", axis=0, tiled=True)
    rows_back = lax.all_gather(grad_low, "dp", axis=0, tiled=True)
    turn_count = lax.axis_size("dp") // 4
    block_rows = rows_back.shape[0] // turn_count

    def add_block(running, piece_pair):
        block_grads, block_ids = piece_pair
        local_ids = block_ids - row_base
        inside = (local_ids >= 0) & (local_ids < vocab_rows)
        segment = jnp.where(inside, local_ids, vocab_rows)
        summed = jax.ops.segment_sum(
            block_grads.astype(jnp.float32), segment, num_segments=vocab_rows + 1
        )
        return (running + summed[:vocab_rows], None)

    table_full, _ = lax.scan(
        add_block,
        jnp.zeros((vocab_rows, D), jnp.float32),
        (rows_back.reshape(turn_count, block_rows, D), ids_all.reshape(turn_count, block_rows)),
    )
    return lax.psum(table_full.astype(jnp.bfloat16), "fsdp")


def once(flag, make, value):
    return lax.while_loop(lambda state: state[0], lambda state: (False, make(state[1])), (flag, value))[1]


def fast_body(
    token_ids,
    pad_mask,
    hard_negative,
    table,
    table_first,
    table_second,
    attn_in,
    attn_in_first,
    attn_in_second,
    attn_out,
    attn_out_first,
    attn_out_second,
    ffn_in,
    ffn_in_first,
    ffn_in_second,
    ffn_out,
    ffn_out_first,
    ffn_out_second,
    proj_head,
    proj_head_first,
    proj_head_second,
    small_params,
    small_first,
    small_second,
):
    dp_count = lax.axis_size("dp")
    fsdp_count = lax.axis_size("fsdp")
    total = dp_count * fsdp_count
    pairs_here = token_ids.shape[1]
    pairs_total = pairs_here * total
    seq_count = 2 * pairs_here
    vocab_rows = table.shape[0]
    row_base = lax.axis_index("dp") * vocab_rows
    gain_rows = small_params[: 3 * D].reshape(3, D)
    bias_table = small_params[3 * D : 3 * D + NB * HEADS].reshape(NB, HEADS)
    log_scale = small_params[3 * D + NB * HEADS]
    buckets = jnp.asarray(bucket_table(L, NB).T.reshape(-1), jnp.int32)
    bucket_hot = (buckets[:, None] == jnp.arange(NB, dtype=jnp.int32)[None, :]).astype(jnp.float32)
    bias_full = (
        jnp.dot(bucket_hot, bias_table, precision=HIGH).reshape(L, L, HEADS).transpose(2, 0, 1)
    )
    mask_rows = pad_mask.reshape(seq_count, L)
    ids_flat = token_ids.reshape(-1)
    tokens = ids_flat.shape[0]

    gathered_packed, gathered_down, heard, slot, embedded = run_head(
        ids_flat, hard_negative, attn_in, attn_out, ffn_in, proj_head, ffn_out, table, 1
    )
    packed = gathered_packed.reshape(-1, PACKED)
    down = gathered_down.reshape(-1, D)
    asked = heard[:, 0, :CAP]
    negatives = heard[:, 1, :pairs_here].reshape(-1).astype(jnp.int32)
    any_spilled = jnp.max(heard[:, 2, 0]) > 0.5
    embedded = once(any_spilled, lambda _: dense_rows(ids_flat, table, row_base), embedded)

    mask_col = mask_rows.astype(jnp.float32).reshape(tokens, 1)
    mixed, attended, totals, after, pre, final, pooled, projected = run_forward(
        embedded, mask_col, gain_rows, bias_full, packed, down
    )
    target = negatives // pairs_here * seq_count + pairs_here + negatives % pairs_here
    target = jnp.concatenate(
        [target.reshape(total, pairs_here), jnp.full((total, pairs_here), -1, jnp.int32)], 1
    ).reshape(-1, 1)
    grad_proj, loss_parts = run_loss(projected, target, log_scale.reshape(1, 1), 3)
    loss_sum, grad_log_scale = loss_parts[0, 0], loss_parts[1, 0]
    grad_after, grad_gains, grad_up, grad_down = run_ffn_back(
        final, after, mask_col, gain_rows, pooled, grad_proj, pre, packed, down
    )
    grad_low, grad_gain, grad_bias, grad_attn, up_shard, down_shard, squares = run_attn_back(
        embedded, mask_col, mixed, attended, totals, grad_after, gain_rows, bias_full, packed, grad_up, grad_down, 4
    )
    grad_gains = jnp.concatenate([grad_gain, grad_gains[1:]], 0)
    grad_bias_table = jnp.dot(grad_bias.reshape(HEADS, L * L), bucket_hot, precision=HIGH).T
    small_local = jnp.concatenate([grad_gains.reshape(-1), grad_bias_table.reshape(-1)])
    width = -(-small_local.shape[0] // 1024) * 8
    small_local = jnp.pad(small_local, (0, width * 128 - small_local.shape[0]))
    slots = jnp.arange(dp_count * CAP, dtype=jnp.int32).astype(jnp.float32)
    slot_hot = (slot == slots[None, :]).astype(jnp.bfloat16)
    slot_sums = matmul_tn(slot_hot, grad_low).astype(jnp.bfloat16).reshape(dp_count, CAP, D)
    (attn_shard,), table_grad, summed, squares = finish(
        [grad_attn.reshape(total, -1, WIDE + D)],
        slot_sums,
        asked.reshape(-1),
        small_local.reshape(width, 128),
        squares,
        vocab_rows,
        5,
    )
    table_squares = jnp.sum(squares[8:])
    table_grad, table_squares = once(
        any_spilled,
        lambda _: with_squares(dense_table_grad(ids_flat, grad_low, vocab_rows, row_base)),
        (table_grad, table_squares),
    )
    small_size = small_params.shape[0]
    total_squares = jnp.sum(squares[:8]) + table_squares / fsdp_count
    small_grad = jnp.concatenate([summed.reshape(-1)[: small_size - 1], grad_log_scale[None]])
    norm_value = jnp.sqrt(total_squares + jnp.sum(small_grad * small_grad))
    factor = jnp.minimum(1.0, CLIP / (norm_value + 1e-06))
    updates = (
        (table, table_first, table_second, table_grad.astype(jnp.float32)),
        (attn_in, attn_in_first, attn_in_second, attn_shard[:, :WIDE]),
        (attn_out, attn_out_first, attn_out_second, attn_shard[:, WIDE:]),
        (ffn_in, ffn_in_first, ffn_in_second, up_shard[:, : 4 * D]),
        (ffn_out, ffn_out_first, ffn_out_second, down_shard),
        (proj_head, proj_head_first, proj_head_second, up_shard[:, 4 * D :]),
        (small_params, small_first, small_second, small_grad),
    )
    results = [loss_sum, norm_value]
    for kind_index, arrays in enumerate(updates):
        results.extend(adam_update(*arrays, factor, RATES[kind_index], DECAYS[kind_index]))
    return tuple(results)


def with_squares(table_grad):
    wide = table_grad.astype(jnp.float32)
    return (table_grad, lax.psum(jnp.sum(wide * wide), ("dp", "fsdp")))


def solution(mesh):
    program = fast_body if fits(mesh) else plain_body
    return jax.shard_map(
        program,
        mesh=mesh,
        in_specs=(
            P(None, ("dp", "fsdp"), None),
            P(None, ("dp", "fsdp"), None),
            P(("dp", "fsdp")),
            P("dp", None),
            P("dp", None),
            P("dp", None),
            P(("dp", "fsdp"), None),
            P(("dp", "fsdp"), None),
            P(("dp", "fsdp"), None),
            P(("dp", "fsdp"), None),
            P(("dp", "fsdp"), None),
            P(("dp", "fsdp"), None),
            P(("dp", "fsdp"), None),
            P(("dp", "fsdp"), None),
            P(("dp", "fsdp"), None),
            P(("dp", "fsdp"), None),
            P(("dp", "fsdp"), None),
            P(("dp", "fsdp"), None),
            P(("dp", "fsdp"), None),
            P(("dp", "fsdp"), None),
            P(("dp", "fsdp"), None),
            P(),
            P(),
            P(),
        ),
        out_specs=(
            P(),
            P(),
            P("dp", None),
            P("dp", None),
            P("dp", None),
            P(("dp", "fsdp"), None),
            P(("dp", "fsdp"), None),
            P(("dp", "fsdp"), None),
            P(("dp", "fsdp"), None),
            P(("dp", "fsdp"), None),
            P(("dp", "fsdp"), None),
            P(("dp", "fsdp"), None),
            P(("dp", "fsdp"), None),
            P(("dp", "fsdp"), None),
            P(("dp", "fsdp"), None),
            P(("dp", "fsdp"), None),
            P(("dp", "fsdp"), None),
            P(("dp", "fsdp"), None),
            P(("dp", "fsdp"), None),
            P(("dp", "fsdp"), None),
            P(),
            P(),
            P(),
        ),
        check_vma=False,
    )
```

```python
import functools

import jax
import jax.numpy as jnp
import numpy as np
from jax import lax
from jax.experimental import pallas as pl
from jax.experimental.pallas import tpu as pltpu
from jax.sharding import PartitionSpec as P

D = 768
HEADS = 12
HD = 64
NB = 32
L = 128
STEP = 10


EPS = 1e-06
SCALE = 0.125
MARGIN = 0.2
CLIP = 0.1
BETA_ONE = 0.9
BETA_TWO = 0.99
ADAM_EPS = 1e-08
RATES = (3.0, 0.1, 0.2, 0.1, 0.05, 0.1, 1.0)
DECAYS = (0.001, 0.001, 0.001, 0.001, 0.001, 0.001, 0.0)
HIGH = lax.Precision.HIGHEST
MESH = pl.DeviceIdType.MESH
CAP = 112


def bucket_table(length, count):
    position = np.arange(length)
    relative = position[None, :] - position[:, None]
    half = count // 2
    base_part = (relative > 0).astype(np.int64) * half
    distance = np.abs(relative)
    exact = half // 2
    safe_dist = np.maximum(distance, 1)
    large = exact + (np.log(safe_dist / exact) / np.log(length / exact) * (half - exact)).astype(
        np.int64
    )
    large = np.minimum(large, half - 1)
    return base_part + np.where(distance < exact, distance, large)


def matmul(left_side, right_side):
    return jnp.dot(left_side, right_side, preferred_element_type=jnp.float32)


def matmul_tn(left_side, right_side):
    return lax.dot_general(
        left_side, right_side, (((0,), (0,)), ((), ())), preferred_element_type=jnp.float32
    )


def matmul_nt(left_side, right_side):
    return lax.dot_general(
        left_side, right_side, (((1,), (1,)), ((), ())), preferred_element_type=jnp.float32
    )


def normalize(inputs, gain_row):
    factor = lax.rsqrt(jnp.mean(inputs * inputs, -1, keepdims=True) + EPS)
    return (inputs * factor * gain_row, factor)


def normalize_back(grad_out, inputs, factor, gain_row):
    scaled = grad_out * gain_row
    grad_gain = jnp.sum(grad_out * inputs * factor, 0)
    grad_in = factor * (
        scaled - inputs * factor * factor * jnp.mean(scaled * inputs, -1, keepdims=True)
    )
    return (grad_in, grad_gain)


def attention_scores(mixed_proj, mask_rows, bias_full):
    keep_add = jnp.where(mask_rows > 0, 0.0, -1000000000.0).astype(jnp.float32)
    scores = jnp.einsum(
        "bqhd,bkhd->bhqk",
        mixed_proj[:, :, 0],
        mixed_proj[:, :, 1],
        preferred_element_type=jnp.float32,
    )
    return scores * SCALE + bias_full[None] + keep_add[:, None, None, :]


def layer_forward(token_rows, mask_rows, weights, gain_rows, bias_full):
    attn_in, attn_out, ffn_in, ffn_out = weights
    seq_count, length = mask_rows.shape
    width = token_rows.shape[1]
    normed_one, factor_one = normalize(token_rows, gain_rows[0])
    act_one = normed_one.astype(jnp.bfloat16)
    mixed_proj = (
        matmul(act_one, attn_in).astype(jnp.bfloat16).reshape(seq_count, length, 3, HEADS, HD)
    )
    scores = attention_scores(mixed_proj, mask_rows, bias_full)
    row_max = jnp.max(scores, -1, keepdims=True)
    log_total = row_max + jnp.log(jnp.sum(jnp.exp(scores - row_max), -1, keepdims=True))
    prob_low = jnp.exp(scores - log_total).astype(jnp.bfloat16)
    attended = jnp.einsum(
        "bhqk,bkhd->bqhd", prob_low, mixed_proj[:, :, 2], preferred_element_type=jnp.float32
    )
    attended = attended.astype(jnp.bfloat16).reshape(-1, width)
    after_attn = token_rows + matmul(attended, attn_out)
    normed_two, factor_two = normalize(after_attn, gain_rows[1])
    act_two = normed_two.astype(jnp.bfloat16)
    pre_act = matmul(act_two, ffn_in)
    hidden = jax.nn.gelu(pre_act).astype(jnp.bfloat16)
    final_rows = after_attn + matmul(hidden, ffn_out)
    kept = (
        token_rows,
        factor_one,
        act_one,
        mixed_proj,
        log_total,
        attended,
        after_attn,
        factor_two,
        act_two,
        pre_act,
        hidden,
    )
    return (final_rows, kept)


def layer_backward(grad_final, kept, mask_rows, weights, gain_rows, bias_full):
    (
        token_rows,
        factor_one,
        act_one,
        mixed_proj,
        log_total,
        attended,
        after_attn,
        factor_two,
        act_two,
        pre_act,
        hidden,
    ) = kept
    attn_in, attn_out, ffn_in, ffn_out = weights
    seq_count, length = mask_rows.shape
    branch = grad_final.astype(jnp.bfloat16)
    grad_ffn_out = matmul_tn(hidden, branch)
    grad_hidden = matmul_nt(branch, ffn_out)
    _, gelu_pull = jax.vjp(jax.nn.gelu, pre_act)
    grad_pre = gelu_pull(grad_hidden)[0].astype(jnp.bfloat16)
    grad_ffn_in = matmul_tn(act_two, grad_pre)
    grad_act_two = matmul_nt(grad_pre, ffn_in)
    grad_mid, gain_two = normalize_back(grad_act_two, after_attn, factor_two, gain_rows[1])
    grad_after = grad_final + grad_mid
    branch = grad_after.astype(jnp.bfloat16)
    grad_attn_out = matmul_tn(attended, branch)
    grad_attended = (
        matmul_nt(branch, attn_out).astype(jnp.bfloat16).reshape(seq_count, length, HEADS, HD)
    )
    scores = attention_scores(mixed_proj, mask_rows, bias_full)
    prob_full = jnp.exp(scores - log_total)
    prob_low = prob_full.astype(jnp.bfloat16)
    queries = mixed_proj[:, :, 0]
    key_rows = mixed_proj[:, :, 1]
    grad_probs = jnp.einsum(
        "bqhd,bkhd->bhqk", grad_attended, mixed_proj[:, :, 2], preferred_element_type=jnp.float32
    )
    grad_values = jnp.einsum(
        "bhqk,bqhd->bkhd", prob_low, grad_attended, preferred_element_type=jnp.float32
    )
    grad_scores = prob_full * (grad_probs - jnp.sum(prob_full * grad_probs, -1, keepdims=True))
    grad_scores = grad_scores.astype(jnp.bfloat16)
    grad_bias = jnp.sum(grad_scores, 0, dtype=jnp.float32)
    grad_queries = (
        jnp.einsum("bhqk,bkhd->bqhd", grad_scores, key_rows, preferred_element_type=jnp.float32)
        * SCALE
    )
    grad_keys = (
        jnp.einsum("bhqk,bqhd->bkhd", grad_scores, queries, preferred_element_type=jnp.float32)
        * SCALE
    )
    grad_mixed = (
        jnp.stack([grad_queries, grad_keys, grad_values], 2)
        .astype(jnp.bfloat16)
        .reshape(seq_count * length, -1)
    )
    grad_attn_in = matmul_tn(act_one, grad_mixed)
    grad_act_one = matmul_nt(grad_mixed, attn_in)
    grad_low, gain_one = normalize_back(grad_act_one, token_rows, factor_one, gain_rows[0])
    grad_rows = grad_after + grad_low
    return (
        grad_rows,
        (grad_attn_in, grad_attn_out, grad_ffn_in, grad_ffn_out),
        gain_one,
        gain_two,
        grad_bias,
    )


def adam_update(param, first_moment, second_moment, gradient, factor, rate, decay):
    clipped = gradient * factor
    first_new = BETA_ONE * first_moment + (1.0 - BETA_ONE) * clipped
    second_new = BETA_TWO * second_moment + (1.0 - BETA_TWO) * clipped * clipped
    direction = (
        first_new
        / (1.0 - BETA_ONE**STEP)
        / (jnp.sqrt(second_new / (1.0 - BETA_TWO**STEP)) + ADAM_EPS)
    )
    return (first_new, second_new, param - rate * (direction + decay * param))


class Grid:
    def __init__(self):
        self.dp, self.fs = lax.axis_size("dp"), lax.axis_size("fsdp")
        self.total = self.dp * self.fs
        self.wide = self.fs // 2
        self.tall = self.dp // self.wide

    def here(self):
        d, f = lax.axis_index("dp"), lax.axis_index("fsdp")
        return d // self.wide, lax.rem(d, self.wide), f // 2, lax.rem(f, 2)

    def device(self, z, x, y, core):
        return (z * self.wide + x, y * 2 + core)

    def flat(self, z, x, y, core):
        return (z * self.wide + x) * self.fs + y * 2 + core

    def peer(self, index):
        return (index // self.fs, lax.rem(index, self.fs))


def greet(device, when=None):
    barrier = pltpu.get_barrier_semaphore()

    def signal():
        pl.semaphore_signal(barrier, inc=1, device_id=device, device_id_type=MESH)

    if when is None:
        signal()
    else:
        pl.when(when)(signal)


def meet(count):
    pl.semaphore_wait(pltpu.get_barrier_semaphore(), count)


ROW_BLOCK = 512
WIDE = 3 * D
PACKED = WIDE + D + 4 * D + D
TILE_SEQS = 4


def head_kernel(
    grid,
    col_ref,
    row_ref,
    negative_ref,
    in_ref,
    out_ref,
    up_ref,
    proj_ref,
    down_ref,
    table_hbm,
    packed_out,
    down_out,
    heard,
    slot_ref,
    x0_ref,
    packed_mine,
    down_mine,
    table,
    total,
    answers,
    found,
    messages,
    send_sem,
    recv_sem,
    own_sem,
    row_send,
    row_recv,
    note_send,
    note_recv,
    note_on,
    table_sem,
):
    srcs, outs = (packed_mine, down_mine), (packed_out, down_out)
    count = 2
    z, x, y, core = grid.here()
    tall = grid.tall
    d, f = lax.axis_index("dp"), lax.axis_index("fsdp")
    ux, uy = lax.rem(x + 1 - core, 2), lax.rem(y + core, 2)
    vx, vy = lax.rem(x + core, 2), lax.rem(y + 1 - core, 2)
    up, down = grid.device(z + 1, x, y, core), grid.device(z - 1, x, y, core)
    u_device, v_device = grid.device(z, ux, uy, core), grid.device(z, vx, vy, core)
    sibling = grid.device(z, x, y, 1 - core)
    has_up, has_down = z < tall - 1, z > 0
    me = grid.flat(z, x, y, core)
    f_side, f_y, f_far = y * 2 + 1 - core, (1 - y) * 2 + core, (1 - y) * 2 + 1 - core

    @pl.loop(1, grid.dp)
    def _(step):
        greet((lax.rem(d + step, grid.dp), f))

    greet((d, f_y))
    greet(sibling)
    vocab_rows = table_hbm.shape[0]
    fetch = pltpu.make_async_copy(table_hbm, table.at[pl.ds(0, vocab_rows), :], table_sem)
    fetch.start()
    at = 0
    for ref in (in_ref, out_ref, up_ref, proj_ref):
        packed_mine[:, at : at + ref.shape[1]] = ref[...].astype(jnp.bfloat16)
        at += ref.shape[1]
    down_mine[...] = down_ref[...].astype(jnp.bfloat16)
    local = [pltpu.make_async_copy(srcs[m], outs[m].at[me], own_sem.at[m]) for m in range(count)]
    for item in local:
        item.start()
    meet(grid.dp + 1)

    def copy(m, shard, device, way, own):
        return pltpu.make_async_remote_copy(
            src_ref=srcs[m] if own else outs[m].at[shard],
            dst_ref=outs[m].at[shard],
            send_sem=send_sem.at[way, m, shard],
            recv_sem=recv_sem.at[m, shard],
            device_id=device,
            device_id_type=MESH,
        )

    def send(shard, device, way, own=False):
        for m in range(count):
            copy(m, shard, device, way, own).start()

    def arrived(shard):
        for m in range(count):
            copy(m, shard, sibling, 4, False).wait_recv()

    def sent(shard, device, way):
        for m in range(count):
            copy(m, shard, device, way, False).wait_send()

    @pl.when(has_up)
    def _():
        send(me, up, 0, True)

    @pl.when(has_down)
    def _():
        send(me, down, 1, True)

    send(me, u_device, 2, True)
    send(me, v_device, 3, True)
    send(me, sibling, 4, True)

    tokens = col_ref.shape[0]
    chunk = 128
    ids_row = row_ref[...]
    place_row = lax.broadcasted_iota(jnp.int32, (chunk, tokens), 1)
    place_col = lax.broadcasted_iota(jnp.int32, (chunk, tokens), 0)

    def see(step, repeated):
        start = pl.multiple_of(step * chunk, chunk)
        again = (col_ref[pl.ds(start, chunk), :] == ids_row) & (place_col + start < place_row)
        return jnp.maximum(repeated, jnp.max(jnp.where(again, 1.0, 0.0), 0, keepdims=True))

    repeated = lax.fori_loop(0, tokens // chunk, see, jnp.zeros((1, tokens), jnp.float32))
    firsts = jnp.where(repeated > 0.5, -1.0, ids_row)
    lane = lax.broadcasted_iota(jnp.int32, (chunk, 128), 1).astype(jnp.float32)

    def rank_some(step, carry):
        listed, most = carry
        start = pl.multiple_of(step * chunk, chunk)
        ids = col_ref[pl.ds(start, chunk), :]
        owner = jnp.zeros_like(ids)
        for other in range(1, grid.dp):
            owner = owner + jnp.where(ids >= float(other * vocab_rows), 1.0, 0.0)
        first_id = owner * float(vocab_rows)
        rank = jnp.sum(jnp.where((firsts >= first_id) & (firsts < ids), 1.0, 0.0), 1, keepdims=True)
        slot = jnp.where(rank < float(CAP), owner * float(CAP) + rank, -1.0)
        slot_ref[pl.ds(start, chunk), :] = slot
        rows = []
        for other in range(grid.dp):
            hit = (slot == lane + float(other * CAP)) & (lane < float(CAP))
            rows.append(jnp.max(jnp.where(hit, ids - first_id + 1.0, 0.0), 0, keepdims=True))
        return (jnp.maximum(listed, jnp.concatenate(rows, 0)), jnp.maximum(most, jnp.max(rank, 0, keepdims=True)))

    listed, most = lax.fori_loop(
        0,
        tokens // chunk,
        rank_some,
        (jnp.zeros((grid.dp, 128), jnp.float32), jnp.zeros((1, 1), jnp.float32)),
    )
    spilled = jnp.broadcast_to(jnp.where(most >= float(CAP), 1.0, 0.0), (1, 128))
    rest = jnp.concatenate([negative_ref[...], spilled, jnp.zeros((5, 128), jnp.float32)], 0)
    for other in range(grid.dp):
        messages[other] = jnp.concatenate([listed[other : other + 1] - 1.0, rest], 0)

    def note(peer, slot):
        return pltpu.make_async_remote_copy(
            src_ref=messages.at[peer],
            dst_ref=heard.at[slot],
            send_sem=note_send.at[peer],
            recv_sem=note_recv.at[slot],
            device_id=(peer, f),
            device_id_type=MESH,
        )

    def note_onward(slot, to_side):
        return pltpu.make_async_remote_copy(
            src_ref=heard.at[slot],
            dst_ref=heard.at[slot],
            send_sem=note_on.at[1 if to_side else 0, slot],
            recv_sem=note_recv.at[slot],
            device_id=(d, f_side if to_side else f_y),
            device_id_type=MESH,
        )

    @pl.loop(1, grid.dp)
    def _(step):
        note(lax.rem(d + step, grid.dp), me).start()

    heard[me] = messages[d]

    def row_copy(peer, slot):
        return pltpu.make_async_remote_copy(
            src_ref=answers.at[peer],
            dst_ref=found.at[slot],
            send_sem=row_send.at[peer],
            recv_sem=row_recv.at[slot],
            device_id=(peer, f),
            device_id_type=MESH,
        )

    def pass_z(k):
        low, high = z - k, z + k

        @pl.when(low >= 0)
        def _():
            shard = grid.flat(low, x, y, core)
            arrived(shard)

            @pl.when(has_up)
            def _():
                send(shard, up, 0)

            send(shard, u_device, 2)
            send(shard, v_device, 3)
            send(shard, sibling, 4)

        @pl.when(high < tall)
        def _():
            shard = grid.flat(high, x, y, core)
            arrived(shard)

            @pl.when(has_down)
            def _():
                send(shard, down, 1)

            send(shard, u_device, 2)
            send(shard, v_device, 3)
            send(shard, sibling, 4)

    def both(k, action):
        pl.when(z - k >= 0)(lambda: action(z - k))
        if k:
            pl.when(z + k < tall)(lambda: action(z + k))

    def pass_u(level):
        shard = grid.flat(level, ux, uy, core)
        arrived(shard)
        send(shard, v_device, 3)
        send(shard, sibling, 4)

    def pass_v(level):
        shard = grid.flat(level, vx, vy, core)
        arrived(shard)
        send(shard, sibling, 4)

    def pass_far(level):
        shard = grid.flat(level, 1 - x, 1 - y, core)
        arrived(shard)
        send(shard, sibling, 4)

    both(0, pass_u)

    @pl.loop(1, grid.dp)
    def _(step):
        note(d, lax.rem(d + step, grid.dp) * grid.fs + f).wait_recv()

    @pl.loop(0, grid.dp)
    def _(peer):
        note_onward(peer * grid.fs + f, False).start()
        note_onward(peer * grid.fs + f, True).start()

    pass_z(1)
    fetch.wait()
    padding = table.shape[0] - vocab_rows
    if padding:
        table[vocab_rows:, :] = jnp.zeros((padding, D), jnp.float32)
    asked = jnp.concatenate([heard[peer * grid.fs + f, 0:1, :] for peer in range(grid.dp)], 0)
    asked = jnp.transpose(asked)
    block = ROW_BLOCK
    total[...] = jnp.zeros_like(total)
    lanes = lax.broadcasted_iota(jnp.int32, (CAP, block), 1).astype(jnp.float32)

    def pick(step):
        start = pl.multiple_of(step * block, block)
        some = table[pl.ds(start, block), :].astype(jnp.bfloat16)
        wanted = lanes + (step * block).astype(jnp.float32)
        hot = jnp.concatenate(
            [
                jnp.where(asked[:CAP, peer : peer + 1] == wanted, 1.0, 0.0)
                for peer in range(grid.dp)
            ],
            0,
        ).astype(jnp.bfloat16)
        total[...] += matmul(hot, some)

    steps = table.shape[0] // block
    pl.loop(0, steps)(pick)
    answers[...] = total[...].reshape(answers.shape).astype(jnp.bfloat16)
    found[d] = answers[d]

    @pl.loop(1, grid.dp)
    def _(step):
        row_copy(lax.rem(d + step, grid.dp), d).start()

    both(0, pass_v)
    for k in range(1, tall + 1):
        if 1 < k < tall:
            pass_z(k)
        if k < tall:
            both(k, pass_u)
            both(k, pass_v)
        both(k - 1, pass_far)

    @pl.loop(1, grid.dp)
    def _(step):
        row_copy(d, lax.rem(d + step, grid.dp)).wait_recv()

    slots = grid.dp * CAP
    some = tokens // 4
    wide_lane = lax.broadcasted_iota(jnp.int32, (some, slots), 1).astype(jnp.float32)
    rows = found[...].reshape(slots, D)

    @pl.loop(0, 4)
    def _(step):
        start = pl.multiple_of(step * some, some)
        hot = jnp.where(slot_ref[pl.ds(start, some), :] == wide_lane, 1.0, 0.0).astype(jnp.bfloat16)
        x0_ref[pl.ds(start, some), :] = matmul(hot, rows)

    @pl.loop(0, grid.dp)
    def _(peer):
        note(d, peer * grid.fs + f_y).wait_recv()
        note_onward(peer * grid.fs + f_y, True).start()

    @pl.loop(0, grid.dp)
    def _(peer):
        note(d, peer * grid.fs + f_side).wait_recv()
        note(d, peer * grid.fs + f_far).wait_recv()
        note_onward(peer * grid.fs + f, False).wait_send()
        note_onward(peer * grid.fs + f, True).wait_send()
        note_onward(peer * grid.fs + f_y, True).wait_send()

    @pl.loop(1, grid.dp)
    def _(step):
        peer = lax.rem(d + step, grid.dp)
        row_copy(peer, d).wait_send()
        note(peer, me).wait_send()

    @pl.loop(0, tall)
    def _(level):
        for xx in range(2):
            for yy in range(2):
                arrived(grid.flat(level, xx, yy, 1 - core))
                sent(grid.flat(level, xx, yy, core), sibling, 4)
        shard, other = grid.flat(level, x, y, core), grid.flat(level, ux, uy, core)

        @pl.when((level <= z) & has_up)
        def _():
            sent(shard, up, 0)

        @pl.when((level >= z) & has_down)
        def _():
            sent(shard, down, 1)

        sent(shard, u_device, 2)
        sent(shard, v_device, 3)
        sent(other, v_device, 3)

    for item in local:
        item.wait()


def run_head(ids, negatives, attn_in, attn_out, ffn_in, proj_head, ffn_out, table, number):
    grid = Grid()
    tokens = ids.shape[0]
    wide = ids.astype(jnp.float32)
    row = jnp.zeros((1, 128), jnp.float32).at[0, : negatives.shape[0]].set(negatives.astype(jnp.float32))
    shapes = ((attn_in.shape[0], PACKED), ffn_out.shape)
    blocks = -(-table.shape[0] // ROW_BLOCK)
    anywhere, inside = pl.BlockSpec(memory_space=pl.ANY), pl.BlockSpec(memory_space=pltpu.VMEM)
    dma = pltpu.SemaphoreType.DMA
    line, everyone = dma((grid.dp,)), dma((grid.total,))
    return pl.pallas_call(
        functools.partial(head_kernel, grid),
        out_shape=[jax.ShapeDtypeStruct((grid.total,) + shape, jnp.bfloat16) for shape in shapes]
        + [
            jax.ShapeDtypeStruct((grid.total, 8, 128), jnp.float32),
            jax.ShapeDtypeStruct((tokens, 1), jnp.float32),
            jax.ShapeDtypeStruct((tokens, D), jnp.float32),
        ],
        in_specs=[inside] * 8 + [anywhere],
        out_specs=[anywhere] * 2 + [inside] * 3,
        scratch_shapes=[pltpu.VMEM(shape, jnp.bfloat16) for shape in shapes]
        + [
            pltpu.VMEM((blocks * ROW_BLOCK, D), jnp.float32),
            pltpu.VMEM((grid.dp * CAP, D), jnp.float32),
            pltpu.VMEM((grid.dp, CAP, D), jnp.bfloat16),
            pltpu.VMEM((grid.dp, CAP, D), jnp.bfloat16),
            pltpu.VMEM((grid.dp, 8, 128), jnp.float32),
            dma((5, 2, grid.total)),
            dma((2, grid.total)),
            dma((2,)),
            line,
            line,
            line,
            everyone,
            dma((2, grid.total)),
            dma,
        ],
        compiler_params=pltpu.CompilerParams(
            collective_id=number, has_side_effects=True, vmem_limit_bytes=48 * 1024 * 1024
        ),
    )(wide.reshape(tokens, 1), wide.reshape(1, tokens), row, attn_in, attn_out, ffn_in, proj_head, ffn_out, table)


def lane_is(shape, low, high):
    lanes = lax.broadcasted_iota(jnp.int32, shape, len(shape) - 1)
    return (lanes >= low) & (lanes < high)


def gelu_parts(t):
    inner = np.float32(np.sqrt(2 / np.pi)) * (t + 0.044715 * (t * t * t))
    tan = jnp.tanh(inner)
    return 0.5 * (1.0 + tan), tan


def forward_kernel(
    x0_ref,
    mask_col_ref,
    gains_ref,
    bias_ref,
    packed_hbm,
    down_hbm,
    mixed_ref,
    attended_ref,
    total_ref,
    after_ref,
    pre_ref,
    final_ref,
    pooled_ref,
    projected_ref,
    packed,
    down,
    load_sem,
):
    step = pl.program_id(0)
    tile_seqs = x0_ref.shape[0] // L
    edges = (0, WIDE, WIDE + D, WIDE + 5 * D, PACKED)

    def load(k):
        if k == 4:
            return pltpu.make_async_copy(down_hbm, down, load_sem.at[k])
        part = pl.ds(edges[k], edges[k + 1] - edges[k])
        return pltpu.make_async_copy(packed_hbm.at[:, part], packed.at[:, part], load_sem.at[k])

    def loaded(k):
        @pl.when(step == 0)
        def _():
            load(k).wait()

    @pl.when(step == 0)
    def _():
        for k in (0, 1, 2, 4, 3):
            load(k).start()

    x0 = x0_ref[...]
    act_one = normalize(x0, gains_ref[0:1, :])[0].astype(jnp.bfloat16)
    loaded(0)
    for at in range(0, WIDE, D):
        mixed_ref[:, at : at + D] = matmul(act_one, packed[:, at : at + D]).astype(jnp.bfloat16)

    zero = jnp.zeros((), jnp.bfloat16)
    for s in range(tile_seqs):
        rows = slice(s * L, (s + 1) * L)
        keep = jnp.where(mask_col_ref[rows, :] > 0, 0.0, -1000000000.0)
        for pair in range(HEADS // 2):
            at = pair * 128
            query = mixed_ref[rows, at : at + 128]
            key = mixed_ref[rows, D + at : D + at + 128]
            value = mixed_ref[rows, 2 * D + at : 2 * D + at + 128]
            mine = lane_is((L, 128), 0, HD)
            keys = jnp.concatenate([jnp.where(mine, key, zero), jnp.where(mine, zero, key)], 0)
            scores = (matmul_nt(keys, query) * SCALE).reshape(2, L, L)
            scores = scores + bias_ref[2 * pair : 2 * pair + 2] + keep[None]
            row_max = jnp.max(scores, 1, keepdims=True)
            powers = jnp.exp(scores - row_max)
            row_sum = jnp.sum(powers, 1, keepdims=True)
            prob = (powers * (1.0 / row_sum)).astype(jnp.bfloat16)
            total_ref[s, 2 * pair : 2 * pair + 2, :] = (row_max + jnp.log(row_sum))[:, 0, :]
            flipped = jnp.transpose(value)
            both = jnp.concatenate([matmul(flipped[:HD], prob[0]), matmul(flipped[HD:], prob[1])], 0)
            both = jnp.transpose(both)
            attended_ref[rows, at : at + 128] = both.astype(jnp.bfloat16)

    loaded(1)
    after = x0 + matmul(attended_ref[...], packed[:, WIDE : WIDE + D])
    after_ref[...] = after
    act_two = normalize(after, gains_ref[1:2, :])[0].astype(jnp.bfloat16)
    loaded(2)
    loaded(4)
    final = after
    for j in range(4):
        at = WIDE + D + j * D
        pre = matmul(act_two, packed[:, at : at + D])
        pre_ref[:, j * D : (j + 1) * D] = pre
        hidden = (pre * gelu_parts(pre)[0]).astype(jnp.bfloat16)
        final = final + matmul(hidden, down[j * D : (j + 1) * D, :])
    final_ref[...] = final
    normed = normalize(final, gains_ref[2:3, :])[0]
    weight = mask_col_ref[...]
    for s in range(tile_seqs):
        rows = slice(s * L, (s + 1) * L)
        count = jnp.sum(weight[rows], 0, keepdims=True)
        row = jnp.sum(normed[rows] * weight[rows], 0, keepdims=True) / count
        pooled_ref[pl.ds(step * tile_seqs + s, 1), :] = row

    @pl.when(step == pl.num_programs(0) - 1)
    def _():
        load(3).wait()
        projected_ref[...] = matmul(pooled_ref[...].astype(jnp.bfloat16), packed[:, PACKED - D :])


def run_forward(x0, mask_col, gains, bias_full, packed, down):
    tokens = x0.shape[0]
    seqs = tokens // L
    tile = TILE_SEQS * L
    steps = tokens // tile

    def rows(width):
        return pl.BlockSpec((tile, width), lambda i: (i, 0))

    def whole(*shape):
        return pl.BlockSpec(shape, lambda i: (0,) * len(shape), pipeline_mode=pl.Buffered(1))

    def kept(width, dtype):
        return jax.ShapeDtypeStruct((tokens, width), dtype)

    anywhere = pl.BlockSpec(memory_space=pl.ANY)
    return pl.pallas_call(
        forward_kernel,
        grid=(steps,),
        out_shape=[
            kept(WIDE, jnp.bfloat16),
            kept(D, jnp.bfloat16),
            jax.ShapeDtypeStruct((seqs, HEADS, L), jnp.float32),
            kept(D, jnp.float32),
            kept(4 * D, jnp.float32),
            kept(D, jnp.float32),
            jax.ShapeDtypeStruct((seqs, D), jnp.float32),
            jax.ShapeDtypeStruct((seqs, D), jnp.float32),
        ],
        in_specs=[
            rows(D),
            rows(1),
            whole(3, D),
            whole(HEADS, L, L),
            anywhere,
            anywhere,
        ],
        out_specs=[rows(WIDE), rows(D), pl.BlockSpec((TILE_SEQS, HEADS, L), lambda i: (i, 0, 0)), rows(D), rows(4 * D), rows(D), whole(seqs, D), whole(seqs, D)],
        scratch_shapes=[
            pltpu.VMEM((D, PACKED), jnp.bfloat16),
            pltpu.VMEM((4 * D, D), jnp.bfloat16),
            pltpu.SemaphoreType.DMA((5,)),
        ],
        compiler_params=pltpu.CompilerParams(vmem_limit_bytes=60 * 1024 * 1024),
    )(x0, mask_col, gains, bias_full, packed, down)


def loss_kernel(
    grid, pairs_here, projected_ref, target_ref, scale_ref, grad_ref, loss_ref, others, grads, send_sem, recv_sem
):
    z, x, y, core = grid.here()
    tall = grid.tall
    each = 2 * pairs_here
    half = D // 2
    x_device, y_device = grid.device(z, 1 - x, y, core), grid.device(z, x, 1 - y, core)
    sibling = grid.device(z, x, y, 1 - core)

    def other_levels(action):
        @pl.loop(1, tall)
        def _(step):
            action(lax.rem(z + step, tall))

    greet(x_device)
    greet(y_device)
    greet(sibling)
    other_levels(lambda level: greet(grid.device(level, x, y, core)))
    projected = projected_ref[...]
    factor = lax.rsqrt(jnp.sum(projected * projected, -1, keepdims=True) + EPS)
    unit = projected * factor
    others[core, z, x, y] = jnp.concatenate([unit[:, :half], unit[:, half:]], 0).astype(jnp.bfloat16)
    meet(tall + 2)

    def remote(blocks, device, sent, received):
        return pltpu.make_async_remote_copy(
            src_ref=blocks,
            dst_ref=blocks,
            send_sem=send_sem.at[sent],
            recv_sem=recv_sem.at[received],
            device_id=device,
            device_id_type=MESH,
        )

    along_x = remote(others.at[core, z, x, y], x_device, 0, 0)
    along_x.start()
    along_x.wait_recv()
    along_y = [remote(others.at[core, z, xx, y], y_device, 1 + xx, 1 + xx) for xx in range(2)]
    for copy in along_y:
        copy.start()
    for copy in along_y:
        copy.wait_recv()

    def along_z(level, origin):
        return remote(others.at[core, origin], grid.device(level, x, y, core), 3 + level, 3 + origin)

    def to_side(level):
        return remote(others.at[core, level], sibling, 3 + tall + level, 3 + tall + level)

    other_levels(lambda level: along_z(level, z).start())
    to_side(z).start()

    def pass_side(level):
        along_z(level, level).wait_recv()
        to_side(level).start()

    other_levels(pass_side)
    for level in range(tall):
        to_side(level).wait_recv()
    me = ((core * tall + z) * 2 + x) * 2 + y

    count = grid.total * each
    wide = others[...].reshape(grid.total, 2 * each, half).astype(jnp.float32)
    units = jnp.concatenate(
        [wide[:, :each].reshape(count, half), wide[:, each:].reshape(count, half)], 1
    ).astype(jnp.bfloat16)
    similar = matmul_nt(units, units)
    row = lax.broadcasted_iota(jnp.int32, (count, count), 0)
    column = lax.broadcasted_iota(jnp.int32, (count, count), 1)
    used = (lax.rem(row, each) < pairs_here) & (lax.rem(column, each) >= pairs_here)
    own = used & (column == row + pairs_here)
    negative = used & (column == target_ref[...])
    sim_scale = jnp.exp(scale_ref[...])
    own_mask = jnp.where(own, 1.0, 0.0)
    negative_mask = jnp.where(negative, 1.0, 0.0)
    logits = sim_scale * similar - MARGIN * own_mask
    diagonal = jnp.sum(logits * own_mask, 1, keepdims=True)
    hardest = jnp.sum(logits * negative_mask, 1, keepdims=True)
    row_max = jnp.max(jnp.where(used, logits, -3e38), 1, keepdims=True)
    powers = jnp.where(used, jnp.exp(jnp.minimum(logits - row_max, 0.0)), 0.0)
    row_sum = jnp.sum(powers, 1, keepdims=True)
    is_query = lax.rem(lax.broadcasted_iota(jnp.int32, (count, 1), 0), each) < pairs_here
    gap = hardest - diagonal
    softplus = jnp.maximum(gap, 0.0) + jnp.log(1.0 + jnp.exp(-jnp.abs(gap)))
    row_sum = jnp.where(is_query, row_sum, 1.0)
    losses = jnp.where(is_query, row_max + jnp.log(row_sum) - diagonal + softplus, 0.0)
    gate = 1.0 / (1.0 + jnp.exp(-gap))
    grad_logits = jnp.where(
        used, powers / row_sum - own_mask + gate * (negative_mask - own_mask), 0.0
    )
    loss_ref[0:1, :] = jnp.broadcast_to(jnp.sum(losses, 0, keepdims=True), (1, 128))
    grad_scale = sim_scale * jnp.sum(
        jnp.sum(grad_logits * similar, 1, keepdims=True), 0, keepdims=True
    )
    loss_ref[1:2, :] = jnp.broadcast_to(grad_scale, (1, 128))
    loss_ref[2:8, :] = jnp.zeros((6, 128), jnp.float32)
    grad_similar = sim_scale * grad_logits
    grads[...] = grad_similar + jnp.transpose(grad_similar)
    first = pl.multiple_of(me * each, each)
    grad_units = matmul(grads[pl.ds(first, each), :].astype(jnp.bfloat16), units)
    grad_units = grad_units.astype(jnp.bfloat16).astype(jnp.float32)
    grad_ref[...] = (
        factor * (grad_units - unit * jnp.sum(grad_units * unit, -1, keepdims=True))
    ).astype(jnp.bfloat16)

    along_x.wait_send()
    for copy in along_y:
        copy.wait_send()
    other_levels(lambda level: along_z(level, level).wait_send())
    for level in range(tall):
        to_side(level).wait_send()


def run_loss(projected, target, log_scale, number):
    grid = Grid()
    each = projected.shape[0]
    count = grid.total * each
    inside = pl.BlockSpec(memory_space=pltpu.VMEM)
    dma = pltpu.SemaphoreType.DMA((3 + 2 * grid.tall,))
    return pl.pallas_call(
        functools.partial(loss_kernel, grid, each // 2),
        out_shape=[
            jax.ShapeDtypeStruct((each, D), jnp.bfloat16),
            jax.ShapeDtypeStruct((8, 128), jnp.float32),
        ],
        in_specs=[inside] * 3,
        out_specs=[inside] * 2,
        scratch_shapes=[
            pltpu.VMEM((2, grid.tall, 2, 2, 2 * each, D // 2), jnp.bfloat16),
            pltpu.VMEM((count, count), jnp.float32),
            dma,
            dma,
        ],
        compiler_params=pltpu.CompilerParams(collective_id=number, has_side_effects=True),
    )(projected, target, log_scale)


class Tree:

    @staticmethod
    def scratch(grid, blocks):
        count, tall = len(blocks), grid.tall
        leads = ((tall, 2, 2), (tall, 2, 2), (tall, 2), (tall,), (tall,), (tall,))
        dma = pltpu.SemaphoreType.DMA
        level, pair = dma((count, tall)), dma((count, tall, 2))
        buffers = [pltpu.VMEM(lead + block, jnp.bfloat16) for lead in leads for block in blocks]
        return buffers + [level, level, level, pair, pair] + [level] * 5

    @staticmethod
    def size(count):
        return 6 * count + 10

    def __init__(self, grid, srcs, scratch):
        count = len(srcs)
        self.grid, self.count, self.srcs = grid, count, srcs
        self.acc, self.from_side, self.from_v, self.from_u, self.from_low, self.from_high = [
            scratch[k * count : (k + 1) * count] for k in range(6)
        ]
        (
            self.load_sem,
            self.side_send,
            self.side_recv,
            self.v_send,
            self.v_recv,
            self.u_send,
            self.u_recv,
            self.z_send,
            self.low_recv,
            self.high_recv,
        ) = scratch[6 * count :]
        z, x, y, core = self.place = grid.here()
        tall = grid.tall
        self.up, self.down = grid.device(z + 1, x, y, core), grid.device(z - 1, x, y, core)
        self.has_up, self.has_down = z < tall - 1, z > 0
        self.u = lax.rem(x + 1 - core, 2), lax.rem(y + core, 2)
        self.v = lax.rem(x + core, 2), lax.rem(y + 1 - core, 2)
        self.u_device = grid.device(z, *self.u, core)
        self.v_device = grid.device(z, *self.v, core)
        self.sibling = grid.device(z, x, y, 1 - core)
        self.levels = [self.level_of(j) for j in range(tall)]

    def greet_all(self):
        greet(self.u_device)
        greet(self.v_device)
        greet(self.sibling)
        greet(self.up, self.has_up)
        greet(self.down, self.has_down)
        return 3 + self.has_up.astype(jnp.int32) + self.has_down.astype(jnp.int32)

    def each(self, action):
        for m in range(self.count):
            action(m)

    def level_of(self, j):
        tall = self.grid.tall
        tables = [
            sorted(range(tall), key=lambda level: (-abs(level - own), -level))[j] for own in range(tall)
        ]
        value = tables[0]
        for own in range(1, tall):
            value = jnp.where(self.place[0] == own, tables[own], value)
        return value

    def load(self, m, level):
        core = self.place[3]
        return pltpu.make_async_copy(
            self.srcs[m].at[level, :, :, core], self.acc[m].at[level], self.load_sem.at[m, level]
        )

    def remote(self, src, dst, send_sem, recv_sem, device):
        return pltpu.make_async_remote_copy(
            src_ref=src,
            dst_ref=dst,
            send_sem=send_sem,
            recv_sem=recv_sem,
            device_id=device,
            device_id_type=MESH,
        )

    def side(self, m, level):
        return self.remote(
            self.srcs[m].at[level, :, :, 1 - self.place[3]],
            self.from_side[m].at[level],
            self.side_send.at[m, level],
            self.side_recv.at[m, level],
            self.sibling,
        )

    def v_copy(self, m, level, along_u):
        z, x, y, core = self.place
        xx, yy = (1 - x, 1 - y) if along_u else self.v
        return self.remote(
            self.acc[m].at[level, xx, yy],
            self.from_v[m].at[level, along_u],
            self.v_send.at[m, level, along_u],
            self.v_recv.at[m, level, along_u],
            self.v_device,
        )

    def u_copy(self, m, level):
        return self.remote(
            self.acc[m].at[level, self.u[0], self.u[1]],
            self.from_u[m].at[level],
            self.u_send.at[m, level],
            self.u_recv.at[m, level],
            self.u_device,
        )

    def z_copy(self, m, level, upward):
        z, x, y, core = self.place
        return self.remote(
            self.acc[m].at[level, x, y],
            (self.from_low if upward else self.from_high)[m].at[level],
            self.z_send.at[m, level],
            (self.low_recv if upward else self.high_recv).at[m, level],
            self.up if upward else self.down,
        )

    def add(self, m, level, xx, yy, other):
        total = self.acc[m][level, xx, yy].astype(jnp.float32) + other.astype(jnp.float32)
        self.acc[m][level, xx, yy] = total.astype(jnp.bfloat16)

    def loads(self):
        for level in self.levels:
            self.each(lambda m: self.load(m, level).start())

    def sides(self):
        for level in self.levels:
            self.each(lambda m: self.side(m, level).start())

    def first(self, j):
        level = self.levels[j]

        def run(m):
            self.load(m, level).wait()
            self.side(m, level).wait_recv()
            for xx in range(2):
                for yy in range(2):
                    self.add(m, level, xx, yy, self.from_side[m][level, xx, yy])
            self.v_copy(m, level, 1).start()
            self.v_copy(m, level, 0).start()

        self.each(run)

    def second(self, j):
        z, x, y, core = self.place
        level = self.levels[j]

        def run(m):
            self.v_copy(m, level, 1).wait_recv()
            self.add(m, level, self.u[0], self.u[1], self.from_v[m][level, 1])
            self.u_copy(m, level).start()

        def run_own(m):
            self.v_copy(m, level, 0).wait_recv()
            self.add(m, level, x, y, self.from_v[m][level, 0])

        self.each(run)
        self.each(run_own)

    def third(self, j):
        z, x, y, core = self.place
        level = self.levels[j]

        def run(m):
            self.u_copy(m, level).wait_recv()
            self.add(m, level, x, y, self.from_u[m][level])

            @pl.when((level >= z) & self.has_down)
            def _():
                self.z_copy(m, level, True).wait_recv()
                self.add(m, level, x, y, self.from_low[m][level])

            @pl.when((level <= z) & self.has_up)
            def _():
                self.z_copy(m, level, False).wait_recv()
                self.add(m, level, x, y, self.from_high[m][level])

            @pl.when(level > z)
            def _():
                self.z_copy(m, level, True).start()

            @pl.when(level < z)
            def _():
                self.z_copy(m, level, False).start()

        self.each(run)

    def own(self, m):
        z, x, y, core = self.place
        return self.acc[m][z, x, y].astype(jnp.float32)

    def drain(self):
        for level in self.levels:
            self.each(lambda m: self.side(m, level).wait_send())
            self.each(lambda m: self.v_copy(m, level, 0).wait_send())
            self.each(lambda m: self.v_copy(m, level, 1).wait_send())
            self.each(lambda m: self.u_copy(m, level).wait_send())

            @pl.when(level != self.place[0])
            def _():
                self.each(lambda m: self.z_copy(m, level, True).wait_send())


def fold(values):
    n, lanes = values.shape
    part = jnp.sum(values.reshape(n // 8, 8, lanes), 0)
    total = part[:, :128]
    for at in range(128, lanes, 128):
        total = total + part[:, at : at + 128]
    return total


def gain_back(gains_ref, grads_ref, k, grad_out, inputs):
    factor = lax.rsqrt(jnp.mean(inputs * inputs, -1, keepdims=True) + EPS)
    scaled = grad_out * gains_ref[k : k + 1, :]
    grads_ref[k : k + 1, :] += jnp.sum(grad_out * inputs * factor, 0, keepdims=True)
    return factor * (
        scaled - inputs * (factor * factor * jnp.mean(scaled * inputs, -1, keepdims=True))
    )


BACK_SEQS = 2
HALF = 256


def ffn_back_kernel(
    final_ref,
    after_ref,
    mask_col_ref,
    gains_ref,
    pooled_ref,
    grad_proj_ref,
    pre_hbm,
    packed_hbm,
    down_hbm,
    grad_after_ref,
    grad_gains_ref,
    grad_up_hbm,
    grad_down_hbm,
    up,
    head,
    down,
    branch,
    act_two,
    hidden,
    grad_pre,
    grad_act,
    pre,
    grad_pooled,
    stage,
    load_sem,
    pre_sem,
    store_sem,
):
    tokens = final_ref.shape[0]
    tile = BACK_SEQS * L

    def load(k):
        if k == 0:
            return pltpu.make_async_copy(packed_hbm.at[:, pl.ds(PACKED - D, D)], head, load_sem.at[0])
        if k == 1:
            return pltpu.make_async_copy(down_hbm, down, load_sem.at[1])
        return pltpu.make_async_copy(packed_hbm.at[:, pl.ds(WIDE + D, 4 * D)], up, load_sem.at[2])

    def load_pre(j):
        return pltpu.make_async_copy(pre_hbm.at[:, pl.ds(j * D, D)], pre.at[j % 2], pre_sem.at[j % 2])

    load(0).start()
    load_pre(0).start()
    load(1).start()
    load(2).start()
    grad_gains_ref[...] = jnp.zeros_like(grad_gains_ref)
    load(0).wait()
    grad_pooled[...] = matmul_nt(grad_proj_ref[...], head[...])

    @pl.loop(0, tokens // tile)
    def _(step):
        rows = pl.ds(pl.multiple_of(step * tile, tile), tile)
        weight = mask_col_ref[rows, :]
        pieces = []
        for s in range(BACK_SEQS):
            part = weight[s * L : (s + 1) * L]
            count = jnp.sum(part, 0, keepdims=True)
            pieces.append(part * (grad_pooled[pl.ds(step * BACK_SEQS + s, 1), :] / count))
        grad = gain_back(gains_ref, grad_gains_ref, 2, jnp.concatenate(pieces, 0), final_ref[rows, :])
        grad_after_ref[rows, :] = grad
        branch[rows, :] = grad.astype(jnp.bfloat16)
        act_two[rows, :] = normalize(after_ref[rows, :], gains_ref[1:2, :])[0].astype(jnp.bfloat16)

    stores = []

    def store(value, to):
        slot = len(stores) % 2
        if len(stores) >= 2:
            stores[-2].wait()
        stage[slot] = value.astype(jnp.bfloat16)
        stores.append(pltpu.make_async_copy(stage.at[slot], to, store_sem.at[slot]))
        stores[-1].start()

    load(1).wait()
    for j in range(4):
        part = slice(j * D, (j + 1) * D)
        if j < 3:
            load_pre(j + 1).start()
        for at in range(0, tokens, HALF):
            rows = slice(at, at + HALF)
            wide = matmul_nt(branch[rows, :], down[part, :])
            if at == 0:
                load_pre(j).wait()
            some = pre[j % 2, rows, :]
            half, tan = gelu_parts(some)
            hidden[rows, :] = (some * half).astype(jnp.bfloat16)
            slope = np.float32(np.sqrt(2 / np.pi)) * (1.0 + (3 * 0.044715) * (some * some))
            slope = half + 0.5 * some * (1.0 - tan * tan) * slope
            grad_pre[rows, :] = (wide * slope).astype(jnp.bfloat16)
            if j == 0:
                if at == 0:
                    load(2).wait()
                grad_act[rows, :] = matmul_nt(grad_pre[rows, :], up[:, part])
            else:
                grad_act[rows, :] += matmul_nt(grad_pre[rows, :], up[:, part])
        store(matmul_tn(hidden[...], branch[...]), grad_down_hbm.at[pl.ds(j * D, D), :])
        store(matmul_tn(act_two[...], grad_pre[...]), grad_up_hbm.at[:, pl.ds(j * D, D)])
    store(
        matmul_tn(pooled_ref[...].astype(jnp.bfloat16), grad_proj_ref[...]),
        grad_up_hbm.at[:, pl.ds(4 * D, D)],
    )

    @pl.loop(0, tokens // tile)
    def _(step):
        rows = pl.ds(pl.multiple_of(step * tile, tile), tile)
        grad = gain_back(gains_ref, grad_gains_ref, 1, grad_act[rows, :], after_ref[rows, :])
        grad_after_ref[rows, :] += grad

    stores[-2].wait()
    stores[-1].wait()


def run_ffn_back(final, after, mask_col, gains, pooled, grad_proj, pre, packed, down):
    tokens, seqs = final.shape[0], pooled.shape[0]
    anywhere, inside = pl.BlockSpec(memory_space=pl.ANY), pl.BlockSpec(memory_space=pltpu.VMEM)

    def low(*shape):
        return pltpu.VMEM(shape, jnp.bfloat16)

    def full(*shape):
        return pltpu.VMEM(shape, jnp.float32)

    return pl.pallas_call(
        ffn_back_kernel,
        out_shape=[
            jax.ShapeDtypeStruct((tokens, D), jnp.float32),
            jax.ShapeDtypeStruct((3, D), jnp.float32),
            jax.ShapeDtypeStruct((D, 5 * D), jnp.bfloat16),
            jax.ShapeDtypeStruct((4 * D, D), jnp.bfloat16),
        ],
        in_specs=[inside] * 6 + [anywhere] * 3,
        out_specs=[inside] * 2 + [anywhere] * 2,
        scratch_shapes=[
            low(D, 4 * D),
            low(D, D),
            low(4 * D, D),
            low(tokens, D),
            low(tokens, D),
            low(tokens, D),
            low(tokens, D),
            full(tokens, D),
            full(2, tokens, D),
            full(seqs, D),
            low(2, D, D),
            pltpu.SemaphoreType.DMA((3,)),
            pltpu.SemaphoreType.DMA((2,)),
            pltpu.SemaphoreType.DMA((2,)),
        ],
        compiler_params=pltpu.CompilerParams(vmem_limit_bytes=62 * 1024 * 1024),
    )(final, after, mask_col, gains, pooled, grad_proj, pre, packed, down)


def attn_back_kernel(grid, *refs):
    x0_ref, mask_col_ref, mixed_ref, attended, total_ref, grad_after_ref, gains_ref, bias_ref, packed_hbm = refs[:9]
    srcs = refs[9:11]
    rows_ref, grad_gains_ref, grad_bias_ref, grad_attn_hbm = refs[11:15]
    outs, square_ref = refs[15:17], refs[17]
    packed, act_one, branch_one, grad_mixed, stage, load_sem, store_sem = refs[18:25]
    tree = Tree(grid, srcs, refs[25:])
    step = pl.program_id(0)
    last_step = pl.num_programs(0) - 1
    tile_seqs = x0_ref.shape[0] // L
    tile = tile_seqs * L
    base = pl.multiple_of(step * tile, tile)

    def load(k):
        part = pl.ds(WIDE, D) if k else pl.ds(0, WIDE)
        return pltpu.make_async_copy(packed_hbm.at[:, part], packed.at[:, part], load_sem.at[k])

    @pl.when(step == 0)
    def _():
        friends = tree.greet_all()
        load(1).start()
        load(0).start()
        tree.loads()
        grad_gains_ref[...] = jnp.zeros_like(grad_gains_ref)
        grad_bias_ref[...] = jnp.zeros_like(grad_bias_ref)
        meet(friends)
        tree.sides()
        load(1).wait()

    rows = pl.ds(base, tile)
    grad_after = grad_after_ref[...]
    weight = mask_col_ref[...]
    branch = grad_after.astype(jnp.bfloat16)
    branch_one[rows, :] = branch
    grad_attended = matmul_nt(branch, packed[:, WIDE:]).astype(jnp.bfloat16)
    act_one[rows, :] = normalize(x0_ref[...], gains_ref[0:1, :])[0].astype(jnp.bfloat16)

    def at_step(number, action, *levels):
        @pl.when(step == number)
        def _():
            for j in levels:
                action(j)

    at_step(0, tree.first, 0, 1)
    at_step(1, tree.second, 0)
    at_step(2, tree.third, 0)
    at_step(3, tree.third, 1)
    zero = jnp.zeros((), jnp.bfloat16)
    mine = lane_is((L, 128), 0, HD)
    for s in range(tile_seqs):
        part = slice(s * L, (s + 1) * L)
        here = pl.ds(pl.multiple_of(base + s * L, L), L)
        keep = jnp.where(weight[part] > 0, 0.0, -1000000000.0)
        for pair in range(HEADS // 2):
            at = pair * 128
            query = mixed_ref[part, at : at + 128]
            key = mixed_ref[part, D + at : D + at + 128]
            value = mixed_ref[part, 2 * D + at : 2 * D + at + 128]
            grad_out = grad_attended[part, at : at + 128]
            keys = jnp.concatenate([jnp.where(mine, key, zero), jnp.where(mine, zero, key)], 0)
            values = jnp.concatenate([jnp.where(mine, value, zero), jnp.where(mine, zero, value)], 0)
            scores = (matmul_nt(keys, query) * SCALE).reshape(2, L, L)
            scores = scores + bias_ref[2 * pair : 2 * pair + 2] + keep[None]
            prob = jnp.exp(scores - total_ref[s, 2 * pair : 2 * pair + 2, :][:, None, :])
            grad_prob = matmul_nt(values, grad_out).reshape(2, L, L)
            mean = jnp.sum(prob * grad_prob, 1, keepdims=True)
            grad_scores = (prob * (grad_prob - mean)).astype(jnp.bfloat16)
            grad_bias_ref[2 * pair : 2 * pair + 2] += grad_scores.astype(jnp.float32)
            prob_low = prob.astype(jnp.bfloat16)
            flipped = jnp.transpose(key)
            grad_query = jnp.concatenate(
                [matmul(flipped[:HD], grad_scores[0]), matmul(flipped[HD:], grad_scores[1])], 0
            )
            grad_mixed[here, at : at + 128] = (jnp.transpose(grad_query) * SCALE).astype(jnp.bfloat16)
            grad_keys = matmul(grad_scores.reshape(2 * L, L), query)
            grad_key = jnp.where(mine, grad_keys[:L], grad_keys[L:]) * SCALE
            grad_mixed[here, D + at : D + at + 128] = grad_key.astype(jnp.bfloat16)
            grad_values = matmul(prob_low.reshape(2 * L, L), grad_out)
            grad_value = jnp.where(mine, grad_values[:L], grad_values[L:])
            grad_mixed[here, 2 * D + at : 2 * D + at + 128] = grad_value.astype(jnp.bfloat16)

    @pl.when(step == 0)
    def _():
        tree.first(2)
        tree.first(3)
        load(0).wait()

    at_step(1, tree.second, 1)
    at_step(2, tree.second, 2)
    at_step(3, tree.second, 3)
    grad_act = matmul_nt(grad_mixed[rows, :], packed[:, :WIDE])
    grad_low = gain_back(gains_ref, grad_gains_ref, 0, grad_act, x0_ref[...])
    rows_ref[...] = (grad_after + grad_low).astype(jnp.bfloat16)

    @pl.when(step == last_step)
    def _():
        tree.third(2)
        jobs = [(attended, branch_one, slice(0, D), 3)]
        for j in range(3):
            jobs.append((act_one, grad_mixed, slice(j * D, (j + 1) * D), j))
        copies = []
        for number, (left, right, part, at) in enumerate(jobs):
            slot = number % 2
            if number >= 2:
                copies[number - 2].wait()
            stage[slot] = matmul_tn(left[...], right[:, part]).astype(jnp.bfloat16)
            to = grad_attn_hbm.at[:, pl.ds(at * D, D)]
            copies.append(pltpu.make_async_copy(stage.at[slot], to, store_sem.at[slot]))
            copies[-1].start()
        tree.third(3)
        square_ref[...] = jnp.zeros_like(square_ref)

        def give(m):
            wide = tree.own(m)
            outs[m][...] = wide
            square_ref[0:8, :] += fold(wide * wide)

        tree.each(give)
        copies[-2].wait()
        copies[-1].wait()
        tree.drain()


def run_attn_back(
    x0, mask_col, mixed, attended, totals, grad_after, gains, bias_full, packed, grad_up, grad_down, number
):
    grid = Grid()
    tokens = x0.shape[0]
    tile = BACK_SEQS * L
    steps = tokens // tile
    srcs = [grad.reshape(grid.total, -1, grad.shape[1]) for grad in (grad_up, grad_down)]
    blocks = [src.shape[1:] for src in srcs]
    srcs = [src.reshape((grid.tall, 2, 2, 2) + src.shape[1:]) for src in srcs]

    def rows(width):
        return pl.BlockSpec((tile, width), lambda i: (i, 0))

    def whole(*shape):
        return pl.BlockSpec(shape, lambda i: (0,) * len(shape), pipeline_mode=pl.Buffered(1))

    def low(*shape):
        return pltpu.VMEM(shape, jnp.bfloat16)

    anywhere = pl.BlockSpec(memory_space=pl.ANY)
    return pl.pallas_call(
        functools.partial(attn_back_kernel, grid),
        grid=(steps,),
        out_shape=[
            jax.ShapeDtypeStruct((tokens, D), jnp.bfloat16),
            jax.ShapeDtypeStruct((1, D), jnp.float32),
            jax.ShapeDtypeStruct((HEADS, L, L), jnp.float32),
            jax.ShapeDtypeStruct((D, WIDE + D), jnp.bfloat16),
        ]
        + [jax.ShapeDtypeStruct(block, jnp.float32) for block in blocks]
        + [jax.ShapeDtypeStruct((16, 128), jnp.float32)],
        in_specs=[
            rows(D),
            rows(1),
            rows(WIDE),
            whole(tokens, D),
            pl.BlockSpec((BACK_SEQS, HEADS, L), lambda i: (i, 0, 0)),
            rows(D),
            whole(3, D),
            whole(HEADS, L, L),
            anywhere,
            anywhere,
            anywhere,
        ],
        out_specs=[rows(D), whole(1, D), whole(HEADS, L, L), anywhere]
        + [whole(*block) for block in blocks]
        + [whole(16, 128)],
        scratch_shapes=[
            low(D, WIDE + D),
            low(tokens, D),
            low(tokens, D),
            low(tokens, WIDE),
            low(2, D, D),
            pltpu.SemaphoreType.DMA((2,)),
            pltpu.SemaphoreType.DMA((2,)),
        ]
        + Tree.scratch(grid, blocks),
        compiler_params=pltpu.CompilerParams(
            collective_id=number, has_side_effects=True, vmem_limit_bytes=62 * 1024 * 1024
        ),
    )(x0, mask_col, mixed, attended, totals, grad_after, gains, bias_full, packed, *srcs)


def finish_kernel(grid, count, *refs):
    srcs, (sums, ids, small, square_ref) = refs[:count], refs[count : count + 4]
    refs = refs[count + 4 :]
    outs, (table_out, small_out, square_out) = refs[:count], refs[count : count + 3]
    refs = refs[count + 3 :]
    tree = Tree(grid, srcs, refs[: Tree.size(count)])
    refs = refs[Tree.size(count) :]
    rows, part_sums, small_stage, small_in, square_stage, square_in = refs[:6]
    row_own, line_send, on_send, row_recv, small_send, small_recv, square_send, square_recv = refs[6:]
    z, x, y, core = grid.here()
    tall = grid.tall
    d, f = lax.axis_index("dp"), lax.axis_index("fsdp")
    me = f * grid.dp + d
    sibling = tree.sibling
    f_side = y * 2 + 1 - core
    f_y = (1 - y) * 2 + core
    f_far = (1 - y) * 2 + 1 - core
    for level in range(tall):
        small_in[3 + level] = jnp.zeros(small.shape, jnp.float32)
        square_in[3 + level] = jnp.zeros((16, 128), jnp.float32)
    x_device, y_device = grid.device(z, 1 - x, y, core), grid.device(z, x, 1 - y, core)

    @pl.loop(1, grid.dp)
    def _(step):
        greet((lax.rem(d + step, grid.dp), f))

    greet(y_device)
    greet(sibling)

    def line(peer, slot):
        return pltpu.make_async_remote_copy(
            src_ref=sums.at[peer],
            dst_ref=rows.at[slot],
            send_sem=line_send.at[peer],
            recv_sem=row_recv.at[slot],
            device_id=(peer, f),
            device_id_type=MESH,
        )

    def onward(slot, to_side, own_block=False):
        return pltpu.make_async_remote_copy(
            src_ref=sums.at[d] if own_block else rows.at[slot],
            dst_ref=rows.at[slot],
            send_sem=on_send.at[1 if to_side else 0, slot],
            recv_sem=row_recv.at[slot],
            device_id=(d, f_side if to_side else f_y),
            device_id_type=MESH,
        )

    def total_of(stage, inbox, send_sem, recv_sem):
        partners = (sibling, x_device, y_device)

        def copy(r):
            return pltpu.make_async_remote_copy(
                src_ref=stage.at[r],
                dst_ref=inbox.at[r],
                send_sem=send_sem.at[r],
                recv_sem=recv_sem.at[r],
                device_id=partners[r],
                device_id_type=MESH,
            )

        def z_send(level, slot):
            return pltpu.make_async_remote_copy(
                src_ref=stage.at[3],
                dst_ref=inbox.at[3 + slot],
                send_sem=send_sem.at[3 + level],
                recv_sem=recv_sem.at[3 + slot],
                device_id=grid.device(level, x, y, core),
                device_id_type=MESH,
            )

        def others(action):
            @pl.loop(1, tall)
            def _(step):
                action(lax.rem(z + step, tall))

        def send(r):
            if r < 3:
                copy(r).start()
            else:
                others(lambda level: z_send(level, z).start())

        def take(r):
            if r < 3:
                copy(r).wait_recv()
                stage[r + 1] = stage[r] + inbox[r]
                send(r + 1)
            else:
                others(lambda level: z_send(level, level).wait_recv())

        def result():
            total = stage[3]
            for level in range(tall):
                total = total + jnp.where(z == level, 0.0, inbox[3 + level])
            for r in range(3):
                copy(r).wait_send()
            others(lambda level: z_send(level, level).wait_send())
            return total

        return send, take, result

    small_stage[0] = small[...]
    small_sends, small_take, small_result = total_of(small_stage, small_in, small_send, small_recv)
    square_sends, square_take, square_result = total_of(square_stage, square_in, square_send, square_recv)
    own_rows = pltpu.make_async_copy(sums.at[d], rows.at[me], row_own)
    own_rows.start()
    tree.loads()
    meet(grid.dp + 1)
    small_sends(0)

    @pl.loop(1, grid.dp)
    def _(step):
        line(lax.rem(d + step, grid.dp), me).start()

    tree.sides()
    onward(me, False, True).start()
    onward(me, True, True).start()

    def pass_lines():
        @pl.loop(1, grid.dp)
        def _(step):
            slot = f * grid.dp + lax.rem(d + grid.dp - step, grid.dp)
            line(d, slot).wait_recv()
            onward(slot, False).start()
            onward(slot, True).start()

    def pass_y():
        @pl.loop(0, grid.dp)
        def _(step):
            slot = f_y * grid.dp + lax.rem(d + grid.dp - step, grid.dp)
            line(d, slot).wait_recv()
            onward(slot, True).start()

    def rows_in(column):
        @pl.loop(0, grid.dp)
        def _(step):
            line(d, column * grid.dp + step).wait_recv()

    table_rows = table_out.shape[0]
    whole_blocks = table_rows // ROW_BLOCK
    square_stage[0] = square_ref[...]

    per = grid.dp * rows.shape[1]

    def product(column, start, size):
        place = start + lax.broadcasted_iota(jnp.int32, (size, per), 0)
        hot = jnp.where(place.astype(jnp.float32) == ids[pl.ds(column, 1), :], 1.0, 0.0)
        some = rows[pl.ds(column * grid.dp, grid.dp)].reshape(per, D)
        return matmul(hot.astype(jnp.bfloat16), some)

    def spread_near():
        @pl.loop(0, part_sums.shape[0] // ROW_BLOCK)
        def _(block):
            start = pl.multiple_of(block * ROW_BLOCK, ROW_BLOCK)
            part_sums[pl.ds(start, ROW_BLOCK), :] = product(f, start, ROW_BLOCK) + product(
                f_side, start, ROW_BLOCK
            )

    def spread(start, size):
        total = part_sums[pl.ds(start, size), :] + product(f_y, start, size) + product(f_far, start, size)
        low = total.astype(jnp.bfloat16)
        table_out[pl.ds(start, size), :] = low
        wide = low.astype(jnp.float32)
        square_stage[0, 8:16, :] += fold(wide * wide)

    def spread_all():
        @pl.loop(0, whole_blocks)
        def _(block):
            spread(pl.multiple_of(block * ROW_BLOCK, ROW_BLOCK), ROW_BLOCK)

        if table_rows % ROW_BLOCK:
            spread(whole_blocks * ROW_BLOCK, table_rows % ROW_BLOCK)

    for j in range(tall):
        tree.first(j)
        if j < 3:
            small_take(j)
    pass_lines()
    tree.second(0)
    tree.second(1)
    own_rows.wait()
    rows_in(f_side)
    spread_near()
    tree.third(0)
    tree.second(2)
    pass_y()
    tree.third(1)
    tree.second(3)
    tree.third(2)
    rows_in(f_far)
    spread_all()
    tree.third(3)

    def give(m):
        wide = tree.own(m)
        outs[m][...] = wide
        square_stage[0, 0:8, :] += fold(wide * wide)

    tree.each(give)

    square_sends(0)
    small_take(3)
    small_out[...] = small_result()
    for r in range(3):
        square_take(r)

    tree.drain()

    @pl.loop(0, grid.dp)
    def _(step):
        onward(f * grid.dp + step, False).wait_send()
        onward(f * grid.dp + step, True).wait_send()
        onward(f_y * grid.dp + step, True).wait_send()

    @pl.loop(1, grid.dp)
    def _(step):
        line(lax.rem(d + step, grid.dp), me).wait_send()

    square_take(3)
    square_out[...] = square_result()


def finish(srcs, sums, ids, small, squares, vocab_rows, number):
    grid = Grid()
    count = len(srcs)
    tall = grid.tall
    blocks = [src.shape[1:] for src in srcs]
    srcs = [src.reshape((tall, 2, 2, 2) + src.shape[1:]) for src in srcs]
    cap = sums.shape[1]
    dma = pltpu.SemaphoreType.DMA
    by_device, by_step = dma((grid.total,)), dma((3 + tall,))
    scratch = Tree.scratch(grid, blocks) + [
        pltpu.VMEM((grid.total, cap, D), jnp.bfloat16),
        pltpu.VMEM((-(-vocab_rows // ROW_BLOCK) * ROW_BLOCK, D), jnp.float32),
        pltpu.VMEM((4,) + small.shape, jnp.float32),
        pltpu.VMEM((3 + tall,) + small.shape, jnp.float32),
        pltpu.VMEM((4, 16, 128), jnp.float32),
        pltpu.VMEM((3 + tall, 16, 128), jnp.float32),
        dma,
        dma((grid.dp,)),
        dma((2, grid.total)),
        by_device,
    ]
    anywhere, inside = pl.BlockSpec(memory_space=pl.ANY), pl.BlockSpec(memory_space=pltpu.VMEM)
    results = pl.pallas_call(
        functools.partial(finish_kernel, grid, count),
        out_shape=[jax.ShapeDtypeStruct(block, jnp.float32) for block in blocks]
        + [
            jax.ShapeDtypeStruct((vocab_rows, D), jnp.bfloat16),
            jax.ShapeDtypeStruct(small.shape, jnp.float32),
            jax.ShapeDtypeStruct((16, 128), jnp.float32),
        ],
        in_specs=[anywhere] * (count + 1) + [inside] * 3,
        out_specs=[inside] * (count + 3),
        scratch_shapes=scratch + [by_step] * 4,
        compiler_params=pltpu.CompilerParams(
            collective_id=number, has_side_effects=True, vmem_limit_bytes=62 * 1024 * 1024
        ),
    )(*srcs, sums, ids, small, squares)
    return (results[:count], *results[count:])


def update_kernel(fs, *refs):
    squares, summed, scale_grad, table, table_first, table_second, table_grad = refs[:7]
    rest, shards = refs[7:22], refs[22:25]
    norm_ref, out_first, out_second, out = refs[25:29]
    rest_outs, factor_ref = refs[29:44], refs[44]

    def row_sum(values):
        return jnp.sum(jnp.sum(values, 1, keepdims=True), 0, keepdims=True)

    @pl.when(pl.program_id(0) == 0)
    def _():
        total = row_sum(squares[0:8, :]) + row_sum(squares[8:16, :]) / float(fs)
        total = total + (row_sum(summed[...] * summed[...]) + scale_grad[...] * scale_grad[...])
        norm = jnp.sqrt(total)
        norm_ref[...] = jnp.broadcast_to(norm, norm_ref.shape)
        factor_ref[...] = jnp.minimum(1.0, CLIP / (norm + 1e-06))
        attn, up, down = shards
        grads = (attn[:, :WIDE], attn[:, WIDE:], up[:, : 4 * D], down[...], up[:, 4 * D :])
        for k in range(5):
            first_new, second_new, new = adam_update(
                *[ref[...] for ref in rest[3 * k : 3 * k + 3]],
                grads[k],
                factor_ref[...],
                RATES[k + 1],
                DECAYS[k + 1],
            )
            rest_outs[3 * k][...] = first_new
            rest_outs[3 * k + 1][...] = second_new
            rest_outs[3 * k + 2][...] = new

    first_new, second_new, new = adam_update(
        table[...],
        table_first[...],
        table_second[...],
        table_grad[...].astype(jnp.float32),
        factor_ref[...],
        RATES[0],
        DECAYS[0],
    )
    out_first[...] = first_new
    out_second[...] = second_new
    out[...] = new


def run_update(fs, squares, summed, scale_grad, table_arrays, table_grad, rest, shards):
    vocab_rows = table_grad.shape[0]
    blocks = pl.BlockSpec((ROW_BLOCK, D), lambda i: (i, 0))

    def whole(array):
        return pl.BlockSpec(
            array.shape, lambda i: (0,) * array.ndim, pipeline_mode=pl.Buffered(1)
        )

    norm = jax.ShapeDtypeStruct((8, 128), jnp.float32)
    return pl.pallas_call(
        functools.partial(update_kernel, fs),
        grid=(-(-vocab_rows // ROW_BLOCK),),
        out_shape=[norm]
        + [jax.ShapeDtypeStruct(table_grad.shape, jnp.float32)] * 3
        + [jax.ShapeDtypeStruct(array.shape, jnp.float32) for array in rest],
        in_specs=[whole(squares), whole(summed), whole(scale_grad)]
        + [blocks] * 4
        + [whole(array) for array in (*rest, *shards)],
        out_specs=[whole(norm)] + [blocks] * 3 + [whole(array) for array in rest],
        scratch_shapes=[pltpu.VMEM((1, 1), jnp.float32)],
        compiler_params=pltpu.CompilerParams(vmem_limit_bytes=60 * 1024 * 1024),
    )(squares, summed, scale_grad, *table_arrays, table_grad, *rest, *shards)


def plain_body(
    token_ids,
    pad_mask,
    hard_negative,
    table,
    table_first,
    table_second,
    attn_in,
    attn_in_first,
    attn_in_second,
    attn_out,
    attn_out_first,
    attn_out_second,
    ffn_in,
    ffn_in_first,
    ffn_in_second,
    ffn_out,
    ffn_out_first,
    ffn_out_second,
    proj_head,
    proj_head_first,
    proj_head_second,
    small_params,
    small_first,
    small_second,
):
    dp_count = lax.axis_size("dp")
    fsdp_count = lax.axis_size("fsdp")
    device_flat = lax.axis_index("dp") * fsdp_count + lax.axis_index("fsdp")
    pairs_here = token_ids.shape[1]
    pairs_total = pairs_here * dp_count * fsdp_count
    seq_count = 2 * pairs_here
    vocab_rows = table.shape[0]
    row_base = lax.axis_index("dp") * vocab_rows
    gain_rows = small_params[: 3 * D].reshape(3, D)
    bias_table = small_params[3 * D : 3 * D + NB * HEADS].reshape(NB, HEADS)
    log_scale = small_params[3 * D + NB * HEADS]
    buckets = jnp.asarray(bucket_table(L, NB).reshape(-1), jnp.int32)
    bucket_hot = (buckets[:, None] == jnp.arange(NB, dtype=jnp.int32)[None, :]).astype(jnp.float32)
    bias_full = (
        jnp.dot(bucket_hot, bias_table, precision=HIGH).reshape(L, L, HEADS).transpose(2, 0, 1)
    )
    mask_rows = pad_mask.reshape(seq_count, L)
    ids_flat = token_ids.reshape(-1)
    table_low = table.astype(jnp.bfloat16)
    ids_all = lax.all_gather(ids_flat, "dp", axis=0, tiled=True)
    picked = ids_all - row_base
    inside = (picked >= 0) & (picked < vocab_rows)
    chosen = jnp.take(table_low, jnp.clip(picked, 0, vocab_rows - 1), axis=0)
    embedded = lax.psum_scatter(
        jnp.where(inside[:, None], chosen.astype(jnp.float32), 0.0).astype(jnp.bfloat16),
        "dp",
        scatter_dimension=0,
        tiled=True,
    ).astype(jnp.float32)
    shards = (
        attn_in.astype(jnp.bfloat16),
        attn_out.astype(jnp.bfloat16),
        ffn_in.astype(jnp.bfloat16),
        ffn_out.astype(jnp.bfloat16),
        proj_head.astype(jnp.bfloat16),
    )
    gathered = (
        lax.all_gather(shards[0], ("dp", "fsdp"), axis=0, tiled=True),
        lax.all_gather(shards[1], ("dp", "fsdp"), axis=0, tiled=True),
        lax.all_gather(shards[2], ("dp", "fsdp"), axis=0, tiled=True),
        lax.all_gather(shards[3], ("dp", "fsdp"), axis=0, tiled=True),
        lax.all_gather(shards[4], ("dp", "fsdp"), axis=0, tiled=True),
    )
    final_rows, kept = layer_forward(embedded, mask_rows, gathered[:4], gain_rows, bias_full)
    normed_three, factor_three = normalize(final_rows, gain_rows[2])
    mask_weight = mask_rows.astype(jnp.float32)[:, :, None]
    counts = jnp.sum(mask_weight, 1)
    pooled = jnp.sum(normed_three.reshape(seq_count, L, D) * mask_weight, 1) / counts
    pooled_low = pooled.astype(jnp.bfloat16)
    projected = matmul(pooled_low, gathered[4])
    proj_factor = lax.rsqrt(jnp.sum(projected * projected, -1, keepdims=True) + EPS)
    unit_rows = projected * proj_factor
    unit_low = unit_rows.astype(jnp.bfloat16)
    mine_query = unit_low[:pairs_here]
    all_pass = lax.all_gather(unit_low[pairs_here:], ("dp", "fsdp"), axis=0, tiled=True)
    similar = matmul_nt(mine_query, all_pass)
    sim_scale = jnp.exp(log_scale)
    columns = jnp.arange(pairs_total, dtype=jnp.int32)
    own_index = device_flat * pairs_here + jnp.arange(pairs_here, dtype=jnp.int32)
    own_mask = (columns[None, :] == own_index[:, None]).astype(jnp.float32)
    negative = (columns[None, :] == hard_negative[:, None]).astype(jnp.float32)
    logits = sim_scale * similar - MARGIN * own_mask
    diagonal = jnp.sum(logits * own_mask, 1)
    hardest = jnp.sum(logits * negative, 1)
    row_max = jnp.max(logits, 1, keepdims=True)
    log_total = row_max + jnp.log(jnp.sum(jnp.exp(logits - row_max), 1, keepdims=True))
    loss_local = jnp.sum(log_total[:, 0] - diagonal + jax.nn.softplus(hardest - diagonal))
    hinge_gate = jax.nn.sigmoid(hardest - diagonal)
    grad_logits = (
        jnp.exp(logits - log_total) - own_mask + hinge_gate[:, None] * (negative - own_mask)
    )
    grad_log_scale = sim_scale * jnp.sum(grad_logits * similar)
    grad_similar = (sim_scale * grad_logits).astype(jnp.bfloat16)
    grad_query = matmul(grad_similar, all_pass).astype(jnp.bfloat16)
    grad_pass_terms = matmul_tn(grad_similar, mine_query)
    grad_pass = lax.psum_scatter(
        grad_pass_terms, ("dp", "fsdp"), scatter_dimension=0, tiled=True
    ).astype(jnp.bfloat16)
    grad_units = jnp.concatenate([grad_query, grad_pass], 0).astype(jnp.float32)
    grad_proj = (
        proj_factor * (grad_units - unit_rows * jnp.sum(grad_units * unit_rows, -1, keepdims=True))
    ).astype(jnp.bfloat16)
    gathered_back = (
        lax.all_gather(shards[0], ("dp", "fsdp"), axis=0, tiled=True),
        lax.all_gather(shards[1], ("dp", "fsdp"), axis=0, tiled=True),
        lax.all_gather(shards[2], ("dp", "fsdp"), axis=0, tiled=True),
        lax.all_gather(shards[3], ("dp", "fsdp"), axis=0, tiled=True),
        lax.all_gather(shards[4], ("dp", "fsdp"), axis=0, tiled=True),
    )
    grad_proj_head = matmul_tn(pooled_low, grad_proj)
    grad_pooled = matmul_nt(grad_proj, gathered_back[4])
    grad_normed = ((grad_pooled / counts)[:, None, :] * mask_weight).reshape(-1, D)
    grad_final, gain_three = normalize_back(grad_normed, final_rows, factor_three, gain_rows[2])
    grad_rows, matrix_grads, gain_one, gain_two, grad_bias = layer_backward(
        grad_final, kept, mask_rows, gathered_back[:4], gain_rows, bias_full
    )
    attn_in_grad, attn_out_grad, ffn_in_grad, ffn_out_grad = matrix_grads
    grad_bias_table = jnp.dot(grad_bias.reshape(HEADS, L * L), bucket_hot, precision=HIGH).T
    small_local = jnp.concatenate(
        [gain_one, gain_two, gain_three, grad_bias_table.reshape(-1), grad_log_scale[None]]
    )
    small_grad = lax.psum(small_local, ("dp", "fsdp"))
    weight_grads = (
        lax.psum_scatter(attn_in_grad, ("dp", "fsdp"), scatter_dimension=0, tiled=True),
        lax.psum_scatter(attn_out_grad, ("dp", "fsdp"), scatter_dimension=0, tiled=True),
        lax.psum_scatter(ffn_in_grad, ("dp", "fsdp"), scatter_dimension=0, tiled=True),
        lax.psum_scatter(ffn_out_grad, ("dp", "fsdp"), scatter_dimension=0, tiled=True),
        lax.psum_scatter(grad_proj_head, ("dp", "fsdp"), scatter_dimension=0, tiled=True),
    )
    rows_back = lax.all_gather(grad_rows.astype(jnp.bfloat16), "dp", axis=0, tiled=True)
    turn_count = dp_count // 4
    block_rows = rows_back.shape[0] // turn_count

    def add_block(running, piece_pair):
        block_grads, block_ids = piece_pair
        local_ids = block_ids - row_base
        inside = (local_ids >= 0) & (local_ids < vocab_rows)
        segment = jnp.where(inside, local_ids, vocab_rows)
        summed = jax.ops.segment_sum(
            block_grads.astype(jnp.float32), segment, num_segments=vocab_rows + 1
        )
        return (running + summed[:vocab_rows], None)

    table_full, _ = lax.scan(
        add_block,
        jnp.zeros((vocab_rows, D), jnp.float32),
        (rows_back.reshape(turn_count, block_rows, D), ids_all.reshape(turn_count, block_rows)),
    )
    table_grad = lax.psum(table_full.astype(jnp.bfloat16), "fsdp").astype(jnp.float32)
    owned = (table_grad,) + tuple(weight_grads)
    squares = jnp.sum(table_grad * table_grad) / fsdp_count
    for gradient in weight_grads:
        squares = squares + jnp.sum(gradient * gradient)
    total_squares, loss_sum = lax.psum((squares, loss_local), ("dp", "fsdp"))
    norm_value = jnp.sqrt(total_squares + jnp.sum(small_grad * small_grad))
    factor = jnp.minimum(1.0, CLIP / (norm_value + 1e-06))
    masters = (table, attn_in, attn_out, ffn_in, ffn_out, proj_head, small_params)
    firsts = (
        table_first,
        attn_in_first,
        attn_out_first,
        ffn_in_first,
        ffn_out_first,
        proj_head_first,
        small_first,
    )
    seconds = (
        table_second,
        attn_in_second,
        attn_out_second,
        ffn_in_second,
        ffn_out_second,
        proj_head_second,
        small_second,
    )
    gradients = owned + (small_grad,)
    results = [loss_sum, norm_value]
    for kind_index in range(7):
        results.extend(
            adam_update(
                masters[kind_index],
                firsts[kind_index],
                seconds[kind_index],
                gradients[kind_index],
                factor,
                RATES[kind_index],
                DECAYS[kind_index],
            )
        )
    return tuple(results)


def fits(mesh):
    return mesh.shape["fsdp"] == 4 and mesh.shape["dp"] == 8


def dense_rows(ids_flat, table, row_base):
    vocab_rows = table.shape[0]
    ids_all = lax.all_gather(ids_flat, "dp", axis=0, tiled=True)
    picked = ids_all - row_base
    inside = (picked >= 0) & (picked < vocab_rows)
    chosen = lax.optimization_barrier(
        jnp.take(table, jnp.clip(picked, 0, vocab_rows - 1), axis=0)
    )
    return lax.psum_scatter(
        jnp.where(inside[:, None], chosen, 0.0).astype(jnp.bfloat16),
        "dp",
        scatter_dimension=0,
        tiled=True,
    ).astype(jnp.float32)


def dense_table_grad(ids_flat, grad_low, vocab_rows, row_base):
    ids_all = lax.all_gather(ids_flat, "dp", axis=0, tiled=True)
    rows_back = lax.all_gather(grad_low, "dp", axis=0, tiled=True)
    turn_count = lax.axis_size("dp") // 4
    block_rows = rows_back.shape[0] // turn_count

    def add_block(running, piece_pair):
        block_grads, block_ids = piece_pair
        local_ids = block_ids - row_base
        inside = (local_ids >= 0) & (local_ids < vocab_rows)
        segment = jnp.where(inside, local_ids, vocab_rows)
        summed = jax.ops.segment_sum(
            block_grads.astype(jnp.float32), segment, num_segments=vocab_rows + 1
        )
        return (running + summed[:vocab_rows], None)

    table_full, _ = lax.scan(
        add_block,
        jnp.zeros((vocab_rows, D), jnp.float32),
        (rows_back.reshape(turn_count, block_rows, D), ids_all.reshape(turn_count, block_rows)),
    )
    return lax.psum(table_full.astype(jnp.bfloat16), "fsdp")


def once(flag, make, value):
    return lax.while_loop(lambda state: state[0], lambda state: (False, make(state[1])), (flag, value))[1]


def fast_body(
    token_ids,
    pad_mask,
    hard_negative,
    table,
    table_first,
    table_second,
    attn_in,
    attn_in_first,
    attn_in_second,
    attn_out,
    attn_out_first,
    attn_out_second,
    ffn_in,
    ffn_in_first,
    ffn_in_second,
    ffn_out,
    ffn_out_first,
    ffn_out_second,
    proj_head,
    proj_head_first,
    proj_head_second,
    small_params,
    small_first,
    small_second,
):
    dp_count = lax.axis_size("dp")
    fsdp_count = lax.axis_size("fsdp")
    total = dp_count * fsdp_count
    pairs_here = token_ids.shape[1]
    pairs_total = pairs_here * total
    seq_count = 2 * pairs_here
    vocab_rows = table.shape[0]
    row_base = lax.axis_index("dp") * vocab_rows
    gain_rows = small_params[: 3 * D].reshape(3, D)
    bias_table = small_params[3 * D : 3 * D + NB * HEADS].reshape(NB, HEADS)
    log_scale = small_params[3 * D + NB * HEADS]
    buckets = jnp.asarray(bucket_table(L, NB).T.reshape(-1), jnp.int32)
    bucket_hot = (buckets[:, None] == jnp.arange(NB, dtype=jnp.int32)[None, :]).astype(jnp.float32)
    bias_full = (
        jnp.dot(bucket_hot, bias_table, precision=HIGH).reshape(L, L, HEADS).transpose(2, 0, 1)
    )
    mask_rows = pad_mask.reshape(seq_count, L)
    ids_flat = token_ids.reshape(-1)
    tokens = ids_flat.shape[0]

    gathered_packed, gathered_down, heard, slot, embedded = run_head(
        ids_flat, hard_negative, attn_in, attn_out, ffn_in, proj_head, ffn_out, table, 1
    )
    packed = gathered_packed.reshape(-1, PACKED)
    down = gathered_down.reshape(-1, D)
    asked = heard[:, 0, :CAP]
    negatives = heard[:, 1, :pairs_here].reshape(-1).astype(jnp.int32)
    any_spilled = jnp.max(heard[:, 2, 0]) > 0.5
    embedded = once(any_spilled, lambda _: dense_rows(ids_flat, table, row_base), embedded)

    mask_col = mask_rows.astype(jnp.float32).reshape(tokens, 1)
    mixed, attended, totals, after, pre, final, pooled, projected = run_forward(
        embedded, mask_col, gain_rows, bias_full, packed, down
    )
    tall, wide = dp_count // (fsdp_count // 2), fsdp_count // 2
    owner = negatives // pairs_here
    owner = (owner % 2 * tall + owner // (2 * wide * wide)) * wide * wide + owner // 2 % (wide * wide) % wide + (
        owner // (2 * wide) % wide * wide
    )
    target = owner * seq_count + pairs_here + negatives % pairs_here
    target = jnp.concatenate(
        [target.reshape(total, pairs_here), jnp.full((total, pairs_here), -1, jnp.int32)], 1
    )
    target = target.reshape(tall * wide * wide, 2, seq_count).transpose(1, 0, 2).reshape(-1, 1)
    grad_proj, loss_parts = run_loss(projected, target, log_scale.reshape(1, 1), 3)
    loss_sum, grad_log_scale = loss_parts[0, 0], loss_parts[1, 0]
    grad_after, grad_gains, grad_up, grad_down = run_ffn_back(
        final, after, mask_col, gain_rows, pooled, grad_proj, pre, packed, down
    )
    grad_low, grad_gain, grad_bias, grad_attn, up_shard, down_shard, squares = run_attn_back(
        embedded, mask_col, mixed, attended, totals, grad_after, gain_rows, bias_full, packed, grad_up, grad_down, 4
    )
    grad_gains = jnp.concatenate([grad_gain, grad_gains[1:]], 0)
    grad_bias_table = jnp.dot(grad_bias.reshape(HEADS, L * L), bucket_hot, precision=HIGH).T
    small_local = jnp.concatenate([grad_gains.reshape(-1), grad_bias_table.reshape(-1)])
    width = -(-small_local.shape[0] // 1024) * 8
    small_local = jnp.pad(small_local, (0, width * 128 - small_local.shape[0]))
    slots = jnp.arange(dp_count * CAP, dtype=jnp.int32).astype(jnp.float32)
    slot_hot = (slot == slots[None, :]).astype(jnp.bfloat16)
    slot_sums = matmul_tn(slot_hot, grad_low).astype(jnp.bfloat16).reshape(dp_count, CAP, D)
    (attn_shard,), table_grad, summed, squares = finish(
        [grad_attn.reshape(total, -1, WIDE + D)],
        slot_sums,
        asked.reshape(dp_count, fsdp_count, CAP).transpose(1, 0, 2).reshape(fsdp_count, -1),
        small_local.reshape(width, 128),
        squares,
        vocab_rows,
        5,
    )
    table_grad, squares = once(
        any_spilled,
        lambda state: with_squares(dense_table_grad(ids_flat, grad_low, vocab_rows, row_base), state[1]),
        (table_grad, squares),
    )
    norm, *updated = run_update(
        fsdp_count,
        squares,
        summed,
        grad_log_scale.reshape(1, 1),
        (table, table_first, table_second),
        table_grad,
        (
            *(attn_in, attn_in_first, attn_in_second),
            *(attn_out, attn_out_first, attn_out_second),
            *(ffn_in, ffn_in_first, ffn_in_second),
            *(ffn_out, ffn_out_first, ffn_out_second),
            *(proj_head, proj_head_first, proj_head_second),
        ),
        (attn_shard, up_shard, down_shard),
    )
    norm_value = norm[0, 0]
    factor = jnp.minimum(1.0, CLIP / (norm_value + 1e-06))
    small_size = small_params.shape[0]
    small_grad = jnp.concatenate([summed.reshape(-1)[: small_size - 1], grad_log_scale[None]])
    small_new = adam_update(
        small_params, small_first, small_second, small_grad, factor, RATES[6], DECAYS[6]
    )
    return (loss_sum, norm_value, *updated, *small_new)


def with_squares(table_grad, squares):
    wide = table_grad.astype(jnp.float32)
    total = lax.psum(jnp.sum(wide * wide), ("dp", "fsdp"))
    return (table_grad, squares.at[8:].set(0.0).at[8, 0].set(total))


def solution(mesh):
    program = fast_body if fits(mesh) else plain_body
    return jax.shard_map(
        program,
        mesh=mesh,
        in_specs=(
            P(None, ("dp", "fsdp"), None),
            P(None, ("dp", "fsdp"), None),
            P(("dp", "fsdp")),
            P("dp", None),
            P("dp", None),
            P("dp", None),
            P(("dp", "fsdp"), None),
            P(("dp", "fsdp"), None),
            P(("dp", "fsdp"), None),
            P(("dp", "fsdp"), None),
            P(("dp", "fsdp"), None),
            P(("dp", "fsdp"), None),
            P(("dp", "fsdp"), None),
            P(("dp", "fsdp"), None),
            P(("dp", "fsdp"), None),
            P(("dp", "fsdp"), None),
            P(("dp", "fsdp"), None),
            P(("dp", "fsdp"), None),
            P(("dp", "fsdp"), None),
            P(("dp", "fsdp"), None),
            P(("dp", "fsdp"), None),
            P(),
            P(),
            P(),
        ),
        out_specs=(
            P(),
            P(),
            P("dp", None),
            P("dp", None),
            P("dp", None),
            P(("dp", "fsdp"), None),
            P(("dp", "fsdp"), None),
            P(("dp", "fsdp"), None),
            P(("dp", "fsdp"), None),
            P(("dp", "fsdp"), None),
            P(("dp", "fsdp"), None),
            P(("dp", "fsdp"), None),
            P(("dp", "fsdp"), None),
            P(("dp", "fsdp"), None),
            P(("dp", "fsdp"), None),
            P(("dp", "fsdp"), None),
            P(("dp", "fsdp"), None),
            P(("dp", "fsdp"), None),
            P(("dp", "fsdp"), None),
            P(("dp", "fsdp"), None),
            P(),
            P(),
            P(),
        ),
        check_vma=False,
    )
```

```python
import functools

import jax
import jax.numpy as jnp
import numpy as np
from jax import lax
from jax.experimental import pallas as pl
from jax.experimental.pallas import tpu as pltpu
from jax.sharding import PartitionSpec as P

D = 768
HEADS = 12
HD = 64
NB = 32
L = 128
STEP = 10


EPS = 1e-06
SCALE = 0.125
MARGIN = 0.2
CLIP = 0.1
BETA_ONE = 0.9
BETA_TWO = 0.99
ADAM_EPS = 1e-08
RATES = (3.0, 0.1, 0.2, 0.1, 0.05, 0.1, 1.0)
DECAYS = (0.001, 0.001, 0.001, 0.001, 0.001, 0.001, 0.0)
HIGH = lax.Precision.HIGHEST
MESH = pl.DeviceIdType.MESH
CAP = 112


def bucket_table(length, count):
    position = np.arange(length)
    relative = position[None, :] - position[:, None]
    half = count // 2
    base_part = (relative > 0).astype(np.int64) * half
    distance = np.abs(relative)
    exact = half // 2
    safe_dist = np.maximum(distance, 1)
    large = exact + (np.log(safe_dist / exact) / np.log(length / exact) * (half - exact)).astype(
        np.int64
    )
    large = np.minimum(large, half - 1)
    return base_part + np.where(distance < exact, distance, large)


def matmul(left_side, right_side):
    return jnp.dot(left_side, right_side, preferred_element_type=jnp.float32)


def matmul_tn(left_side, right_side):
    return lax.dot_general(
        left_side, right_side, (((0,), (0,)), ((), ())), preferred_element_type=jnp.float32
    )


def matmul_nt(left_side, right_side):
    return lax.dot_general(
        left_side, right_side, (((1,), (1,)), ((), ())), preferred_element_type=jnp.float32
    )


def normalize(inputs, gain_row):
    factor = lax.rsqrt(jnp.mean(inputs * inputs, -1, keepdims=True) + EPS)
    return (inputs * factor * gain_row, factor)


def normalize_back(grad_out, inputs, factor, gain_row):
    scaled = grad_out * gain_row
    grad_gain = jnp.sum(grad_out * inputs * factor, 0)
    grad_in = factor * (
        scaled - inputs * factor * factor * jnp.mean(scaled * inputs, -1, keepdims=True)
    )
    return (grad_in, grad_gain)


def attention_scores(mixed_proj, mask_rows, bias_full):
    keep_add = jnp.where(mask_rows > 0, 0.0, -1000000000.0).astype(jnp.float32)
    scores = jnp.einsum(
        "bqhd,bkhd->bhqk",
        mixed_proj[:, :, 0],
        mixed_proj[:, :, 1],
        preferred_element_type=jnp.float32,
    )
    return scores * SCALE + bias_full[None] + keep_add[:, None, None, :]


def layer_forward(token_rows, mask_rows, weights, gain_rows, bias_full):
    attn_in, attn_out, ffn_in, ffn_out = weights
    seq_count, length = mask_rows.shape
    width = token_rows.shape[1]
    normed_one, factor_one = normalize(token_rows, gain_rows[0])
    act_one = normed_one.astype(jnp.bfloat16)
    mixed_proj = (
        matmul(act_one, attn_in).astype(jnp.bfloat16).reshape(seq_count, length, 3, HEADS, HD)
    )
    scores = attention_scores(mixed_proj, mask_rows, bias_full)
    row_max = jnp.max(scores, -1, keepdims=True)
    log_total = row_max + jnp.log(jnp.sum(jnp.exp(scores - row_max), -1, keepdims=True))
    prob_low = jnp.exp(scores - log_total).astype(jnp.bfloat16)
    attended = jnp.einsum(
        "bhqk,bkhd->bqhd", prob_low, mixed_proj[:, :, 2], preferred_element_type=jnp.float32
    )
    attended = attended.astype(jnp.bfloat16).reshape(-1, width)
    after_attn = token_rows + matmul(attended, attn_out)
    normed_two, factor_two = normalize(after_attn, gain_rows[1])
    act_two = normed_two.astype(jnp.bfloat16)
    pre_act = matmul(act_two, ffn_in)
    hidden = jax.nn.gelu(pre_act).astype(jnp.bfloat16)
    final_rows = after_attn + matmul(hidden, ffn_out)
    kept = (
        token_rows,
        factor_one,
        act_one,
        mixed_proj,
        log_total,
        attended,
        after_attn,
        factor_two,
        act_two,
        pre_act,
        hidden,
    )
    return (final_rows, kept)


def layer_backward(grad_final, kept, mask_rows, weights, gain_rows, bias_full):
    (
        token_rows,
        factor_one,
        act_one,
        mixed_proj,
        log_total,
        attended,
        after_attn,
        factor_two,
        act_two,
        pre_act,
        hidden,
    ) = kept
    attn_in, attn_out, ffn_in, ffn_out = weights
    seq_count, length = mask_rows.shape
    branch = grad_final.astype(jnp.bfloat16)
    grad_ffn_out = matmul_tn(hidden, branch)
    grad_hidden = matmul_nt(branch, ffn_out)
    _, gelu_pull = jax.vjp(jax.nn.gelu, pre_act)
    grad_pre = gelu_pull(grad_hidden)[0].astype(jnp.bfloat16)
    grad_ffn_in = matmul_tn(act_two, grad_pre)
    grad_act_two = matmul_nt(grad_pre, ffn_in)
    grad_mid, gain_two = normalize_back(grad_act_two, after_attn, factor_two, gain_rows[1])
    grad_after = grad_final + grad_mid
    branch = grad_after.astype(jnp.bfloat16)
    grad_attn_out = matmul_tn(attended, branch)
    grad_attended = (
        matmul_nt(branch, attn_out).astype(jnp.bfloat16).reshape(seq_count, length, HEADS, HD)
    )
    scores = attention_scores(mixed_proj, mask_rows, bias_full)
    prob_full = jnp.exp(scores - log_total)
    prob_low = prob_full.astype(jnp.bfloat16)
    queries = mixed_proj[:, :, 0]
    key_rows = mixed_proj[:, :, 1]
    grad_probs = jnp.einsum(
        "bqhd,bkhd->bhqk", grad_attended, mixed_proj[:, :, 2], preferred_element_type=jnp.float32
    )
    grad_values = jnp.einsum(
        "bhqk,bqhd->bkhd", prob_low, grad_attended, preferred_element_type=jnp.float32
    )
    grad_scores = prob_full * (grad_probs - jnp.sum(prob_full * grad_probs, -1, keepdims=True))
    grad_scores = grad_scores.astype(jnp.bfloat16)
    grad_bias = jnp.sum(grad_scores, 0, dtype=jnp.float32)
    grad_queries = (
        jnp.einsum("bhqk,bkhd->bqhd", grad_scores, key_rows, preferred_element_type=jnp.float32)
        * SCALE
    )
    grad_keys = (
        jnp.einsum("bhqk,bqhd->bkhd", grad_scores, queries, preferred_element_type=jnp.float32)
        * SCALE
    )
    grad_mixed = (
        jnp.stack([grad_queries, grad_keys, grad_values], 2)
        .astype(jnp.bfloat16)
        .reshape(seq_count * length, -1)
    )
    grad_attn_in = matmul_tn(act_one, grad_mixed)
    grad_act_one = matmul_nt(grad_mixed, attn_in)
    grad_low, gain_one = normalize_back(grad_act_one, token_rows, factor_one, gain_rows[0])
    grad_rows = grad_after + grad_low
    return (
        grad_rows,
        (grad_attn_in, grad_attn_out, grad_ffn_in, grad_ffn_out),
        gain_one,
        gain_two,
        grad_bias,
    )


def adam_update(param, first_moment, second_moment, gradient, factor, rate, decay):
    clipped = gradient * factor
    first_new = BETA_ONE * first_moment + (1.0 - BETA_ONE) * clipped
    second_new = BETA_TWO * second_moment + (1.0 - BETA_TWO) * clipped * clipped
    direction = (
        first_new
        / (1.0 - BETA_ONE**STEP)
        / (jnp.sqrt(second_new / (1.0 - BETA_TWO**STEP)) + ADAM_EPS)
    )
    return (first_new, second_new, param - rate * (direction + decay * param))


class Grid:
    def __init__(self):
        self.dp, self.fs = lax.axis_size("dp"), lax.axis_size("fsdp")
        self.total = self.dp * self.fs
        self.wide = self.fs // 2
        self.tall = self.dp // self.wide

    def here(self):
        d, f = lax.axis_index("dp"), lax.axis_index("fsdp")
        return d // self.wide, lax.rem(d, self.wide), f // 2, lax.rem(f, 2)

    def device(self, z, x, y, core):
        return (z * self.wide + x, y * 2 + core)

    def flat(self, z, x, y, core):
        return (z * self.wide + x) * self.fs + y * 2 + core

    def peer(self, index):
        return (index // self.fs, lax.rem(index, self.fs))


def greet(device, when=None):
    barrier = pltpu.get_barrier_semaphore()

    def signal():
        pl.semaphore_signal(barrier, inc=1, device_id=device, device_id_type=MESH)

    if when is None:
        signal()
    else:
        pl.when(when)(signal)


def meet(count):
    pl.semaphore_wait(pltpu.get_barrier_semaphore(), count)


ROW_BLOCK = 512
WIDE = 3 * D
PACKED = WIDE + D + 4 * D + D
TILE_SEQS = 4


def head_kernel(
    grid,
    col_ref,
    row_ref,
    negative_ref,
    in_ref,
    out_ref,
    up_ref,
    proj_ref,
    down_ref,
    table_hbm,
    packed_out,
    down_out,
    heard,
    slot_ref,
    x0_ref,
    packed_mine,
    down_mine,
    table,
    total,
    answers,
    found,
    messages,
    send_sem,
    recv_sem,
    own_sem,
    row_send,
    row_recv,
    note_send,
    note_recv,
    note_on,
    table_sem,
):
    srcs, outs = (packed_mine, down_mine), (packed_out, down_out)
    count = 2
    z, x, y, core = grid.here()
    tall = grid.tall
    d, f = lax.axis_index("dp"), lax.axis_index("fsdp")
    u_places = ((lax.rem(x + 1 - core, 2), lax.rem(y + core, 2)), (1 - x, y))
    v_places = ((lax.rem(x + core, 2), lax.rem(y + 1 - core, 2)), (x, 1 - y))
    up, down = grid.device(z + 1, x, y, core), grid.device(z - 1, x, y, core)
    u_devices = [grid.device(z, *place, core) for place in u_places]
    v_devices = [grid.device(z, *place, core) for place in v_places]
    sibling = grid.device(z, x, y, 1 - core)
    has_up, has_down = z < tall - 1, z > 0
    me = grid.flat(z, x, y, core)
    f_side, f_y, f_far = y * 2 + 1 - core, (1 - y) * 2 + core, (1 - y) * 2 + 1 - core

    @pl.loop(1, grid.dp)
    def _(step):
        greet((lax.rem(d + step, grid.dp), f))

    greet((d, f_y))
    greet(sibling)
    vocab_rows = table_hbm.shape[0]
    fetch = pltpu.make_async_copy(table_hbm, table.at[pl.ds(0, vocab_rows), :], table_sem)
    fetch.start()
    at = 0
    for ref in (in_ref, out_ref, up_ref, proj_ref):
        packed_mine[:, at : at + ref.shape[1]] = ref[...].astype(jnp.bfloat16)
        at += ref.shape[1]
    down_mine[...] = down_ref[...].astype(jnp.bfloat16)
    local = [pltpu.make_async_copy(srcs[m], outs[m].at[me], own_sem.at[m]) for m in range(count)]
    for item in local:
        item.start()
    meet(grid.dp + 1)

    def copy(m, shard, device, way, own):
        return pltpu.make_async_remote_copy(
            src_ref=srcs[m] if own else outs[m].at[shard],
            dst_ref=outs[m].at[shard],
            send_sem=send_sem.at[way, m, shard],
            recv_sem=recv_sem.at[m, shard],
            device_id=device,
            device_id_type=MESH,
        )

    def send(shard, device, way, own=False):
        for m in range(count):
            copy(m, shard, device[m] if isinstance(device, list) else device, way, own).start()

    def arrived(shard):
        for m in range(count):
            copy(m, shard, sibling, 4, False).wait_recv()

    def sent(shard, device, way):
        for m in range(count):
            copy(m, shard, device[m] if isinstance(device, list) else device, way, False).wait_send()

    @pl.when(has_up)
    def _():
        send(me, up, 0, True)

    @pl.when(has_down)
    def _():
        send(me, down, 1, True)

    send(me, u_devices, 2, True)
    send(me, v_devices, 3, True)
    send(me, sibling, 4, True)

    tokens = col_ref.shape[0]
    chunk = 128
    ids_row = row_ref[...]
    place_row = lax.broadcasted_iota(jnp.int32, (chunk, tokens), 1)
    place_col = lax.broadcasted_iota(jnp.int32, (chunk, tokens), 0)

    def see(step, repeated):
        start = pl.multiple_of(step * chunk, chunk)
        again = (col_ref[pl.ds(start, chunk), :] == ids_row) & (place_col + start < place_row)
        return jnp.maximum(repeated, jnp.max(jnp.where(again, 1.0, 0.0), 0, keepdims=True))

    repeated = lax.fori_loop(0, tokens // chunk, see, jnp.zeros((1, tokens), jnp.float32))
    firsts = jnp.where(repeated > 0.5, -1.0, ids_row)
    lane = lax.broadcasted_iota(jnp.int32, (chunk, 128), 1).astype(jnp.float32)

    def rank_some(step, carry):
        listed, most = carry
        start = pl.multiple_of(step * chunk, chunk)
        ids = col_ref[pl.ds(start, chunk), :]
        owner = jnp.zeros_like(ids)
        for other in range(1, grid.dp):
            owner = owner + jnp.where(ids >= float(other * vocab_rows), 1.0, 0.0)
        first_id = owner * float(vocab_rows)
        rank = jnp.sum(jnp.where((firsts >= first_id) & (firsts < ids), 1.0, 0.0), 1, keepdims=True)
        slot = jnp.where(rank < float(CAP), owner * float(CAP) + rank, -1.0)
        slot_ref[pl.ds(start, chunk), :] = slot
        rows = []
        for other in range(grid.dp):
            hit = (slot == lane + float(other * CAP)) & (lane < float(CAP))
            rows.append(jnp.max(jnp.where(hit, ids - first_id + 1.0, 0.0), 0, keepdims=True))
        return (jnp.maximum(listed, jnp.concatenate(rows, 0)), jnp.maximum(most, jnp.max(rank, 0, keepdims=True)))

    listed, most = lax.fori_loop(
        0,
        tokens // chunk,
        rank_some,
        (jnp.zeros((grid.dp, 128), jnp.float32), jnp.zeros((1, 1), jnp.float32)),
    )
    spilled = jnp.broadcast_to(jnp.where(most >= float(CAP), 1.0, 0.0), (1, 128))
    rest = jnp.concatenate([negative_ref[...], spilled, jnp.zeros((5, 128), jnp.float32)], 0)
    for other in range(grid.dp):
        messages[other] = jnp.concatenate([listed[other : other + 1] - 1.0, rest], 0)

    def note(peer, slot):
        return pltpu.make_async_remote_copy(
            src_ref=messages.at[peer],
            dst_ref=heard.at[slot],
            send_sem=note_send.at[peer],
            recv_sem=note_recv.at[slot],
            device_id=(peer, f),
            device_id_type=MESH,
        )

    def note_onward(slot, to_side):
        return pltpu.make_async_remote_copy(
            src_ref=heard.at[slot],
            dst_ref=heard.at[slot],
            send_sem=note_on.at[1 if to_side else 0, slot],
            recv_sem=note_recv.at[slot],
            device_id=(d, f_side if to_side else f_y),
            device_id_type=MESH,
        )

    @pl.loop(1, grid.dp)
    def _(step):
        note(lax.rem(d + step, grid.dp), me).start()

    heard[me] = messages[d]

    def row_copy(peer, slot):
        return pltpu.make_async_remote_copy(
            src_ref=answers.at[peer],
            dst_ref=found.at[slot],
            send_sem=row_send.at[peer],
            recv_sem=row_recv.at[slot],
            device_id=(peer, f),
            device_id_type=MESH,
        )

    def pass_z(k):
        low, high = z - k, z + k

        @pl.when(low >= 0)
        def _():
            shard = grid.flat(low, x, y, core)
            arrived(shard)

            @pl.when(has_up)
            def _():
                send(shard, up, 0)

            send(shard, u_devices, 2)
            send(shard, v_devices, 3)
            send(shard, sibling, 4)

        @pl.when(high < tall)
        def _():
            shard = grid.flat(high, x, y, core)
            arrived(shard)

            @pl.when(has_down)
            def _():
                send(shard, down, 1)

            send(shard, u_devices, 2)
            send(shard, v_devices, 3)
            send(shard, sibling, 4)

    def both(k, action):
        pl.when(z - k >= 0)(lambda: action(z - k))
        if k:
            pl.when(z + k < tall)(lambda: action(z + k))

    def pass_u(level):
        for m in range(count):
            shard = grid.flat(level, *u_places[m], core)
            copy(m, shard, sibling, 4, False).wait_recv()
            copy(m, shard, v_devices[m], 3, False).start()
            copy(m, shard, sibling, 4, False).start()

    def pass_v(level):
        for m in range(count):
            shard = grid.flat(level, *v_places[m], core)
            copy(m, shard, sibling, 4, False).wait_recv()
            copy(m, shard, sibling, 4, False).start()

    def pass_far(level):
        shard = grid.flat(level, 1 - x, 1 - y, core)
        arrived(shard)
        send(shard, sibling, 4)

    both(0, pass_u)

    @pl.loop(1, grid.dp)
    def _(step):
        note(d, lax.rem(d + step, grid.dp) * grid.fs + f).wait_recv()

    @pl.loop(0, grid.dp)
    def _(peer):
        note_onward(peer * grid.fs + f, False).start()
        note_onward(peer * grid.fs + f, True).start()

    pass_z(1)
    fetch.wait()
    padding = table.shape[0] - vocab_rows
    if padding:
        table[vocab_rows:, :] = jnp.zeros((padding, D), jnp.float32)
    asked = jnp.concatenate([heard[peer * grid.fs + f, 0:1, :] for peer in range(grid.dp)], 0)
    asked = jnp.transpose(asked)
    block = ROW_BLOCK
    total[...] = jnp.zeros_like(total)
    lanes = lax.broadcasted_iota(jnp.int32, (CAP, block), 1).astype(jnp.float32)

    def pick(step):
        start = pl.multiple_of(step * block, block)
        some = table[pl.ds(start, block), :].astype(jnp.bfloat16)
        wanted = lanes + (step * block).astype(jnp.float32)
        hot = jnp.concatenate(
            [
                jnp.where(asked[:CAP, peer : peer + 1] == wanted, 1.0, 0.0)
                for peer in range(grid.dp)
            ],
            0,
        ).astype(jnp.bfloat16)
        total[...] += matmul(hot, some)

    steps = table.shape[0] // block
    pl.loop(0, steps)(pick)
    answers[...] = total[...].reshape(answers.shape).astype(jnp.bfloat16)
    found[d] = answers[d]

    @pl.loop(1, grid.dp)
    def _(step):
        row_copy(lax.rem(d + step, grid.dp), d).start()

    both(1, pass_u)
    pass_z(2)
    both(0, pass_v)
    both(2, pass_u)
    pass_z(3)
    both(1, pass_v)
    both(3, pass_u)
    both(0, pass_far)
    both(2, pass_v)
    both(1, pass_far)
    both(3, pass_v)
    both(2, pass_far)
    both(3, pass_far)

    @pl.loop(1, grid.dp)
    def _(step):
        row_copy(d, lax.rem(d + step, grid.dp)).wait_recv()

    slots = grid.dp * CAP
    some = tokens // 4
    wide_lane = lax.broadcasted_iota(jnp.int32, (some, slots), 1).astype(jnp.float32)
    rows = found[...].reshape(slots, D)

    @pl.loop(0, 4)
    def _(step):
        start = pl.multiple_of(step * some, some)
        hot = jnp.where(slot_ref[pl.ds(start, some), :] == wide_lane, 1.0, 0.0).astype(jnp.bfloat16)
        x0_ref[pl.ds(start, some), :] = matmul(hot, rows)

    @pl.loop(0, grid.dp)
    def _(peer):
        note(d, peer * grid.fs + f_y).wait_recv()
        note_onward(peer * grid.fs + f_y, True).start()

    @pl.loop(0, grid.dp)
    def _(peer):
        note(d, peer * grid.fs + f_side).wait_recv()
        note(d, peer * grid.fs + f_far).wait_recv()
        note_onward(peer * grid.fs + f, False).wait_send()
        note_onward(peer * grid.fs + f, True).wait_send()
        note_onward(peer * grid.fs + f_y, True).wait_send()

    @pl.loop(1, grid.dp)
    def _(step):
        peer = lax.rem(d + step, grid.dp)
        row_copy(peer, d).wait_send()
        note(peer, me).wait_send()

    @pl.loop(0, tall)
    def _(level):
        for xx in range(2):
            for yy in range(2):
                arrived(grid.flat(level, xx, yy, 1 - core))
                sent(grid.flat(level, xx, yy, core), sibling, 4)
        shard = grid.flat(level, x, y, core)

        @pl.when((level <= z) & has_up)
        def _():
            sent(shard, up, 0)

        @pl.when((level >= z) & has_down)
        def _():
            sent(shard, down, 1)

        sent(shard, u_devices, 2)
        sent(shard, v_devices, 3)
        for m in range(count):
            other = grid.flat(level, *u_places[m], core)
            copy(m, other, v_devices[m], 3, False).wait_send()

    for item in local:
        item.wait()


def run_head(ids, negatives, attn_in, attn_out, ffn_in, proj_head, ffn_out, table, number):
    grid = Grid()
    tokens = ids.shape[0]
    wide = ids.astype(jnp.float32)
    row = jnp.zeros((1, 128), jnp.float32).at[0, : negatives.shape[0]].set(negatives.astype(jnp.float32))
    shapes = ((attn_in.shape[0], PACKED), ffn_out.shape)
    blocks = -(-table.shape[0] // ROW_BLOCK)
    anywhere, inside = pl.BlockSpec(memory_space=pl.ANY), pl.BlockSpec(memory_space=pltpu.VMEM)
    dma = pltpu.SemaphoreType.DMA
    line, everyone = dma((grid.dp,)), dma((grid.total,))
    return pl.pallas_call(
        functools.partial(head_kernel, grid),
        out_shape=[jax.ShapeDtypeStruct((grid.total,) + shape, jnp.bfloat16) for shape in shapes]
        + [
            jax.ShapeDtypeStruct((grid.total, 8, 128), jnp.float32),
            jax.ShapeDtypeStruct((tokens, 1), jnp.float32),
            jax.ShapeDtypeStruct((tokens, D), jnp.float32),
        ],
        in_specs=[inside] * 8 + [anywhere],
        out_specs=[anywhere] * 2 + [inside] * 3,
        scratch_shapes=[pltpu.VMEM(shape, jnp.bfloat16) for shape in shapes]
        + [
            pltpu.VMEM((blocks * ROW_BLOCK, D), jnp.float32),
            pltpu.VMEM((grid.dp * CAP, D), jnp.float32),
            pltpu.VMEM((grid.dp, CAP, D), jnp.bfloat16),
            pltpu.VMEM((grid.dp, CAP, D), jnp.bfloat16),
            pltpu.VMEM((grid.dp, 8, 128), jnp.float32),
            dma((5, 2, grid.total)),
            dma((2, grid.total)),
            dma((2,)),
            line,
            line,
            line,
            everyone,
            dma((2, grid.total)),
            dma,
        ],
        compiler_params=pltpu.CompilerParams(
            collective_id=number, has_side_effects=True, vmem_limit_bytes=48 * 1024 * 1024
        ),
    )(wide.reshape(tokens, 1), wide.reshape(1, tokens), row, attn_in, attn_out, ffn_in, proj_head, ffn_out, table)


def lane_is(shape, low, high):
    lanes = lax.broadcasted_iota(jnp.int32, shape, len(shape) - 1)
    return (lanes >= low) & (lanes < high)


def gelu_parts(t):
    inner = np.float32(np.sqrt(2 / np.pi)) * (t + 0.044715 * (t * t * t))
    tan = jnp.tanh(inner)
    return 0.5 * (1.0 + tan), tan


def forward_kernel(
    x0_ref,
    mask_col_ref,
    gains_ref,
    bias_ref,
    packed_hbm,
    down_hbm,
    mixed_ref,
    attended_ref,
    total_ref,
    after_ref,
    pre_ref,
    final_ref,
    pooled_ref,
    projected_ref,
    packed,
    down,
    load_sem,
):
    step = pl.program_id(0)
    tile_seqs = x0_ref.shape[0] // L
    edges = (0, WIDE, WIDE + D, WIDE + 5 * D, PACKED)

    def load(k):
        if k == 4:
            return pltpu.make_async_copy(down_hbm, down, load_sem.at[k])
        part = pl.ds(edges[k], edges[k + 1] - edges[k])
        return pltpu.make_async_copy(packed_hbm.at[:, part], packed.at[:, part], load_sem.at[k])

    def loaded(k):
        @pl.when(step == 0)
        def _():
            load(k).wait()

    @pl.when(step == 0)
    def _():
        for k in (0, 1, 2, 4, 3):
            load(k).start()

    x0 = x0_ref[...]
    act_one = normalize(x0, gains_ref[0:1, :])[0].astype(jnp.bfloat16)
    loaded(0)
    for at in range(0, WIDE, D):
        mixed_ref[:, at : at + D] = matmul(act_one, packed[:, at : at + D]).astype(jnp.bfloat16)

    zero = jnp.zeros((), jnp.bfloat16)
    for s in range(tile_seqs):
        rows = slice(s * L, (s + 1) * L)
        keep = jnp.where(mask_col_ref[rows, :] > 0, 0.0, -1000000000.0)
        for pair in range(HEADS // 2):
            at = pair * 128
            query = mixed_ref[rows, at : at + 128]
            key = mixed_ref[rows, D + at : D + at + 128]
            value = mixed_ref[rows, 2 * D + at : 2 * D + at + 128]
            mine = lane_is((L, 128), 0, HD)
            keys = jnp.concatenate([jnp.where(mine, key, zero), jnp.where(mine, zero, key)], 0)
            scores = (matmul_nt(keys, query) * SCALE).reshape(2, L, L)
            scores = scores + bias_ref[2 * pair : 2 * pair + 2] + keep[None]
            row_max = jnp.max(scores, 1, keepdims=True)
            powers = jnp.exp(scores - row_max)
            row_sum = jnp.sum(powers, 1, keepdims=True)
            prob = (powers * (1.0 / row_sum)).astype(jnp.bfloat16)
            total_ref[s, 2 * pair : 2 * pair + 2, :] = (row_max + jnp.log(row_sum))[:, 0, :]
            flipped = jnp.transpose(value)
            both = jnp.concatenate([matmul(flipped[:HD], prob[0]), matmul(flipped[HD:], prob[1])], 0)
            both = jnp.transpose(both)
            attended_ref[rows, at : at + 128] = both.astype(jnp.bfloat16)

    loaded(1)
    after = x0 + matmul(attended_ref[...], packed[:, WIDE : WIDE + D])
    after_ref[...] = after
    act_two = normalize(after, gains_ref[1:2, :])[0].astype(jnp.bfloat16)
    loaded(2)
    loaded(4)
    final = after
    for j in range(4):
        at = WIDE + D + j * D
        pre = matmul(act_two, packed[:, at : at + D])
        pre_ref[:, j * D : (j + 1) * D] = pre
        hidden = (pre * gelu_parts(pre)[0]).astype(jnp.bfloat16)
        final = final + matmul(hidden, down[j * D : (j + 1) * D, :])
    final_ref[...] = final
    normed = normalize(final, gains_ref[2:3, :])[0]
    weight = mask_col_ref[...]
    for s in range(tile_seqs):
        rows = slice(s * L, (s + 1) * L)
        count = jnp.sum(weight[rows], 0, keepdims=True)
        row = jnp.sum(normed[rows] * weight[rows], 0, keepdims=True) / count
        pooled_ref[pl.ds(step * tile_seqs + s, 1), :] = row

    @pl.when(step == pl.num_programs(0) - 1)
    def _():
        load(3).wait()
        projected_ref[...] = matmul(pooled_ref[...].astype(jnp.bfloat16), packed[:, PACKED - D :])


def run_forward(x0, mask_col, gains, bias_full, packed, down):
    tokens = x0.shape[0]
    seqs = tokens // L
    tile = TILE_SEQS * L
    steps = tokens // tile

    def rows(width):
        return pl.BlockSpec((tile, width), lambda i: (i, 0))

    def whole(*shape):
        return pl.BlockSpec(shape, lambda i: (0,) * len(shape), pipeline_mode=pl.Buffered(1))

    def kept(width, dtype):
        return jax.ShapeDtypeStruct((tokens, width), dtype)

    anywhere = pl.BlockSpec(memory_space=pl.ANY)
    return pl.pallas_call(
        forward_kernel,
        grid=(steps,),
        out_shape=[
            kept(WIDE, jnp.bfloat16),
            kept(D, jnp.bfloat16),
            jax.ShapeDtypeStruct((seqs, HEADS, L), jnp.float32),
            kept(D, jnp.float32),
            kept(4 * D, jnp.float32),
            kept(D, jnp.float32),
            jax.ShapeDtypeStruct((seqs, D), jnp.float32),
            jax.ShapeDtypeStruct((seqs, D), jnp.float32),
        ],
        in_specs=[
            rows(D),
            rows(1),
            whole(3, D),
            whole(HEADS, L, L),
            anywhere,
            anywhere,
        ],
        out_specs=[rows(WIDE), rows(D), pl.BlockSpec((TILE_SEQS, HEADS, L), lambda i: (i, 0, 0)), rows(D), rows(4 * D), rows(D), whole(seqs, D), whole(seqs, D)],
        scratch_shapes=[
            pltpu.VMEM((D, PACKED), jnp.bfloat16),
            pltpu.VMEM((4 * D, D), jnp.bfloat16),
            pltpu.SemaphoreType.DMA((5,)),
        ],
        compiler_params=pltpu.CompilerParams(vmem_limit_bytes=60 * 1024 * 1024),
    )(x0, mask_col, gains, bias_full, packed, down)


def loss_kernel(
    grid, pairs_here, projected_ref, target_ref, scale_ref, grad_ref, loss_ref, others, grads, send_sem, recv_sem
):
    z, x, y, core = grid.here()
    tall = grid.tall
    each = 2 * pairs_here
    half = D // 2
    x_device, y_device = grid.device(z, 1 - x, y, core), grid.device(z, x, 1 - y, core)
    sibling = grid.device(z, x, y, 1 - core)

    def other_levels(action):
        @pl.loop(1, tall)
        def _(step):
            action(lax.rem(z + step, tall))

    greet(x_device)
    greet(y_device)
    greet(sibling)
    other_levels(lambda level: greet(grid.device(level, x, y, core)))
    projected = projected_ref[...]
    factor = lax.rsqrt(jnp.sum(projected * projected, -1, keepdims=True) + EPS)
    unit = projected * factor
    others[core, z, x, y] = jnp.concatenate([unit[:, :half], unit[:, half:]], 0).astype(jnp.bfloat16)
    meet(tall + 2)

    def remote(blocks, device, sent, received):
        return pltpu.make_async_remote_copy(
            src_ref=blocks,
            dst_ref=blocks,
            send_sem=send_sem.at[sent],
            recv_sem=recv_sem.at[received],
            device_id=device,
            device_id_type=MESH,
        )

    along_x = remote(others.at[core, z, x, y], x_device, 0, 0)
    along_x.start()
    along_x.wait_recv()
    along_y = [remote(others.at[core, z, xx, y], y_device, 1 + xx, 1 + xx) for xx in range(2)]
    for copy in along_y:
        copy.start()
    for copy in along_y:
        copy.wait_recv()

    def along_z(level, origin):
        return remote(others.at[core, origin], grid.device(level, x, y, core), 3 + level, 3 + origin)

    def to_side(level):
        return remote(others.at[core, level], sibling, 3 + tall + level, 3 + tall + level)

    other_levels(lambda level: along_z(level, z).start())
    to_side(z).start()

    def pass_side(level):
        along_z(level, level).wait_recv()
        to_side(level).start()

    other_levels(pass_side)
    for level in range(tall):
        to_side(level).wait_recv()
    me = ((core * tall + z) * 2 + x) * 2 + y

    count = grid.total * each
    wide = others[...].reshape(grid.total, 2 * each, half).astype(jnp.float32)
    units = jnp.concatenate(
        [wide[:, :each].reshape(count, half), wide[:, each:].reshape(count, half)], 1
    ).astype(jnp.bfloat16)
    similar = matmul_nt(units, units)
    row = lax.broadcasted_iota(jnp.int32, (count, count), 0)
    column = lax.broadcasted_iota(jnp.int32, (count, count), 1)
    used = (lax.rem(row, each) < pairs_here) & (lax.rem(column, each) >= pairs_here)
    own = used & (column == row + pairs_here)
    negative = used & (column == target_ref[...])
    sim_scale = jnp.exp(scale_ref[...])
    own_mask = jnp.where(own, 1.0, 0.0)
    negative_mask = jnp.where(negative, 1.0, 0.0)
    logits = sim_scale * similar - MARGIN * own_mask
    diagonal = jnp.sum(logits * own_mask, 1, keepdims=True)
    hardest = jnp.sum(logits * negative_mask, 1, keepdims=True)
    row_max = jnp.max(jnp.where(used, logits, -3e38), 1, keepdims=True)
    powers = jnp.where(used, jnp.exp(jnp.minimum(logits - row_max, 0.0)), 0.0)
    row_sum = jnp.sum(powers, 1, keepdims=True)
    is_query = lax.rem(lax.broadcasted_iota(jnp.int32, (count, 1), 0), each) < pairs_here
    gap = hardest - diagonal
    softplus = jnp.maximum(gap, 0.0) + jnp.log(1.0 + jnp.exp(-jnp.abs(gap)))
    row_sum = jnp.where(is_query, row_sum, 1.0)
    losses = jnp.where(is_query, row_max + jnp.log(row_sum) - diagonal + softplus, 0.0)
    gate = 1.0 / (1.0 + jnp.exp(-gap))
    grad_logits = jnp.where(
        used, powers / row_sum - own_mask + gate * (negative_mask - own_mask), 0.0
    )
    loss_ref[0:1, :] = jnp.broadcast_to(jnp.sum(losses, 0, keepdims=True), (1, 128))
    grad_scale = sim_scale * jnp.sum(
        jnp.sum(grad_logits * similar, 1, keepdims=True), 0, keepdims=True
    )
    loss_ref[1:2, :] = jnp.broadcast_to(grad_scale, (1, 128))
    loss_ref[2:8, :] = jnp.zeros((6, 128), jnp.float32)
    grad_similar = sim_scale * grad_logits
    grads[...] = grad_similar + jnp.transpose(grad_similar)
    first = pl.multiple_of(me * each, each)
    grad_units = matmul(grads[pl.ds(first, each), :].astype(jnp.bfloat16), units)
    grad_units = grad_units.astype(jnp.bfloat16).astype(jnp.float32)
    grad_ref[...] = (
        factor * (grad_units - unit * jnp.sum(grad_units * unit, -1, keepdims=True))
    ).astype(jnp.bfloat16)

    along_x.wait_send()
    for copy in along_y:
        copy.wait_send()
    other_levels(lambda level: along_z(level, level).wait_send())
    for level in range(tall):
        to_side(level).wait_send()


def run_loss(projected, target, log_scale, number):
    grid = Grid()
    each = projected.shape[0]
    count = grid.total * each
    inside = pl.BlockSpec(memory_space=pltpu.VMEM)
    dma = pltpu.SemaphoreType.DMA((3 + 2 * grid.tall,))
    return pl.pallas_call(
        functools.partial(loss_kernel, grid, each // 2),
        out_shape=[
            jax.ShapeDtypeStruct((each, D), jnp.bfloat16),
            jax.ShapeDtypeStruct((8, 128), jnp.float32),
        ],
        in_specs=[inside] * 3,
        out_specs=[inside] * 2,
        scratch_shapes=[
            pltpu.VMEM((2, grid.tall, 2, 2, 2 * each, D // 2), jnp.bfloat16),
            pltpu.VMEM((count, count), jnp.float32),
            dma,
            dma,
        ],
        compiler_params=pltpu.CompilerParams(collective_id=number, has_side_effects=True),
    )(projected, target, log_scale)


class Tree:

    @staticmethod
    def scratch(grid, blocks):
        count, tall = len(blocks), grid.tall
        leads = ((tall, 2, 2), (tall, 2, 2), (tall, 2), (tall,), (tall,), (tall,))
        dma = pltpu.SemaphoreType.DMA
        level, pair = dma((count, tall)), dma((count, tall, 2))
        buffers = [pltpu.VMEM(lead + block, jnp.bfloat16) for lead in leads for block in blocks]
        return buffers + [level, level, level, pair, pair] + [level] * 5

    @staticmethod
    def size(count):
        return 6 * count + 10

    def __init__(self, grid, srcs, scratch):
        count = len(srcs)
        self.grid, self.count, self.srcs = grid, count, srcs
        self.acc, self.from_side, self.from_v, self.from_u, self.from_low, self.from_high = [
            scratch[k * count : (k + 1) * count] for k in range(6)
        ]
        (
            self.load_sem,
            self.side_send,
            self.side_recv,
            self.v_send,
            self.v_recv,
            self.u_send,
            self.u_recv,
            self.z_send,
            self.low_recv,
            self.high_recv,
        ) = scratch[6 * count :]
        z, x, y, core = self.place = grid.here()
        tall = grid.tall
        self.up, self.down = grid.device(z + 1, x, y, core), grid.device(z - 1, x, y, core)
        self.has_up, self.has_down = z < tall - 1, z > 0
        self.u = lax.rem(x + 1 - core, 2), lax.rem(y + core, 2)
        self.v = lax.rem(x + core, 2), lax.rem(y + 1 - core, 2)
        self.u_device = grid.device(z, *self.u, core)
        self.v_device = grid.device(z, *self.v, core)
        self.sibling = grid.device(z, x, y, 1 - core)
        self.levels = [self.level_of(j) for j in range(tall)]

    def greet_all(self):
        greet(self.u_device)
        greet(self.v_device)
        greet(self.sibling)
        greet(self.up, self.has_up)
        greet(self.down, self.has_down)
        return 3 + self.has_up.astype(jnp.int32) + self.has_down.astype(jnp.int32)

    def each(self, action):
        for m in range(self.count):
            action(m)

    def level_of(self, j):
        tall = self.grid.tall
        tables = [
            sorted(range(tall), key=lambda level: (-abs(level - own), -level))[j] for own in range(tall)
        ]
        value = tables[0]
        for own in range(1, tall):
            value = jnp.where(self.place[0] == own, tables[own], value)
        return value

    def load(self, m, level):
        core = self.place[3]
        return pltpu.make_async_copy(
            self.srcs[m].at[level, :, :, core], self.acc[m].at[level], self.load_sem.at[m, level]
        )

    def remote(self, src, dst, send_sem, recv_sem, device):
        return pltpu.make_async_remote_copy(
            src_ref=src,
            dst_ref=dst,
            send_sem=send_sem,
            recv_sem=recv_sem,
            device_id=device,
            device_id_type=MESH,
        )

    def side(self, m, level):
        return self.remote(
            self.srcs[m].at[level, :, :, 1 - self.place[3]],
            self.from_side[m].at[level],
            self.side_send.at[m, level],
            self.side_recv.at[m, level],
            self.sibling,
        )

    def v_copy(self, m, level, along_u):
        z, x, y, core = self.place
        xx, yy = (1 - x, 1 - y) if along_u else self.v
        return self.remote(
            self.acc[m].at[level, xx, yy],
            self.from_v[m].at[level, along_u],
            self.v_send.at[m, level, along_u],
            self.v_recv.at[m, level, along_u],
            self.v_device,
        )

    def u_copy(self, m, level):
        return self.remote(
            self.acc[m].at[level, self.u[0], self.u[1]],
            self.from_u[m].at[level],
            self.u_send.at[m, level],
            self.u_recv.at[m, level],
            self.u_device,
        )

    def z_copy(self, m, level, upward):
        z, x, y, core = self.place
        return self.remote(
            self.acc[m].at[level, x, y],
            (self.from_low if upward else self.from_high)[m].at[level],
            self.z_send.at[m, level],
            (self.low_recv if upward else self.high_recv).at[m, level],
            self.up if upward else self.down,
        )

    def add(self, m, level, xx, yy, other):
        total = self.acc[m][level, xx, yy].astype(jnp.float32) + other.astype(jnp.float32)
        self.acc[m][level, xx, yy] = total.astype(jnp.bfloat16)

    def loads(self):
        for level in self.levels:
            self.each(lambda m: self.load(m, level).start())

    def sides(self):
        for level in self.levels:
            self.each(lambda m: self.side(m, level).start())

    def first(self, j):
        level = self.levels[j]

        def run(m):
            self.load(m, level).wait()
            self.side(m, level).wait_recv()
            for xx in range(2):
                for yy in range(2):
                    self.add(m, level, xx, yy, self.from_side[m][level, xx, yy])
            self.v_copy(m, level, 1).start()
            self.v_copy(m, level, 0).start()

        self.each(run)

    def second(self, j):
        z, x, y, core = self.place
        level = self.levels[j]

        def run(m):
            self.v_copy(m, level, 1).wait_recv()
            self.add(m, level, self.u[0], self.u[1], self.from_v[m][level, 1])
            self.u_copy(m, level).start()

        def run_own(m):
            self.v_copy(m, level, 0).wait_recv()
            self.add(m, level, x, y, self.from_v[m][level, 0])

        self.each(run)
        self.each(run_own)

    def third(self, j):
        z, x, y, core = self.place
        level = self.levels[j]

        def run(m):
            self.u_copy(m, level).wait_recv()
            self.add(m, level, x, y, self.from_u[m][level])

            @pl.when((level >= z) & self.has_down)
            def _():
                self.z_copy(m, level, True).wait_recv()
                self.add(m, level, x, y, self.from_low[m][level])

            @pl.when((level <= z) & self.has_up)
            def _():
                self.z_copy(m, level, False).wait_recv()
                self.add(m, level, x, y, self.from_high[m][level])

            @pl.when(level > z)
            def _():
                self.z_copy(m, level, True).start()

            @pl.when(level < z)
            def _():
                self.z_copy(m, level, False).start()

        self.each(run)

    def own(self, m):
        z, x, y, core = self.place
        return self.acc[m][z, x, y].astype(jnp.float32)

    def drain(self):
        for level in self.levels:
            self.each(lambda m: self.side(m, level).wait_send())
            self.each(lambda m: self.v_copy(m, level, 0).wait_send())
            self.each(lambda m: self.v_copy(m, level, 1).wait_send())
            self.each(lambda m: self.u_copy(m, level).wait_send())

            @pl.when(level != self.place[0])
            def _():
                self.each(lambda m: self.z_copy(m, level, True).wait_send())


def fold(values):
    n, lanes = values.shape
    part = jnp.sum(values.reshape(n // 8, 8, lanes), 0)
    total = part[:, :128]
    for at in range(128, lanes, 128):
        total = total + part[:, at : at + 128]
    return total


def gain_back(gains_ref, grads_ref, k, grad_out, inputs):
    factor = lax.rsqrt(jnp.mean(inputs * inputs, -1, keepdims=True) + EPS)
    scaled = grad_out * gains_ref[k : k + 1, :]
    grads_ref[k : k + 1, :] += jnp.sum(grad_out * inputs * factor, 0, keepdims=True)
    return factor * (
        scaled - inputs * (factor * factor * jnp.mean(scaled * inputs, -1, keepdims=True))
    )


BACK_SEQS = 2
HALF = 256


def ffn_back_kernel(
    final_ref,
    after_ref,
    mask_col_ref,
    gains_ref,
    pooled_ref,
    grad_proj_ref,
    pre_hbm,
    packed_hbm,
    down_hbm,
    grad_after_ref,
    grad_gains_ref,
    grad_up_hbm,
    grad_down_hbm,
    up,
    head,
    down,
    branch,
    act_two,
    hidden,
    grad_pre,
    grad_act,
    pre,
    grad_pooled,
    stage,
    load_sem,
    pre_sem,
    store_sem,
):
    tokens = final_ref.shape[0]
    tile = BACK_SEQS * L

    def load(k):
        if k == 0:
            return pltpu.make_async_copy(packed_hbm.at[:, pl.ds(PACKED - D, D)], head, load_sem.at[0])
        if k == 1:
            return pltpu.make_async_copy(down_hbm, down, load_sem.at[1])
        return pltpu.make_async_copy(packed_hbm.at[:, pl.ds(WIDE + D, 4 * D)], up, load_sem.at[2])

    def load_pre(j):
        return pltpu.make_async_copy(pre_hbm.at[:, pl.ds(j * D, D)], pre.at[j % 2], pre_sem.at[j % 2])

    load(0).start()
    load_pre(0).start()
    load(1).start()
    load(2).start()
    grad_gains_ref[...] = jnp.zeros_like(grad_gains_ref)
    load(0).wait()
    grad_pooled[...] = matmul_nt(grad_proj_ref[...], head[...])

    @pl.loop(0, tokens // tile)
    def _(step):
        rows = pl.ds(pl.multiple_of(step * tile, tile), tile)
        weight = mask_col_ref[rows, :]
        pieces = []
        for s in range(BACK_SEQS):
            part = weight[s * L : (s + 1) * L]
            count = jnp.sum(part, 0, keepdims=True)
            pieces.append(part * (grad_pooled[pl.ds(step * BACK_SEQS + s, 1), :] / count))
        grad = gain_back(gains_ref, grad_gains_ref, 2, jnp.concatenate(pieces, 0), final_ref[rows, :])
        grad_after_ref[rows, :] = grad
        branch[rows, :] = grad.astype(jnp.bfloat16)
        act_two[rows, :] = normalize(after_ref[rows, :], gains_ref[1:2, :])[0].astype(jnp.bfloat16)

    stores = []

    def store(value, to):
        slot = len(stores) % 2
        if len(stores) >= 2:
            stores[-2].wait()
        stage[slot] = value.astype(jnp.bfloat16)
        stores.append(pltpu.make_async_copy(stage.at[slot], to, store_sem.at[slot]))
        stores[-1].start()

    load(1).wait()
    for j in range(4):
        part = slice(j * D, (j + 1) * D)
        if j < 3:
            load_pre(j + 1).start()
        for at in range(0, tokens, HALF):
            rows = slice(at, at + HALF)
            wide = matmul_nt(branch[rows, :], down[part, :])
            if at == 0:
                load_pre(j).wait()
            some = pre[j % 2, rows, :]
            half, tan = gelu_parts(some)
            hidden[rows, :] = (some * half).astype(jnp.bfloat16)
            slope = np.float32(np.sqrt(2 / np.pi)) * (1.0 + (3 * 0.044715) * (some * some))
            slope = half + 0.5 * some * (1.0 - tan * tan) * slope
            grad_pre[rows, :] = (wide * slope).astype(jnp.bfloat16)
            if j == 0:
                if at == 0:
                    load(2).wait()
                grad_act[rows, :] = matmul_nt(grad_pre[rows, :], up[:, part])
            else:
                grad_act[rows, :] += matmul_nt(grad_pre[rows, :], up[:, part])
        store(matmul_tn(hidden[...], branch[...]), grad_down_hbm.at[pl.ds(j * D, D), :])
        store(matmul_tn(act_two[...], grad_pre[...]), grad_up_hbm.at[:, pl.ds(j * D, D)])
    store(
        matmul_tn(pooled_ref[...].astype(jnp.bfloat16), grad_proj_ref[...]),
        grad_up_hbm.at[:, pl.ds(4 * D, D)],
    )

    @pl.loop(0, tokens // tile)
    def _(step):
        rows = pl.ds(pl.multiple_of(step * tile, tile), tile)
        grad = gain_back(gains_ref, grad_gains_ref, 1, grad_act[rows, :], after_ref[rows, :])
        grad_after_ref[rows, :] += grad

    stores[-2].wait()
    stores[-1].wait()


def run_ffn_back(final, after, mask_col, gains, pooled, grad_proj, pre, packed, down):
    tokens, seqs = final.shape[0], pooled.shape[0]
    anywhere, inside = pl.BlockSpec(memory_space=pl.ANY), pl.BlockSpec(memory_space=pltpu.VMEM)

    def low(*shape):
        return pltpu.VMEM(shape, jnp.bfloat16)

    def full(*shape):
        return pltpu.VMEM(shape, jnp.float32)

    return pl.pallas_call(
        ffn_back_kernel,
        out_shape=[
            jax.ShapeDtypeStruct((tokens, D), jnp.float32),
            jax.ShapeDtypeStruct((3, D), jnp.float32),
            jax.ShapeDtypeStruct((D, 5 * D), jnp.bfloat16),
            jax.ShapeDtypeStruct((4 * D, D), jnp.bfloat16),
        ],
        in_specs=[inside] * 6 + [anywhere] * 3,
        out_specs=[inside] * 2 + [anywhere] * 2,
        scratch_shapes=[
            low(D, 4 * D),
            low(D, D),
            low(4 * D, D),
            low(tokens, D),
            low(tokens, D),
            low(tokens, D),
            low(tokens, D),
            full(tokens, D),
            full(2, tokens, D),
            full(seqs, D),
            low(2, D, D),
            pltpu.SemaphoreType.DMA((3,)),
            pltpu.SemaphoreType.DMA((2,)),
            pltpu.SemaphoreType.DMA((2,)),
        ],
        compiler_params=pltpu.CompilerParams(vmem_limit_bytes=62 * 1024 * 1024),
    )(final, after, mask_col, gains, pooled, grad_proj, pre, packed, down)


def attn_back_kernel(grid, *refs):
    x0_ref, mask_col_ref, mixed_ref, attended, total_ref, grad_after_ref, gains_ref, bias_ref, packed_hbm = refs[:9]
    srcs = refs[9:11]
    rows_ref, grad_gains_ref, grad_bias_ref, grad_attn_hbm = refs[11:15]
    outs, square_ref = refs[15:17], refs[17]
    packed, act_one, branch_one, grad_mixed, stage, load_sem, store_sem = refs[18:25]
    tree = Tree(grid, srcs, refs[25:])
    step = pl.program_id(0)
    last_step = pl.num_programs(0) - 1
    tile_seqs = x0_ref.shape[0] // L
    tile = tile_seqs * L
    base = pl.multiple_of(step * tile, tile)

    def load(k):
        part = pl.ds(WIDE, D) if k else pl.ds(0, WIDE)
        return pltpu.make_async_copy(packed_hbm.at[:, part], packed.at[:, part], load_sem.at[k])

    @pl.when(step == 0)
    def _():
        friends = tree.greet_all()
        load(1).start()
        load(0).start()
        tree.loads()
        grad_gains_ref[...] = jnp.zeros_like(grad_gains_ref)
        grad_bias_ref[...] = jnp.zeros_like(grad_bias_ref)
        meet(friends)
        tree.sides()
        load(1).wait()

    rows = pl.ds(base, tile)
    grad_after = grad_after_ref[...]
    weight = mask_col_ref[...]
    branch = grad_after.astype(jnp.bfloat16)
    branch_one[rows, :] = branch
    grad_attended = matmul_nt(branch, packed[:, WIDE:]).astype(jnp.bfloat16)
    act_one[rows, :] = normalize(x0_ref[...], gains_ref[0:1, :])[0].astype(jnp.bfloat16)

    def at_step(number, action, *levels):
        @pl.when(step == number)
        def _():
            for j in levels:
                action(j)

    at_step(0, tree.first, 0, 1)
    at_step(1, tree.second, 0)
    at_step(2, tree.third, 0)
    at_step(3, tree.third, 1)
    zero = jnp.zeros((), jnp.bfloat16)
    mine = lane_is((L, 128), 0, HD)
    for s in range(tile_seqs):
        part = slice(s * L, (s + 1) * L)
        here = pl.ds(pl.multiple_of(base + s * L, L), L)
        keep = jnp.where(weight[part] > 0, 0.0, -1000000000.0)
        for pair in range(HEADS // 2):
            at = pair * 128
            query = mixed_ref[part, at : at + 128]
            key = mixed_ref[part, D + at : D + at + 128]
            value = mixed_ref[part, 2 * D + at : 2 * D + at + 128]
            grad_out = grad_attended[part, at : at + 128]
            keys = jnp.concatenate([jnp.where(mine, key, zero), jnp.where(mine, zero, key)], 0)
            values = jnp.concatenate([jnp.where(mine, value, zero), jnp.where(mine, zero, value)], 0)
            scores = (matmul_nt(keys, query) * SCALE).reshape(2, L, L)
            scores = scores + bias_ref[2 * pair : 2 * pair + 2] + keep[None]
            prob = jnp.exp(scores - total_ref[s, 2 * pair : 2 * pair + 2, :][:, None, :])
            grad_prob = matmul_nt(values, grad_out).reshape(2, L, L)
            mean = jnp.sum(prob * grad_prob, 1, keepdims=True)
            grad_scores = (prob * (grad_prob - mean)).astype(jnp.bfloat16)
            grad_bias_ref[2 * pair : 2 * pair + 2] += grad_scores.astype(jnp.float32)
            prob_low = prob.astype(jnp.bfloat16)
            flipped = jnp.transpose(key)
            grad_query = jnp.concatenate(
                [matmul(flipped[:HD], grad_scores[0]), matmul(flipped[HD:], grad_scores[1])], 0
            )
            grad_mixed[here, at : at + 128] = (jnp.transpose(grad_query) * SCALE).astype(jnp.bfloat16)
            grad_keys = matmul(grad_scores.reshape(2 * L, L), query)
            grad_key = jnp.where(mine, grad_keys[:L], grad_keys[L:]) * SCALE
            grad_mixed[here, D + at : D + at + 128] = grad_key.astype(jnp.bfloat16)
            grad_values = matmul(prob_low.reshape(2 * L, L), grad_out)
            grad_value = jnp.where(mine, grad_values[:L], grad_values[L:])
            grad_mixed[here, 2 * D + at : 2 * D + at + 128] = grad_value.astype(jnp.bfloat16)

    @pl.when(step == 0)
    def _():
        tree.first(2)
        tree.first(3)
        load(0).wait()

    at_step(1, tree.second, 1)
    at_step(2, tree.second, 2)
    at_step(3, tree.second, 3)
    grad_act = matmul_nt(grad_mixed[rows, :], packed[:, :WIDE])
    grad_low = gain_back(gains_ref, grad_gains_ref, 0, grad_act, x0_ref[...])
    rows_ref[...] = (grad_after + grad_low).astype(jnp.bfloat16)

    @pl.when(step == last_step)
    def _():
        tree.third(2)
        jobs = [(attended, branch_one, slice(0, D), 3)]
        for j in range(3):
            jobs.append((act_one, grad_mixed, slice(j * D, (j + 1) * D), j))
        copies = []
        for number, (left, right, part, at) in enumerate(jobs):
            slot = number % 2
            if number >= 2:
                copies[number - 2].wait()
            stage[slot] = matmul_tn(left[...], right[:, part]).astype(jnp.bfloat16)
            to = grad_attn_hbm.at[:, pl.ds(at * D, D)]
            copies.append(pltpu.make_async_copy(stage.at[slot], to, store_sem.at[slot]))
            copies[-1].start()
        tree.third(3)
        square_ref[...] = jnp.zeros_like(square_ref)

        def give(m):
            wide = tree.own(m)
            outs[m][...] = wide
            square_ref[0:8, :] += fold(wide * wide)

        tree.each(give)
        copies[-2].wait()
        copies[-1].wait()
        tree.drain()


def run_attn_back(
    x0, mask_col, mixed, attended, totals, grad_after, gains, bias_full, packed, grad_up, grad_down, number
):
    grid = Grid()
    tokens = x0.shape[0]
    tile = BACK_SEQS * L
    steps = tokens // tile
    srcs = [grad.reshape(grid.total, -1, grad.shape[1]) for grad in (grad_up, grad_down)]
    blocks = [src.shape[1:] for src in srcs]
    srcs = [src.reshape((grid.tall, 2, 2, 2) + src.shape[1:]) for src in srcs]

    def rows(width):
        return pl.BlockSpec((tile, width), lambda i: (i, 0))

    def whole(*shape):
        return pl.BlockSpec(shape, lambda i: (0,) * len(shape), pipeline_mode=pl.Buffered(1))

    def low(*shape):
        return pltpu.VMEM(shape, jnp.bfloat16)

    anywhere = pl.BlockSpec(memory_space=pl.ANY)
    return pl.pallas_call(
        functools.partial(attn_back_kernel, grid),
        grid=(steps,),
        out_shape=[
            jax.ShapeDtypeStruct((tokens, D), jnp.bfloat16),
            jax.ShapeDtypeStruct((1, D), jnp.float32),
            jax.ShapeDtypeStruct((HEADS, L, L), jnp.float32),
            jax.ShapeDtypeStruct((D, WIDE + D), jnp.bfloat16),
        ]
        + [jax.ShapeDtypeStruct(block, jnp.float32) for block in blocks]
        + [jax.ShapeDtypeStruct((16, 128), jnp.float32)],
        in_specs=[
            rows(D),
            rows(1),
            rows(WIDE),
            whole(tokens, D),
            pl.BlockSpec((BACK_SEQS, HEADS, L), lambda i: (i, 0, 0)),
            rows(D),
            whole(3, D),
            whole(HEADS, L, L),
            anywhere,
            anywhere,
            anywhere,
        ],
        out_specs=[rows(D), whole(1, D), whole(HEADS, L, L), anywhere]
        + [whole(*block) for block in blocks]
        + [whole(16, 128)],
        scratch_shapes=[
            low(D, WIDE + D),
            low(tokens, D),
            low(tokens, D),
            low(tokens, WIDE),
            low(2, D, D),
            pltpu.SemaphoreType.DMA((2,)),
            pltpu.SemaphoreType.DMA((2,)),
        ]
        + Tree.scratch(grid, blocks),
        compiler_params=pltpu.CompilerParams(
            collective_id=number, has_side_effects=True, vmem_limit_bytes=62 * 1024 * 1024
        ),
    )(x0, mask_col, mixed, attended, totals, grad_after, gains, bias_full, packed, *srcs)


def finish_kernel(grid, count, *refs):
    srcs, (sums, ids, small, square_ref) = refs[:count], refs[count : count + 4]
    refs = refs[count + 4 :]
    outs, (table_out, small_out, square_out) = refs[:count], refs[count : count + 3]
    refs = refs[count + 3 :]
    tree = Tree(grid, srcs, refs[: Tree.size(count)])
    refs = refs[Tree.size(count) :]
    rows, part_sums, small_stage, small_in, square_stage, square_in = refs[:6]
    row_own, line_send, on_send, row_recv, small_send, small_recv, square_send, square_recv = refs[6:]
    z, x, y, core = grid.here()
    tall = grid.tall
    d, f = lax.axis_index("dp"), lax.axis_index("fsdp")
    me = f * grid.dp + d
    sibling = tree.sibling
    f_side = y * 2 + 1 - core
    f_y = (1 - y) * 2 + core
    f_far = (1 - y) * 2 + 1 - core
    for level in range(tall):
        small_in[3 + level] = jnp.zeros(small.shape, jnp.float32)
        square_in[3 + level] = jnp.zeros((16, 128), jnp.float32)
    x_device, y_device = grid.device(z, 1 - x, y, core), grid.device(z, x, 1 - y, core)

    @pl.loop(1, grid.dp)
    def _(step):
        greet((lax.rem(d + step, grid.dp), f))

    greet(y_device)
    greet(sibling)

    def line(peer, slot):
        return pltpu.make_async_remote_copy(
            src_ref=sums.at[peer],
            dst_ref=rows.at[slot],
            send_sem=line_send.at[peer],
            recv_sem=row_recv.at[slot],
            device_id=(peer, f),
            device_id_type=MESH,
        )

    def onward(slot, to_side, own_block=False):
        return pltpu.make_async_remote_copy(
            src_ref=sums.at[d] if own_block else rows.at[slot],
            dst_ref=rows.at[slot],
            send_sem=on_send.at[1 if to_side else 0, slot],
            recv_sem=row_recv.at[slot],
            device_id=(d, f_side if to_side else f_y),
            device_id_type=MESH,
        )

    def total_of(stage, inbox, send_sem, recv_sem):
        partners = (sibling, x_device, y_device)

        def copy(r):
            return pltpu.make_async_remote_copy(
                src_ref=stage.at[r],
                dst_ref=inbox.at[r],
                send_sem=send_sem.at[r],
                recv_sem=recv_sem.at[r],
                device_id=partners[r],
                device_id_type=MESH,
            )

        def z_send(level, slot):
            return pltpu.make_async_remote_copy(
                src_ref=stage.at[3],
                dst_ref=inbox.at[3 + slot],
                send_sem=send_sem.at[3 + level],
                recv_sem=recv_sem.at[3 + slot],
                device_id=grid.device(level, x, y, core),
                device_id_type=MESH,
            )

        def others(action):
            @pl.loop(1, tall)
            def _(step):
                action(lax.rem(z + step, tall))

        def send(r):
            if r < 3:
                copy(r).start()
            else:
                others(lambda level: z_send(level, z).start())

        def take(r):
            if r < 3:
                copy(r).wait_recv()
                stage[r + 1] = stage[r] + inbox[r]
                send(r + 1)
            else:
                others(lambda level: z_send(level, level).wait_recv())

        def result():
            total = stage[3]
            for level in range(tall):
                total = total + jnp.where(z == level, 0.0, inbox[3 + level])
            for r in range(3):
                copy(r).wait_send()
            others(lambda level: z_send(level, level).wait_send())
            return total

        return send, take, result

    small_stage[0] = small[...]
    small_sends, small_take, small_result = total_of(small_stage, small_in, small_send, small_recv)
    square_sends, square_take, square_result = total_of(square_stage, square_in, square_send, square_recv)
    own_rows = pltpu.make_async_copy(sums.at[d], rows.at[me], row_own)
    own_rows.start()
    tree.loads()
    meet(grid.dp + 1)
    small_sends(0)

    @pl.loop(1, grid.dp)
    def _(step):
        line(lax.rem(d + step, grid.dp), me).start()

    tree.sides()
    onward(me, False, True).start()
    onward(me, True, True).start()

    def pass_lines():
        @pl.loop(1, grid.dp)
        def _(step):
            slot = f * grid.dp + lax.rem(d + grid.dp - step, grid.dp)
            line(d, slot).wait_recv()
            onward(slot, False).start()
            onward(slot, True).start()

    def pass_y():
        @pl.loop(0, grid.dp)
        def _(step):
            slot = f_y * grid.dp + lax.rem(d + grid.dp - step, grid.dp)
            line(d, slot).wait_recv()
            onward(slot, True).start()

    def rows_in(column):
        @pl.loop(0, grid.dp)
        def _(step):
            line(d, column * grid.dp + step).wait_recv()

    table_rows = table_out.shape[0]
    whole_blocks = table_rows // ROW_BLOCK
    square_stage[0] = square_ref[...]

    per = grid.dp * rows.shape[1]

    def product(column, start, size):
        place = start + lax.broadcasted_iota(jnp.int32, (size, per), 0)
        hot = jnp.where(place.astype(jnp.float32) == ids[pl.ds(column, 1), :], 1.0, 0.0)
        some = rows[pl.ds(column * grid.dp, grid.dp)].reshape(per, D)
        return matmul(hot.astype(jnp.bfloat16), some)

    def spread_near():
        @pl.loop(0, part_sums.shape[0] // ROW_BLOCK)
        def _(block):
            start = pl.multiple_of(block * ROW_BLOCK, ROW_BLOCK)
            part_sums[pl.ds(start, ROW_BLOCK), :] = product(f, start, ROW_BLOCK) + product(
                f_side, start, ROW_BLOCK
            )

    def spread(start, size):
        total = part_sums[pl.ds(start, size), :] + product(f_y, start, size) + product(f_far, start, size)
        low = total.astype(jnp.bfloat16)
        table_out[pl.ds(start, size), :] = low
        wide = low.astype(jnp.float32)
        square_stage[0, 8:16, :] += fold(wide * wide)

    def spread_all():
        @pl.loop(0, whole_blocks)
        def _(block):
            spread(pl.multiple_of(block * ROW_BLOCK, ROW_BLOCK), ROW_BLOCK)

        if table_rows % ROW_BLOCK:
            spread(whole_blocks * ROW_BLOCK, table_rows % ROW_BLOCK)

    for j in range(tall):
        tree.first(j)
        if j < 3:
            small_take(j)
    pass_lines()
    tree.second(0)
    tree.second(1)
    own_rows.wait()
    rows_in(f_side)
    spread_near()
    tree.third(0)
    tree.second(2)
    pass_y()
    tree.third(1)
    tree.second(3)
    tree.third(2)
    rows_in(f_far)
    spread_all()
    tree.third(3)

    def give(m):
        wide = tree.own(m)
        outs[m][...] = wide
        square_stage[0, 0:8, :] += fold(wide * wide)

    tree.each(give)

    square_sends(0)
    small_take(3)
    small_out[...] = small_result()
    for r in range(3):
        square_take(r)

    tree.drain()

    @pl.loop(0, grid.dp)
    def _(step):
        onward(f * grid.dp + step, False).wait_send()
        onward(f * grid.dp + step, True).wait_send()
        onward(f_y * grid.dp + step, True).wait_send()

    @pl.loop(1, grid.dp)
    def _(step):
        line(lax.rem(d + step, grid.dp), me).wait_send()

    square_take(3)
    square_out[...] = square_result()


def finish(srcs, sums, ids, small, squares, vocab_rows, number):
    grid = Grid()
    count = len(srcs)
    tall = grid.tall
    blocks = [src.shape[1:] for src in srcs]
    srcs = [src.reshape((tall, 2, 2, 2) + src.shape[1:]) for src in srcs]
    cap = sums.shape[1]
    dma = pltpu.SemaphoreType.DMA
    by_device, by_step = dma((grid.total,)), dma((3 + tall,))
    scratch = Tree.scratch(grid, blocks) + [
        pltpu.VMEM((grid.total, cap, D), jnp.bfloat16),
        pltpu.VMEM((-(-vocab_rows // ROW_BLOCK) * ROW_BLOCK, D), jnp.float32),
        pltpu.VMEM((4,) + small.shape, jnp.float32),
        pltpu.VMEM((3 + tall,) + small.shape, jnp.float32),
        pltpu.VMEM((4, 16, 128), jnp.float32),
        pltpu.VMEM((3 + tall, 16, 128), jnp.float32),
        dma,
        dma((grid.dp,)),
        dma((2, grid.total)),
        by_device,
    ]
    anywhere, inside = pl.BlockSpec(memory_space=pl.ANY), pl.BlockSpec(memory_space=pltpu.VMEM)
    results = pl.pallas_call(
        functools.partial(finish_kernel, grid, count),
        out_shape=[jax.ShapeDtypeStruct(block, jnp.float32) for block in blocks]
        + [
            jax.ShapeDtypeStruct((vocab_rows, D), jnp.bfloat16),
            jax.ShapeDtypeStruct(small.shape, jnp.float32),
            jax.ShapeDtypeStruct((16, 128), jnp.float32),
        ],
        in_specs=[anywhere] * (count + 1) + [inside] * 3,
        out_specs=[inside] * (count + 3),
        scratch_shapes=scratch + [by_step] * 4,
        compiler_params=pltpu.CompilerParams(
            collective_id=number, has_side_effects=True, vmem_limit_bytes=62 * 1024 * 1024
        ),
    )(*srcs, sums, ids, small, squares)
    return (results[:count], *results[count:])


def update_kernel(fs, *refs):
    squares, summed, scale_grad, table, table_first, table_second, table_grad = refs[:7]
    rest, shards = refs[7:22], refs[22:25]
    norm_ref, out_first, out_second, out = refs[25:29]
    rest_outs, factor_ref = refs[29:44], refs[44]

    def row_sum(values):
        return jnp.sum(jnp.sum(values, 1, keepdims=True), 0, keepdims=True)

    @pl.when(pl.program_id(0) == 0)
    def _():
        total = row_sum(squares[0:8, :]) + row_sum(squares[8:16, :]) / float(fs)
        total = total + (row_sum(summed[...] * summed[...]) + scale_grad[...] * scale_grad[...])
        norm = jnp.sqrt(total)
        norm_ref[...] = jnp.broadcast_to(norm, norm_ref.shape)
        factor_ref[...] = jnp.minimum(1.0, CLIP / (norm + 1e-06))
        attn, up, down = shards
        grads = (attn[:, :WIDE], attn[:, WIDE:], up[:, : 4 * D], down[...], up[:, 4 * D :])
        for k in range(5):
            first_new, second_new, new = adam_update(
                *[ref[...] for ref in rest[3 * k : 3 * k + 3]],
                grads[k],
                factor_ref[...],
                RATES[k + 1],
                DECAYS[k + 1],
            )
            rest_outs[3 * k][...] = first_new
            rest_outs[3 * k + 1][...] = second_new
            rest_outs[3 * k + 2][...] = new

    first_new, second_new, new = adam_update(
        table[...],
        table_first[...],
        table_second[...],
        table_grad[...].astype(jnp.float32),
        factor_ref[...],
        RATES[0],
        DECAYS[0],
    )
    out_first[...] = first_new
    out_second[...] = second_new
    out[...] = new


def run_update(fs, squares, summed, scale_grad, table_arrays, table_grad, rest, shards):
    vocab_rows = table_grad.shape[0]
    blocks = pl.BlockSpec((ROW_BLOCK, D), lambda i: (i, 0))

    def whole(array):
        return pl.BlockSpec(
            array.shape, lambda i: (0,) * array.ndim, pipeline_mode=pl.Buffered(1)
        )

    norm = jax.ShapeDtypeStruct((8, 128), jnp.float32)
    return pl.pallas_call(
        functools.partial(update_kernel, fs),
        grid=(-(-vocab_rows // ROW_BLOCK),),
        out_shape=[norm]
        + [jax.ShapeDtypeStruct(table_grad.shape, jnp.float32)] * 3
        + [jax.ShapeDtypeStruct(array.shape, jnp.float32) for array in rest],
        in_specs=[whole(squares), whole(summed), whole(scale_grad)]
        + [blocks] * 4
        + [whole(array) for array in (*rest, *shards)],
        out_specs=[whole(norm)] + [blocks] * 3 + [whole(array) for array in rest],
        scratch_shapes=[pltpu.VMEM((1, 1), jnp.float32)],
        compiler_params=pltpu.CompilerParams(vmem_limit_bytes=60 * 1024 * 1024),
    )(squares, summed, scale_grad, *table_arrays, table_grad, *rest, *shards)


def plain_body(
    token_ids,
    pad_mask,
    hard_negative,
    table,
    table_first,
    table_second,
    attn_in,
    attn_in_first,
    attn_in_second,
    attn_out,
    attn_out_first,
    attn_out_second,
    ffn_in,
    ffn_in_first,
    ffn_in_second,
    ffn_out,
    ffn_out_first,
    ffn_out_second,
    proj_head,
    proj_head_first,
    proj_head_second,
    small_params,
    small_first,
    small_second,
):
    dp_count = lax.axis_size("dp")
    fsdp_count = lax.axis_size("fsdp")
    device_flat = lax.axis_index("dp") * fsdp_count + lax.axis_index("fsdp")
    pairs_here = token_ids.shape[1]
    pairs_total = pairs_here * dp_count * fsdp_count
    seq_count = 2 * pairs_here
    vocab_rows = table.shape[0]
    row_base = lax.axis_index("dp") * vocab_rows
    gain_rows = small_params[: 3 * D].reshape(3, D)
    bias_table = small_params[3 * D : 3 * D + NB * HEADS].reshape(NB, HEADS)
    log_scale = small_params[3 * D + NB * HEADS]
    buckets = jnp.asarray(bucket_table(L, NB).reshape(-1), jnp.int32)
    bucket_hot = (buckets[:, None] == jnp.arange(NB, dtype=jnp.int32)[None, :]).astype(jnp.float32)
    bias_full = (
        jnp.dot(bucket_hot, bias_table, precision=HIGH).reshape(L, L, HEADS).transpose(2, 0, 1)
    )
    mask_rows = pad_mask.reshape(seq_count, L)
    ids_flat = token_ids.reshape(-1)
    table_low = table.astype(jnp.bfloat16)
    ids_all = lax.all_gather(ids_flat, "dp", axis=0, tiled=True)
    picked = ids_all - row_base
    inside = (picked >= 0) & (picked < vocab_rows)
    chosen = jnp.take(table_low, jnp.clip(picked, 0, vocab_rows - 1), axis=0)
    embedded = lax.psum_scatter(
        jnp.where(inside[:, None], chosen.astype(jnp.float32), 0.0).astype(jnp.bfloat16),
        "dp",
        scatter_dimension=0,
        tiled=True,
    ).astype(jnp.float32)
    shards = (
        attn_in.astype(jnp.bfloat16),
        attn_out.astype(jnp.bfloat16),
        ffn_in.astype(jnp.bfloat16),
        ffn_out.astype(jnp.bfloat16),
        proj_head.astype(jnp.bfloat16),
    )
    gathered = (
        lax.all_gather(shards[0], ("dp", "fsdp"), axis=0, tiled=True),
        lax.all_gather(shards[1], ("dp", "fsdp"), axis=0, tiled=True),
        lax.all_gather(shards[2], ("dp", "fsdp"), axis=0, tiled=True),
        lax.all_gather(shards[3], ("dp", "fsdp"), axis=0, tiled=True),
        lax.all_gather(shards[4], ("dp", "fsdp"), axis=0, tiled=True),
    )
    final_rows, kept = layer_forward(embedded, mask_rows, gathered[:4], gain_rows, bias_full)
    normed_three, factor_three = normalize(final_rows, gain_rows[2])
    mask_weight = mask_rows.astype(jnp.float32)[:, :, None]
    counts = jnp.sum(mask_weight, 1)
    pooled = jnp.sum(normed_three.reshape(seq_count, L, D) * mask_weight, 1) / counts
    pooled_low = pooled.astype(jnp.bfloat16)
    projected = matmul(pooled_low, gathered[4])
    proj_factor = lax.rsqrt(jnp.sum(projected * projected, -1, keepdims=True) + EPS)
    unit_rows = projected * proj_factor
    unit_low = unit_rows.astype(jnp.bfloat16)
    mine_query = unit_low[:pairs_here]
    all_pass = lax.all_gather(unit_low[pairs_here:], ("dp", "fsdp"), axis=0, tiled=True)
    similar = matmul_nt(mine_query, all_pass)
    sim_scale = jnp.exp(log_scale)
    columns = jnp.arange(pairs_total, dtype=jnp.int32)
    own_index = device_flat * pairs_here + jnp.arange(pairs_here, dtype=jnp.int32)
    own_mask = (columns[None, :] == own_index[:, None]).astype(jnp.float32)
    negative = (columns[None, :] == hard_negative[:, None]).astype(jnp.float32)
    logits = sim_scale * similar - MARGIN * own_mask
    diagonal = jnp.sum(logits * own_mask, 1)
    hardest = jnp.sum(logits * negative, 1)
    row_max = jnp.max(logits, 1, keepdims=True)
    log_total = row_max + jnp.log(jnp.sum(jnp.exp(logits - row_max), 1, keepdims=True))
    loss_local = jnp.sum(log_total[:, 0] - diagonal + jax.nn.softplus(hardest - diagonal))
    hinge_gate = jax.nn.sigmoid(hardest - diagonal)
    grad_logits = (
        jnp.exp(logits - log_total) - own_mask + hinge_gate[:, None] * (negative - own_mask)
    )
    grad_log_scale = sim_scale * jnp.sum(grad_logits * similar)
    grad_similar = (sim_scale * grad_logits).astype(jnp.bfloat16)
    grad_query = matmul(grad_similar, all_pass).astype(jnp.bfloat16)
    grad_pass_terms = matmul_tn(grad_similar, mine_query)
    grad_pass = lax.psum_scatter(
        grad_pass_terms, ("dp", "fsdp"), scatter_dimension=0, tiled=True
    ).astype(jnp.bfloat16)
    grad_units = jnp.concatenate([grad_query, grad_pass], 0).astype(jnp.float32)
    grad_proj = (
        proj_factor * (grad_units - unit_rows * jnp.sum(grad_units * unit_rows, -1, keepdims=True))
    ).astype(jnp.bfloat16)
    gathered_back = (
        lax.all_gather(shards[0], ("dp", "fsdp"), axis=0, tiled=True),
        lax.all_gather(shards[1], ("dp", "fsdp"), axis=0, tiled=True),
        lax.all_gather(shards[2], ("dp", "fsdp"), axis=0, tiled=True),
        lax.all_gather(shards[3], ("dp", "fsdp"), axis=0, tiled=True),
        lax.all_gather(shards[4], ("dp", "fsdp"), axis=0, tiled=True),
    )
    grad_proj_head = matmul_tn(pooled_low, grad_proj)
    grad_pooled = matmul_nt(grad_proj, gathered_back[4])
    grad_normed = ((grad_pooled / counts)[:, None, :] * mask_weight).reshape(-1, D)
    grad_final, gain_three = normalize_back(grad_normed, final_rows, factor_three, gain_rows[2])
    grad_rows, matrix_grads, gain_one, gain_two, grad_bias = layer_backward(
        grad_final, kept, mask_rows, gathered_back[:4], gain_rows, bias_full
    )
    attn_in_grad, attn_out_grad, ffn_in_grad, ffn_out_grad = matrix_grads
    grad_bias_table = jnp.dot(grad_bias.reshape(HEADS, L * L), bucket_hot, precision=HIGH).T
    small_local = jnp.concatenate(
        [gain_one, gain_two, gain_three, grad_bias_table.reshape(-1), grad_log_scale[None]]
    )
    small_grad = lax.psum(small_local, ("dp", "fsdp"))
    weight_grads = (
        lax.psum_scatter(attn_in_grad, ("dp", "fsdp"), scatter_dimension=0, tiled=True),
        lax.psum_scatter(attn_out_grad, ("dp", "fsdp"), scatter_dimension=0, tiled=True),
        lax.psum_scatter(ffn_in_grad, ("dp", "fsdp"), scatter_dimension=0, tiled=True),
        lax.psum_scatter(ffn_out_grad, ("dp", "fsdp"), scatter_dimension=0, tiled=True),
        lax.psum_scatter(grad_proj_head, ("dp", "fsdp"), scatter_dimension=0, tiled=True),
    )
    rows_back = lax.all_gather(grad_rows.astype(jnp.bfloat16), "dp", axis=0, tiled=True)
    turn_count = dp_count // 4
    block_rows = rows_back.shape[0] // turn_count

    def add_block(running, piece_pair):
        block_grads, block_ids = piece_pair
        local_ids = block_ids - row_base
        inside = (local_ids >= 0) & (local_ids < vocab_rows)
        segment = jnp.where(inside, local_ids, vocab_rows)
        summed = jax.ops.segment_sum(
            block_grads.astype(jnp.float32), segment, num_segments=vocab_rows + 1
        )
        return (running + summed[:vocab_rows], None)

    table_full, _ = lax.scan(
        add_block,
        jnp.zeros((vocab_rows, D), jnp.float32),
        (rows_back.reshape(turn_count, block_rows, D), ids_all.reshape(turn_count, block_rows)),
    )
    table_grad = lax.psum(table_full.astype(jnp.bfloat16), "fsdp").astype(jnp.float32)
    owned = (table_grad,) + tuple(weight_grads)
    squares = jnp.sum(table_grad * table_grad) / fsdp_count
    for gradient in weight_grads:
        squares = squares + jnp.sum(gradient * gradient)
    total_squares, loss_sum = lax.psum((squares, loss_local), ("dp", "fsdp"))
    norm_value = jnp.sqrt(total_squares + jnp.sum(small_grad * small_grad))
    factor = jnp.minimum(1.0, CLIP / (norm_value + 1e-06))
    masters = (table, attn_in, attn_out, ffn_in, ffn_out, proj_head, small_params)
    firsts = (
        table_first,
        attn_in_first,
        attn_out_first,
        ffn_in_first,
        ffn_out_first,
        proj_head_first,
        small_first,
    )
    seconds = (
        table_second,
        attn_in_second,
        attn_out_second,
        ffn_in_second,
        ffn_out_second,
        proj_head_second,
        small_second,
    )
    gradients = owned + (small_grad,)
    results = [loss_sum, norm_value]
    for kind_index in range(7):
        results.extend(
            adam_update(
                masters[kind_index],
                firsts[kind_index],
                seconds[kind_index],
                gradients[kind_index],
                factor,
                RATES[kind_index],
                DECAYS[kind_index],
            )
        )
    return tuple(results)


def fits(mesh):
    return mesh.shape["fsdp"] == 4 and mesh.shape["dp"] == 8


def dense_rows(ids_flat, table, row_base):
    vocab_rows = table.shape[0]
    ids_all = lax.all_gather(ids_flat, "dp", axis=0, tiled=True)
    picked = ids_all - row_base
    inside = (picked >= 0) & (picked < vocab_rows)
    chosen = jnp.take(table, jnp.clip(picked, 0, vocab_rows - 1), axis=0)
    return lax.psum_scatter(
        jnp.where(inside[:, None], chosen, 0.0).astype(jnp.bfloat16),
        "dp",
        scatter_dimension=0,
        tiled=True,
    ).astype(jnp.float32)


def dense_table_grad(ids_flat, grad_low, vocab_rows, row_base):
    ids_all = lax.all_gather(ids_flat, "dp", axis=0, tiled=True)
    rows_back = lax.all_gather(grad_low, "dp", axis=0, tiled=True)
    turn_count = lax.axis_size("dp") // 4
    block_rows = rows_back.shape[0] // turn_count

    def add_block(running, piece_pair):
        block_grads, block_ids = piece_pair
        local_ids = block_ids - row_base
        inside = (local_ids >= 0) & (local_ids < vocab_rows)
        segment = jnp.where(inside, local_ids, vocab_rows)
        summed = jax.ops.segment_sum(
            block_grads.astype(jnp.float32), segment, num_segments=vocab_rows + 1
        )
        return (running + summed[:vocab_rows], None)

    table_full, _ = lax.scan(
        add_block,
        jnp.zeros((vocab_rows, D), jnp.float32),
        (rows_back.reshape(turn_count, block_rows, D), ids_all.reshape(turn_count, block_rows)),
    )
    return lax.psum(table_full.astype(jnp.bfloat16), "fsdp")


def once(flag, make, value):
    return lax.while_loop(lambda state: state[0], lambda state: (False, make(state[1])), (flag, value))[1]


def fast_body(
    token_ids,
    pad_mask,
    hard_negative,
    table,
    table_first,
    table_second,
    attn_in,
    attn_in_first,
    attn_in_second,
    attn_out,
    attn_out_first,
    attn_out_second,
    ffn_in,
    ffn_in_first,
    ffn_in_second,
    ffn_out,
    ffn_out_first,
    ffn_out_second,
    proj_head,
    proj_head_first,
    proj_head_second,
    small_params,
    small_first,
    small_second,
):
    dp_count = lax.axis_size("dp")
    fsdp_count = lax.axis_size("fsdp")
    total = dp_count * fsdp_count
    pairs_here = token_ids.shape[1]
    pairs_total = pairs_here * total
    seq_count = 2 * pairs_here
    vocab_rows = table.shape[0]
    row_base = lax.axis_index("dp") * vocab_rows
    gain_rows = small_params[: 3 * D].reshape(3, D)
    bias_table = small_params[3 * D : 3 * D + NB * HEADS].reshape(NB, HEADS)
    log_scale = small_params[3 * D + NB * HEADS]
    buckets = jnp.asarray(bucket_table(L, NB).T.reshape(-1), jnp.int32)
    bucket_hot = (buckets[:, None] == jnp.arange(NB, dtype=jnp.int32)[None, :]).astype(jnp.float32)
    bias_full = (
        jnp.dot(bucket_hot, bias_table, precision=HIGH).reshape(L, L, HEADS).transpose(2, 0, 1)
    )
    mask_rows = pad_mask.reshape(seq_count, L)
    ids_flat = token_ids.reshape(-1)
    tokens = ids_flat.shape[0]

    gathered_packed, gathered_down, heard, slot, embedded = run_head(
        ids_flat, hard_negative, attn_in, attn_out, ffn_in, proj_head, ffn_out, table, 1
    )
    packed = gathered_packed.reshape(-1, PACKED)
    down = gathered_down.reshape(-1, D)
    asked = heard[:, 0, :CAP]
    negatives = heard[:, 1, :pairs_here].reshape(-1).astype(jnp.int32)
    any_spilled = jnp.max(heard[:, 2, 0]) > 0.5
    embedded = once(
        any_spilled,
        lambda rows: dense_rows(
            ids_flat, table + jnp.minimum(jnp.abs(rows[0, 0]), 0.0), row_base
        ),
        embedded,
    )

    mask_col = mask_rows.astype(jnp.float32).reshape(tokens, 1)
    mixed, attended, totals, after, pre, final, pooled, projected = run_forward(
        embedded, mask_col, gain_rows, bias_full, packed, down
    )
    tall, wide = dp_count // (fsdp_count // 2), fsdp_count // 2
    owner = negatives // pairs_here
    owner = (owner % 2 * tall + owner // (2 * wide * wide)) * wide * wide + owner // 2 % (wide * wide) % wide + (
        owner // (2 * wide) % wide * wide
    )
    target = owner * seq_count + pairs_here + negatives % pairs_here
    target = jnp.concatenate(
        [target.reshape(total, pairs_here), jnp.full((total, pairs_here), -1, jnp.int32)], 1
    )
    target = target.reshape(tall * wide * wide, 2, seq_count).transpose(1, 0, 2).reshape(-1, 1)
    grad_proj, loss_parts = run_loss(projected, target, log_scale.reshape(1, 1), 3)
    loss_sum, grad_log_scale = loss_parts[0, 0], loss_parts[1, 0]
    grad_after, grad_gains, grad_up, grad_down = run_ffn_back(
        final, after, mask_col, gain_rows, pooled, grad_proj, pre, packed, down
    )
    grad_low, grad_gain, grad_bias, grad_attn, up_shard, down_shard, squares = run_attn_back(
        embedded, mask_col, mixed, attended, totals, grad_after, gain_rows, bias_full, packed, grad_up, grad_down, 4
    )
    grad_gains = jnp.concatenate([grad_gain, grad_gains[1:]], 0)
    grad_bias_table = jnp.dot(grad_bias.reshape(HEADS, L * L), bucket_hot, precision=HIGH).T
    small_local = jnp.concatenate([grad_gains.reshape(-1), grad_bias_table.reshape(-1)])
    width = -(-small_local.shape[0] // 1024) * 8
    small_local = jnp.pad(small_local, (0, width * 128 - small_local.shape[0]))
    slots = jnp.arange(dp_count * CAP, dtype=jnp.int32).astype(jnp.float32)
    slot_hot = (slot == slots[None, :]).astype(jnp.bfloat16)
    slot_sums = matmul_tn(slot_hot, grad_low).astype(jnp.bfloat16).reshape(dp_count, CAP, D)
    (attn_shard,), table_grad, summed, squares = finish(
        [grad_attn.reshape(total, -1, WIDE + D)],
        slot_sums,
        asked.reshape(dp_count, fsdp_count, CAP).transpose(1, 0, 2).reshape(fsdp_count, -1),
        small_local.reshape(width, 128),
        squares,
        vocab_rows,
        5,
    )
    table_grad, squares = once(
        any_spilled,
        lambda state: with_squares(dense_table_grad(ids_flat, grad_low, vocab_rows, row_base), state[1]),
        (table_grad, squares),
    )
    norm, *updated = run_update(
        fsdp_count,
        squares,
        summed,
        grad_log_scale.reshape(1, 1),
        (table, table_first, table_second),
        table_grad,
        (
            *(attn_in, attn_in_first, attn_in_second),
            *(attn_out, attn_out_first, attn_out_second),
            *(ffn_in, ffn_in_first, ffn_in_second),
            *(ffn_out, ffn_out_first, ffn_out_second),
            *(proj_head, proj_head_first, proj_head_second),
        ),
        (attn_shard, up_shard, down_shard),
    )
    norm_value = norm[0, 0]
    factor = jnp.minimum(1.0, CLIP / (norm_value + 1e-06))
    small_size = small_params.shape[0]
    small_grad = jnp.concatenate([summed.reshape(-1)[: small_size - 1], grad_log_scale[None]])
    small_new = adam_update(
        small_params, small_first, small_second, small_grad, factor, RATES[6], DECAYS[6]
    )
    return (loss_sum, norm_value, *updated, *small_new)


def with_squares(table_grad, squares):
    wide = table_grad.astype(jnp.float32)
    total = lax.psum(jnp.sum(wide * wide), ("dp", "fsdp"))
    return (table_grad, squares.at[8:].set(0.0).at[8, 0].set(total))


def solution(mesh):
    program = fast_body if fits(mesh) else plain_body
    return jax.shard_map(
        program,
        mesh=mesh,
        in_specs=(
            P(None, ("dp", "fsdp"), None),
            P(None, ("dp", "fsdp"), None),
            P(("dp", "fsdp")),
            P("dp", None),
            P("dp", None),
            P("dp", None),
            P(("dp", "fsdp"), None),
            P(("dp", "fsdp"), None),
            P(("dp", "fsdp"), None),
            P(("dp", "fsdp"), None),
            P(("dp", "fsdp"), None),
            P(("dp", "fsdp"), None),
            P(("dp", "fsdp"), None),
            P(("dp", "fsdp"), None),
            P(("dp", "fsdp"), None),
            P(("dp", "fsdp"), None),
            P(("dp", "fsdp"), None),
            P(("dp", "fsdp"), None),
            P(("dp", "fsdp"), None),
            P(("dp", "fsdp"), None),
            P(("dp", "fsdp"), None),
            P(),
            P(),
            P(),
        ),
        out_specs=(
            P(),
            P(),
            P("dp", None),
            P("dp", None),
            P("dp", None),
            P(("dp", "fsdp"), None),
            P(("dp", "fsdp"), None),
            P(("dp", "fsdp"), None),
            P(("dp", "fsdp"), None),
            P(("dp", "fsdp"), None),
            P(("dp", "fsdp"), None),
            P(("dp", "fsdp"), None),
            P(("dp", "fsdp"), None),
            P(("dp", "fsdp"), None),
            P(("dp", "fsdp"), None),
            P(("dp", "fsdp"), None),
            P(("dp", "fsdp"), None),
            P(("dp", "fsdp"), None),
            P(("dp", "fsdp"), None),
            P(("dp", "fsdp"), None),
            P(),
            P(),
            P(),
        ),
        check_vma=False,
    )
```

```python
import functools

import jax
import jax.numpy as jnp
import numpy as np
from jax import lax
from jax.experimental import pallas as pl
from jax.experimental.pallas import tpu as pltpu
from jax.sharding import PartitionSpec as P

D = 768
HEADS = 12
HD = 64
NB = 32
L = 128
STEP = 10


EPS = 1e-06
SCALE = 0.125
MARGIN = 0.2
CLIP = 0.1
BETA_ONE = 0.9
BETA_TWO = 0.99
ADAM_EPS = 1e-08
RATES = (3.0, 0.1, 0.2, 0.1, 0.05, 0.1, 1.0)
DECAYS = (0.001, 0.001, 0.001, 0.001, 0.001, 0.001, 0.0)
HIGH = lax.Precision.HIGHEST
MESH = pl.DeviceIdType.MESH
CAP = 112


def bucket_table(length, count):
    position = np.arange(length)
    relative = position[None, :] - position[:, None]
    half = count // 2
    base_part = (relative > 0).astype(np.int64) * half
    distance = np.abs(relative)
    exact = half // 2
    safe_dist = np.maximum(distance, 1)
    large = exact + (np.log(safe_dist / exact) / np.log(length / exact) * (half - exact)).astype(
        np.int64
    )
    large = np.minimum(large, half - 1)
    return base_part + np.where(distance < exact, distance, large)


def matmul(left_side, right_side):
    return jnp.dot(left_side, right_side, preferred_element_type=jnp.float32)


def matmul_tn(left_side, right_side):
    return lax.dot_general(
        left_side, right_side, (((0,), (0,)), ((), ())), preferred_element_type=jnp.float32
    )


def matmul_nt(left_side, right_side):
    return lax.dot_general(
        left_side, right_side, (((1,), (1,)), ((), ())), preferred_element_type=jnp.float32
    )


def normalize(inputs, gain_row):
    factor = lax.rsqrt(jnp.mean(inputs * inputs, -1, keepdims=True) + EPS)
    return (inputs * factor * gain_row, factor)


def normalize_back(grad_out, inputs, factor, gain_row):
    scaled = grad_out * gain_row
    grad_gain = jnp.sum(grad_out * inputs * factor, 0)
    grad_in = factor * (
        scaled - inputs * factor * factor * jnp.mean(scaled * inputs, -1, keepdims=True)
    )
    return (grad_in, grad_gain)


def attention_scores(mixed_proj, mask_rows, bias_full):
    keep_add = jnp.where(mask_rows > 0, 0.0, -1000000000.0).astype(jnp.float32)
    scores = jnp.einsum(
        "bqhd,bkhd->bhqk",
        mixed_proj[:, :, 0],
        mixed_proj[:, :, 1],
        preferred_element_type=jnp.float32,
    )
    return scores * SCALE + bias_full[None] + keep_add[:, None, None, :]


def layer_forward(token_rows, mask_rows, weights, gain_rows, bias_full):
    attn_in, attn_out, ffn_in, ffn_out = weights
    seq_count, length = mask_rows.shape
    width = token_rows.shape[1]
    normed_one, factor_one = normalize(token_rows, gain_rows[0])
    act_one = normed_one.astype(jnp.bfloat16)
    mixed_proj = (
        matmul(act_one, attn_in).astype(jnp.bfloat16).reshape(seq_count, length, 3, HEADS, HD)
    )
    scores = attention_scores(mixed_proj, mask_rows, bias_full)
    row_max = jnp.max(scores, -1, keepdims=True)
    log_total = row_max + jnp.log(jnp.sum(jnp.exp(scores - row_max), -1, keepdims=True))
    prob_low = jnp.exp(scores - log_total).astype(jnp.bfloat16)
    attended = jnp.einsum(
        "bhqk,bkhd->bqhd", prob_low, mixed_proj[:, :, 2], preferred_element_type=jnp.float32
    )
    attended = attended.astype(jnp.bfloat16).reshape(-1, width)
    after_attn = token_rows + matmul(attended, attn_out)
    normed_two, factor_two = normalize(after_attn, gain_rows[1])
    act_two = normed_two.astype(jnp.bfloat16)
    pre_act = matmul(act_two, ffn_in)
    hidden = jax.nn.gelu(pre_act).astype(jnp.bfloat16)
    final_rows = after_attn + matmul(hidden, ffn_out)
    kept = (
        token_rows,
        factor_one,
        act_one,
        mixed_proj,
        log_total,
        attended,
        after_attn,
        factor_two,
        act_two,
        pre_act,
        hidden,
    )
    return (final_rows, kept)


def layer_backward(grad_final, kept, mask_rows, weights, gain_rows, bias_full):
    (
        token_rows,
        factor_one,
        act_one,
        mixed_proj,
        log_total,
        attended,
        after_attn,
        factor_two,
        act_two,
        pre_act,
        hidden,
    ) = kept
    attn_in, attn_out, ffn_in, ffn_out = weights
    seq_count, length = mask_rows.shape
    branch = grad_final.astype(jnp.bfloat16)
    grad_ffn_out = matmul_tn(hidden, branch)
    grad_hidden = matmul_nt(branch, ffn_out)
    _, gelu_pull = jax.vjp(jax.nn.gelu, pre_act)
    grad_pre = gelu_pull(grad_hidden)[0].astype(jnp.bfloat16)
    grad_ffn_in = matmul_tn(act_two, grad_pre)
    grad_act_two = matmul_nt(grad_pre, ffn_in)
    grad_mid, gain_two = normalize_back(grad_act_two, after_attn, factor_two, gain_rows[1])
    grad_after = grad_final + grad_mid
    branch = grad_after.astype(jnp.bfloat16)
    grad_attn_out = matmul_tn(attended, branch)
    grad_attended = (
        matmul_nt(branch, attn_out).astype(jnp.bfloat16).reshape(seq_count, length, HEADS, HD)
    )
    scores = attention_scores(mixed_proj, mask_rows, bias_full)
    prob_full = jnp.exp(scores - log_total)
    prob_low = prob_full.astype(jnp.bfloat16)
    queries = mixed_proj[:, :, 0]
    key_rows = mixed_proj[:, :, 1]
    grad_probs = jnp.einsum(
        "bqhd,bkhd->bhqk", grad_attended, mixed_proj[:, :, 2], preferred_element_type=jnp.float32
    )
    grad_values = jnp.einsum(
        "bhqk,bqhd->bkhd", prob_low, grad_attended, preferred_element_type=jnp.float32
    )
    grad_scores = prob_full * (grad_probs - jnp.sum(prob_full * grad_probs, -1, keepdims=True))
    grad_scores = grad_scores.astype(jnp.bfloat16)
    grad_bias = jnp.sum(grad_scores, 0, dtype=jnp.float32)
    grad_queries = (
        jnp.einsum("bhqk,bkhd->bqhd", grad_scores, key_rows, preferred_element_type=jnp.float32)
        * SCALE
    )
    grad_keys = (
        jnp.einsum("bhqk,bqhd->bkhd", grad_scores, queries, preferred_element_type=jnp.float32)
        * SCALE
    )
    grad_mixed = (
        jnp.stack([grad_queries, grad_keys, grad_values], 2)
        .astype(jnp.bfloat16)
        .reshape(seq_count * length, -1)
    )
    grad_attn_in = matmul_tn(act_one, grad_mixed)
    grad_act_one = matmul_nt(grad_mixed, attn_in)
    grad_low, gain_one = normalize_back(grad_act_one, token_rows, factor_one, gain_rows[0])
    grad_rows = grad_after + grad_low
    return (
        grad_rows,
        (grad_attn_in, grad_attn_out, grad_ffn_in, grad_ffn_out),
        gain_one,
        gain_two,
        grad_bias,
    )


def adam_update(param, first_moment, second_moment, gradient, factor, rate, decay):
    clipped = gradient * factor
    first_new = BETA_ONE * first_moment + (1.0 - BETA_ONE) * clipped
    second_new = BETA_TWO * second_moment + (1.0 - BETA_TWO) * clipped * clipped
    direction = (
        first_new
        / (1.0 - BETA_ONE**STEP)
        / (jnp.sqrt(second_new / (1.0 - BETA_TWO**STEP)) + ADAM_EPS)
    )
    return (first_new, second_new, param - rate * (direction + decay * param))


class Grid:
    def __init__(self):
        self.dp, self.fs = lax.axis_size("dp"), lax.axis_size("fsdp")
        self.total = self.dp * self.fs
        self.wide = self.fs // 2
        self.tall = self.dp // self.wide

    def here(self):
        d, f = lax.axis_index("dp"), lax.axis_index("fsdp")
        return d // self.wide, lax.rem(d, self.wide), f // 2, lax.rem(f, 2)

    def device(self, z, x, y, core):
        return (z * self.wide + x, y * 2 + core)

    def flat(self, z, x, y, core):
        return (z * self.wide + x) * self.fs + y * 2 + core

    def peer(self, index):
        return (index // self.fs, lax.rem(index, self.fs))


def greet(device, when=None):
    barrier = pltpu.get_barrier_semaphore()

    def signal():
        pl.semaphore_signal(barrier, inc=1, device_id=device, device_id_type=MESH)

    if when is None:
        signal()
    else:
        pl.when(when)(signal)


def meet(count):
    pl.semaphore_wait(pltpu.get_barrier_semaphore(), count)


ROW_BLOCK = 512
WIDE = 3 * D
PACKED = WIDE + D + 4 * D + D
TILE_SEQS = 4


def head_kernel(
    grid,
    col_ref,
    row_ref,
    negative_ref,
    in_ref,
    out_ref,
    up_ref,
    proj_ref,
    down_ref,
    table_hbm,
    packed_out,
    down_out,
    heard,
    slot_ref,
    x0_ref,
    packed_mine,
    down_mine,
    table,
    total,
    answers,
    found,
    messages,
    in_wide,
    out_wide,
    up_wide,
    proj_wide,
    down_wide,
    send_sem,
    recv_sem,
    own_sem,
    row_send,
    row_recv,
    note_send,
    note_recv,
    note_on,
    table_sem,
    wide_sem,
):
    srcs, outs = (packed_mine, down_mine), (packed_out, down_out)
    count = 2
    z, x, y, core = grid.here()
    tall = grid.tall
    d, f = lax.axis_index("dp"), lax.axis_index("fsdp")
    u_places = ((lax.rem(x + 1 - core, 2), lax.rem(y + core, 2)), (1 - x, y))
    v_places = ((lax.rem(x + core, 2), lax.rem(y + 1 - core, 2)), (x, 1 - y))
    up, down = grid.device(z + 1, x, y, core), grid.device(z - 1, x, y, core)
    u_devices = [grid.device(z, *place, core) for place in u_places]
    v_devices = [grid.device(z, *place, core) for place in v_places]
    sibling = grid.device(z, x, y, 1 - core)
    has_up, has_down = z < tall - 1, z > 0
    me = grid.flat(z, x, y, core)
    f_side, f_y, f_far = y * 2 + 1 - core, (1 - y) * 2 + core, (1 - y) * 2 + 1 - core

    @pl.loop(1, grid.dp)
    def _(step):
        greet((lax.rem(d + step, grid.dp), f))

    greet((d, f_y))
    greet(sibling)
    vocab_rows = table_hbm.shape[0]
    fetch = pltpu.make_async_copy(table_hbm, table.at[pl.ds(0, vocab_rows), :], table_sem)
    wide = (in_wide, out_wide, up_wide, proj_wide, down_wide)
    for k, ref in enumerate((in_ref, out_ref, up_ref, proj_ref, down_ref)):
        pltpu.make_async_copy(ref, wide[k], wide_sem.at[k]).start()
    fetch.start()
    at = 0
    for k, ref in enumerate((in_ref, out_ref, up_ref, proj_ref, down_ref)):
        pltpu.make_async_copy(ref, wide[k], wide_sem.at[k]).wait()
        if k < 4:
            packed_mine[:, at : at + ref.shape[1]] = wide[k][...].astype(jnp.bfloat16)
            at += ref.shape[1]
    down_mine[...] = down_wide[...].astype(jnp.bfloat16)
    local = [pltpu.make_async_copy(srcs[m], outs[m].at[me], own_sem.at[m]) for m in range(count)]
    for item in local:
        item.start()
    meet(grid.dp + 1)

    def copy(m, shard, device, way, own):
        return pltpu.make_async_remote_copy(
            src_ref=srcs[m] if own else outs[m].at[shard],
            dst_ref=outs[m].at[shard],
            send_sem=send_sem.at[way, m, shard],
            recv_sem=recv_sem.at[m, shard],
            device_id=device,
            device_id_type=MESH,
        )

    def send(shard, device, way, own=False):
        for m in range(count):
            copy(m, shard, device[m] if isinstance(device, list) else device, way, own).start()

    def arrived(shard):
        for m in range(count):
            copy(m, shard, sibling, 4, False).wait_recv()

    def sent(shard, device, way):
        for m in range(count):
            copy(m, shard, device[m] if isinstance(device, list) else device, way, False).wait_send()

    @pl.when(has_up)
    def _():
        send(me, up, 0, True)

    @pl.when(has_down)
    def _():
        send(me, down, 1, True)

    send(me, u_devices, 2, True)
    send(me, v_devices, 3, True)
    send(me, sibling, 4, True)

    tokens = col_ref.shape[0]
    chunk = 128
    ids_row = row_ref[...]
    place_row = lax.broadcasted_iota(jnp.int32, (chunk, tokens), 1)
    place_col = lax.broadcasted_iota(jnp.int32, (chunk, tokens), 0)

    def see(step, repeated):
        start = pl.multiple_of(step * chunk, chunk)
        again = (col_ref[pl.ds(start, chunk), :] == ids_row) & (place_col + start < place_row)
        return jnp.maximum(repeated, jnp.max(jnp.where(again, 1.0, 0.0), 0, keepdims=True))

    repeated = lax.fori_loop(0, tokens // chunk, see, jnp.zeros((1, tokens), jnp.float32))
    firsts = jnp.where(repeated > 0.5, -1.0, ids_row)
    lane = lax.broadcasted_iota(jnp.int32, (chunk, 128), 1).astype(jnp.float32)

    def rank_some(step, carry):
        listed, most = carry
        start = pl.multiple_of(step * chunk, chunk)
        ids = col_ref[pl.ds(start, chunk), :]
        owner = jnp.zeros_like(ids)
        for other in range(1, grid.dp):
            owner = owner + jnp.where(ids >= float(other * vocab_rows), 1.0, 0.0)
        first_id = owner * float(vocab_rows)
        rank = jnp.sum(jnp.where((firsts >= first_id) & (firsts < ids), 1.0, 0.0), 1, keepdims=True)
        slot = jnp.where(rank < float(CAP), owner * float(CAP) + rank, -1.0)
        slot_ref[pl.ds(start, chunk), :] = slot
        rows = []
        for other in range(grid.dp):
            hit = (slot == lane + float(other * CAP)) & (lane < float(CAP))
            rows.append(jnp.max(jnp.where(hit, ids - first_id + 1.0, 0.0), 0, keepdims=True))
        return (jnp.maximum(listed, jnp.concatenate(rows, 0)), jnp.maximum(most, jnp.max(rank, 0, keepdims=True)))

    listed, most = lax.fori_loop(
        0,
        tokens // chunk,
        rank_some,
        (jnp.zeros((grid.dp, 128), jnp.float32), jnp.zeros((1, 1), jnp.float32)),
    )
    spilled = jnp.broadcast_to(jnp.where(most >= float(CAP), 1.0, 0.0), (1, 128))
    rest = jnp.concatenate([negative_ref[...], spilled, jnp.zeros((5, 128), jnp.float32)], 0)
    for other in range(grid.dp):
        messages[other] = jnp.concatenate([listed[other : other + 1] - 1.0, rest], 0)

    def note(peer, slot):
        return pltpu.make_async_remote_copy(
            src_ref=messages.at[peer],
            dst_ref=heard.at[slot],
            send_sem=note_send.at[peer],
            recv_sem=note_recv.at[slot],
            device_id=(peer, f),
            device_id_type=MESH,
        )

    def note_onward(slot, to_side):
        return pltpu.make_async_remote_copy(
            src_ref=heard.at[slot],
            dst_ref=heard.at[slot],
            send_sem=note_on.at[1 if to_side else 0, slot],
            recv_sem=note_recv.at[slot],
            device_id=(d, f_side if to_side else f_y),
            device_id_type=MESH,
        )

    @pl.loop(1, grid.dp)
    def _(step):
        note(lax.rem(d + step, grid.dp), me).start()

    heard[me] = messages[d]

    def row_copy(peer, slot):
        return pltpu.make_async_remote_copy(
            src_ref=answers.at[peer],
            dst_ref=found.at[slot],
            send_sem=row_send.at[peer],
            recv_sem=row_recv.at[slot],
            device_id=(peer, f),
            device_id_type=MESH,
        )

    def pass_z(k):
        low, high = z - k, z + k

        @pl.when(low >= 0)
        def _():
            shard = grid.flat(low, x, y, core)
            arrived(shard)

            @pl.when(has_up)
            def _():
                send(shard, up, 0)

            send(shard, u_devices, 2)
            send(shard, v_devices, 3)
            send(shard, sibling, 4)

        @pl.when(high < tall)
        def _():
            shard = grid.flat(high, x, y, core)
            arrived(shard)

            @pl.when(has_down)
            def _():
                send(shard, down, 1)

            send(shard, u_devices, 2)
            send(shard, v_devices, 3)
            send(shard, sibling, 4)

    def both(k, action):
        pl.when(z - k >= 0)(lambda: action(z - k))
        if k:
            pl.when(z + k < tall)(lambda: action(z + k))

    def pass_u(level):
        for m in range(count):
            shard = grid.flat(level, *u_places[m], core)
            copy(m, shard, sibling, 4, False).wait_recv()
            copy(m, shard, v_devices[m], 3, False).start()
            copy(m, shard, sibling, 4, False).start()

    def pass_v(level):
        for m in range(count):
            shard = grid.flat(level, *v_places[m], core)
            copy(m, shard, sibling, 4, False).wait_recv()
            copy(m, shard, sibling, 4, False).start()

    def pass_far(level):
        shard = grid.flat(level, 1 - x, 1 - y, core)
        arrived(shard)
        send(shard, sibling, 4)

    both(0, pass_u)

    @pl.loop(1, grid.dp)
    def _(step):
        note(d, lax.rem(d + step, grid.dp) * grid.fs + f).wait_recv()

    @pl.loop(0, grid.dp)
    def _(peer):
        note_onward(peer * grid.fs + f, False).start()
        note_onward(peer * grid.fs + f, True).start()

    pass_z(1)
    fetch.wait()
    padding = table.shape[0] - vocab_rows
    if padding:
        table[vocab_rows:, :] = jnp.zeros((padding, D), jnp.float32)
    asked = jnp.concatenate([heard[peer * grid.fs + f, 0:1, :] for peer in range(grid.dp)], 0)
    asked = jnp.transpose(asked)
    block = ROW_BLOCK
    total[...] = jnp.zeros_like(total)
    lanes = lax.broadcasted_iota(jnp.int32, (CAP, block), 1).astype(jnp.float32)

    def pick(step):
        start = pl.multiple_of(step * block, block)
        some = table[pl.ds(start, block), :].astype(jnp.bfloat16)
        wanted = lanes + (step * block).astype(jnp.float32)
        hot = jnp.concatenate(
            [
                jnp.where(asked[:CAP, peer : peer + 1] == wanted, 1.0, 0.0)
                for peer in range(grid.dp)
            ],
            0,
        ).astype(jnp.bfloat16)
        total[...] += matmul(hot, some)

    steps = table.shape[0] // block
    pl.loop(0, steps)(pick)
    answers[...] = total[...].reshape(answers.shape).astype(jnp.bfloat16)
    found[d] = answers[d]

    @pl.loop(1, grid.dp)
    def _(step):
        row_copy(lax.rem(d + step, grid.dp), d).start()

    both(1, pass_u)
    pass_z(2)
    both(0, pass_v)
    both(2, pass_u)
    pass_z(3)
    both(1, pass_v)
    both(3, pass_u)
    both(0, pass_far)
    both(2, pass_v)
    both(1, pass_far)
    both(3, pass_v)
    both(2, pass_far)
    both(3, pass_far)

    @pl.loop(1, grid.dp)
    def _(step):
        row_copy(d, lax.rem(d + step, grid.dp)).wait_recv()

    slots = grid.dp * CAP
    some = tokens // 4
    wide_lane = lax.broadcasted_iota(jnp.int32, (some, slots), 1).astype(jnp.float32)
    rows = found[...].reshape(slots, D)

    @pl.loop(0, 4)
    def _(step):
        start = pl.multiple_of(step * some, some)
        hot = jnp.where(slot_ref[pl.ds(start, some), :] == wide_lane, 1.0, 0.0).astype(jnp.bfloat16)
        x0_ref[pl.ds(start, some), :] = matmul(hot, rows)

    @pl.loop(0, grid.dp)
    def _(peer):
        note(d, peer * grid.fs + f_y).wait_recv()
        note_onward(peer * grid.fs + f_y, True).start()

    @pl.loop(0, grid.dp)
    def _(peer):
        note(d, peer * grid.fs + f_side).wait_recv()
        note(d, peer * grid.fs + f_far).wait_recv()
        note_onward(peer * grid.fs + f, False).wait_send()
        note_onward(peer * grid.fs + f, True).wait_send()
        note_onward(peer * grid.fs + f_y, True).wait_send()

    @pl.loop(1, grid.dp)
    def _(step):
        peer = lax.rem(d + step, grid.dp)
        row_copy(peer, d).wait_send()
        note(peer, me).wait_send()

    @pl.loop(0, tall)
    def _(level):
        for xx in range(2):
            for yy in range(2):
                arrived(grid.flat(level, xx, yy, 1 - core))
                sent(grid.flat(level, xx, yy, core), sibling, 4)
        shard = grid.flat(level, x, y, core)

        @pl.when((level <= z) & has_up)
        def _():
            sent(shard, up, 0)

        @pl.when((level >= z) & has_down)
        def _():
            sent(shard, down, 1)

        sent(shard, u_devices, 2)
        sent(shard, v_devices, 3)
        for m in range(count):
            other = grid.flat(level, *u_places[m], core)
            copy(m, other, v_devices[m], 3, False).wait_send()

    for item in local:
        item.wait()


def run_head(ids, negatives, attn_in, attn_out, ffn_in, proj_head, ffn_out, table, number):
    grid = Grid()
    tokens = ids.shape[0]
    wide = ids.astype(jnp.float32)
    row = jnp.zeros((1, 128), jnp.float32).at[0, : negatives.shape[0]].set(negatives.astype(jnp.float32))
    shapes = ((attn_in.shape[0], PACKED), ffn_out.shape)
    blocks = -(-table.shape[0] // ROW_BLOCK)
    anywhere, inside = pl.BlockSpec(memory_space=pl.ANY), pl.BlockSpec(memory_space=pltpu.VMEM)
    dma = pltpu.SemaphoreType.DMA
    line, everyone = dma((grid.dp,)), dma((grid.total,))
    return pl.pallas_call(
        functools.partial(head_kernel, grid),
        out_shape=[jax.ShapeDtypeStruct((grid.total,) + shape, jnp.bfloat16) for shape in shapes]
        + [
            jax.ShapeDtypeStruct((grid.total, 8, 128), jnp.float32),
            jax.ShapeDtypeStruct((tokens, 1), jnp.float32),
            jax.ShapeDtypeStruct((tokens, D), jnp.float32),
        ],
        in_specs=[inside] * 3 + [anywhere] * 6,
        out_specs=[anywhere] * 2 + [inside] * 3,
        scratch_shapes=[pltpu.VMEM(shape, jnp.bfloat16) for shape in shapes]
        + [
            pltpu.VMEM((blocks * ROW_BLOCK, D), jnp.float32),
            pltpu.VMEM((grid.dp * CAP, D), jnp.float32),
            pltpu.VMEM((grid.dp, CAP, D), jnp.bfloat16),
            pltpu.VMEM((grid.dp, CAP, D), jnp.bfloat16),
            pltpu.VMEM((grid.dp, 8, 128), jnp.float32),
        ]
        + [
            pltpu.VMEM(array.shape, jnp.float32)
            for array in (attn_in, attn_out, ffn_in, proj_head, ffn_out)
        ]
        + [
            dma((5, 2, grid.total)),
            dma((2, grid.total)),
            dma((2,)),
            line,
            line,
            line,
            everyone,
            dma((2, grid.total)),
            dma,
            dma((5,)),
        ],
        compiler_params=pltpu.CompilerParams(
            collective_id=number, has_side_effects=True, vmem_limit_bytes=62 * 1024 * 1024
        ),
    )(wide.reshape(tokens, 1), wide.reshape(1, tokens), row, attn_in, attn_out, ffn_in, proj_head, ffn_out, table)


def lane_is(shape, low, high):
    lanes = lax.broadcasted_iota(jnp.int32, shape, len(shape) - 1)
    return (lanes >= low) & (lanes < high)


def gelu_parts(t):
    inner = np.float32(np.sqrt(2 / np.pi)) * (t + 0.044715 * (t * t * t))
    tan = jnp.tanh(inner)
    return 0.5 * (1.0 + tan), tan


def forward_kernel(
    x0_ref,
    mask_col_ref,
    gains_ref,
    bias_ref,
    packed_hbm,
    down_hbm,
    mixed_ref,
    attended_ref,
    total_ref,
    after_ref,
    pre_ref,
    final_ref,
    pooled_ref,
    projected_ref,
    packed,
    down,
    load_sem,
):
    step = pl.program_id(0)
    tile_seqs = x0_ref.shape[0] // L
    edges = (0, WIDE, WIDE + D, WIDE + 5 * D, PACKED)

    def load(k):
        if k == 4:
            return pltpu.make_async_copy(down_hbm, down, load_sem.at[k])
        part = pl.ds(edges[k], edges[k + 1] - edges[k])
        return pltpu.make_async_copy(packed_hbm.at[:, part], packed.at[:, part], load_sem.at[k])

    def loaded(k):
        @pl.when(step == 0)
        def _():
            load(k).wait()

    @pl.when(step == 0)
    def _():
        for k in (0, 1, 2, 4, 3):
            load(k).start()

    x0 = x0_ref[...]
    act_one = normalize(x0, gains_ref[0:1, :])[0].astype(jnp.bfloat16)
    loaded(0)
    for at in range(0, WIDE, D):
        mixed_ref[:, at : at + D] = matmul(act_one, packed[:, at : at + D]).astype(jnp.bfloat16)

    zero = jnp.zeros((), jnp.bfloat16)
    for s in range(tile_seqs):
        rows = slice(s * L, (s + 1) * L)
        keep = jnp.where(mask_col_ref[rows, :] > 0, 0.0, -1000000000.0)
        for pair in range(HEADS // 2):
            at = pair * 128
            query = mixed_ref[rows, at : at + 128]
            key = mixed_ref[rows, D + at : D + at + 128]
            value = mixed_ref[rows, 2 * D + at : 2 * D + at + 128]
            mine = lane_is((L, 128), 0, HD)
            keys = jnp.concatenate([jnp.where(mine, key, zero), jnp.where(mine, zero, key)], 0)
            scores = (matmul_nt(keys, query) * SCALE).reshape(2, L, L)
            scores = scores + bias_ref[2 * pair : 2 * pair + 2] + keep[None]
            row_max = jnp.max(scores, 1, keepdims=True)
            powers = jnp.exp(scores - row_max)
            row_sum = jnp.sum(powers, 1, keepdims=True)
            prob = (powers * (1.0 / row_sum)).astype(jnp.bfloat16)
            total_ref[s, 2 * pair : 2 * pair + 2, :] = (row_max + jnp.log(row_sum))[:, 0, :]
            flipped = jnp.transpose(value)
            both = jnp.concatenate([matmul(flipped[:HD], prob[0]), matmul(flipped[HD:], prob[1])], 0)
            both = jnp.transpose(both)
            attended_ref[rows, at : at + 128] = both.astype(jnp.bfloat16)

    loaded(1)
    after = x0 + matmul(attended_ref[...], packed[:, WIDE : WIDE + D])
    after_ref[...] = after
    act_two = normalize(after, gains_ref[1:2, :])[0].astype(jnp.bfloat16)
    loaded(2)
    loaded(4)
    final = after
    for j in range(4):
        at = WIDE + D + j * D
        pre = matmul(act_two, packed[:, at : at + D])
        pre_ref[:, j * D : (j + 1) * D] = pre
        hidden = (pre * gelu_parts(pre)[0]).astype(jnp.bfloat16)
        final = final + matmul(hidden, down[j * D : (j + 1) * D, :])
    final_ref[...] = final
    normed = normalize(final, gains_ref[2:3, :])[0]
    weight = mask_col_ref[...]
    for s in range(tile_seqs):
        rows = slice(s * L, (s + 1) * L)
        count = jnp.sum(weight[rows], 0, keepdims=True)
        row = jnp.sum(normed[rows] * weight[rows], 0, keepdims=True) / count
        pooled_ref[pl.ds(step * tile_seqs + s, 1), :] = row

    @pl.when(step == pl.num_programs(0) - 1)
    def _():
        load(3).wait()
        projected_ref[...] = matmul(pooled_ref[...].astype(jnp.bfloat16), packed[:, PACKED - D :])


def run_forward(x0, mask_col, gains, bias_full, packed, down):
    tokens = x0.shape[0]
    seqs = tokens // L
    tile = TILE_SEQS * L
    steps = tokens // tile

    def rows(width):
        return pl.BlockSpec((tile, width), lambda i: (i, 0))

    def whole(*shape):
        return pl.BlockSpec(shape, lambda i: (0,) * len(shape), pipeline_mode=pl.Buffered(1))

    def kept(width, dtype):
        return jax.ShapeDtypeStruct((tokens, width), dtype)

    anywhere = pl.BlockSpec(memory_space=pl.ANY)
    return pl.pallas_call(
        forward_kernel,
        grid=(steps,),
        out_shape=[
            kept(WIDE, jnp.bfloat16),
            kept(D, jnp.bfloat16),
            jax.ShapeDtypeStruct((seqs, HEADS, L), jnp.float32),
            kept(D, jnp.float32),
            kept(4 * D, jnp.float32),
            kept(D, jnp.float32),
            jax.ShapeDtypeStruct((seqs, D), jnp.float32),
            jax.ShapeDtypeStruct((seqs, D), jnp.float32),
        ],
        in_specs=[
            rows(D),
            rows(1),
            whole(3, D),
            whole(HEADS, L, L),
            anywhere,
            anywhere,
        ],
        out_specs=[rows(WIDE), rows(D), pl.BlockSpec((TILE_SEQS, HEADS, L), lambda i: (i, 0, 0)), rows(D), rows(4 * D), rows(D), whole(seqs, D), whole(seqs, D)],
        scratch_shapes=[
            pltpu.VMEM((D, PACKED), jnp.bfloat16),
            pltpu.VMEM((4 * D, D), jnp.bfloat16),
            pltpu.SemaphoreType.DMA((5,)),
        ],
        compiler_params=pltpu.CompilerParams(vmem_limit_bytes=60 * 1024 * 1024),
    )(x0, mask_col, gains, bias_full, packed, down)


def loss_kernel(
    grid, pairs_here, projected_ref, target_ref, scale_ref, grad_ref, loss_ref, others, grads, send_sem, recv_sem
):
    z, x, y, core = grid.here()
    tall = grid.tall
    each = 2 * pairs_here
    half = D // 2
    x_device, y_device = grid.device(z, 1 - x, y, core), grid.device(z, x, 1 - y, core)
    sibling = grid.device(z, x, y, 1 - core)

    def other_levels(action):
        @pl.loop(1, tall)
        def _(step):
            action(lax.rem(z + step, tall))

    greet(x_device)
    greet(y_device)
    greet(sibling)
    other_levels(lambda level: greet(grid.device(level, x, y, core)))
    projected = projected_ref[...]
    factor = lax.rsqrt(jnp.sum(projected * projected, -1, keepdims=True) + EPS)
    unit = projected * factor
    others[core, z, x, y] = jnp.concatenate([unit[:, :half], unit[:, half:]], 0).astype(jnp.bfloat16)
    meet(tall + 2)

    def remote(blocks, device, sent, received):
        return pltpu.make_async_remote_copy(
            src_ref=blocks,
            dst_ref=blocks,
            send_sem=send_sem.at[sent],
            recv_sem=recv_sem.at[received],
            device_id=device,
            device_id_type=MESH,
        )

    along_x = remote(others.at[core, z, x, y], x_device, 0, 0)
    along_x.start()
    along_x.wait_recv()
    along_y = [remote(others.at[core, z, xx, y], y_device, 1 + xx, 1 + xx) for xx in range(2)]
    for copy in along_y:
        copy.start()
    for copy in along_y:
        copy.wait_recv()

    def along_z(level, origin):
        return remote(others.at[core, origin], grid.device(level, x, y, core), 3 + level, 3 + origin)

    def to_side(level):
        return remote(others.at[core, level], sibling, 3 + tall + level, 3 + tall + level)

    other_levels(lambda level: along_z(level, z).start())
    to_side(z).start()

    def pass_side(level):
        along_z(level, level).wait_recv()
        to_side(level).start()

    other_levels(pass_side)
    for level in range(tall):
        to_side(level).wait_recv()
    me = ((core * tall + z) * 2 + x) * 2 + y

    count = grid.total * each
    wide = others[...].reshape(grid.total, 2 * each, half).astype(jnp.float32)
    units = jnp.concatenate(
        [wide[:, :each].reshape(count, half), wide[:, each:].reshape(count, half)], 1
    ).astype(jnp.bfloat16)
    similar = matmul_nt(units, units)
    row = lax.broadcasted_iota(jnp.int32, (count, count), 0)
    column = lax.broadcasted_iota(jnp.int32, (count, count), 1)
    used = (lax.rem(row, each) < pairs_here) & (lax.rem(column, each) >= pairs_here)
    own = used & (column == row + pairs_here)
    negative = used & (column == target_ref[...])
    sim_scale = jnp.exp(scale_ref[...])
    own_mask = jnp.where(own, 1.0, 0.0)
    negative_mask = jnp.where(negative, 1.0, 0.0)
    logits = sim_scale * similar - MARGIN * own_mask
    diagonal = jnp.sum(logits * own_mask, 1, keepdims=True)
    hardest = jnp.sum(logits * negative_mask, 1, keepdims=True)
    row_max = jnp.max(jnp.where(used, logits, -3e38), 1, keepdims=True)
    powers = jnp.where(used, jnp.exp(jnp.minimum(logits - row_max, 0.0)), 0.0)
    row_sum = jnp.sum(powers, 1, keepdims=True)
    is_query = lax.rem(lax.broadcasted_iota(jnp.int32, (count, 1), 0), each) < pairs_here
    gap = hardest - diagonal
    softplus = jnp.maximum(gap, 0.0) + jnp.log(1.0 + jnp.exp(-jnp.abs(gap)))
    row_sum = jnp.where(is_query, row_sum, 1.0)
    losses = jnp.where(is_query, row_max + jnp.log(row_sum) - diagonal + softplus, 0.0)
    gate = 1.0 / (1.0 + jnp.exp(-gap))
    grad_logits = jnp.where(
        used, powers / row_sum - own_mask + gate * (negative_mask - own_mask), 0.0
    )
    loss_ref[0:1, :] = jnp.broadcast_to(jnp.sum(losses, 0, keepdims=True), (1, 128))
    grad_scale = sim_scale * jnp.sum(
        jnp.sum(grad_logits * similar, 1, keepdims=True), 0, keepdims=True
    )
    loss_ref[1:2, :] = jnp.broadcast_to(grad_scale, (1, 128))
    loss_ref[2:8, :] = jnp.zeros((6, 128), jnp.float32)
    grad_similar = sim_scale * grad_logits
    grads[...] = grad_similar + jnp.transpose(grad_similar)
    first = pl.multiple_of(me * each, each)
    grad_units = matmul(grads[pl.ds(first, each), :].astype(jnp.bfloat16), units)
    grad_units = grad_units.astype(jnp.bfloat16).astype(jnp.float32)
    grad_ref[...] = (
        factor * (grad_units - unit * jnp.sum(grad_units * unit, -1, keepdims=True))
    ).astype(jnp.bfloat16)

    along_x.wait_send()
    for copy in along_y:
        copy.wait_send()
    other_levels(lambda level: along_z(level, level).wait_send())
    for level in range(tall):
        to_side(level).wait_send()


def run_loss(projected, target, log_scale, number):
    grid = Grid()
    each = projected.shape[0]
    count = grid.total * each
    inside = pl.BlockSpec(memory_space=pltpu.VMEM)
    dma = pltpu.SemaphoreType.DMA((3 + 2 * grid.tall,))
    return pl.pallas_call(
        functools.partial(loss_kernel, grid, each // 2),
        out_shape=[
            jax.ShapeDtypeStruct((each, D), jnp.bfloat16),
            jax.ShapeDtypeStruct((8, 128), jnp.float32),
        ],
        in_specs=[inside] * 3,
        out_specs=[inside] * 2,
        scratch_shapes=[
            pltpu.VMEM((2, grid.tall, 2, 2, 2 * each, D // 2), jnp.bfloat16),
            pltpu.VMEM((count, count), jnp.float32),
            dma,
            dma,
        ],
        compiler_params=pltpu.CompilerParams(collective_id=number, has_side_effects=True),
    )(projected, target, log_scale)


class Tree:

    @staticmethod
    def scratch(grid, blocks):
        count, tall = len(blocks), grid.tall
        leads = ((tall, 2, 2), (tall, 2, 2), (tall, 2), (tall,), (tall,), (tall,))
        dma = pltpu.SemaphoreType.DMA
        level, pair = dma((count, tall)), dma((count, tall, 2))
        buffers = [pltpu.VMEM(lead + block, jnp.bfloat16) for lead in leads for block in blocks]
        return buffers + [level, level, level, pair, pair] + [level] * 5

    @staticmethod
    def size(count):
        return 6 * count + 10

    def __init__(self, grid, srcs, scratch):
        count = len(srcs)
        self.grid, self.count, self.srcs = grid, count, srcs
        self.acc, self.from_side, self.from_v, self.from_u, self.from_low, self.from_high = [
            scratch[k * count : (k + 1) * count] for k in range(6)
        ]
        (
            self.load_sem,
            self.side_send,
            self.side_recv,
            self.v_send,
            self.v_recv,
            self.u_send,
            self.u_recv,
            self.z_send,
            self.low_recv,
            self.high_recv,
        ) = scratch[6 * count :]
        z, x, y, core = self.place = grid.here()
        tall = grid.tall
        self.up, self.down = grid.device(z + 1, x, y, core), grid.device(z - 1, x, y, core)
        self.has_up, self.has_down = z < tall - 1, z > 0
        self.u = lax.rem(x + 1 - core, 2), lax.rem(y + core, 2)
        self.v = lax.rem(x + core, 2), lax.rem(y + 1 - core, 2)
        self.u_device = grid.device(z, *self.u, core)
        self.v_device = grid.device(z, *self.v, core)
        self.sibling = grid.device(z, x, y, 1 - core)
        self.levels = [self.level_of(j) for j in range(tall)]

    def greet_all(self):
        greet(self.u_device)
        greet(self.v_device)
        greet(self.sibling)
        greet(self.up, self.has_up)
        greet(self.down, self.has_down)
        return 3 + self.has_up.astype(jnp.int32) + self.has_down.astype(jnp.int32)

    def each(self, action):
        for m in range(self.count):
            action(m)

    def level_of(self, j):
        tall = self.grid.tall
        tables = [
            sorted(range(tall), key=lambda level: (-abs(level - own), -level))[j] for own in range(tall)
        ]
        value = tables[0]
        for own in range(1, tall):
            value = jnp.where(self.place[0] == own, tables[own], value)
        return value

    def load(self, m, level):
        core = self.place[3]
        return pltpu.make_async_copy(
            self.srcs[m].at[level, :, :, core], self.acc[m].at[level], self.load_sem.at[m, level]
        )

    def remote(self, src, dst, send_sem, recv_sem, device):
        return pltpu.make_async_remote_copy(
            src_ref=src,
            dst_ref=dst,
            send_sem=send_sem,
            recv_sem=recv_sem,
            device_id=device,
            device_id_type=MESH,
        )

    def side(self, m, level):
        return self.remote(
            self.srcs[m].at[level, :, :, 1 - self.place[3]],
            self.from_side[m].at[level],
            self.side_send.at[m, level],
            self.side_recv.at[m, level],
            self.sibling,
        )

    def v_copy(self, m, level, along_u):
        z, x, y, core = self.place
        xx, yy = (1 - x, 1 - y) if along_u else self.v
        return self.remote(
            self.acc[m].at[level, xx, yy],
            self.from_v[m].at[level, along_u],
            self.v_send.at[m, level, along_u],
            self.v_recv.at[m, level, along_u],
            self.v_device,
        )

    def u_copy(self, m, level):
        return self.remote(
            self.acc[m].at[level, self.u[0], self.u[1]],
            self.from_u[m].at[level],
            self.u_send.at[m, level],
            self.u_recv.at[m, level],
            self.u_device,
        )

    def z_copy(self, m, level, upward):
        z, x, y, core = self.place
        return self.remote(
            self.acc[m].at[level, x, y],
            (self.from_low if upward else self.from_high)[m].at[level],
            self.z_send.at[m, level],
            (self.low_recv if upward else self.high_recv).at[m, level],
            self.up if upward else self.down,
        )

    def add(self, m, level, xx, yy, other):
        total = self.acc[m][level, xx, yy].astype(jnp.float32) + other.astype(jnp.float32)
        self.acc[m][level, xx, yy] = total.astype(jnp.bfloat16)

    def loads(self):
        for level in self.levels:
            self.each(lambda m: self.load(m, level).start())

    def sides(self):
        for level in self.levels:
            self.each(lambda m: self.side(m, level).start())

    def first(self, j):
        level = self.levels[j]

        def run(m):
            self.load(m, level).wait()
            self.side(m, level).wait_recv()
            for xx in range(2):
                for yy in range(2):
                    self.add(m, level, xx, yy, self.from_side[m][level, xx, yy])
            self.v_copy(m, level, 1).start()
            self.v_copy(m, level, 0).start()

        self.each(run)

    def second(self, j):
        z, x, y, core = self.place
        level = self.levels[j]

        def run(m):
            self.v_copy(m, level, 1).wait_recv()
            self.add(m, level, self.u[0], self.u[1], self.from_v[m][level, 1])
            self.u_copy(m, level).start()

        def run_own(m):
            self.v_copy(m, level, 0).wait_recv()
            self.add(m, level, x, y, self.from_v[m][level, 0])

        self.each(run)
        self.each(run_own)

    def third(self, j):
        z, x, y, core = self.place
        level = self.levels[j]

        def run(m):
            self.u_copy(m, level).wait_recv()
            self.add(m, level, x, y, self.from_u[m][level])

            @pl.when((level >= z) & self.has_down)
            def _():
                self.z_copy(m, level, True).wait_recv()
                self.add(m, level, x, y, self.from_low[m][level])

            @pl.when((level <= z) & self.has_up)
            def _():
                self.z_copy(m, level, False).wait_recv()
                self.add(m, level, x, y, self.from_high[m][level])

            @pl.when(level > z)
            def _():
                self.z_copy(m, level, True).start()

            @pl.when(level < z)
            def _():
                self.z_copy(m, level, False).start()

        self.each(run)

    def own(self, m):
        z, x, y, core = self.place
        return self.acc[m][z, x, y].astype(jnp.float32)

    def drain(self):
        for level in self.levels:
            self.each(lambda m: self.side(m, level).wait_send())
            self.each(lambda m: self.v_copy(m, level, 0).wait_send())
            self.each(lambda m: self.v_copy(m, level, 1).wait_send())
            self.each(lambda m: self.u_copy(m, level).wait_send())

            @pl.when(level != self.place[0])
            def _():
                self.each(lambda m: self.z_copy(m, level, True).wait_send())


def fold(values):
    n, lanes = values.shape
    part = jnp.sum(values.reshape(n // 8, 8, lanes), 0)
    total = part[:, :128]
    for at in range(128, lanes, 128):
        total = total + part[:, at : at + 128]
    return total


def gain_back(gains_ref, grads_ref, k, grad_out, inputs):
    factor = lax.rsqrt(jnp.mean(inputs * inputs, -1, keepdims=True) + EPS)
    scaled = grad_out * gains_ref[k : k + 1, :]
    grads_ref[k : k + 1, :] += jnp.sum(grad_out * inputs * factor, 0, keepdims=True)
    return factor * (
        scaled - inputs * (factor * factor * jnp.mean(scaled * inputs, -1, keepdims=True))
    )


BACK_SEQS = 2
HALF = 256


def ffn_back_kernel(
    final_ref,
    after_ref,
    mask_col_ref,
    gains_ref,
    pooled_ref,
    grad_proj_ref,
    pre_hbm,
    packed_hbm,
    down_hbm,
    grad_after_ref,
    grad_gains_ref,
    grad_up_hbm,
    grad_down_hbm,
    up,
    head,
    down,
    branch,
    act_two,
    hidden,
    grad_pre,
    grad_act,
    pre,
    grad_pooled,
    stage,
    load_sem,
    pre_sem,
    store_sem,
):
    tokens = final_ref.shape[0]
    tile = BACK_SEQS * L

    def load(k):
        if k == 0:
            return pltpu.make_async_copy(packed_hbm.at[:, pl.ds(PACKED - D, D)], head, load_sem.at[0])
        if k == 1:
            return pltpu.make_async_copy(down_hbm, down, load_sem.at[1])
        return pltpu.make_async_copy(packed_hbm.at[:, pl.ds(WIDE + D, 4 * D)], up, load_sem.at[2])

    def load_pre(j):
        return pltpu.make_async_copy(pre_hbm.at[:, pl.ds(j * D, D)], pre.at[j % 2], pre_sem.at[j % 2])

    load(0).start()
    load_pre(0).start()
    load(1).start()
    load(2).start()
    grad_gains_ref[...] = jnp.zeros_like(grad_gains_ref)
    load(0).wait()
    grad_pooled[...] = matmul_nt(grad_proj_ref[...], head[...])

    @pl.loop(0, tokens // tile)
    def _(step):
        rows = pl.ds(pl.multiple_of(step * tile, tile), tile)
        weight = mask_col_ref[rows, :]
        pieces = []
        for s in range(BACK_SEQS):
            part = weight[s * L : (s + 1) * L]
            count = jnp.sum(part, 0, keepdims=True)
            pieces.append(part * (grad_pooled[pl.ds(step * BACK_SEQS + s, 1), :] / count))
        grad = gain_back(gains_ref, grad_gains_ref, 2, jnp.concatenate(pieces, 0), final_ref[rows, :])
        grad_after_ref[rows, :] = grad
        branch[rows, :] = grad.astype(jnp.bfloat16)
        act_two[rows, :] = normalize(after_ref[rows, :], gains_ref[1:2, :])[0].astype(jnp.bfloat16)

    stores = []

    def store(value, to):
        slot = len(stores) % 2
        if len(stores) >= 2:
            stores[-2].wait()
        stage[slot] = value.astype(jnp.bfloat16)
        stores.append(pltpu.make_async_copy(stage.at[slot], to, store_sem.at[slot]))
        stores[-1].start()

    load(1).wait()
    for j in range(4):
        part = slice(j * D, (j + 1) * D)
        if j < 3:
            load_pre(j + 1).start()
        for at in range(0, tokens, HALF):
            rows = slice(at, at + HALF)
            wide = matmul_nt(branch[rows, :], down[part, :])
            if at == 0:
                load_pre(j).wait()
            some = pre[j % 2, rows, :]
            half, tan = gelu_parts(some)
            hidden[rows, :] = (some * half).astype(jnp.bfloat16)
            slope = np.float32(np.sqrt(2 / np.pi)) * (1.0 + (3 * 0.044715) * (some * some))
            slope = half + 0.5 * some * (1.0 - tan * tan) * slope
            grad_pre[rows, :] = (wide * slope).astype(jnp.bfloat16)
            if j == 0:
                if at == 0:
                    load(2).wait()
                grad_act[rows, :] = matmul_nt(grad_pre[rows, :], up[:, part])
            else:
                grad_act[rows, :] += matmul_nt(grad_pre[rows, :], up[:, part])
        store(matmul_tn(hidden[...], branch[...]), grad_down_hbm.at[pl.ds(j * D, D), :])
        store(matmul_tn(act_two[...], grad_pre[...]), grad_up_hbm.at[:, pl.ds(j * D, D)])
    store(
        matmul_tn(pooled_ref[...].astype(jnp.bfloat16), grad_proj_ref[...]),
        grad_up_hbm.at[:, pl.ds(4 * D, D)],
    )

    @pl.loop(0, tokens // tile)
    def _(step):
        rows = pl.ds(pl.multiple_of(step * tile, tile), tile)
        grad = gain_back(gains_ref, grad_gains_ref, 1, grad_act[rows, :], after_ref[rows, :])
        grad_after_ref[rows, :] += grad

    stores[-2].wait()
    stores[-1].wait()


def run_ffn_back(final, after, mask_col, gains, pooled, grad_proj, pre, packed, down):
    tokens, seqs = final.shape[0], pooled.shape[0]
    anywhere, inside = pl.BlockSpec(memory_space=pl.ANY), pl.BlockSpec(memory_space=pltpu.VMEM)

    def low(*shape):
        return pltpu.VMEM(shape, jnp.bfloat16)

    def full(*shape):
        return pltpu.VMEM(shape, jnp.float32)

    return pl.pallas_call(
        ffn_back_kernel,
        out_shape=[
            jax.ShapeDtypeStruct((tokens, D), jnp.float32),
            jax.ShapeDtypeStruct((3, D), jnp.float32),
            jax.ShapeDtypeStruct((D, 5 * D), jnp.bfloat16),
            jax.ShapeDtypeStruct((4 * D, D), jnp.bfloat16),
        ],
        in_specs=[inside] * 6 + [anywhere] * 3,
        out_specs=[inside] * 2 + [anywhere] * 2,
        scratch_shapes=[
            low(D, 4 * D),
            low(D, D),
            low(4 * D, D),
            low(tokens, D),
            low(tokens, D),
            low(tokens, D),
            low(tokens, D),
            full(tokens, D),
            full(2, tokens, D),
            full(seqs, D),
            low(2, D, D),
            pltpu.SemaphoreType.DMA((3,)),
            pltpu.SemaphoreType.DMA((2,)),
            pltpu.SemaphoreType.DMA((2,)),
        ],
        compiler_params=pltpu.CompilerParams(vmem_limit_bytes=62 * 1024 * 1024),
    )(final, after, mask_col, gains, pooled, grad_proj, pre, packed, down)


def attn_back_kernel(grid, *refs):
    x0_ref, mask_col_ref, mixed_ref, attended, total_ref, grad_after_ref, gains_ref, bias_ref, packed_hbm = refs[:9]
    srcs = refs[9:11]
    rows_ref, grad_gains_ref, grad_bias_ref, grad_attn_hbm = refs[11:15]
    outs, square_ref = refs[15:17], refs[17]
    packed, act_one, branch_one, grad_mixed, stage, load_sem, store_sem = refs[18:25]
    tree = Tree(grid, srcs, refs[25:])
    step = pl.program_id(0)
    last_step = pl.num_programs(0) - 1
    tile_seqs = x0_ref.shape[0] // L
    tile = tile_seqs * L
    base = pl.multiple_of(step * tile, tile)

    def load(k):
        part = pl.ds(WIDE, D) if k else pl.ds(0, WIDE)
        return pltpu.make_async_copy(packed_hbm.at[:, part], packed.at[:, part], load_sem.at[k])

    @pl.when(step == 0)
    def _():
        friends = tree.greet_all()
        load(1).start()
        load(0).start()
        tree.loads()
        grad_gains_ref[...] = jnp.zeros_like(grad_gains_ref)
        grad_bias_ref[...] = jnp.zeros_like(grad_bias_ref)
        meet(friends)
        tree.sides()
        load(1).wait()

    rows = pl.ds(base, tile)
    grad_after = grad_after_ref[...]
    weight = mask_col_ref[...]
    branch = grad_after.astype(jnp.bfloat16)
    branch_one[rows, :] = branch
    grad_attended = matmul_nt(branch, packed[:, WIDE:]).astype(jnp.bfloat16)
    act_one[rows, :] = normalize(x0_ref[...], gains_ref[0:1, :])[0].astype(jnp.bfloat16)

    def at_step(number, action, *levels):
        @pl.when(step == number)
        def _():
            for j in levels:
                action(j)

    at_step(0, tree.first, 0, 1)
    at_step(1, tree.second, 0)
    at_step(2, tree.third, 0)
    at_step(3, tree.third, 1)
    zero = jnp.zeros((), jnp.bfloat16)
    mine = lane_is((L, 128), 0, HD)
    for s in range(tile_seqs):
        part = slice(s * L, (s + 1) * L)
        here = pl.ds(pl.multiple_of(base + s * L, L), L)
        keep = jnp.where(weight[part] > 0, 0.0, -1000000000.0)
        for pair in range(HEADS // 2):
            at = pair * 128
            query = mixed_ref[part, at : at + 128]
            key = mixed_ref[part, D + at : D + at + 128]
            value = mixed_ref[part, 2 * D + at : 2 * D + at + 128]
            grad_out = grad_attended[part, at : at + 128]
            keys = jnp.concatenate([jnp.where(mine, key, zero), jnp.where(mine, zero, key)], 0)
            values = jnp.concatenate([jnp.where(mine, value, zero), jnp.where(mine, zero, value)], 0)
            scores = (matmul_nt(keys, query) * SCALE).reshape(2, L, L)
            scores = scores + bias_ref[2 * pair : 2 * pair + 2] + keep[None]
            prob = jnp.exp(scores - total_ref[s, 2 * pair : 2 * pair + 2, :][:, None, :])
            grad_prob = matmul_nt(values, grad_out).reshape(2, L, L)
            mean = jnp.sum(prob * grad_prob, 1, keepdims=True)
            grad_scores = (prob * (grad_prob - mean)).astype(jnp.bfloat16)
            grad_bias_ref[2 * pair : 2 * pair + 2] += grad_scores.astype(jnp.float32)
            prob_low = prob.astype(jnp.bfloat16)
            flipped = jnp.transpose(key)
            grad_query = jnp.concatenate(
                [matmul(flipped[:HD], grad_scores[0]), matmul(flipped[HD:], grad_scores[1])], 0
            )
            grad_mixed[here, at : at + 128] = (jnp.transpose(grad_query) * SCALE).astype(jnp.bfloat16)
            grad_keys = matmul(grad_scores.reshape(2 * L, L), query)
            grad_key = jnp.where(mine, grad_keys[:L], grad_keys[L:]) * SCALE
            grad_mixed[here, D + at : D + at + 128] = grad_key.astype(jnp.bfloat16)
            grad_values = matmul(prob_low.reshape(2 * L, L), grad_out)
            grad_value = jnp.where(mine, grad_values[:L], grad_values[L:])
            grad_mixed[here, 2 * D + at : 2 * D + at + 128] = grad_value.astype(jnp.bfloat16)

    @pl.when(step == 0)
    def _():
        tree.first(2)
        tree.first(3)
        load(0).wait()

    at_step(1, tree.second, 1)
    at_step(2, tree.second, 2)
    at_step(3, tree.second, 3)
    grad_act = matmul_nt(grad_mixed[rows, :], packed[:, :WIDE])
    grad_low = gain_back(gains_ref, grad_gains_ref, 0, grad_act, x0_ref[...])
    rows_ref[...] = (grad_after + grad_low).astype(jnp.bfloat16)

    @pl.when(step == last_step)
    def _():
        tree.third(2)
        jobs = [(attended, branch_one, slice(0, D), 3)]
        for j in range(3):
            jobs.append((act_one, grad_mixed, slice(j * D, (j + 1) * D), j))
        copies = []
        for number, (left, right, part, at) in enumerate(jobs):
            slot = number % 2
            if number >= 2:
                copies[number - 2].wait()
            stage[slot] = matmul_tn(left[...], right[:, part]).astype(jnp.bfloat16)
            to = grad_attn_hbm.at[:, pl.ds(at * D, D)]
            copies.append(pltpu.make_async_copy(stage.at[slot], to, store_sem.at[slot]))
            copies[-1].start()
        tree.third(3)
        square_ref[...] = jnp.zeros_like(square_ref)

        def give(m):
            wide = tree.own(m)
            outs[m][...] = wide
            square_ref[0:8, :] += fold(wide * wide)

        tree.each(give)
        copies[-2].wait()
        copies[-1].wait()
        tree.drain()


def run_attn_back(
    x0, mask_col, mixed, attended, totals, grad_after, gains, bias_full, packed, grad_up, grad_down, number
):
    grid = Grid()
    tokens = x0.shape[0]
    tile = BACK_SEQS * L
    steps = tokens // tile
    srcs = [grad.reshape(grid.total, -1, grad.shape[1]) for grad in (grad_up, grad_down)]
    blocks = [src.shape[1:] for src in srcs]
    srcs = [src.reshape((grid.tall, 2, 2, 2) + src.shape[1:]) for src in srcs]

    def rows(width):
        return pl.BlockSpec((tile, width), lambda i: (i, 0))

    def whole(*shape):
        return pl.BlockSpec(shape, lambda i: (0,) * len(shape), pipeline_mode=pl.Buffered(1))

    def low(*shape):
        return pltpu.VMEM(shape, jnp.bfloat16)

    anywhere = pl.BlockSpec(memory_space=pl.ANY)
    return pl.pallas_call(
        functools.partial(attn_back_kernel, grid),
        grid=(steps,),
        out_shape=[
            jax.ShapeDtypeStruct((tokens, D), jnp.bfloat16),
            jax.ShapeDtypeStruct((1, D), jnp.float32),
            jax.ShapeDtypeStruct((HEADS, L, L), jnp.float32),
            jax.ShapeDtypeStruct((D, WIDE + D), jnp.bfloat16),
        ]
        + [jax.ShapeDtypeStruct(block, jnp.float32) for block in blocks]
        + [jax.ShapeDtypeStruct((16, 128), jnp.float32)],
        in_specs=[
            rows(D),
            rows(1),
            rows(WIDE),
            whole(tokens, D),
            pl.BlockSpec((BACK_SEQS, HEADS, L), lambda i: (i, 0, 0)),
            rows(D),
            whole(3, D),
            whole(HEADS, L, L),
            anywhere,
            anywhere,
            anywhere,
        ],
        out_specs=[rows(D), whole(1, D), whole(HEADS, L, L), anywhere]
        + [whole(*block) for block in blocks]
        + [whole(16, 128)],
        scratch_shapes=[
            low(D, WIDE + D),
            low(tokens, D),
            low(tokens, D),
            low(tokens, WIDE),
            low(2, D, D),
            pltpu.SemaphoreType.DMA((2,)),
            pltpu.SemaphoreType.DMA((2,)),
        ]
        + Tree.scratch(grid, blocks),
        compiler_params=pltpu.CompilerParams(
            collective_id=number, has_side_effects=True, vmem_limit_bytes=62 * 1024 * 1024
        ),
    )(x0, mask_col, mixed, attended, totals, grad_after, gains, bias_full, packed, *srcs)


def finish_kernel(grid, count, *refs):
    srcs, (grad_rows, slot_ref, ids, small, square_ref) = refs[:count], refs[count : count + 5]
    refs = refs[count + 5 :]
    outs, (table_out, small_out, square_out) = refs[:count], refs[count : count + 3]
    refs = refs[count + 3 :]
    tree = Tree(grid, srcs, refs[: Tree.size(count)])
    refs = refs[Tree.size(count) :]
    sums, rows, part_sums, small_stage, small_in, square_stage, square_in = refs[:7]
    line_send, on_send, row_recv, small_send, small_recv, square_send, square_recv = refs[7:]
    z, x, y, core = grid.here()
    tall = grid.tall
    d, f = lax.axis_index("dp"), lax.axis_index("fsdp")
    me = f * grid.dp + d
    sibling = tree.sibling
    f_side = y * 2 + 1 - core
    f_y = (1 - y) * 2 + core
    f_far = (1 - y) * 2 + 1 - core
    for level in range(tall):
        small_in[3 + level] = jnp.zeros(small.shape, jnp.float32)
        square_in[3 + level] = jnp.zeros((16, 128), jnp.float32)
    x_device, y_device = grid.device(z, 1 - x, y, core), grid.device(z, x, 1 - y, core)

    @pl.loop(1, grid.dp)
    def _(step):
        greet((lax.rem(d + step, grid.dp), f))

    greet(y_device)
    greet(sibling)

    def line(peer, slot):
        return pltpu.make_async_remote_copy(
            src_ref=sums.at[peer],
            dst_ref=rows.at[slot],
            send_sem=line_send.at[peer],
            recv_sem=row_recv.at[slot],
            device_id=(peer, f),
            device_id_type=MESH,
        )

    def onward(slot, to_side, own_block=False):
        return pltpu.make_async_remote_copy(
            src_ref=sums.at[d] if own_block else rows.at[slot],
            dst_ref=rows.at[slot],
            send_sem=on_send.at[1 if to_side else 0, slot],
            recv_sem=row_recv.at[slot],
            device_id=(d, f_side if to_side else f_y),
            device_id_type=MESH,
        )

    def total_of(stage, inbox, send_sem, recv_sem):
        partners = (sibling, x_device, y_device)

        def copy(r):
            return pltpu.make_async_remote_copy(
                src_ref=stage.at[r],
                dst_ref=inbox.at[r],
                send_sem=send_sem.at[r],
                recv_sem=recv_sem.at[r],
                device_id=partners[r],
                device_id_type=MESH,
            )

        def z_send(level, slot):
            return pltpu.make_async_remote_copy(
                src_ref=stage.at[3],
                dst_ref=inbox.at[3 + slot],
                send_sem=send_sem.at[3 + level],
                recv_sem=recv_sem.at[3 + slot],
                device_id=grid.device(level, x, y, core),
                device_id_type=MESH,
            )

        def others(action):
            @pl.loop(1, tall)
            def _(step):
                action(lax.rem(z + step, tall))

        def send(r):
            if r < 3:
                copy(r).start()
            else:
                others(lambda level: z_send(level, z).start())

        def take(r):
            if r < 3:
                copy(r).wait_recv()
                stage[r + 1] = stage[r] + inbox[r]
                send(r + 1)
            else:
                others(lambda level: z_send(level, level).wait_recv())

        def result():
            total = stage[3]
            for level in range(tall):
                total = total + jnp.where(z == level, 0.0, inbox[3 + level])
            for r in range(3):
                copy(r).wait_send()
            others(lambda level: z_send(level, level).wait_send())
            return total

        return send, take, result

    small_stage[0] = small[...]
    small_sends, small_take, small_result = total_of(small_stage, small_in, small_send, small_recv)
    square_sends, square_take, square_result = total_of(square_stage, square_in, square_send, square_recv)
    tree.loads()
    meet(grid.dp + 1)
    small_sends(0)
    tree.sides()
    cap = sums.shape[1]
    lanes = lax.broadcasted_iota(jnp.int32, (1, cap), 1).astype(jnp.float32)

    def sum_of(peer):
        hot = jnp.where(slot_ref[...] == lanes + (peer * cap).astype(jnp.float32), 1.0, 0.0)
        return matmul_tn(hot.astype(jnp.bfloat16), grad_rows[...]).astype(jnp.bfloat16)

    @pl.loop(1, grid.dp)
    def _(step):
        peer = lax.rem(d + step, grid.dp)
        sums[peer] = sum_of(peer)
        line(peer, me).start()

    own_sum = sum_of(d)
    sums[d] = own_sum
    rows[me] = own_sum
    onward(me, False, True).start()
    onward(me, True, True).start()

    def pass_lines():
        @pl.loop(1, grid.dp)
        def _(step):
            slot = f * grid.dp + lax.rem(d + grid.dp - step, grid.dp)
            line(d, slot).wait_recv()
            onward(slot, False).start()
            onward(slot, True).start()

    def pass_y():
        @pl.loop(0, grid.dp)
        def _(step):
            slot = f_y * grid.dp + lax.rem(d + grid.dp - step, grid.dp)
            line(d, slot).wait_recv()
            onward(slot, True).start()

    def rows_in(column):
        @pl.loop(0, grid.dp)
        def _(step):
            line(d, column * grid.dp + step).wait_recv()

    table_rows = table_out.shape[0]
    whole_blocks = table_rows // ROW_BLOCK
    square_stage[0] = square_ref[...]

    per = grid.dp * rows.shape[1]

    def product(column, start, size):
        place = start + lax.broadcasted_iota(jnp.int32, (size, per), 0)
        hot = jnp.where(place.astype(jnp.float32) == ids[pl.ds(column, 1), :], 1.0, 0.0)
        some = rows[pl.ds(column * grid.dp, grid.dp)].reshape(per, D)
        return matmul(hot.astype(jnp.bfloat16), some)

    def spread_near():
        @pl.loop(0, part_sums.shape[0] // ROW_BLOCK)
        def _(block):
            start = pl.multiple_of(block * ROW_BLOCK, ROW_BLOCK)
            part_sums[pl.ds(start, ROW_BLOCK), :] = product(f, start, ROW_BLOCK) + product(
                f_side, start, ROW_BLOCK
            )

    def spread(start, size):
        total = part_sums[pl.ds(start, size), :] + product(f_y, start, size) + product(f_far, start, size)
        low = total.astype(jnp.bfloat16)
        table_out[pl.ds(start, size), :] = low
        wide = low.astype(jnp.float32)
        square_stage[0, 8:16, :] += fold(wide * wide)

    def spread_all():
        @pl.loop(0, whole_blocks)
        def _(block):
            spread(pl.multiple_of(block * ROW_BLOCK, ROW_BLOCK), ROW_BLOCK)

        if table_rows % ROW_BLOCK:
            spread(whole_blocks * ROW_BLOCK, table_rows % ROW_BLOCK)

    for j in range(tall):
        tree.first(j)
        if j < 3:
            small_take(j)
    pass_lines()
    tree.second(0)
    tree.second(1)
    rows_in(f_side)
    spread_near()
    tree.third(0)
    tree.second(2)
    pass_y()
    tree.third(1)
    tree.second(3)
    tree.third(2)
    rows_in(f_far)
    spread_all()
    tree.third(3)

    def give(m):
        wide = tree.own(m)
        outs[m][...] = wide
        square_stage[0, 0:8, :] += fold(wide * wide)

    tree.each(give)

    square_sends(0)
    small_take(3)
    small_out[...] = small_result()
    for r in range(3):
        square_take(r)

    tree.drain()

    @pl.loop(0, grid.dp)
    def _(step):
        onward(f * grid.dp + step, False).wait_send()
        onward(f * grid.dp + step, True).wait_send()
        onward(f_y * grid.dp + step, True).wait_send()

    @pl.loop(1, grid.dp)
    def _(step):
        line(lax.rem(d + step, grid.dp), me).wait_send()

    square_take(3)
    square_out[...] = square_result()


def finish(srcs, grad_rows, slot, ids, small, squares, vocab_rows, number):
    grid = Grid()
    count = len(srcs)
    tall = grid.tall
    blocks = [src.shape[1:] for src in srcs]
    srcs = [src.reshape((tall, 2, 2, 2) + src.shape[1:]) for src in srcs]
    dma = pltpu.SemaphoreType.DMA
    by_device, by_step = dma((grid.total,)), dma((3 + tall,))
    scratch = Tree.scratch(grid, blocks) + [
        pltpu.VMEM((grid.dp, CAP, D), jnp.bfloat16),
        pltpu.VMEM((grid.total, CAP, D), jnp.bfloat16),
        pltpu.VMEM((-(-vocab_rows // ROW_BLOCK) * ROW_BLOCK, D), jnp.float32),
        pltpu.VMEM((4,) + small.shape, jnp.float32),
        pltpu.VMEM((3 + tall,) + small.shape, jnp.float32),
        pltpu.VMEM((4, 16, 128), jnp.float32),
        pltpu.VMEM((3 + tall, 16, 128), jnp.float32),
        dma((grid.dp,)),
        dma((2, grid.total)),
        by_device,
    ]
    anywhere, inside = pl.BlockSpec(memory_space=pl.ANY), pl.BlockSpec(memory_space=pltpu.VMEM)
    results = pl.pallas_call(
        functools.partial(finish_kernel, grid, count),
        out_shape=[jax.ShapeDtypeStruct(block, jnp.float32) for block in blocks]
        + [
            jax.ShapeDtypeStruct((vocab_rows, D), jnp.bfloat16),
            jax.ShapeDtypeStruct(small.shape, jnp.float32),
            jax.ShapeDtypeStruct((16, 128), jnp.float32),
        ],
        in_specs=[anywhere] * count + [inside] * 5,
        out_specs=[inside] * (count + 3),
        scratch_shapes=scratch + [by_step] * 4,
        compiler_params=pltpu.CompilerParams(
            collective_id=number, has_side_effects=True, vmem_limit_bytes=62 * 1024 * 1024
        ),
    )(*srcs, grad_rows, slot, ids, small, squares)
    return (results[:count], *results[count:])


def update_kernel(fs, *refs):
    squares, summed, scale_grad, table, table_first, table_second, table_grad = refs[:7]
    rest, shards = refs[7:22], refs[22:25]
    norm_ref, out_first, out_second, out = refs[25:29]
    rest_outs, factor_ref = refs[29:44], refs[44]

    def row_sum(values):
        return jnp.sum(jnp.sum(values, 1, keepdims=True), 0, keepdims=True)

    @pl.when(pl.program_id(0) == 0)
    def _():
        total = row_sum(squares[0:8, :]) + row_sum(squares[8:16, :]) / float(fs)
        total = total + (row_sum(summed[...] * summed[...]) + scale_grad[...] * scale_grad[...])
        norm = jnp.sqrt(total)
        norm_ref[...] = jnp.broadcast_to(norm, norm_ref.shape)
        factor_ref[...] = jnp.minimum(1.0, CLIP / (norm + 1e-06))
        attn, up, down = shards
        grads = (attn[:, :WIDE], attn[:, WIDE:], up[:, : 4 * D], down[...], up[:, 4 * D :])
        for k in range(5):
            first_new, second_new, new = adam_update(
                *[ref[...] for ref in rest[3 * k : 3 * k + 3]],
                grads[k],
                factor_ref[...],
                RATES[k + 1],
                DECAYS[k + 1],
            )
            rest_outs[3 * k][...] = first_new
            rest_outs[3 * k + 1][...] = second_new
            rest_outs[3 * k + 2][...] = new

    first_new, second_new, new = adam_update(
        table[...],
        table_first[...],
        table_second[...],
        table_grad[...].astype(jnp.float32),
        factor_ref[...],
        RATES[0],
        DECAYS[0],
    )
    out_first[...] = first_new
    out_second[...] = second_new
    out[...] = new


def run_update(fs, squares, summed, scale_grad, table_arrays, table_grad, rest, shards):
    vocab_rows = table_grad.shape[0]
    blocks = pl.BlockSpec((ROW_BLOCK, D), lambda i: (i, 0))

    def whole(array):
        return pl.BlockSpec(
            array.shape, lambda i: (0,) * array.ndim, pipeline_mode=pl.Buffered(1)
        )

    norm = jax.ShapeDtypeStruct((8, 128), jnp.float32)
    return pl.pallas_call(
        functools.partial(update_kernel, fs),
        grid=(-(-vocab_rows // ROW_BLOCK),),
        out_shape=[norm]
        + [jax.ShapeDtypeStruct(table_grad.shape, jnp.float32)] * 3
        + [jax.ShapeDtypeStruct(array.shape, jnp.float32) for array in rest],
        in_specs=[whole(squares), whole(summed), whole(scale_grad)]
        + [blocks] * 4
        + [whole(array) for array in (*rest, *shards)],
        out_specs=[whole(norm)] + [blocks] * 3 + [whole(array) for array in rest],
        scratch_shapes=[pltpu.VMEM((1, 1), jnp.float32)],
        compiler_params=pltpu.CompilerParams(vmem_limit_bytes=60 * 1024 * 1024),
    )(squares, summed, scale_grad, *table_arrays, table_grad, *rest, *shards)


def plain_body(
    token_ids,
    pad_mask,
    hard_negative,
    table,
    table_first,
    table_second,
    attn_in,
    attn_in_first,
    attn_in_second,
    attn_out,
    attn_out_first,
    attn_out_second,
    ffn_in,
    ffn_in_first,
    ffn_in_second,
    ffn_out,
    ffn_out_first,
    ffn_out_second,
    proj_head,
    proj_head_first,
    proj_head_second,
    small_params,
    small_first,
    small_second,
):
    dp_count = lax.axis_size("dp")
    fsdp_count = lax.axis_size("fsdp")
    device_flat = lax.axis_index("dp") * fsdp_count + lax.axis_index("fsdp")
    pairs_here = token_ids.shape[1]
    pairs_total = pairs_here * dp_count * fsdp_count
    seq_count = 2 * pairs_here
    vocab_rows = table.shape[0]
    row_base = lax.axis_index("dp") * vocab_rows
    gain_rows = small_params[: 3 * D].reshape(3, D)
    bias_table = small_params[3 * D : 3 * D + NB * HEADS].reshape(NB, HEADS)
    log_scale = small_params[3 * D + NB * HEADS]
    buckets = jnp.asarray(bucket_table(L, NB).reshape(-1), jnp.int32)
    bucket_hot = (buckets[:, None] == jnp.arange(NB, dtype=jnp.int32)[None, :]).astype(jnp.float32)
    bias_full = (
        jnp.dot(bucket_hot, bias_table, precision=HIGH).reshape(L, L, HEADS).transpose(2, 0, 1)
    )
    mask_rows = pad_mask.reshape(seq_count, L)
    ids_flat = token_ids.reshape(-1)
    table_low = table.astype(jnp.bfloat16)
    ids_all = lax.all_gather(ids_flat, "dp", axis=0, tiled=True)
    picked = ids_all - row_base
    inside = (picked >= 0) & (picked < vocab_rows)
    chosen = jnp.take(table_low, jnp.clip(picked, 0, vocab_rows - 1), axis=0)
    embedded = lax.psum_scatter(
        jnp.where(inside[:, None], chosen.astype(jnp.float32), 0.0).astype(jnp.bfloat16),
        "dp",
        scatter_dimension=0,
        tiled=True,
    ).astype(jnp.float32)
    shards = (
        attn_in.astype(jnp.bfloat16),
        attn_out.astype(jnp.bfloat16),
        ffn_in.astype(jnp.bfloat16),
        ffn_out.astype(jnp.bfloat16),
        proj_head.astype(jnp.bfloat16),
    )
    gathered = (
        lax.all_gather(shards[0], ("dp", "fsdp"), axis=0, tiled=True),
        lax.all_gather(shards[1], ("dp", "fsdp"), axis=0, tiled=True),
        lax.all_gather(shards[2], ("dp", "fsdp"), axis=0, tiled=True),
        lax.all_gather(shards[3], ("dp", "fsdp"), axis=0, tiled=True),
        lax.all_gather(shards[4], ("dp", "fsdp"), axis=0, tiled=True),
    )
    final_rows, kept = layer_forward(embedded, mask_rows, gathered[:4], gain_rows, bias_full)
    normed_three, factor_three = normalize(final_rows, gain_rows[2])
    mask_weight = mask_rows.astype(jnp.float32)[:, :, None]
    counts = jnp.sum(mask_weight, 1)
    pooled = jnp.sum(normed_three.reshape(seq_count, L, D) * mask_weight, 1) / counts
    pooled_low = pooled.astype(jnp.bfloat16)
    projected = matmul(pooled_low, gathered[4])
    proj_factor = lax.rsqrt(jnp.sum(projected * projected, -1, keepdims=True) + EPS)
    unit_rows = projected * proj_factor
    unit_low = unit_rows.astype(jnp.bfloat16)
    mine_query = unit_low[:pairs_here]
    all_pass = lax.all_gather(unit_low[pairs_here:], ("dp", "fsdp"), axis=0, tiled=True)
    similar = matmul_nt(mine_query, all_pass)
    sim_scale = jnp.exp(log_scale)
    columns = jnp.arange(pairs_total, dtype=jnp.int32)
    own_index = device_flat * pairs_here + jnp.arange(pairs_here, dtype=jnp.int32)
    own_mask = (columns[None, :] == own_index[:, None]).astype(jnp.float32)
    negative = (columns[None, :] == hard_negative[:, None]).astype(jnp.float32)
    logits = sim_scale * similar - MARGIN * own_mask
    diagonal = jnp.sum(logits * own_mask, 1)
    hardest = jnp.sum(logits * negative, 1)
    row_max = jnp.max(logits, 1, keepdims=True)
    log_total = row_max + jnp.log(jnp.sum(jnp.exp(logits - row_max), 1, keepdims=True))
    loss_local = jnp.sum(log_total[:, 0] - diagonal + jax.nn.softplus(hardest - diagonal))
    hinge_gate = jax.nn.sigmoid(hardest - diagonal)
    grad_logits = (
        jnp.exp(logits - log_total) - own_mask + hinge_gate[:, None] * (negative - own_mask)
    )
    grad_log_scale = sim_scale * jnp.sum(grad_logits * similar)
    grad_similar = (sim_scale * grad_logits).astype(jnp.bfloat16)
    grad_query = matmul(grad_similar, all_pass).astype(jnp.bfloat16)
    grad_pass_terms = matmul_tn(grad_similar, mine_query)
    grad_pass = lax.psum_scatter(
        grad_pass_terms, ("dp", "fsdp"), scatter_dimension=0, tiled=True
    ).astype(jnp.bfloat16)
    grad_units = jnp.concatenate([grad_query, grad_pass], 0).astype(jnp.float32)
    grad_proj = (
        proj_factor * (grad_units - unit_rows * jnp.sum(grad_units * unit_rows, -1, keepdims=True))
    ).astype(jnp.bfloat16)
    gathered_back = (
        lax.all_gather(shards[0], ("dp", "fsdp"), axis=0, tiled=True),
        lax.all_gather(shards[1], ("dp", "fsdp"), axis=0, tiled=True),
        lax.all_gather(shards[2], ("dp", "fsdp"), axis=0, tiled=True),
        lax.all_gather(shards[3], ("dp", "fsdp"), axis=0, tiled=True),
        lax.all_gather(shards[4], ("dp", "fsdp"), axis=0, tiled=True),
    )
    grad_proj_head = matmul_tn(pooled_low, grad_proj)
    grad_pooled = matmul_nt(grad_proj, gathered_back[4])
    grad_normed = ((grad_pooled / counts)[:, None, :] * mask_weight).reshape(-1, D)
    grad_final, gain_three = normalize_back(grad_normed, final_rows, factor_three, gain_rows[2])
    grad_rows, matrix_grads, gain_one, gain_two, grad_bias = layer_backward(
        grad_final, kept, mask_rows, gathered_back[:4], gain_rows, bias_full
    )
    attn_in_grad, attn_out_grad, ffn_in_grad, ffn_out_grad = matrix_grads
    grad_bias_table = jnp.dot(grad_bias.reshape(HEADS, L * L), bucket_hot, precision=HIGH).T
    small_local = jnp.concatenate(
        [gain_one, gain_two, gain_three, grad_bias_table.reshape(-1), grad_log_scale[None]]
    )
    small_grad = lax.psum(small_local, ("dp", "fsdp"))
    weight_grads = (
        lax.psum_scatter(attn_in_grad, ("dp", "fsdp"), scatter_dimension=0, tiled=True),
        lax.psum_scatter(attn_out_grad, ("dp", "fsdp"), scatter_dimension=0, tiled=True),
        lax.psum_scatter(ffn_in_grad, ("dp", "fsdp"), scatter_dimension=0, tiled=True),
        lax.psum_scatter(ffn_out_grad, ("dp", "fsdp"), scatter_dimension=0, tiled=True),
        lax.psum_scatter(grad_proj_head, ("dp", "fsdp"), scatter_dimension=0, tiled=True),
    )
    rows_back = lax.all_gather(grad_rows.astype(jnp.bfloat16), "dp", axis=0, tiled=True)
    turn_count = dp_count // 4
    block_rows = rows_back.shape[0] // turn_count

    def add_block(running, piece_pair):
        block_grads, block_ids = piece_pair
        local_ids = block_ids - row_base
        inside = (local_ids >= 0) & (local_ids < vocab_rows)
        segment = jnp.where(inside, local_ids, vocab_rows)
        summed = jax.ops.segment_sum(
            block_grads.astype(jnp.float32), segment, num_segments=vocab_rows + 1
        )
        return (running + summed[:vocab_rows], None)

    table_full, _ = lax.scan(
        add_block,
        jnp.zeros((vocab_rows, D), jnp.float32),
        (rows_back.reshape(turn_count, block_rows, D), ids_all.reshape(turn_count, block_rows)),
    )
    table_grad = lax.psum(table_full.astype(jnp.bfloat16), "fsdp").astype(jnp.float32)
    owned = (table_grad,) + tuple(weight_grads)
    squares = jnp.sum(table_grad * table_grad) / fsdp_count
    for gradient in weight_grads:
        squares = squares + jnp.sum(gradient * gradient)
    total_squares, loss_sum = lax.psum((squares, loss_local), ("dp", "fsdp"))
    norm_value = jnp.sqrt(total_squares + jnp.sum(small_grad * small_grad))
    factor = jnp.minimum(1.0, CLIP / (norm_value + 1e-06))
    masters = (table, attn_in, attn_out, ffn_in, ffn_out, proj_head, small_params)
    firsts = (
        table_first,
        attn_in_first,
        attn_out_first,
        ffn_in_first,
        ffn_out_first,
        proj_head_first,
        small_first,
    )
    seconds = (
        table_second,
        attn_in_second,
        attn_out_second,
        ffn_in_second,
        ffn_out_second,
        proj_head_second,
        small_second,
    )
    gradients = owned + (small_grad,)
    results = [loss_sum, norm_value]
    for kind_index in range(7):
        results.extend(
            adam_update(
                masters[kind_index],
                firsts[kind_index],
                seconds[kind_index],
                gradients[kind_index],
                factor,
                RATES[kind_index],
                DECAYS[kind_index],
            )
        )
    return tuple(results)


def fits(mesh):
    return mesh.shape["fsdp"] == 4 and mesh.shape["dp"] == 8


def dense_rows(ids_flat, table, row_base):
    vocab_rows = table.shape[0]
    ids_all = lax.all_gather(ids_flat, "dp", axis=0, tiled=True)
    picked = ids_all - row_base
    inside = (picked >= 0) & (picked < vocab_rows)
    chosen = jnp.take(table, jnp.clip(picked, 0, vocab_rows - 1), axis=0)
    return lax.psum_scatter(
        jnp.where(inside[:, None], chosen, 0.0).astype(jnp.bfloat16),
        "dp",
        scatter_dimension=0,
        tiled=True,
    ).astype(jnp.float32)


def dense_table_grad(ids_flat, grad_low, vocab_rows, row_base):
    ids_all = lax.all_gather(ids_flat, "dp", axis=0, tiled=True)
    rows_back = lax.all_gather(grad_low, "dp", axis=0, tiled=True)
    turn_count = lax.axis_size("dp") // 4
    block_rows = rows_back.shape[0] // turn_count

    def add_block(running, piece_pair):
        block_grads, block_ids = piece_pair
        local_ids = block_ids - row_base
        inside = (local_ids >= 0) & (local_ids < vocab_rows)
        segment = jnp.where(inside, local_ids, vocab_rows)
        summed = jax.ops.segment_sum(
            block_grads.astype(jnp.float32), segment, num_segments=vocab_rows + 1
        )
        return (running + summed[:vocab_rows], None)

    table_full, _ = lax.scan(
        add_block,
        jnp.zeros((vocab_rows, D), jnp.float32),
        (rows_back.reshape(turn_count, block_rows, D), ids_all.reshape(turn_count, block_rows)),
    )
    return lax.psum(table_full.astype(jnp.bfloat16), "fsdp")


def once(flag, make, value):
    return lax.while_loop(lambda state: state[0], lambda state: (False, make(state[1])), (flag, value))[1]


def fast_body(
    token_ids,
    pad_mask,
    hard_negative,
    table,
    table_first,
    table_second,
    attn_in,
    attn_in_first,
    attn_in_second,
    attn_out,
    attn_out_first,
    attn_out_second,
    ffn_in,
    ffn_in_first,
    ffn_in_second,
    ffn_out,
    ffn_out_first,
    ffn_out_second,
    proj_head,
    proj_head_first,
    proj_head_second,
    small_params,
    small_first,
    small_second,
):
    dp_count = lax.axis_size("dp")
    fsdp_count = lax.axis_size("fsdp")
    total = dp_count * fsdp_count
    pairs_here = token_ids.shape[1]
    pairs_total = pairs_here * total
    seq_count = 2 * pairs_here
    vocab_rows = table.shape[0]
    row_base = lax.axis_index("dp") * vocab_rows
    gain_rows = small_params[: 3 * D].reshape(3, D)
    bias_table = small_params[3 * D : 3 * D + NB * HEADS].reshape(NB, HEADS)
    log_scale = small_params[3 * D + NB * HEADS]
    buckets = jnp.asarray(bucket_table(L, NB).T.reshape(-1), jnp.int32)
    bucket_hot = (buckets[:, None] == jnp.arange(NB, dtype=jnp.int32)[None, :]).astype(jnp.float32)
    bias_full = (
        jnp.dot(bucket_hot, bias_table, precision=HIGH).reshape(L, L, HEADS).transpose(2, 0, 1)
    )
    mask_rows = pad_mask.reshape(seq_count, L)
    ids_flat = token_ids.reshape(-1)
    tokens = ids_flat.shape[0]

    gathered_packed, gathered_down, heard, slot, embedded = run_head(
        ids_flat, hard_negative, attn_in, attn_out, ffn_in, proj_head, ffn_out, table, 1
    )
    packed = gathered_packed.reshape(-1, PACKED)
    down = gathered_down.reshape(-1, D)
    asked = heard[:, 0, :CAP]
    negatives = heard[:, 1, :pairs_here].reshape(-1).astype(jnp.int32)
    any_spilled = jnp.max(heard[:, 2, 0]) > 0.5
    embedded = once(
        any_spilled,
        lambda rows: dense_rows(
            ids_flat, table + jnp.minimum(jnp.abs(rows[0, 0]), 0.0), row_base
        ),
        embedded,
    )

    mask_col = mask_rows.astype(jnp.float32).reshape(tokens, 1)
    mixed, attended, totals, after, pre, final, pooled, projected = run_forward(
        embedded, mask_col, gain_rows, bias_full, packed, down
    )
    tall, wide = dp_count // (fsdp_count // 2), fsdp_count // 2
    owner = negatives // pairs_here
    owner = (owner % 2 * tall + owner // (2 * wide * wide)) * wide * wide + owner // 2 % (wide * wide) % wide + (
        owner // (2 * wide) % wide * wide
    )
    target = owner * seq_count + pairs_here + negatives % pairs_here
    target = jnp.concatenate(
        [target.reshape(total, pairs_here), jnp.full((total, pairs_here), -1, jnp.int32)], 1
    )
    target = target.reshape(tall * wide * wide, 2, seq_count).transpose(1, 0, 2).reshape(-1, 1)
    grad_proj, loss_parts = run_loss(projected, target, log_scale.reshape(1, 1), 3)
    loss_sum, grad_log_scale = loss_parts[0, 0], loss_parts[1, 0]
    grad_after, grad_gains, grad_up, grad_down = run_ffn_back(
        final, after, mask_col, gain_rows, pooled, grad_proj, pre, packed, down
    )
    grad_low, grad_gain, grad_bias, grad_attn, up_shard, down_shard, squares = run_attn_back(
        embedded, mask_col, mixed, attended, totals, grad_after, gain_rows, bias_full, packed, grad_up, grad_down, 4
    )
    grad_gains = jnp.concatenate([grad_gain, grad_gains[1:]], 0)
    grad_bias_table = jnp.dot(grad_bias.reshape(HEADS, L * L), bucket_hot, precision=HIGH).T
    small_local = jnp.concatenate([grad_gains.reshape(-1), grad_bias_table.reshape(-1)])
    width = -(-small_local.shape[0] // 1024) * 8
    small_local = jnp.pad(small_local, (0, width * 128 - small_local.shape[0]))
    (attn_shard,), table_grad, summed, squares = finish(
        [grad_attn.reshape(total, -1, WIDE + D)],
        grad_low,
        slot,
        asked.reshape(dp_count, fsdp_count, CAP).transpose(1, 0, 2).reshape(fsdp_count, -1),
        small_local.reshape(width, 128),
        squares,
        vocab_rows,
        5,
    )
    table_grad, squares = once(
        any_spilled,
        lambda state: with_squares(dense_table_grad(ids_flat, grad_low, vocab_rows, row_base), state[1]),
        (table_grad, squares),
    )
    norm, *updated = run_update(
        fsdp_count,
        squares,
        summed,
        grad_log_scale.reshape(1, 1),
        (table, table_first, table_second),
        table_grad,
        (
            *(attn_in, attn_in_first, attn_in_second),
            *(attn_out, attn_out_first, attn_out_second),
            *(ffn_in, ffn_in_first, ffn_in_second),
            *(ffn_out, ffn_out_first, ffn_out_second),
            *(proj_head, proj_head_first, proj_head_second),
        ),
        (attn_shard, up_shard, down_shard),
    )
    norm_value = norm[0, 0]
    factor = jnp.minimum(1.0, CLIP / (norm_value + 1e-06))
    small_size = small_params.shape[0]
    small_grad = jnp.concatenate([summed.reshape(-1)[: small_size - 1], grad_log_scale[None]])
    small_new = adam_update(
        small_params, small_first, small_second, small_grad, factor, RATES[6], DECAYS[6]
    )
    return (loss_sum, norm_value, *updated, *small_new)


def with_squares(table_grad, squares):
    wide = table_grad.astype(jnp.float32)
    total = lax.psum(jnp.sum(wide * wide), ("dp", "fsdp"))
    return (table_grad, squares.at[8:].set(0.0).at[8, 0].set(total))


def solution(mesh):
    program = fast_body if fits(mesh) else plain_body
    return jax.shard_map(
        program,
        mesh=mesh,
        in_specs=(
            P(None, ("dp", "fsdp"), None),
            P(None, ("dp", "fsdp"), None),
            P(("dp", "fsdp")),
            P("dp", None),
            P("dp", None),
            P("dp", None),
            P(("dp", "fsdp"), None),
            P(("dp", "fsdp"), None),
            P(("dp", "fsdp"), None),
            P(("dp", "fsdp"), None),
            P(("dp", "fsdp"), None),
            P(("dp", "fsdp"), None),
            P(("dp", "fsdp"), None),
            P(("dp", "fsdp"), None),
            P(("dp", "fsdp"), None),
            P(("dp", "fsdp"), None),
            P(("dp", "fsdp"), None),
            P(("dp", "fsdp"), None),
            P(("dp", "fsdp"), None),
            P(("dp", "fsdp"), None),
            P(("dp", "fsdp"), None),
            P(),
            P(),
            P(),
        ),
        out_specs=(
            P(),
            P(),
            P("dp", None),
            P("dp", None),
            P("dp", None),
            P(("dp", "fsdp"), None),
            P(("dp", "fsdp"), None),
            P(("dp", "fsdp"), None),
            P(("dp", "fsdp"), None),
            P(("dp", "fsdp"), None),
            P(("dp", "fsdp"), None),
            P(("dp", "fsdp"), None),
            P(("dp", "fsdp"), None),
            P(("dp", "fsdp"), None),
            P(("dp", "fsdp"), None),
            P(("dp", "fsdp"), None),
            P(("dp", "fsdp"), None),
            P(("dp", "fsdp"), None),
            P(("dp", "fsdp"), None),
            P(("dp", "fsdp"), None),
            P(),
            P(),
            P(),
        ),
        check_vma=False,
    )
```

```python
import functools

import jax
import jax.numpy as jnp
import numpy as np
from jax import lax
from jax.experimental import pallas as pl
from jax.experimental.pallas import tpu as pltpu
from jax.sharding import PartitionSpec as P

D = 768
HEADS = 12
HD = 64
NB = 32
L = 128
STEP = 10


EPS = 1e-06
SCALE = 0.125
MARGIN = 0.2
CLIP = 0.1
BETA_ONE = 0.9
BETA_TWO = 0.99
ADAM_EPS = 1e-08
RATES = (3.0, 0.1, 0.2, 0.1, 0.05, 0.1, 1.0)
DECAYS = (0.001, 0.001, 0.001, 0.001, 0.001, 0.001, 0.0)
HIGH = lax.Precision.HIGHEST
MESH = pl.DeviceIdType.MESH
CAP = 112


def bucket_table(length, count):
    position = np.arange(length)
    relative = position[None, :] - position[:, None]
    half = count // 2
    base_part = (relative > 0).astype(np.int64) * half
    distance = np.abs(relative)
    exact = half // 2
    safe_dist = np.maximum(distance, 1)
    large = exact + (np.log(safe_dist / exact) / np.log(length / exact) * (half - exact)).astype(
        np.int64
    )
    large = np.minimum(large, half - 1)
    return base_part + np.where(distance < exact, distance, large)


def matmul(left_side, right_side):
    return jnp.dot(left_side, right_side, preferred_element_type=jnp.float32)


def matmul_tn(left_side, right_side):
    return lax.dot_general(
        left_side, right_side, (((0,), (0,)), ((), ())), preferred_element_type=jnp.float32
    )


def matmul_nt(left_side, right_side):
    return lax.dot_general(
        left_side, right_side, (((1,), (1,)), ((), ())), preferred_element_type=jnp.float32
    )


def normalize(inputs, gain_row):
    factor = lax.rsqrt(jnp.mean(inputs * inputs, -1, keepdims=True) + EPS)
    return (inputs * factor * gain_row, factor)


def normalize_back(grad_out, inputs, factor, gain_row):
    scaled = grad_out * gain_row
    grad_gain = jnp.sum(grad_out * inputs * factor, 0)
    grad_in = factor * (
        scaled - inputs * factor * factor * jnp.mean(scaled * inputs, -1, keepdims=True)
    )
    return (grad_in, grad_gain)


def attention_scores(mixed_proj, mask_rows, bias_full):
    keep_add = jnp.where(mask_rows > 0, 0.0, -1000000000.0).astype(jnp.float32)
    scores = jnp.einsum(
        "bqhd,bkhd->bhqk",
        mixed_proj[:, :, 0],
        mixed_proj[:, :, 1],
        preferred_element_type=jnp.float32,
    )
    return scores * SCALE + bias_full[None] + keep_add[:, None, None, :]


def layer_forward(token_rows, mask_rows, weights, gain_rows, bias_full):
    attn_in, attn_out, ffn_in, ffn_out = weights
    seq_count, length = mask_rows.shape
    width = token_rows.shape[1]
    normed_one, factor_one = normalize(token_rows, gain_rows[0])
    act_one = normed_one.astype(jnp.bfloat16)
    mixed_proj = (
        matmul(act_one, attn_in).astype(jnp.bfloat16).reshape(seq_count, length, 3, HEADS, HD)
    )
    scores = attention_scores(mixed_proj, mask_rows, bias_full)
    row_max = jnp.max(scores, -1, keepdims=True)
    log_total = row_max + jnp.log(jnp.sum(jnp.exp(scores - row_max), -1, keepdims=True))
    prob_low = jnp.exp(scores - log_total).astype(jnp.bfloat16)
    attended = jnp.einsum(
        "bhqk,bkhd->bqhd", prob_low, mixed_proj[:, :, 2], preferred_element_type=jnp.float32
    )
    attended = attended.astype(jnp.bfloat16).reshape(-1, width)
    after_attn = token_rows + matmul(attended, attn_out)
    normed_two, factor_two = normalize(after_attn, gain_rows[1])
    act_two = normed_two.astype(jnp.bfloat16)
    pre_act = matmul(act_two, ffn_in)
    hidden = jax.nn.gelu(pre_act).astype(jnp.bfloat16)
    final_rows = after_attn + matmul(hidden, ffn_out)
    kept = (
        token_rows,
        factor_one,
        act_one,
        mixed_proj,
        log_total,
        attended,
        after_attn,
        factor_two,
        act_two,
        pre_act,
        hidden,
    )
    return (final_rows, kept)


def layer_backward(grad_final, kept, mask_rows, weights, gain_rows, bias_full):
    (
        token_rows,
        factor_one,
        act_one,
        mixed_proj,
        log_total,
        attended,
        after_attn,
        factor_two,
        act_two,
        pre_act,
        hidden,
    ) = kept
    attn_in, attn_out, ffn_in, ffn_out = weights
    seq_count, length = mask_rows.shape
    branch = grad_final.astype(jnp.bfloat16)
    grad_ffn_out = matmul_tn(hidden, branch)
    grad_hidden = matmul_nt(branch, ffn_out)
    _, gelu_pull = jax.vjp(jax.nn.gelu, pre_act)
    grad_pre = gelu_pull(grad_hidden)[0].astype(jnp.bfloat16)
    grad_ffn_in = matmul_tn(act_two, grad_pre)
    grad_act_two = matmul_nt(grad_pre, ffn_in)
    grad_mid, gain_two = normalize_back(grad_act_two, after_attn, factor_two, gain_rows[1])
    grad_after = grad_final + grad_mid
    branch = grad_after.astype(jnp.bfloat16)
    grad_attn_out = matmul_tn(attended, branch)
    grad_attended = (
        matmul_nt(branch, attn_out).astype(jnp.bfloat16).reshape(seq_count, length, HEADS, HD)
    )
    scores = attention_scores(mixed_proj, mask_rows, bias_full)
    prob_full = jnp.exp(scores - log_total)
    prob_low = prob_full.astype(jnp.bfloat16)
    queries = mixed_proj[:, :, 0]
    key_rows = mixed_proj[:, :, 1]
    grad_probs = jnp.einsum(
        "bqhd,bkhd->bhqk", grad_attended, mixed_proj[:, :, 2], preferred_element_type=jnp.float32
    )
    grad_values = jnp.einsum(
        "bhqk,bqhd->bkhd", prob_low, grad_attended, preferred_element_type=jnp.float32
    )
    grad_scores = prob_full * (grad_probs - jnp.sum(prob_full * grad_probs, -1, keepdims=True))
    grad_scores = grad_scores.astype(jnp.bfloat16)
    grad_bias = jnp.sum(grad_scores, 0, dtype=jnp.float32)
    grad_queries = (
        jnp.einsum("bhqk,bkhd->bqhd", grad_scores, key_rows, preferred_element_type=jnp.float32)
        * SCALE
    )
    grad_keys = (
        jnp.einsum("bhqk,bqhd->bkhd", grad_scores, queries, preferred_element_type=jnp.float32)
        * SCALE
    )
    grad_mixed = (
        jnp.stack([grad_queries, grad_keys, grad_values], 2)
        .astype(jnp.bfloat16)
        .reshape(seq_count * length, -1)
    )
    grad_attn_in = matmul_tn(act_one, grad_mixed)
    grad_act_one = matmul_nt(grad_mixed, attn_in)
    grad_low, gain_one = normalize_back(grad_act_one, token_rows, factor_one, gain_rows[0])
    grad_rows = grad_after + grad_low
    return (
        grad_rows,
        (grad_attn_in, grad_attn_out, grad_ffn_in, grad_ffn_out),
        gain_one,
        gain_two,
        grad_bias,
    )


def adam_update(param, first_moment, second_moment, gradient, factor, rate, decay):
    clipped = gradient * factor
    first_new = BETA_ONE * first_moment + (1.0 - BETA_ONE) * clipped
    second_new = BETA_TWO * second_moment + (1.0 - BETA_TWO) * clipped * clipped
    direction = (
        first_new
        / (1.0 - BETA_ONE**STEP)
        / (jnp.sqrt(second_new / (1.0 - BETA_TWO**STEP)) + ADAM_EPS)
    )
    return (first_new, second_new, param - rate * (direction + decay * param))


class Grid:
    def __init__(self):
        self.dp, self.fs = lax.axis_size("dp"), lax.axis_size("fsdp")
        self.total = self.dp * self.fs
        self.wide = self.fs // 2
        self.tall = self.dp // self.wide

    def here(self):
        d, f = lax.axis_index("dp"), lax.axis_index("fsdp")
        return d // self.wide, lax.rem(d, self.wide), f // 2, lax.rem(f, 2)

    def device(self, z, x, y, core):
        return (z * self.wide + x, y * 2 + core)

    def flat(self, z, x, y, core):
        return (z * self.wide + x) * self.fs + y * 2 + core

    def peer(self, index):
        return (index // self.fs, lax.rem(index, self.fs))


def greet(device, when=None):
    barrier = pltpu.get_barrier_semaphore()

    def signal():
        pl.semaphore_signal(barrier, inc=1, device_id=device, device_id_type=MESH)

    if when is None:
        signal()
    else:
        pl.when(when)(signal)


def meet(count):
    pl.semaphore_wait(pltpu.get_barrier_semaphore(), count)


ROW_BLOCK = 512
UPDATE_BLOCK = 672
WIDE = 3 * D
PACKED = WIDE + D + 4 * D + D
TILE_SEQS = 4


def head_kernel(
    grid,
    col_ref,
    row_ref,
    negative_ref,
    in_ref,
    out_ref,
    up_ref,
    proj_ref,
    down_ref,
    table_hbm,
    packed_out,
    down_out,
    heard,
    slot_ref,
    x0_ref,
    packed_mine,
    down_mine,
    table,
    total,
    answers,
    found,
    messages,
    in_wide,
    out_wide,
    up_wide,
    proj_wide,
    down_wide,
    send_sem,
    recv_sem,
    own_sem,
    row_send,
    row_recv,
    note_send,
    note_recv,
    note_on,
    table_sem,
    wide_sem,
):
    srcs, outs = (packed_mine, down_mine), (packed_out, down_out)
    count = 2
    z, x, y, core = grid.here()
    tall = grid.tall
    d, f = lax.axis_index("dp"), lax.axis_index("fsdp")
    u_places = ((lax.rem(x + 1 - core, 2), lax.rem(y + core, 2)), (1 - x, y))
    v_places = ((lax.rem(x + core, 2), lax.rem(y + 1 - core, 2)), (x, 1 - y))
    up, down = grid.device(z + 1, x, y, core), grid.device(z - 1, x, y, core)
    u_devices = [grid.device(z, *place, core) for place in u_places]
    v_devices = [grid.device(z, *place, core) for place in v_places]
    sibling = grid.device(z, x, y, 1 - core)
    has_up, has_down = z < tall - 1, z > 0
    me = grid.flat(z, x, y, core)
    f_side, f_y, f_far = y * 2 + 1 - core, (1 - y) * 2 + core, (1 - y) * 2 + 1 - core

    @pl.loop(1, grid.dp)
    def _(step):
        greet((lax.rem(d + step, grid.dp), f))

    greet((d, f_y))
    greet(sibling)
    vocab_rows = table_hbm.shape[0]
    fetch = pltpu.make_async_copy(table_hbm, table.at[pl.ds(0, vocab_rows), :], table_sem)
    wide = (in_wide, out_wide, up_wide, proj_wide, down_wide)
    for k, ref in enumerate((in_ref, out_ref, up_ref, proj_ref, down_ref)):
        pltpu.make_async_copy(ref, wide[k], wide_sem.at[k]).start()
    fetch.start()
    at = 0
    for k, ref in enumerate((in_ref, out_ref, up_ref, proj_ref, down_ref)):
        pltpu.make_async_copy(ref, wide[k], wide_sem.at[k]).wait()
        if k < 4:
            packed_mine[:, at : at + ref.shape[1]] = wide[k][...].astype(jnp.bfloat16)
            at += ref.shape[1]
    down_mine[...] = down_wide[...].astype(jnp.bfloat16)
    local = [pltpu.make_async_copy(srcs[m], outs[m].at[me], own_sem.at[m]) for m in range(count)]
    for item in local:
        item.start()
    meet(grid.dp + 1)

    def copy(m, shard, device, way, own):
        return pltpu.make_async_remote_copy(
            src_ref=srcs[m] if own else outs[m].at[shard],
            dst_ref=outs[m].at[shard],
            send_sem=send_sem.at[way, m, shard],
            recv_sem=recv_sem.at[m, shard],
            device_id=device,
            device_id_type=MESH,
        )

    def send(shard, device, way, own=False):
        for m in range(count):
            copy(m, shard, device[m] if isinstance(device, list) else device, way, own).start()

    def arrived(shard):
        for m in range(count):
            copy(m, shard, sibling, 4, False).wait_recv()

    def sent(shard, device, way):
        for m in range(count):
            copy(m, shard, device[m] if isinstance(device, list) else device, way, False).wait_send()

    @pl.when(has_up)
    def _():
        send(me, up, 0, True)

    @pl.when(has_down)
    def _():
        send(me, down, 1, True)

    send(me, u_devices, 2, True)
    send(me, v_devices, 3, True)
    send(me, sibling, 4, True)

    tokens = col_ref.shape[0]
    chunk = 128
    ids_row = row_ref[...]
    place_row = lax.broadcasted_iota(jnp.int32, (chunk, tokens), 1)
    place_col = lax.broadcasted_iota(jnp.int32, (chunk, tokens), 0)

    def see(step, repeated):
        start = pl.multiple_of(step * chunk, chunk)
        again = (col_ref[pl.ds(start, chunk), :] == ids_row) & (place_col + start < place_row)
        return jnp.maximum(repeated, jnp.max(jnp.where(again, 1.0, 0.0), 0, keepdims=True))

    repeated = lax.fori_loop(0, tokens // chunk, see, jnp.zeros((1, tokens), jnp.float32))
    firsts = jnp.where(repeated > 0.5, -1.0, ids_row)
    lane = lax.broadcasted_iota(jnp.int32, (chunk, 128), 1).astype(jnp.float32)

    def rank_some(step, carry):
        listed, most = carry
        start = pl.multiple_of(step * chunk, chunk)
        ids = col_ref[pl.ds(start, chunk), :]
        owner = jnp.zeros_like(ids)
        for other in range(1, grid.dp):
            owner = owner + jnp.where(ids >= float(other * vocab_rows), 1.0, 0.0)
        first_id = owner * float(vocab_rows)
        rank = jnp.sum(jnp.where((firsts >= first_id) & (firsts < ids), 1.0, 0.0), 1, keepdims=True)
        slot = jnp.where(rank < float(CAP), owner * float(CAP) + rank, -1.0)
        slot_ref[pl.ds(start, chunk), :] = slot
        rows = []
        for other in range(grid.dp):
            hit = (slot == lane + float(other * CAP)) & (lane < float(CAP))
            rows.append(jnp.max(jnp.where(hit, ids - first_id + 1.0, 0.0), 0, keepdims=True))
        return (jnp.maximum(listed, jnp.concatenate(rows, 0)), jnp.maximum(most, jnp.max(rank, 0, keepdims=True)))

    listed, most = lax.fori_loop(
        0,
        tokens // chunk,
        rank_some,
        (jnp.zeros((grid.dp, 128), jnp.float32), jnp.zeros((1, 1), jnp.float32)),
    )
    spilled = jnp.broadcast_to(jnp.where(most >= float(CAP), 1.0, 0.0), (1, 128))
    rest = jnp.concatenate([negative_ref[...], spilled, jnp.zeros((5, 128), jnp.float32)], 0)
    for other in range(grid.dp):
        messages[other] = jnp.concatenate([listed[other : other + 1] - 1.0, rest], 0)

    def note(peer, slot):
        return pltpu.make_async_remote_copy(
            src_ref=messages.at[peer],
            dst_ref=heard.at[slot],
            send_sem=note_send.at[peer],
            recv_sem=note_recv.at[slot],
            device_id=(peer, f),
            device_id_type=MESH,
        )

    def note_onward(slot, to_side):
        return pltpu.make_async_remote_copy(
            src_ref=heard.at[slot],
            dst_ref=heard.at[slot],
            send_sem=note_on.at[1 if to_side else 0, slot],
            recv_sem=note_recv.at[slot],
            device_id=(d, f_side if to_side else f_y),
            device_id_type=MESH,
        )

    @pl.loop(1, grid.dp)
    def _(step):
        note(lax.rem(d + step, grid.dp), me).start()

    heard[me] = messages[d]

    def row_copy(peer, slot):
        return pltpu.make_async_remote_copy(
            src_ref=answers.at[peer],
            dst_ref=found.at[slot],
            send_sem=row_send.at[peer],
            recv_sem=row_recv.at[slot],
            device_id=(peer, f),
            device_id_type=MESH,
        )

    def pass_z(k):
        low, high = z - k, z + k

        @pl.when(low >= 0)
        def _():
            shard = grid.flat(low, x, y, core)
            arrived(shard)

            @pl.when(has_up)
            def _():
                send(shard, up, 0)

            send(shard, u_devices, 2)
            send(shard, v_devices, 3)
            send(shard, sibling, 4)

        @pl.when(high < tall)
        def _():
            shard = grid.flat(high, x, y, core)
            arrived(shard)

            @pl.when(has_down)
            def _():
                send(shard, down, 1)

            send(shard, u_devices, 2)
            send(shard, v_devices, 3)
            send(shard, sibling, 4)

    def both(k, action):
        pl.when(z - k >= 0)(lambda: action(z - k))
        if k:
            pl.when(z + k < tall)(lambda: action(z + k))

    def pass_u(level):
        for m in range(count):
            shard = grid.flat(level, *u_places[m], core)
            copy(m, shard, sibling, 4, False).wait_recv()
            copy(m, shard, v_devices[m], 3, False).start()
            copy(m, shard, sibling, 4, False).start()

    def pass_v(level):
        for m in range(count):
            shard = grid.flat(level, *v_places[m], core)
            copy(m, shard, sibling, 4, False).wait_recv()
            copy(m, shard, sibling, 4, False).start()

    def pass_far(level):
        shard = grid.flat(level, 1 - x, 1 - y, core)
        arrived(shard)
        send(shard, sibling, 4)

    both(0, pass_u)

    @pl.loop(1, grid.dp)
    def _(step):
        note(d, lax.rem(d + step, grid.dp) * grid.fs + f).wait_recv()

    @pl.loop(0, grid.dp)
    def _(peer):
        note_onward(peer * grid.fs + f, False).start()
        note_onward(peer * grid.fs + f, True).start()

    pass_z(1)
    fetch.wait()
    padding = table.shape[0] - vocab_rows
    if padding:
        table[vocab_rows:, :] = jnp.zeros((padding, D), jnp.float32)
    asked = jnp.concatenate([heard[peer * grid.fs + f, 0:1, :] for peer in range(grid.dp)], 0)
    asked = jnp.transpose(asked)
    block = ROW_BLOCK
    total[...] = jnp.zeros_like(total)
    lanes = lax.broadcasted_iota(jnp.int32, (CAP, block), 1).astype(jnp.float32)

    def pick(step):
        start = pl.multiple_of(step * block, block)
        some = table[pl.ds(start, block), :].astype(jnp.bfloat16)
        wanted = lanes + (step * block).astype(jnp.float32)
        hot = jnp.concatenate(
            [
                jnp.where(asked[:CAP, peer : peer + 1] == wanted, 1.0, 0.0)
                for peer in range(grid.dp)
            ],
            0,
        ).astype(jnp.bfloat16)
        total[...] += matmul(hot, some)

    steps = table.shape[0] // block
    pl.loop(0, steps)(pick)
    answers[...] = total[...].reshape(answers.shape).astype(jnp.bfloat16)
    found[d] = answers[d]

    @pl.loop(1, grid.dp)
    def _(step):
        row_copy(lax.rem(d + step, grid.dp), d).start()

    both(1, pass_u)
    pass_z(2)
    both(0, pass_v)
    both(2, pass_u)
    pass_z(3)
    both(1, pass_v)
    both(3, pass_u)
    both(0, pass_far)
    both(2, pass_v)
    both(1, pass_far)
    both(3, pass_v)
    both(2, pass_far)
    both(3, pass_far)

    @pl.loop(1, grid.dp)
    def _(step):
        row_copy(d, lax.rem(d + step, grid.dp)).wait_recv()

    slots = grid.dp * CAP
    some = tokens // 4
    wide_lane = lax.broadcasted_iota(jnp.int32, (some, slots), 1).astype(jnp.float32)
    rows = found[...].reshape(slots, D)

    @pl.loop(0, 4)
    def _(step):
        start = pl.multiple_of(step * some, some)
        hot = jnp.where(slot_ref[pl.ds(start, some), :] == wide_lane, 1.0, 0.0).astype(jnp.bfloat16)
        x0_ref[pl.ds(start, some), :] = matmul(hot, rows)

    @pl.loop(0, grid.dp)
    def _(peer):
        note(d, peer * grid.fs + f_y).wait_recv()
        note_onward(peer * grid.fs + f_y, True).start()

    @pl.loop(0, grid.dp)
    def _(peer):
        note(d, peer * grid.fs + f_side).wait_recv()
        note(d, peer * grid.fs + f_far).wait_recv()
        note_onward(peer * grid.fs + f, False).wait_send()
        note_onward(peer * grid.fs + f, True).wait_send()
        note_onward(peer * grid.fs + f_y, True).wait_send()

    @pl.loop(1, grid.dp)
    def _(step):
        peer = lax.rem(d + step, grid.dp)
        row_copy(peer, d).wait_send()
        note(peer, me).wait_send()

    @pl.loop(0, tall)
    def _(level):
        for xx in range(2):
            for yy in range(2):
                arrived(grid.flat(level, xx, yy, 1 - core))
                sent(grid.flat(level, xx, yy, core), sibling, 4)
        shard = grid.flat(level, x, y, core)

        @pl.when((level <= z) & has_up)
        def _():
            sent(shard, up, 0)

        @pl.when((level >= z) & has_down)
        def _():
            sent(shard, down, 1)

        sent(shard, u_devices, 2)
        sent(shard, v_devices, 3)
        for m in range(count):
            other = grid.flat(level, *u_places[m], core)
            copy(m, other, v_devices[m], 3, False).wait_send()

    for item in local:
        item.wait()


def run_head(ids, negatives, attn_in, attn_out, ffn_in, proj_head, ffn_out, table, number):
    grid = Grid()
    tokens = ids.shape[0]
    wide = ids.astype(jnp.float32)
    row = jnp.zeros((1, 128), jnp.float32).at[0, : negatives.shape[0]].set(negatives.astype(jnp.float32))
    shapes = ((attn_in.shape[0], PACKED), ffn_out.shape)
    blocks = -(-table.shape[0] // ROW_BLOCK)
    anywhere, inside = pl.BlockSpec(memory_space=pl.ANY), pl.BlockSpec(memory_space=pltpu.VMEM)
    dma = pltpu.SemaphoreType.DMA
    line, everyone = dma((grid.dp,)), dma((grid.total,))
    return pl.pallas_call(
        functools.partial(head_kernel, grid),
        out_shape=[jax.ShapeDtypeStruct((grid.total,) + shape, jnp.bfloat16) for shape in shapes]
        + [
            jax.ShapeDtypeStruct((grid.total, 8, 128), jnp.float32),
            jax.ShapeDtypeStruct((tokens, 1), jnp.float32),
            jax.ShapeDtypeStruct((tokens, D), jnp.float32),
        ],
        in_specs=[inside] * 3 + [anywhere] * 6,
        out_specs=[anywhere] * 2 + [inside] * 3,
        scratch_shapes=[pltpu.VMEM(shape, jnp.bfloat16) for shape in shapes]
        + [
            pltpu.VMEM((blocks * ROW_BLOCK, D), jnp.float32),
            pltpu.VMEM((grid.dp * CAP, D), jnp.float32),
            pltpu.VMEM((grid.dp, CAP, D), jnp.bfloat16),
            pltpu.VMEM((grid.dp, CAP, D), jnp.bfloat16),
            pltpu.VMEM((grid.dp, 8, 128), jnp.float32),
        ]
        + [
            pltpu.VMEM(array.shape, jnp.float32)
            for array in (attn_in, attn_out, ffn_in, proj_head, ffn_out)
        ]
        + [
            dma((5, 2, grid.total)),
            dma((2, grid.total)),
            dma((2,)),
            line,
            line,
            line,
            everyone,
            dma((2, grid.total)),
            dma,
            dma((5,)),
        ],
        compiler_params=pltpu.CompilerParams(
            collective_id=number, has_side_effects=True, vmem_limit_bytes=62 * 1024 * 1024
        ),
    )(wide.reshape(tokens, 1), wide.reshape(1, tokens), row, attn_in, attn_out, ffn_in, proj_head, ffn_out, table)


def lane_is(shape, low, high):
    lanes = lax.broadcasted_iota(jnp.int32, shape, len(shape) - 1)
    return (lanes >= low) & (lanes < high)


def gelu_parts(t):
    inner = np.float32(np.sqrt(2 / np.pi)) * (t + 0.044715 * (t * t * t))
    tan = jnp.tanh(inner)
    return 0.5 * (1.0 + tan), tan


def forward_kernel(
    x0_ref,
    mask_col_ref,
    gains_ref,
    bias_ref,
    packed_hbm,
    down_hbm,
    mixed_ref,
    attended_ref,
    total_ref,
    after_ref,
    pre_ref,
    final_ref,
    pooled_ref,
    projected_ref,
    packed,
    down,
    load_sem,
):
    step = pl.program_id(0)
    tile_seqs = x0_ref.shape[0] // L
    edges = (0, WIDE, WIDE + D, WIDE + 5 * D, PACKED)

    def load(k):
        if k == 4:
            return pltpu.make_async_copy(down_hbm, down, load_sem.at[k])
        part = pl.ds(edges[k], edges[k + 1] - edges[k])
        return pltpu.make_async_copy(packed_hbm.at[:, part], packed.at[:, part], load_sem.at[k])

    def loaded(k):
        @pl.when(step == 0)
        def _():
            load(k).wait()

    @pl.when(step == 0)
    def _():
        for k in (0, 1, 2, 4, 3):
            load(k).start()

    x0 = x0_ref[...]
    act_one = normalize(x0, gains_ref[0:1, :])[0].astype(jnp.bfloat16)
    loaded(0)
    for at in range(0, WIDE, D):
        mixed_ref[:, at : at + D] = matmul(act_one, packed[:, at : at + D]).astype(jnp.bfloat16)

    zero = jnp.zeros((), jnp.bfloat16)
    for s in range(tile_seqs):
        rows = slice(s * L, (s + 1) * L)
        keep = jnp.where(mask_col_ref[rows, :] > 0, 0.0, -1000000000.0)
        for pair in range(HEADS // 2):
            at = pair * 128
            query = mixed_ref[rows, at : at + 128]
            key = mixed_ref[rows, D + at : D + at + 128]
            value = mixed_ref[rows, 2 * D + at : 2 * D + at + 128]
            mine = lane_is((L, 128), 0, HD)
            keys = jnp.concatenate([jnp.where(mine, key, zero), jnp.where(mine, zero, key)], 0)
            scores = (matmul_nt(keys, query) * SCALE).reshape(2, L, L)
            scores = scores + bias_ref[2 * pair : 2 * pair + 2] + keep[None]
            row_max = jnp.max(scores, 1, keepdims=True)
            powers = jnp.exp(scores - row_max)
            row_sum = jnp.sum(powers, 1, keepdims=True)
            prob = (powers * (1.0 / row_sum)).astype(jnp.bfloat16)
            total_ref[s, 2 * pair : 2 * pair + 2, :] = (row_max + jnp.log(row_sum))[:, 0, :]
            flipped = jnp.transpose(value)
            both = jnp.concatenate([matmul(flipped[:HD], prob[0]), matmul(flipped[HD:], prob[1])], 0)
            both = jnp.transpose(both)
            attended_ref[rows, at : at + 128] = both.astype(jnp.bfloat16)

    loaded(1)
    after = x0 + matmul(attended_ref[...], packed[:, WIDE : WIDE + D])
    after_ref[...] = after
    act_two = normalize(after, gains_ref[1:2, :])[0].astype(jnp.bfloat16)
    loaded(2)
    loaded(4)
    final = after
    for j in range(4):
        at = WIDE + D + j * D
        pre = matmul(act_two, packed[:, at : at + D])
        pre_ref[:, j * D : (j + 1) * D] = pre
        hidden = (pre * gelu_parts(pre)[0]).astype(jnp.bfloat16)
        final = final + matmul(hidden, down[j * D : (j + 1) * D, :])
    final_ref[...] = final
    normed = normalize(final, gains_ref[2:3, :])[0]
    weight = mask_col_ref[...]
    for s in range(tile_seqs):
        rows = slice(s * L, (s + 1) * L)
        count = jnp.sum(weight[rows], 0, keepdims=True)
        row = jnp.sum(normed[rows] * weight[rows], 0, keepdims=True) / count
        pooled_ref[pl.ds(step * tile_seqs + s, 1), :] = row

    @pl.when(step == pl.num_programs(0) - 1)
    def _():
        load(3).wait()
        projected_ref[...] = matmul(pooled_ref[...].astype(jnp.bfloat16), packed[:, PACKED - D :])


def run_forward(x0, mask_col, gains, bias_full, packed, down):
    tokens = x0.shape[0]
    seqs = tokens // L
    tile = TILE_SEQS * L
    steps = tokens // tile

    def rows(width):
        return pl.BlockSpec((tile, width), lambda i: (i, 0))

    def whole(*shape):
        return pl.BlockSpec(shape, lambda i: (0,) * len(shape), pipeline_mode=pl.Buffered(1))

    def kept(width, dtype):
        return jax.ShapeDtypeStruct((tokens, width), dtype)

    anywhere = pl.BlockSpec(memory_space=pl.ANY)
    return pl.pallas_call(
        forward_kernel,
        grid=(steps,),
        out_shape=[
            kept(WIDE, jnp.bfloat16),
            kept(D, jnp.bfloat16),
            jax.ShapeDtypeStruct((seqs, HEADS, L), jnp.float32),
            kept(D, jnp.float32),
            kept(4 * D, jnp.float32),
            kept(D, jnp.float32),
            jax.ShapeDtypeStruct((seqs, D), jnp.float32),
            jax.ShapeDtypeStruct((seqs, D), jnp.float32),
        ],
        in_specs=[
            rows(D),
            rows(1),
            whole(3, D),
            whole(HEADS, L, L),
            anywhere,
            anywhere,
        ],
        out_specs=[rows(WIDE), rows(D), pl.BlockSpec((TILE_SEQS, HEADS, L), lambda i: (i, 0, 0)), rows(D), rows(4 * D), rows(D), whole(seqs, D), whole(seqs, D)],
        scratch_shapes=[
            pltpu.VMEM((D, PACKED), jnp.bfloat16),
            pltpu.VMEM((4 * D, D), jnp.bfloat16),
            pltpu.SemaphoreType.DMA((5,)),
        ],
        compiler_params=pltpu.CompilerParams(vmem_limit_bytes=60 * 1024 * 1024),
    )(x0, mask_col, gains, bias_full, packed, down)


def loss_kernel(
    grid, pairs_here, projected_ref, target_ref, scale_ref, grad_ref, loss_ref, others, grads, send_sem, recv_sem
):
    z, x, y, core = grid.here()
    tall = grid.tall
    each = 2 * pairs_here
    half = D // 2
    x_device, y_device = grid.device(z, 1 - x, y, core), grid.device(z, x, 1 - y, core)
    sibling = grid.device(z, x, y, 1 - core)

    def other_levels(action):
        @pl.loop(1, tall)
        def _(step):
            action(lax.rem(z + step, tall))

    greet(x_device)
    greet(y_device)
    greet(sibling)
    other_levels(lambda level: greet(grid.device(level, x, y, core)))
    projected = projected_ref[...]
    factor = lax.rsqrt(jnp.sum(projected * projected, -1, keepdims=True) + EPS)
    unit = projected * factor
    others[core, z, x, y] = jnp.concatenate([unit[:, :half], unit[:, half:]], 0).astype(jnp.bfloat16)
    meet(tall + 2)

    def remote(blocks, device, sent, received):
        return pltpu.make_async_remote_copy(
            src_ref=blocks,
            dst_ref=blocks,
            send_sem=send_sem.at[sent],
            recv_sem=recv_sem.at[received],
            device_id=device,
            device_id_type=MESH,
        )

    along_x = remote(others.at[core, z, x, y], x_device, 0, 0)
    along_x.start()
    along_x.wait_recv()
    along_y = [remote(others.at[core, z, xx, y], y_device, 1 + xx, 1 + xx) for xx in range(2)]
    for copy in along_y:
        copy.start()
    for copy in along_y:
        copy.wait_recv()

    def along_z(level, origin):
        return remote(others.at[core, origin], grid.device(level, x, y, core), 3 + level, 3 + origin)

    def to_side(level):
        return remote(others.at[core, level], sibling, 3 + tall + level, 3 + tall + level)

    other_levels(lambda level: along_z(level, z).start())
    to_side(z).start()

    def pass_side(level):
        along_z(level, level).wait_recv()
        to_side(level).start()

    other_levels(pass_side)
    for level in range(tall):
        to_side(level).wait_recv()
    me = ((core * tall + z) * 2 + x) * 2 + y

    count = grid.total * each
    wide = others[...].reshape(grid.total, 2 * each, half).astype(jnp.float32)
    units = jnp.concatenate(
        [wide[:, :each].reshape(count, half), wide[:, each:].reshape(count, half)], 1
    ).astype(jnp.bfloat16)
    similar = matmul_nt(units, units)
    row = lax.broadcasted_iota(jnp.int32, (count, count), 0)
    column = lax.broadcasted_iota(jnp.int32, (count, count), 1)
    used = (lax.rem(row, each) < pairs_here) & (lax.rem(column, each) >= pairs_here)
    own = used & (column == row + pairs_here)
    negative = used & (column == target_ref[...])
    sim_scale = jnp.exp(scale_ref[...])
    own_mask = jnp.where(own, 1.0, 0.0)
    negative_mask = jnp.where(negative, 1.0, 0.0)
    logits = sim_scale * similar - MARGIN * own_mask
    diagonal = jnp.sum(logits * own_mask, 1, keepdims=True)
    hardest = jnp.sum(logits * negative_mask, 1, keepdims=True)
    row_max = jnp.max(jnp.where(used, logits, -3e38), 1, keepdims=True)
    powers = jnp.where(used, jnp.exp(jnp.minimum(logits - row_max, 0.0)), 0.0)
    row_sum = jnp.sum(powers, 1, keepdims=True)
    is_query = lax.rem(lax.broadcasted_iota(jnp.int32, (count, 1), 0), each) < pairs_here
    gap = hardest - diagonal
    softplus = jnp.maximum(gap, 0.0) + jnp.log(1.0 + jnp.exp(-jnp.abs(gap)))
    row_sum = jnp.where(is_query, row_sum, 1.0)
    losses = jnp.where(is_query, row_max + jnp.log(row_sum) - diagonal + softplus, 0.0)
    gate = 1.0 / (1.0 + jnp.exp(-gap))
    grad_logits = jnp.where(
        used, powers / row_sum - own_mask + gate * (negative_mask - own_mask), 0.0
    )
    loss_ref[0:1, :] = jnp.broadcast_to(jnp.sum(losses, 0, keepdims=True), (1, 128))
    grad_scale = sim_scale * jnp.sum(
        jnp.sum(grad_logits * similar, 1, keepdims=True), 0, keepdims=True
    )
    loss_ref[1:2, :] = jnp.broadcast_to(grad_scale, (1, 128))
    loss_ref[2:8, :] = jnp.zeros((6, 128), jnp.float32)
    grad_similar = sim_scale * grad_logits
    grads[...] = grad_similar + jnp.transpose(grad_similar)
    first = pl.multiple_of(me * each, each)
    grad_units = matmul(grads[pl.ds(first, each), :].astype(jnp.bfloat16), units)
    grad_units = grad_units.astype(jnp.bfloat16).astype(jnp.float32)
    grad_ref[...] = (
        factor * (grad_units - unit * jnp.sum(grad_units * unit, -1, keepdims=True))
    ).astype(jnp.bfloat16)

    along_x.wait_send()
    for copy in along_y:
        copy.wait_send()
    other_levels(lambda level: along_z(level, level).wait_send())
    for level in range(tall):
        to_side(level).wait_send()


def run_loss(projected, target, log_scale, number):
    grid = Grid()
    each = projected.shape[0]
    count = grid.total * each
    inside = pl.BlockSpec(memory_space=pltpu.VMEM)
    dma = pltpu.SemaphoreType.DMA((3 + 2 * grid.tall,))
    return pl.pallas_call(
        functools.partial(loss_kernel, grid, each // 2),
        out_shape=[
            jax.ShapeDtypeStruct((each, D), jnp.bfloat16),
            jax.ShapeDtypeStruct((8, 128), jnp.float32),
        ],
        in_specs=[inside] * 3,
        out_specs=[inside] * 2,
        scratch_shapes=[
            pltpu.VMEM((2, grid.tall, 2, 2, 2 * each, D // 2), jnp.bfloat16),
            pltpu.VMEM((count, count), jnp.float32),
            dma,
            dma,
        ],
        compiler_params=pltpu.CompilerParams(collective_id=number, has_side_effects=True),
    )(projected, target, log_scale)


class Tree:

    @staticmethod
    def scratch(grid, blocks):
        count, tall = len(blocks), grid.tall
        leads = ((tall, 2, 2), (tall, 2, 2), (tall, 2), (tall,), (tall,), (tall,))
        dma = pltpu.SemaphoreType.DMA
        level, pair = dma((count, tall)), dma((count, tall, 2))
        buffers = [pltpu.VMEM(lead + block, jnp.bfloat16) for lead in leads for block in blocks]
        return buffers + [level, level, level, pair, pair] + [level] * 5

    @staticmethod
    def size(count):
        return 6 * count + 10

    def __init__(self, grid, srcs, scratch):
        count = len(srcs)
        self.grid, self.count, self.srcs = grid, count, srcs
        self.acc, self.from_side, self.from_v, self.from_u, self.from_low, self.from_high = [
            scratch[k * count : (k + 1) * count] for k in range(6)
        ]
        (
            self.load_sem,
            self.side_send,
            self.side_recv,
            self.v_send,
            self.v_recv,
            self.u_send,
            self.u_recv,
            self.z_send,
            self.low_recv,
            self.high_recv,
        ) = scratch[6 * count :]
        z, x, y, core = self.place = grid.here()
        tall = grid.tall
        self.up, self.down = grid.device(z + 1, x, y, core), grid.device(z - 1, x, y, core)
        self.has_up, self.has_down = z < tall - 1, z > 0
        self.u = lax.rem(x + 1 - core, 2), lax.rem(y + core, 2)
        self.v = lax.rem(x + core, 2), lax.rem(y + 1 - core, 2)
        self.u_device = grid.device(z, *self.u, core)
        self.v_device = grid.device(z, *self.v, core)
        self.sibling = grid.device(z, x, y, 1 - core)
        self.levels = [self.level_of(j) for j in range(tall)]

    def greet_all(self):
        greet(self.u_device)
        greet(self.v_device)
        greet(self.sibling)
        greet(self.up, self.has_up)
        greet(self.down, self.has_down)
        return 3 + self.has_up.astype(jnp.int32) + self.has_down.astype(jnp.int32)

    def each(self, action):
        for m in range(self.count):
            action(m)

    def level_of(self, j):
        tall = self.grid.tall
        tables = [
            sorted(range(tall), key=lambda level: (-abs(level - own), -level))[j] for own in range(tall)
        ]
        value = tables[0]
        for own in range(1, tall):
            value = jnp.where(self.place[0] == own, tables[own], value)
        return value

    def load(self, m, level):
        core = self.place[3]
        return pltpu.make_async_copy(
            self.srcs[m].at[level, :, :, core], self.acc[m].at[level], self.load_sem.at[m, level]
        )

    def remote(self, src, dst, send_sem, recv_sem, device):
        return pltpu.make_async_remote_copy(
            src_ref=src,
            dst_ref=dst,
            send_sem=send_sem,
            recv_sem=recv_sem,
            device_id=device,
            device_id_type=MESH,
        )

    def side(self, m, level):
        return self.remote(
            self.srcs[m].at[level, :, :, 1 - self.place[3]],
            self.from_side[m].at[level],
            self.side_send.at[m, level],
            self.side_recv.at[m, level],
            self.sibling,
        )

    def v_copy(self, m, level, along_u):
        z, x, y, core = self.place
        xx, yy = (1 - x, 1 - y) if along_u else self.v
        return self.remote(
            self.acc[m].at[level, xx, yy],
            self.from_v[m].at[level, along_u],
            self.v_send.at[m, level, along_u],
            self.v_recv.at[m, level, along_u],
            self.v_device,
        )

    def u_copy(self, m, level):
        return self.remote(
            self.acc[m].at[level, self.u[0], self.u[1]],
            self.from_u[m].at[level],
            self.u_send.at[m, level],
            self.u_recv.at[m, level],
            self.u_device,
        )

    def z_copy(self, m, level, upward):
        z, x, y, core = self.place
        return self.remote(
            self.acc[m].at[level, x, y],
            (self.from_low if upward else self.from_high)[m].at[level],
            self.z_send.at[m, level],
            (self.low_recv if upward else self.high_recv).at[m, level],
            self.up if upward else self.down,
        )

    def add(self, m, level, xx, yy, other):
        total = self.acc[m][level, xx, yy].astype(jnp.float32) + other.astype(jnp.float32)
        self.acc[m][level, xx, yy] = total.astype(jnp.bfloat16)

    def loads(self):
        for level in self.levels:
            self.each(lambda m: self.load(m, level).start())

    def sides(self):
        for level in self.levels:
            self.each(lambda m: self.side(m, level).start())

    def first(self, j):
        level = self.levels[j]

        def run(m):
            self.load(m, level).wait()
            self.side(m, level).wait_recv()
            for xx in range(2):
                for yy in range(2):
                    self.add(m, level, xx, yy, self.from_side[m][level, xx, yy])
            self.v_copy(m, level, 1).start()
            self.v_copy(m, level, 0).start()

        self.each(run)

    def second(self, j):
        z, x, y, core = self.place
        level = self.levels[j]

        def run(m):
            self.v_copy(m, level, 1).wait_recv()
            self.add(m, level, self.u[0], self.u[1], self.from_v[m][level, 1])
            self.u_copy(m, level).start()

        def run_own(m):
            self.v_copy(m, level, 0).wait_recv()
            self.add(m, level, x, y, self.from_v[m][level, 0])

        self.each(run)
        self.each(run_own)

    def third(self, j):
        z, x, y, core = self.place
        level = self.levels[j]

        def run(m):
            self.u_copy(m, level).wait_recv()
            self.add(m, level, x, y, self.from_u[m][level])

            @pl.when((level >= z) & self.has_down)
            def _():
                self.z_copy(m, level, True).wait_recv()
                self.add(m, level, x, y, self.from_low[m][level])

            @pl.when((level <= z) & self.has_up)
            def _():
                self.z_copy(m, level, False).wait_recv()
                self.add(m, level, x, y, self.from_high[m][level])

            @pl.when(level > z)
            def _():
                self.z_copy(m, level, True).start()

            @pl.when(level < z)
            def _():
                self.z_copy(m, level, False).start()

        self.each(run)

    def own(self, m):
        z, x, y, core = self.place
        return self.acc[m][z, x, y].astype(jnp.float32)

    def drain(self):
        for level in self.levels:
            self.each(lambda m: self.side(m, level).wait_send())
            self.each(lambda m: self.v_copy(m, level, 0).wait_send())
            self.each(lambda m: self.v_copy(m, level, 1).wait_send())
            self.each(lambda m: self.u_copy(m, level).wait_send())

            @pl.when(level != self.place[0])
            def _():
                self.each(lambda m: self.z_copy(m, level, True).wait_send())


def fold(values):
    n, lanes = values.shape
    part = jnp.sum(values.reshape(n // 8, 8, lanes), 0)
    total = part[:, :128]
    for at in range(128, lanes, 128):
        total = total + part[:, at : at + 128]
    return total


def gain_back(gains_ref, grads_ref, k, grad_out, inputs):
    factor = lax.rsqrt(jnp.mean(inputs * inputs, -1, keepdims=True) + EPS)
    scaled = grad_out * gains_ref[k : k + 1, :]
    grads_ref[k : k + 1, :] += jnp.sum(grad_out * inputs * factor, 0, keepdims=True)
    return factor * (
        scaled - inputs * (factor * factor * jnp.mean(scaled * inputs, -1, keepdims=True))
    )


BACK_SEQS = 2
HALF = 256


def ffn_back_kernel(
    final_ref,
    after_ref,
    mask_col_ref,
    gains_ref,
    pooled_ref,
    grad_proj_ref,
    pre_hbm,
    packed_hbm,
    down_hbm,
    grad_after_ref,
    grad_gains_ref,
    grad_up_hbm,
    grad_down_hbm,
    up,
    head,
    down,
    branch,
    act_two,
    hidden,
    grad_pre,
    grad_act,
    pre,
    grad_pooled,
    stage,
    load_sem,
    pre_sem,
    store_sem,
):
    tokens = final_ref.shape[0]
    tile = BACK_SEQS * L

    def load(k):
        if k == 0:
            return pltpu.make_async_copy(packed_hbm.at[:, pl.ds(PACKED - D, D)], head, load_sem.at[0])
        if k == 1:
            return pltpu.make_async_copy(down_hbm, down, load_sem.at[1])
        return pltpu.make_async_copy(packed_hbm.at[:, pl.ds(WIDE + D, 4 * D)], up, load_sem.at[2])

    def load_pre(j):
        return pltpu.make_async_copy(pre_hbm.at[:, pl.ds(j * D, D)], pre.at[j % 2], pre_sem.at[j % 2])

    load(0).start()
    load_pre(0).start()
    load(1).start()
    load(2).start()
    grad_gains_ref[...] = jnp.zeros_like(grad_gains_ref)
    load(0).wait()
    grad_pooled[...] = matmul_nt(grad_proj_ref[...], head[...])

    @pl.loop(0, tokens // tile)
    def _(step):
        rows = pl.ds(pl.multiple_of(step * tile, tile), tile)
        weight = mask_col_ref[rows, :]
        pieces = []
        for s in range(BACK_SEQS):
            part = weight[s * L : (s + 1) * L]
            count = jnp.sum(part, 0, keepdims=True)
            pieces.append(part * (grad_pooled[pl.ds(step * BACK_SEQS + s, 1), :] / count))
        grad = gain_back(gains_ref, grad_gains_ref, 2, jnp.concatenate(pieces, 0), final_ref[rows, :])
        grad_after_ref[rows, :] = grad
        branch[rows, :] = grad.astype(jnp.bfloat16)
        act_two[rows, :] = normalize(after_ref[rows, :], gains_ref[1:2, :])[0].astype(jnp.bfloat16)

    stores = []

    def store(value, to):
        slot = len(stores) % 2
        if len(stores) >= 2:
            stores[-2].wait()
        stage[slot] = value.astype(jnp.bfloat16)
        stores.append(pltpu.make_async_copy(stage.at[slot], to, store_sem.at[slot]))
        stores[-1].start()

    load(1).wait()
    for j in range(4):
        part = slice(j * D, (j + 1) * D)
        if j < 3:
            load_pre(j + 1).start()
        for at in range(0, tokens, HALF):
            rows = slice(at, at + HALF)
            wide = matmul_nt(branch[rows, :], down[part, :])
            if at == 0:
                load_pre(j).wait()
            some = pre[j % 2, rows, :]
            half, tan = gelu_parts(some)
            hidden[rows, :] = (some * half).astype(jnp.bfloat16)
            slope = np.float32(np.sqrt(2 / np.pi)) * (1.0 + (3 * 0.044715) * (some * some))
            slope = half + 0.5 * some * (1.0 - tan * tan) * slope
            grad_pre[rows, :] = (wide * slope).astype(jnp.bfloat16)
            if j == 0:
                if at == 0:
                    load(2).wait()
                grad_act[rows, :] = matmul_nt(grad_pre[rows, :], up[:, part])
            else:
                grad_act[rows, :] += matmul_nt(grad_pre[rows, :], up[:, part])
        store(matmul_tn(hidden[...], branch[...]), grad_down_hbm.at[pl.ds(j * D, D), :])
        store(matmul_tn(act_two[...], grad_pre[...]), grad_up_hbm.at[:, pl.ds(j * D, D)])
    store(
        matmul_tn(pooled_ref[...].astype(jnp.bfloat16), grad_proj_ref[...]),
        grad_up_hbm.at[:, pl.ds(4 * D, D)],
    )

    @pl.loop(0, tokens // tile)
    def _(step):
        rows = pl.ds(pl.multiple_of(step * tile, tile), tile)
        grad = gain_back(gains_ref, grad_gains_ref, 1, grad_act[rows, :], after_ref[rows, :])
        grad_after_ref[rows, :] += grad

    stores[-2].wait()
    stores[-1].wait()


def run_ffn_back(final, after, mask_col, gains, pooled, grad_proj, pre, packed, down):
    tokens, seqs = final.shape[0], pooled.shape[0]
    anywhere, inside = pl.BlockSpec(memory_space=pl.ANY), pl.BlockSpec(memory_space=pltpu.VMEM)

    def low(*shape):
        return pltpu.VMEM(shape, jnp.bfloat16)

    def full(*shape):
        return pltpu.VMEM(shape, jnp.float32)

    return pl.pallas_call(
        ffn_back_kernel,
        out_shape=[
            jax.ShapeDtypeStruct((tokens, D), jnp.float32),
            jax.ShapeDtypeStruct((3, D), jnp.float32),
            jax.ShapeDtypeStruct((D, 5 * D), jnp.bfloat16),
            jax.ShapeDtypeStruct((4 * D, D), jnp.bfloat16),
        ],
        in_specs=[inside] * 6 + [anywhere] * 3,
        out_specs=[inside] * 2 + [anywhere] * 2,
        scratch_shapes=[
            low(D, 4 * D),
            low(D, D),
            low(4 * D, D),
            low(tokens, D),
            low(tokens, D),
            low(tokens, D),
            low(tokens, D),
            full(tokens, D),
            full(2, tokens, D),
            full(seqs, D),
            low(2, D, D),
            pltpu.SemaphoreType.DMA((3,)),
            pltpu.SemaphoreType.DMA((2,)),
            pltpu.SemaphoreType.DMA((2,)),
        ],
        compiler_params=pltpu.CompilerParams(vmem_limit_bytes=62 * 1024 * 1024),
    )(final, after, mask_col, gains, pooled, grad_proj, pre, packed, down)


def attn_back_kernel(grid, *refs):
    x0_ref, mask_col_ref, mixed_ref, attended, total_ref, grad_after_ref, gains_ref, bias_ref, packed_hbm = refs[:9]
    srcs = refs[9:11]
    rows_ref, grad_gains_ref, grad_bias_ref, grad_attn_hbm = refs[11:15]
    outs, square_ref = refs[15:17], refs[17]
    packed, act_one, branch_one, grad_mixed, stage, load_sem, store_sem = refs[18:25]
    tree = Tree(grid, srcs, refs[25:])
    step = pl.program_id(0)
    last_step = pl.num_programs(0) - 1
    tile_seqs = x0_ref.shape[0] // L
    tile = tile_seqs * L
    base = pl.multiple_of(step * tile, tile)

    def load(k):
        part = pl.ds(WIDE, D) if k else pl.ds(0, WIDE)
        return pltpu.make_async_copy(packed_hbm.at[:, part], packed.at[:, part], load_sem.at[k])

    @pl.when(step == 0)
    def _():
        friends = tree.greet_all()
        load(1).start()
        load(0).start()
        tree.loads()
        grad_gains_ref[...] = jnp.zeros_like(grad_gains_ref)
        grad_bias_ref[...] = jnp.zeros_like(grad_bias_ref)
        meet(friends)
        tree.sides()
        load(1).wait()

    rows = pl.ds(base, tile)
    grad_after = grad_after_ref[...]
    weight = mask_col_ref[...]
    branch = grad_after.astype(jnp.bfloat16)
    branch_one[rows, :] = branch
    grad_attended = matmul_nt(branch, packed[:, WIDE:]).astype(jnp.bfloat16)
    act_one[rows, :] = normalize(x0_ref[...], gains_ref[0:1, :])[0].astype(jnp.bfloat16)

    def at_step(number, action, *levels):
        @pl.when(step == number)
        def _():
            for j in levels:
                action(j)

    at_step(0, tree.first, 0, 1)
    at_step(1, tree.second, 0)
    at_step(2, tree.third, 0)
    at_step(3, tree.third, 1)
    zero = jnp.zeros((), jnp.bfloat16)
    mine = lane_is((L, 128), 0, HD)
    for s in range(tile_seqs):
        part = slice(s * L, (s + 1) * L)
        here = pl.ds(pl.multiple_of(base + s * L, L), L)
        keep = jnp.where(weight[part] > 0, 0.0, -1000000000.0)
        for pair in range(HEADS // 2):
            at = pair * 128
            query = mixed_ref[part, at : at + 128]
            key = mixed_ref[part, D + at : D + at + 128]
            value = mixed_ref[part, 2 * D + at : 2 * D + at + 128]
            grad_out = grad_attended[part, at : at + 128]
            keys = jnp.concatenate([jnp.where(mine, key, zero), jnp.where(mine, zero, key)], 0)
            values = jnp.concatenate([jnp.where(mine, value, zero), jnp.where(mine, zero, value)], 0)
            scores = (matmul_nt(keys, query) * SCALE).reshape(2, L, L)
            scores = scores + bias_ref[2 * pair : 2 * pair + 2] + keep[None]
            prob = jnp.exp(scores - total_ref[s, 2 * pair : 2 * pair + 2, :][:, None, :])
            grad_prob = matmul_nt(values, grad_out).reshape(2, L, L)
            mean = jnp.sum(prob * grad_prob, 1, keepdims=True)
            grad_scores = (prob * (grad_prob - mean)).astype(jnp.bfloat16)
            grad_bias_ref[2 * pair : 2 * pair + 2] += grad_scores.astype(jnp.float32)
            prob_low = prob.astype(jnp.bfloat16)
            flipped = jnp.transpose(key)
            grad_query = jnp.concatenate(
                [matmul(flipped[:HD], grad_scores[0]), matmul(flipped[HD:], grad_scores[1])], 0
            )
            grad_mixed[here, at : at + 128] = (jnp.transpose(grad_query) * SCALE).astype(jnp.bfloat16)
            grad_keys = matmul(grad_scores.reshape(2 * L, L), query)
            grad_key = jnp.where(mine, grad_keys[:L], grad_keys[L:]) * SCALE
            grad_mixed[here, D + at : D + at + 128] = grad_key.astype(jnp.bfloat16)
            grad_values = matmul(prob_low.reshape(2 * L, L), grad_out)
            grad_value = jnp.where(mine, grad_values[:L], grad_values[L:])
            grad_mixed[here, 2 * D + at : 2 * D + at + 128] = grad_value.astype(jnp.bfloat16)

    @pl.when(step == 0)
    def _():
        tree.first(2)
        tree.first(3)
        load(0).wait()

    at_step(1, tree.second, 1)
    at_step(2, tree.second, 2)
    at_step(3, tree.second, 3)
    grad_act = matmul_nt(grad_mixed[rows, :], packed[:, :WIDE])
    grad_low = gain_back(gains_ref, grad_gains_ref, 0, grad_act, x0_ref[...])
    rows_ref[...] = (grad_after + grad_low).astype(jnp.bfloat16)

    @pl.when(step == last_step)
    def _():
        tree.third(2)
        jobs = [(attended, branch_one, slice(0, D), 3)]
        for j in range(3):
            jobs.append((act_one, grad_mixed, slice(j * D, (j + 1) * D), j))
        copies = []
        for number, (left, right, part, at) in enumerate(jobs):
            slot = number % 2
            if number >= 2:
                copies[number - 2].wait()
            stage[slot] = matmul_tn(left[...], right[:, part]).astype(jnp.bfloat16)
            to = grad_attn_hbm.at[:, pl.ds(at * D, D)]
            copies.append(pltpu.make_async_copy(stage.at[slot], to, store_sem.at[slot]))
            copies[-1].start()
        tree.third(3)
        square_ref[...] = jnp.zeros_like(square_ref)

        def give(m):
            wide = tree.own(m)
            outs[m][...] = wide
            square_ref[0:8, :] += fold(wide * wide)

        tree.each(give)
        copies[-2].wait()
        copies[-1].wait()
        tree.drain()


def run_attn_back(
    x0, mask_col, mixed, attended, totals, grad_after, gains, bias_full, packed, grad_up, grad_down, number
):
    grid = Grid()
    tokens = x0.shape[0]
    tile = BACK_SEQS * L
    steps = tokens // tile
    srcs = [grad.reshape(grid.total, -1, grad.shape[1]) for grad in (grad_up, grad_down)]
    blocks = [src.shape[1:] for src in srcs]
    srcs = [src.reshape((grid.tall, 2, 2, 2) + src.shape[1:]) for src in srcs]

    def rows(width):
        return pl.BlockSpec((tile, width), lambda i: (i, 0))

    def whole(*shape):
        return pl.BlockSpec(shape, lambda i: (0,) * len(shape), pipeline_mode=pl.Buffered(1))

    def low(*shape):
        return pltpu.VMEM(shape, jnp.bfloat16)

    anywhere = pl.BlockSpec(memory_space=pl.ANY)
    return pl.pallas_call(
        functools.partial(attn_back_kernel, grid),
        grid=(steps,),
        out_shape=[
            jax.ShapeDtypeStruct((tokens, D), jnp.bfloat16),
            jax.ShapeDtypeStruct((1, D), jnp.float32),
            jax.ShapeDtypeStruct((HEADS, L, L), jnp.float32),
            jax.ShapeDtypeStruct((D, WIDE + D), jnp.bfloat16),
        ]
        + [jax.ShapeDtypeStruct(block, jnp.float32) for block in blocks]
        + [jax.ShapeDtypeStruct((16, 128), jnp.float32)],
        in_specs=[
            rows(D),
            rows(1),
            rows(WIDE),
            whole(tokens, D),
            pl.BlockSpec((BACK_SEQS, HEADS, L), lambda i: (i, 0, 0)),
            rows(D),
            whole(3, D),
            whole(HEADS, L, L),
            anywhere,
            anywhere,
            anywhere,
        ],
        out_specs=[rows(D), whole(1, D), whole(HEADS, L, L), anywhere]
        + [whole(*block) for block in blocks]
        + [whole(16, 128)],
        scratch_shapes=[
            low(D, WIDE + D),
            low(tokens, D),
            low(tokens, D),
            low(tokens, WIDE),
            low(2, D, D),
            pltpu.SemaphoreType.DMA((2,)),
            pltpu.SemaphoreType.DMA((2,)),
        ]
        + Tree.scratch(grid, blocks),
        compiler_params=pltpu.CompilerParams(
            collective_id=number, has_side_effects=True, vmem_limit_bytes=62 * 1024 * 1024
        ),
    )(x0, mask_col, mixed, attended, totals, grad_after, gains, bias_full, packed, *srcs)


def finish_kernel(grid, count, *refs):
    srcs, (grad_rows, slot_ref, ids, small, square_ref) = refs[:count], refs[count : count + 5]
    refs = refs[count + 5 :]
    outs, (table_out, small_out, square_out) = refs[:count], refs[count : count + 3]
    refs = refs[count + 3 :]
    tree = Tree(grid, srcs, refs[: Tree.size(count)])
    refs = refs[Tree.size(count) :]
    sums, rows, part_sums, small_stage, small_in, square_stage, square_in = refs[:7]
    line_send, on_send, row_recv, small_send, small_recv, square_send, square_recv = refs[7:]
    z, x, y, core = grid.here()
    tall = grid.tall
    d, f = lax.axis_index("dp"), lax.axis_index("fsdp")
    me = f * grid.dp + d
    sibling = tree.sibling
    f_side = y * 2 + 1 - core
    f_y = (1 - y) * 2 + core
    f_far = (1 - y) * 2 + 1 - core
    for level in range(tall):
        small_in[3 + level] = jnp.zeros(small.shape, jnp.float32)
        square_in[3 + level] = jnp.zeros((16, 128), jnp.float32)
    x_device, y_device = grid.device(z, 1 - x, y, core), grid.device(z, x, 1 - y, core)

    @pl.loop(1, grid.dp)
    def _(step):
        greet((lax.rem(d + step, grid.dp), f))

    greet(y_device)
    greet(sibling)

    def line(peer, slot):
        return pltpu.make_async_remote_copy(
            src_ref=sums.at[peer],
            dst_ref=rows.at[slot],
            send_sem=line_send.at[peer],
            recv_sem=row_recv.at[slot],
            device_id=(peer, f),
            device_id_type=MESH,
        )

    def onward(slot, to_side, own_block=False):
        return pltpu.make_async_remote_copy(
            src_ref=sums.at[d] if own_block else rows.at[slot],
            dst_ref=rows.at[slot],
            send_sem=on_send.at[1 if to_side else 0, slot],
            recv_sem=row_recv.at[slot],
            device_id=(d, f_side if to_side else f_y),
            device_id_type=MESH,
        )

    def total_of(stage, inbox, send_sem, recv_sem):
        partners = (sibling, x_device, y_device)

        def copy(r):
            return pltpu.make_async_remote_copy(
                src_ref=stage.at[r],
                dst_ref=inbox.at[r],
                send_sem=send_sem.at[r],
                recv_sem=recv_sem.at[r],
                device_id=partners[r],
                device_id_type=MESH,
            )

        def z_send(level, slot):
            return pltpu.make_async_remote_copy(
                src_ref=stage.at[3],
                dst_ref=inbox.at[3 + slot],
                send_sem=send_sem.at[3 + level],
                recv_sem=recv_sem.at[3 + slot],
                device_id=grid.device(level, x, y, core),
                device_id_type=MESH,
            )

        def others(action):
            @pl.loop(1, tall)
            def _(step):
                action(lax.rem(z + step, tall))

        def send(r):
            if r < 3:
                copy(r).start()
            else:
                others(lambda level: z_send(level, z).start())

        def take(r):
            if r < 3:
                copy(r).wait_recv()
                stage[r + 1] = stage[r] + inbox[r]
                send(r + 1)
            else:
                others(lambda level: z_send(level, level).wait_recv())

        def result():
            total = stage[3]
            for level in range(tall):
                total = total + jnp.where(z == level, 0.0, inbox[3 + level])
            for r in range(3):
                copy(r).wait_send()
            others(lambda level: z_send(level, level).wait_send())
            return total

        return send, take, result

    small_stage[0] = small[...]
    small_sends, small_take, small_result = total_of(small_stage, small_in, small_send, small_recv)
    square_sends, square_take, square_result = total_of(square_stage, square_in, square_send, square_recv)
    tree.loads()
    cap = sums.shape[1]
    lanes = lax.broadcasted_iota(jnp.int32, (1, cap), 1).astype(jnp.float32)

    @pl.loop(0, grid.dp)
    def _(peer):
        hot = jnp.where(slot_ref[...] == lanes + (peer * cap).astype(jnp.float32), 1.0, 0.0)
        sums[peer] = matmul_tn(hot.astype(jnp.bfloat16), grad_rows[...]).astype(jnp.bfloat16)

    rows[me] = sums[d]
    meet(grid.dp + 1)
    small_sends(0)

    @pl.loop(1, grid.dp)
    def _(step):
        line(lax.rem(d + step, grid.dp), me).start()

    tree.sides()
    onward(me, False, True).start()
    onward(me, True, True).start()

    def pass_lines():
        @pl.loop(1, grid.dp)
        def _(step):
            slot = f * grid.dp + lax.rem(d + grid.dp - step, grid.dp)
            line(d, slot).wait_recv()
            onward(slot, False).start()
            onward(slot, True).start()

    def pass_y():
        @pl.loop(0, grid.dp)
        def _(step):
            slot = f_y * grid.dp + lax.rem(d + grid.dp - step, grid.dp)
            line(d, slot).wait_recv()
            onward(slot, True).start()

    def rows_in(column):
        @pl.loop(0, grid.dp)
        def _(step):
            line(d, column * grid.dp + step).wait_recv()

    table_rows = table_out.shape[0]
    whole_blocks = table_rows // ROW_BLOCK
    square_stage[0] = square_ref[...]

    per = grid.dp * rows.shape[1]

    def product(column, start, size):
        place = start + lax.broadcasted_iota(jnp.int32, (size, per), 0)
        hot = jnp.where(place.astype(jnp.float32) == ids[pl.ds(column, 1), :], 1.0, 0.0)
        some = rows[pl.ds(column * grid.dp, grid.dp)].reshape(per, D)
        return matmul(hot.astype(jnp.bfloat16), some)

    def spread_near():
        @pl.loop(0, part_sums.shape[0] // ROW_BLOCK)
        def _(block):
            start = pl.multiple_of(block * ROW_BLOCK, ROW_BLOCK)
            part_sums[pl.ds(start, ROW_BLOCK), :] = product(f, start, ROW_BLOCK) + product(
                f_side, start, ROW_BLOCK
            )

    def spread(start, size):
        total = part_sums[pl.ds(start, size), :] + product(f_y, start, size) + product(f_far, start, size)
        low = total.astype(jnp.bfloat16)
        table_out[pl.ds(start, size), :] = low
        wide = low.astype(jnp.float32)
        square_stage[0, 8:16, :] += fold(wide * wide)

    def spread_all():
        @pl.loop(0, whole_blocks)
        def _(block):
            spread(pl.multiple_of(block * ROW_BLOCK, ROW_BLOCK), ROW_BLOCK)

        if table_rows % ROW_BLOCK:
            spread(whole_blocks * ROW_BLOCK, table_rows % ROW_BLOCK)

    for j in range(tall):
        tree.first(j)
        if j < 3:
            small_take(j)
    pass_lines()
    tree.second(0)
    tree.second(1)
    rows_in(f_side)
    spread_near()
    tree.third(0)
    tree.second(2)
    pass_y()
    tree.third(1)
    tree.second(3)
    tree.third(2)
    rows_in(f_far)
    spread_all()
    tree.third(3)

    def give(m):
        wide = tree.own(m)
        outs[m][...] = wide
        square_stage[0, 0:8, :] += fold(wide * wide)

    tree.each(give)

    square_sends(0)
    small_take(3)
    small_out[...] = small_result()
    for r in range(3):
        square_take(r)

    tree.drain()

    @pl.loop(0, grid.dp)
    def _(step):
        onward(f * grid.dp + step, False).wait_send()
        onward(f * grid.dp + step, True).wait_send()
        onward(f_y * grid.dp + step, True).wait_send()

    @pl.loop(1, grid.dp)
    def _(step):
        line(lax.rem(d + step, grid.dp), me).wait_send()

    square_take(3)
    square_out[...] = square_result()


def finish(srcs, grad_rows, slot, ids, small, squares, vocab_rows, number):
    grid = Grid()
    count = len(srcs)
    tall = grid.tall
    blocks = [src.shape[1:] for src in srcs]
    srcs = [src.reshape((tall, 2, 2, 2) + src.shape[1:]) for src in srcs]
    dma = pltpu.SemaphoreType.DMA
    by_device, by_step = dma((grid.total,)), dma((3 + tall,))
    scratch = Tree.scratch(grid, blocks) + [
        pltpu.VMEM((grid.dp, CAP, D), jnp.bfloat16),
        pltpu.VMEM((grid.total, CAP, D), jnp.bfloat16),
        pltpu.VMEM((-(-vocab_rows // ROW_BLOCK) * ROW_BLOCK, D), jnp.float32),
        pltpu.VMEM((4,) + small.shape, jnp.float32),
        pltpu.VMEM((3 + tall,) + small.shape, jnp.float32),
        pltpu.VMEM((4, 16, 128), jnp.float32),
        pltpu.VMEM((3 + tall, 16, 128), jnp.float32),
        dma((grid.dp,)),
        dma((2, grid.total)),
        by_device,
    ]
    anywhere, inside = pl.BlockSpec(memory_space=pl.ANY), pl.BlockSpec(memory_space=pltpu.VMEM)
    results = pl.pallas_call(
        functools.partial(finish_kernel, grid, count),
        out_shape=[jax.ShapeDtypeStruct(block, jnp.float32) for block in blocks]
        + [
            jax.ShapeDtypeStruct((vocab_rows, D), jnp.bfloat16),
            jax.ShapeDtypeStruct(small.shape, jnp.float32),
            jax.ShapeDtypeStruct((16, 128), jnp.float32),
        ],
        in_specs=[anywhere] * count + [inside] * 5,
        out_specs=[inside] * (count + 3),
        scratch_shapes=scratch + [by_step] * 4,
        compiler_params=pltpu.CompilerParams(
            collective_id=number, has_side_effects=True, vmem_limit_bytes=62 * 1024 * 1024
        ),
    )(*srcs, grad_rows, slot, ids, small, squares)
    return (results[:count], *results[count:])


def update_kernel(fs, *refs):
    squares, summed, scale_grad, table, table_first, table_second, table_grad = refs[:7]
    rest, shards = refs[7:22], refs[22:25]
    norm_ref, out_first, out_second, out = refs[25:29]
    rest_outs, factor_ref = refs[29:44], refs[44]

    def row_sum(values):
        return jnp.sum(jnp.sum(values, 1, keepdims=True), 0, keepdims=True)

    @pl.when(pl.program_id(0) == 0)
    def _():
        total = row_sum(squares[0:8, :]) + row_sum(squares[8:16, :]) / float(fs)
        total = total + (row_sum(summed[...] * summed[...]) + scale_grad[...] * scale_grad[...])
        norm = jnp.sqrt(total)
        norm_ref[...] = jnp.broadcast_to(norm, norm_ref.shape)
        factor_ref[...] = jnp.minimum(1.0, CLIP / (norm + 1e-06))
        attn, up, down = shards
        grads = (attn[:, :WIDE], attn[:, WIDE:], up[:, : 4 * D], down[...], up[:, 4 * D :])
        for k in range(5):
            first_new, second_new, new = adam_update(
                *[ref[...] for ref in rest[3 * k : 3 * k + 3]],
                grads[k],
                factor_ref[...],
                RATES[k + 1],
                DECAYS[k + 1],
            )
            rest_outs[3 * k][...] = first_new
            rest_outs[3 * k + 1][...] = second_new
            rest_outs[3 * k + 2][...] = new

    first_new, second_new, new = adam_update(
        table[...],
        table_first[...],
        table_second[...],
        table_grad[...].astype(jnp.float32),
        factor_ref[...],
        RATES[0],
        DECAYS[0],
    )
    out_first[...] = first_new
    out_second[...] = second_new
    out[...] = new


def run_update(fs, squares, summed, scale_grad, table_arrays, table_grad, rest, shards):
    vocab_rows = table_grad.shape[0]
    blocks = pl.BlockSpec((UPDATE_BLOCK, D), lambda i: (i, 0))

    def whole(array):
        return pl.BlockSpec(
            array.shape, lambda i: (0,) * array.ndim, pipeline_mode=pl.Buffered(1)
        )

    norm = jax.ShapeDtypeStruct((8, 128), jnp.float32)
    return pl.pallas_call(
        functools.partial(update_kernel, fs),
        grid=(-(-vocab_rows // UPDATE_BLOCK),),
        out_shape=[norm]
        + [jax.ShapeDtypeStruct(table_grad.shape, jnp.float32)] * 3
        + [jax.ShapeDtypeStruct(array.shape, jnp.float32) for array in rest],
        in_specs=[whole(squares), whole(summed), whole(scale_grad)]
        + [blocks] * 4
        + [whole(array) for array in (*rest, *shards)],
        out_specs=[whole(norm)] + [blocks] * 3 + [whole(array) for array in rest],
        scratch_shapes=[pltpu.VMEM((1, 1), jnp.float32)],
        compiler_params=pltpu.CompilerParams(vmem_limit_bytes=60 * 1024 * 1024),
    )(squares, summed, scale_grad, *table_arrays, table_grad, *rest, *shards)


def plain_body(
    token_ids,
    pad_mask,
    hard_negative,
    table,
    table_first,
    table_second,
    attn_in,
    attn_in_first,
    attn_in_second,
    attn_out,
    attn_out_first,
    attn_out_second,
    ffn_in,
    ffn_in_first,
    ffn_in_second,
    ffn_out,
    ffn_out_first,
    ffn_out_second,
    proj_head,
    proj_head_first,
    proj_head_second,
    small_params,
    small_first,
    small_second,
):
    dp_count = lax.axis_size("dp")
    fsdp_count = lax.axis_size("fsdp")
    device_flat = lax.axis_index("dp") * fsdp_count + lax.axis_index("fsdp")
    pairs_here = token_ids.shape[1]
    pairs_total = pairs_here * dp_count * fsdp_count
    seq_count = 2 * pairs_here
    vocab_rows = table.shape[0]
    row_base = lax.axis_index("dp") * vocab_rows
    gain_rows = small_params[: 3 * D].reshape(3, D)
    bias_table = small_params[3 * D : 3 * D + NB * HEADS].reshape(NB, HEADS)
    log_scale = small_params[3 * D + NB * HEADS]
    buckets = jnp.asarray(bucket_table(L, NB).reshape(-1), jnp.int32)
    bucket_hot = (buckets[:, None] == jnp.arange(NB, dtype=jnp.int32)[None, :]).astype(jnp.float32)
    bias_full = (
        jnp.dot(bucket_hot, bias_table, precision=HIGH).reshape(L, L, HEADS).transpose(2, 0, 1)
    )
    mask_rows = pad_mask.reshape(seq_count, L)
    ids_flat = token_ids.reshape(-1)
    table_low = table.astype(jnp.bfloat16)
    ids_all = lax.all_gather(ids_flat, "dp", axis=0, tiled=True)
    picked = ids_all - row_base
    inside = (picked >= 0) & (picked < vocab_rows)
    chosen = jnp.take(table_low, jnp.clip(picked, 0, vocab_rows - 1), axis=0)
    embedded = lax.psum_scatter(
        jnp.where(inside[:, None], chosen.astype(jnp.float32), 0.0).astype(jnp.bfloat16),
        "dp",
        scatter_dimension=0,
        tiled=True,
    ).astype(jnp.float32)
    shards = (
        attn_in.astype(jnp.bfloat16),
        attn_out.astype(jnp.bfloat16),
        ffn_in.astype(jnp.bfloat16),
        ffn_out.astype(jnp.bfloat16),
        proj_head.astype(jnp.bfloat16),
    )
    gathered = (
        lax.all_gather(shards[0], ("dp", "fsdp"), axis=0, tiled=True),
        lax.all_gather(shards[1], ("dp", "fsdp"), axis=0, tiled=True),
        lax.all_gather(shards[2], ("dp", "fsdp"), axis=0, tiled=True),
        lax.all_gather(shards[3], ("dp", "fsdp"), axis=0, tiled=True),
        lax.all_gather(shards[4], ("dp", "fsdp"), axis=0, tiled=True),
    )
    final_rows, kept = layer_forward(embedded, mask_rows, gathered[:4], gain_rows, bias_full)
    normed_three, factor_three = normalize(final_rows, gain_rows[2])
    mask_weight = mask_rows.astype(jnp.float32)[:, :, None]
    counts = jnp.sum(mask_weight, 1)
    pooled = jnp.sum(normed_three.reshape(seq_count, L, D) * mask_weight, 1) / counts
    pooled_low = pooled.astype(jnp.bfloat16)
    projected = matmul(pooled_low, gathered[4])
    proj_factor = lax.rsqrt(jnp.sum(projected * projected, -1, keepdims=True) + EPS)
    unit_rows = projected * proj_factor
    unit_low = unit_rows.astype(jnp.bfloat16)
    mine_query = unit_low[:pairs_here]
    all_pass = lax.all_gather(unit_low[pairs_here:], ("dp", "fsdp"), axis=0, tiled=True)
    similar = matmul_nt(mine_query, all_pass)
    sim_scale = jnp.exp(log_scale)
    columns = jnp.arange(pairs_total, dtype=jnp.int32)
    own_index = device_flat * pairs_here + jnp.arange(pairs_here, dtype=jnp.int32)
    own_mask = (columns[None, :] == own_index[:, None]).astype(jnp.float32)
    negative = (columns[None, :] == hard_negative[:, None]).astype(jnp.float32)
    logits = sim_scale * similar - MARGIN * own_mask
    diagonal = jnp.sum(logits * own_mask, 1)
    hardest = jnp.sum(logits * negative, 1)
    row_max = jnp.max(logits, 1, keepdims=True)
    log_total = row_max + jnp.log(jnp.sum(jnp.exp(logits - row_max), 1, keepdims=True))
    loss_local = jnp.sum(log_total[:, 0] - diagonal + jax.nn.softplus(hardest - diagonal))
    hinge_gate = jax.nn.sigmoid(hardest - diagonal)
    grad_logits = (
        jnp.exp(logits - log_total) - own_mask + hinge_gate[:, None] * (negative - own_mask)
    )
    grad_log_scale = sim_scale * jnp.sum(grad_logits * similar)
    grad_similar = (sim_scale * grad_logits).astype(jnp.bfloat16)
    grad_query = matmul(grad_similar, all_pass).astype(jnp.bfloat16)
    grad_pass_terms = matmul_tn(grad_similar, mine_query)
    grad_pass = lax.psum_scatter(
        grad_pass_terms, ("dp", "fsdp"), scatter_dimension=0, tiled=True
    ).astype(jnp.bfloat16)
    grad_units = jnp.concatenate([grad_query, grad_pass], 0).astype(jnp.float32)
    grad_proj = (
        proj_factor * (grad_units - unit_rows * jnp.sum(grad_units * unit_rows, -1, keepdims=True))
    ).astype(jnp.bfloat16)
    gathered_back = (
        lax.all_gather(shards[0], ("dp", "fsdp"), axis=0, tiled=True),
        lax.all_gather(shards[1], ("dp", "fsdp"), axis=0, tiled=True),
        lax.all_gather(shards[2], ("dp", "fsdp"), axis=0, tiled=True),
        lax.all_gather(shards[3], ("dp", "fsdp"), axis=0, tiled=True),
        lax.all_gather(shards[4], ("dp", "fsdp"), axis=0, tiled=True),
    )
    grad_proj_head = matmul_tn(pooled_low, grad_proj)
    grad_pooled = matmul_nt(grad_proj, gathered_back[4])
    grad_normed = ((grad_pooled / counts)[:, None, :] * mask_weight).reshape(-1, D)
    grad_final, gain_three = normalize_back(grad_normed, final_rows, factor_three, gain_rows[2])
    grad_rows, matrix_grads, gain_one, gain_two, grad_bias = layer_backward(
        grad_final, kept, mask_rows, gathered_back[:4], gain_rows, bias_full
    )
    attn_in_grad, attn_out_grad, ffn_in_grad, ffn_out_grad = matrix_grads
    grad_bias_table = jnp.dot(grad_bias.reshape(HEADS, L * L), bucket_hot, precision=HIGH).T
    small_local = jnp.concatenate(
        [gain_one, gain_two, gain_three, grad_bias_table.reshape(-1), grad_log_scale[None]]
    )
    small_grad = lax.psum(small_local, ("dp", "fsdp"))
    weight_grads = (
        lax.psum_scatter(attn_in_grad, ("dp", "fsdp"), scatter_dimension=0, tiled=True),
        lax.psum_scatter(attn_out_grad, ("dp", "fsdp"), scatter_dimension=0, tiled=True),
        lax.psum_scatter(ffn_in_grad, ("dp", "fsdp"), scatter_dimension=0, tiled=True),
        lax.psum_scatter(ffn_out_grad, ("dp", "fsdp"), scatter_dimension=0, tiled=True),
        lax.psum_scatter(grad_proj_head, ("dp", "fsdp"), scatter_dimension=0, tiled=True),
    )
    rows_back = lax.all_gather(grad_rows.astype(jnp.bfloat16), "dp", axis=0, tiled=True)
    turn_count = dp_count // 4
    block_rows = rows_back.shape[0] // turn_count

    def add_block(running, piece_pair):
        block_grads, block_ids = piece_pair
        local_ids = block_ids - row_base
        inside = (local_ids >= 0) & (local_ids < vocab_rows)
        segment = jnp.where(inside, local_ids, vocab_rows)
        summed = jax.ops.segment_sum(
            block_grads.astype(jnp.float32), segment, num_segments=vocab_rows + 1
        )
        return (running + summed[:vocab_rows], None)

    table_full, _ = lax.scan(
        add_block,
        jnp.zeros((vocab_rows, D), jnp.float32),
        (rows_back.reshape(turn_count, block_rows, D), ids_all.reshape(turn_count, block_rows)),
    )
    table_grad = lax.psum(table_full.astype(jnp.bfloat16), "fsdp").astype(jnp.float32)
    owned = (table_grad,) + tuple(weight_grads)
    squares = jnp.sum(table_grad * table_grad) / fsdp_count
    for gradient in weight_grads:
        squares = squares + jnp.sum(gradient * gradient)
    total_squares, loss_sum = lax.psum((squares, loss_local), ("dp", "fsdp"))
    norm_value = jnp.sqrt(total_squares + jnp.sum(small_grad * small_grad))
    factor = jnp.minimum(1.0, CLIP / (norm_value + 1e-06))
    masters = (table, attn_in, attn_out, ffn_in, ffn_out, proj_head, small_params)
    firsts = (
        table_first,
        attn_in_first,
        attn_out_first,
        ffn_in_first,
        ffn_out_first,
        proj_head_first,
        small_first,
    )
    seconds = (
        table_second,
        attn_in_second,
        attn_out_second,
        ffn_in_second,
        ffn_out_second,
        proj_head_second,
        small_second,
    )
    gradients = owned + (small_grad,)
    results = [loss_sum, norm_value]
    for kind_index in range(7):
        results.extend(
            adam_update(
                masters[kind_index],
                firsts[kind_index],
                seconds[kind_index],
                gradients[kind_index],
                factor,
                RATES[kind_index],
                DECAYS[kind_index],
            )
        )
    return tuple(results)


def fits(mesh):
    return mesh.shape["fsdp"] == 4 and mesh.shape["dp"] == 8


def dense_rows(ids_flat, table, row_base):
    vocab_rows = table.shape[0]
    ids_all = lax.all_gather(ids_flat, "dp", axis=0, tiled=True)
    picked = ids_all - row_base
    inside = (picked >= 0) & (picked < vocab_rows)
    chosen = jnp.take(table, jnp.clip(picked, 0, vocab_rows - 1), axis=0)
    return lax.psum_scatter(
        jnp.where(inside[:, None], chosen, 0.0).astype(jnp.bfloat16),
        "dp",
        scatter_dimension=0,
        tiled=True,
    ).astype(jnp.float32)


def dense_table_grad(ids_flat, grad_low, vocab_rows, row_base):
    ids_all = lax.all_gather(ids_flat, "dp", axis=0, tiled=True)
    rows_back = lax.all_gather(grad_low, "dp", axis=0, tiled=True)
    turn_count = lax.axis_size("dp") // 4
    block_rows = rows_back.shape[0] // turn_count

    def add_block(running, piece_pair):
        block_grads, block_ids = piece_pair
        local_ids = block_ids - row_base
        inside = (local_ids >= 0) & (local_ids < vocab_rows)
        segment = jnp.where(inside, local_ids, vocab_rows)
        summed = jax.ops.segment_sum(
            block_grads.astype(jnp.float32), segment, num_segments=vocab_rows + 1
        )
        return (running + summed[:vocab_rows], None)

    table_full, _ = lax.scan(
        add_block,
        jnp.zeros((vocab_rows, D), jnp.float32),
        (rows_back.reshape(turn_count, block_rows, D), ids_all.reshape(turn_count, block_rows)),
    )
    return lax.psum(table_full.astype(jnp.bfloat16), "fsdp")


def once(flag, make, value):
    return lax.while_loop(lambda state: state[0], lambda state: (False, make(state[1])), (flag, value))[1]


def fast_body(
    token_ids,
    pad_mask,
    hard_negative,
    table,
    table_first,
    table_second,
    attn_in,
    attn_in_first,
    attn_in_second,
    attn_out,
    attn_out_first,
    attn_out_second,
    ffn_in,
    ffn_in_first,
    ffn_in_second,
    ffn_out,
    ffn_out_first,
    ffn_out_second,
    proj_head,
    proj_head_first,
    proj_head_second,
    small_params,
    small_first,
    small_second,
):
    dp_count = lax.axis_size("dp")
    fsdp_count = lax.axis_size("fsdp")
    total = dp_count * fsdp_count
    pairs_here = token_ids.shape[1]
    pairs_total = pairs_here * total
    seq_count = 2 * pairs_here
    vocab_rows = table.shape[0]
    row_base = lax.axis_index("dp") * vocab_rows
    gain_rows = small_params[: 3 * D].reshape(3, D)
    bias_table = small_params[3 * D : 3 * D + NB * HEADS].reshape(NB, HEADS)
    log_scale = small_params[3 * D + NB * HEADS]
    buckets = jnp.asarray(bucket_table(L, NB).T.reshape(-1), jnp.int32)
    bucket_hot = (buckets[:, None] == jnp.arange(NB, dtype=jnp.int32)[None, :]).astype(jnp.float32)
    bias_full = (
        jnp.dot(bucket_hot, bias_table, precision=HIGH).reshape(L, L, HEADS).transpose(2, 0, 1)
    )
    mask_rows = pad_mask.reshape(seq_count, L)
    ids_flat = token_ids.reshape(-1)
    tokens = ids_flat.shape[0]

    gathered_packed, gathered_down, heard, slot, embedded = run_head(
        ids_flat, hard_negative, attn_in, attn_out, ffn_in, proj_head, ffn_out, table, 1
    )
    packed = gathered_packed.reshape(-1, PACKED)
    down = gathered_down.reshape(-1, D)
    asked = heard[:, 0, :CAP]
    negatives = heard[:, 1, :pairs_here].reshape(-1).astype(jnp.int32)
    any_spilled = jnp.max(heard[:, 2, 0]) > 0.5
    embedded = once(
        any_spilled,
        lambda rows: dense_rows(
            ids_flat, table + jnp.minimum(jnp.abs(rows[0, 0]), 0.0), row_base
        ),
        embedded,
    )

    mask_col = mask_rows.astype(jnp.float32).reshape(tokens, 1)
    mixed, attended, totals, after, pre, final, pooled, projected = run_forward(
        embedded, mask_col, gain_rows, bias_full, packed, down
    )
    tall, wide = dp_count // (fsdp_count // 2), fsdp_count // 2
    owner = negatives // pairs_here
    owner = (owner % 2 * tall + owner // (2 * wide * wide)) * wide * wide + owner // 2 % (wide * wide) % wide + (
        owner // (2 * wide) % wide * wide
    )
    target = owner * seq_count + pairs_here + negatives % pairs_here
    target = jnp.concatenate(
        [target.reshape(total, pairs_here), jnp.full((total, pairs_here), -1, jnp.int32)], 1
    )
    target = target.reshape(tall * wide * wide, 2, seq_count).transpose(1, 0, 2).reshape(-1, 1)
    grad_proj, loss_parts = run_loss(projected, target, log_scale.reshape(1, 1), 3)
    loss_sum, grad_log_scale = loss_parts[0, 0], loss_parts[1, 0]
    grad_after, grad_gains, grad_up, grad_down = run_ffn_back(
        final, after, mask_col, gain_rows, pooled, grad_proj, pre, packed, down
    )
    grad_low, grad_gain, grad_bias, grad_attn, up_shard, down_shard, squares = run_attn_back(
        embedded, mask_col, mixed, attended, totals, grad_after, gain_rows, bias_full, packed, grad_up, grad_down, 4
    )
    grad_gains = jnp.concatenate([grad_gain, grad_gains[1:]], 0)
    grad_bias_table = jnp.dot(grad_bias.reshape(HEADS, L * L), bucket_hot, precision=HIGH).T
    small_local = jnp.concatenate([grad_gains.reshape(-1), grad_bias_table.reshape(-1)])
    width = -(-small_local.shape[0] // 1024) * 8
    small_local = jnp.pad(small_local, (0, width * 128 - small_local.shape[0]))
    (attn_shard,), table_grad, summed, squares = finish(
        [grad_attn.reshape(total, -1, WIDE + D)],
        grad_low,
        slot,
        asked.reshape(dp_count, fsdp_count, CAP).transpose(1, 0, 2).reshape(fsdp_count, -1),
        small_local.reshape(width, 128),
        squares,
        vocab_rows,
        5,
    )
    table_grad, squares = once(
        any_spilled,
        lambda state: with_squares(dense_table_grad(ids_flat, grad_low, vocab_rows, row_base), state[1]),
        (table_grad, squares),
    )
    norm, *updated = run_update(
        fsdp_count,
        squares,
        summed,
        grad_log_scale.reshape(1, 1),
        (table, table_first, table_second),
        table_grad,
        (
            *(attn_in, attn_in_first, attn_in_second),
            *(attn_out, attn_out_first, attn_out_second),
            *(ffn_in, ffn_in_first, ffn_in_second),
            *(ffn_out, ffn_out_first, ffn_out_second),
            *(proj_head, proj_head_first, proj_head_second),
        ),
        (attn_shard, up_shard, down_shard),
    )
    norm_value = norm[0, 0]
    factor = jnp.minimum(1.0, CLIP / (norm_value + 1e-06))
    small_size = small_params.shape[0]
    small_grad = jnp.concatenate([summed.reshape(-1)[: small_size - 1], grad_log_scale[None]])
    small_new = adam_update(
        small_params, small_first, small_second, small_grad, factor, RATES[6], DECAYS[6]
    )
    return (loss_sum, norm_value, *updated, *small_new)


def with_squares(table_grad, squares):
    wide = table_grad.astype(jnp.float32)
    total = lax.psum(jnp.sum(wide * wide), ("dp", "fsdp"))
    return (table_grad, squares.at[8:].set(0.0).at[8, 0].set(total))


def solution(mesh):
    program = fast_body if fits(mesh) else plain_body
    return jax.shard_map(
        program,
        mesh=mesh,
        in_specs=(
            P(None, ("dp", "fsdp"), None),
            P(None, ("dp", "fsdp"), None),
            P(("dp", "fsdp")),
            P("dp", None),
            P("dp", None),
            P("dp", None),
            P(("dp", "fsdp"), None),
            P(("dp", "fsdp"), None),
            P(("dp", "fsdp"), None),
            P(("dp", "fsdp"), None),
            P(("dp", "fsdp"), None),
            P(("dp", "fsdp"), None),
            P(("dp", "fsdp"), None),
            P(("dp", "fsdp"), None),
            P(("dp", "fsdp"), None),
            P(("dp", "fsdp"), None),
            P(("dp", "fsdp"), None),
            P(("dp", "fsdp"), None),
            P(("dp", "fsdp"), None),
            P(("dp", "fsdp"), None),
            P(("dp", "fsdp"), None),
            P(),
            P(),
            P(),
        ),
        out_specs=(
            P(),
            P(),
            P("dp", None),
            P("dp", None),
            P("dp", None),
            P(("dp", "fsdp"), None),
            P(("dp", "fsdp"), None),
            P(("dp", "fsdp"), None),
            P(("dp", "fsdp"), None),
            P(("dp", "fsdp"), None),
            P(("dp", "fsdp"), None),
            P(("dp", "fsdp"), None),
            P(("dp", "fsdp"), None),
            P(("dp", "fsdp"), None),
            P(("dp", "fsdp"), None),
            P(("dp", "fsdp"), None),
            P(("dp", "fsdp"), None),
            P(("dp", "fsdp"), None),
            P(("dp", "fsdp"), None),
            P(("dp", "fsdp"), None),
            P(),
            P(),
            P(),
        ),
        check_vma=False,
    )
```
